32 devices in a mesh: row: 4 (over x, core), chan: 8 (over z, y).
Axes of the slice: x: 2, y: 2, z: 4, core: 2. Of those that a mesh axis runs over, the one named last changes fastest.
Arguments:
- tokens: bfloat16 [16384, 1024], P(('row', 'chan')), may hold values from -6 to 6
- starts: int32 [4, 4096], P('row'), may hold values 0 or 1
- layer_norm_gain: float32 [1024], replicated, may hold values from 0.5 to 1.5
- ln_bias: float32 [1024], replicated, may hold values from -3 to 3
- w_up: bfloat16 [1024, 3072], replicated, may hold values from -0.1875 to 0.1875
- w_val: bfloat16 [1024, 512], replicated, may hold values from -0.1875 to 0.1875
- w_mix: bfloat16 [512, 3072], replicated, may hold values from -0.25 to 0.25
- w_down: bfloat16 [3072, 1024], replicated, may hold values from -0.15625 to 0.15625
- decay_rate: float32 [512, 512], P('chan'), may hold values from 0.0002 to 0.05
- mix_coef: float32 [512, 512], P('chan'), may hold values from -0.006 to 0.006
- out_grad: bfloat16 [16384, 1024], P(('row', 'chan')), may hold values from -6 to 6
Outputs:
- block_out: bfloat16 [16384, 1024], P(('row', 'chan'))
- tokens_grad: float32 [16384, 1024], P(('row', 'chan'))
- gain_grad: float32 [1024], P(('row', 'chan'))
- bias_grad: float32 [1024], P(('row', 'chan'))
- up_grad: float32 [1024, 3072], P(('row', 'chan'))
- val_grad: float32 [1024, 512], P(('row', 'chan'))
- mix_grad: float32 [512, 3072], P(('row', 'chan'))
- down_grad: float32 [3072, 1024], P(('row', 'chan'))
- rate_grad: float32 [512, 512], P('chan', 'row')
- coef_grad: float32 [512, 512], P('chan', 'row')
The draws below stay inside these ranges and needn't reach their ends.
All inputs are finite; a program needn't handle non-finite values. No bound on the sum of `starts` on one device may be relied on, other than what follows from the above.
Results may differ from the reference program's by a relative error of at most 0.007.
Values may be sent and summed in bfloat16 or wider, within the bound.
No kernel may reach another device: no remote copies, remote signals or barrier semaphores. Data moves between devices by JAX's collectives and lax.ppermute only.
A program may use at most 320 MiB of HBM per device.

```python
import math
import jax
import jax.numpy as jnp
from jax import lax

D = 1024
FF = 3072
E = 512
N_STATE = 512
L = 4096
BLK = 256
SEQS = 4
TOKENS = 16384


def set_ends(array, rng, least, largest):
    longest = array.shape.index(max(array.shape))
    spots = []
    for shift in (0, 1):
        where = [jax.random.randint(jax.random.fold_in(rng, axis), (), 0, length) for axis, length in enumerate(array.shape)]
        where[longest] = (where[longest] + shift) % array.shape[longest]
        spots.append(tuple(where))
    return array.at[spots[0]].set(least).at[spots[1]].set(largest)


def steps_of(stream_key, dims, cuts, smallest, high):
    def one(axis_at, parts):
        heights = jax.random.uniform(jax.random.fold_in(jax.random.fold_in(stream_key, 6), axis_at), (parts,), jnp.float32, smallest / len(cuts), high / len(cuts))
        return jnp.repeat(jnp.exp(heights), dims[axis_at] // parts).reshape((-1,) + (1,) * (len(dims) - axis_at - 1))

    loudness = one(*cuts[0])
    for cut in cuts[1:]:
        loudness = loudness * one(*cut)
    return loudness


def bell_draw(key, dims, spread, limit, shards=(), held_as=jnp.bfloat16):
    values = spread * jax.random.normal(key, dims, jnp.float32)
    if shards:
        values = values * steps_of(key, dims, shards, -0.22, 0.18)
    return jnp.clip(values, -limit, limit).astype(held_as)


def setup_inputs(seed: int = 0) -> dict:
    key_list = jax.random.split(jax.random.key(seed), 12)
    tokens = bell_draw(key_list[0], (TOKENS, D), 1.0, 6.0, ((0, 32),))
    starts = set_ends((jax.random.randint(key_list[1], (SEQS, L), 0, L // 8) < 1).astype(jnp.int32), jax.random.fold_in(key_list[1], 1), 0, 1)
    layer_norm_gain = jnp.clip(1.0 + 0.1 * jax.random.normal(key_list[2], (D,), jnp.float32), 0.5, 1.5)
    ln_bias = bell_draw(key_list[3], (D,), 0.5, 3.0, (), jnp.float32)
    w_up = bell_draw(key_list[4], (D, FF), D ** -0.5, 0.1875)
    w_val = bell_draw(key_list[5], (D, E), D ** -0.5, 0.1875)
    w_mix = bell_draw(key_list[6], (E, FF), E ** -0.5, 0.25)
    w_down = bell_draw(key_list[7], (FF, D), (FF // 2) ** -0.5, 0.15625)
    decay_rate = jnp.clip(jnp.exp(math.log(0.05) - 5.521461 * jax.random.uniform(key_list[8], (E, N_STATE), jnp.float32) ** steps_of(key_list[8], (E, N_STATE), ((0, 8),), -0.2, 0.2)), 0.0002, 0.05)
    mix_coef = bell_draw(key_list[9], (E, N_STATE), 0.001, 0.006, ((0, 8),), jnp.float32)
    out_grad = bell_draw(key_list[10], (TOKENS, D), 1.0, 6.0, ((0, 32),))
    return dict(tokens=tokens, starts=starts, layer_norm_gain=layer_norm_gain, ln_bias=ln_bias, w_up=w_up, w_val=w_val, w_mix=w_mix, w_down=w_down, decay_rate=decay_rate, mix_coef=mix_coef, out_grad=out_grad)


@jax.custom_vjp
def low(v):
    return lax.optimization_barrier(v.astype(jnp.bfloat16)).astype(jnp.float32)

@jax.custom_vjp
def low_back(v):
    return v

def low_keep(v):
    return (low(v), None)

def low_pass(kept, grad):
    return (grad,)

def back_keep(v):
    return (v, None)

def back_low(kept, grad):
    return (low(grad),)
low.defvjp(low_keep, low_pass)
low_back.defvjp(back_keep, back_low)
epsilon = 1e-05
highest = lax.Precision.HIGHEST

def ssm_mix(values, decay_rate, mix_coef, starts):
    seq_count, length, channels = values.shape
    block_count = length // BLK
    segment = jnp.cumsum(starts, axis=1).astype(jnp.int32).reshape(seq_count, block_count, BLK)
    values = values.reshape(seq_count, block_count, BLK, channels)
    offsets = jnp.arange(BLK).astype(jnp.float32)
    powers = jnp.exp(-decay_rate[:, :, None] * offsets)
    kernel = jnp.einsum('cn,cnl->cl', mix_coef, powers, precision=highest)
    row_ids = lax.broadcasted_iota(jnp.int32, (BLK, BLK), 0)
    col_ids = lax.broadcasted_iota(jnp.int32, (BLK, BLK), 1)
    lag_ids = jnp.maximum(row_ids - col_ids, 0).astype(jnp.int32)
    causal = (row_ids >= col_ids).astype(jnp.float32)
    toeplitz = jnp.take(kernel, lag_ids, axis=1) * causal
    same_seg = (segment[:, :, :, None] == segment[:, :, None, :]).astype(jnp.float32)
    same_groups = same_seg.reshape(-1, 4, BLK, BLK)
    value_groups = values.reshape(-1, 4, BLK, channels)

    def in_block(pair_in):
        return jnp.einsum('ctu,gtu,guc->gtc', toeplitz, pair_in[0], pair_in[1], precision=highest)
    near_part = lax.map(jax.checkpoint(in_block), (same_groups, value_groups))
    near_part = near_part.reshape(seq_count, block_count, BLK, channels)
    last_seg = segment[:, :, BLK - 1]
    tail_mask = (segment == last_seg[:, :, None]).astype(jnp.float32)
    block_sums = jnp.einsum('cnu,sbu,sbuc->sbcn', powers[:, :, ::-1], tail_mask, values, precision=highest)
    keep_mask = jnp.concatenate([jnp.zeros((seq_count, 1), jnp.float32), (last_seg[:, 1:] == last_seg[:, :-1]).astype(jnp.float32)], axis=1)
    block_fade = jnp.exp(-decay_rate * BLK)

    def carry_step(carried, entry_couple):
        fresh = carried * block_fade * entry_couple[1][:, None, None] + entry_couple[0]
        return (fresh, carried)
    start_state = jnp.zeros((seq_count, channels, decay_rate.shape[1]), jnp.float32)
    _, prev_state = lax.scan(carry_step, start_state, (jnp.moveaxis(block_sums, 1, 0), keep_mask.T))
    prev_state = jnp.moveaxis(prev_state, 0, 1)
    prev_seg = jnp.concatenate([jnp.full((seq_count, 1), -1, jnp.int32), last_seg[:, :-1].astype(jnp.int32)], axis=1)
    head_mask = (segment == prev_seg[:, :, None]).astype(jnp.float32)
    out_decay = mix_coef[:, :, None] * jnp.exp(-decay_rate[:, :, None] * (offsets + 1.0))
    far_part = jnp.einsum('cnt,sbcn,sbt->sbtc', out_decay, prev_state, head_mask, precision=highest)
    return (near_part + far_part).reshape(seq_count, length, channels)

def gelu_exact(values):
    return jax.nn.gelu(values, approximate=False)

def forward(all_tokens, starts, layer_norm_gain, ln_bias, w_up, w_val, w_mix, w_down, decay_rate, mix_coef):
    groups = E // 64
    rate_groups = decay_rate.reshape(groups, 64, N_STATE)
    coef_groups = mix_coef.reshape(groups, 64, N_STATE)

    def per_sequence(pair_in):
        seq_tokens, seq_starts = pair_in
        row_mean = lax.optimization_barrier(jnp.mean(seq_tokens, axis=-1, keepdims=True))
        centred = seq_tokens - row_mean
        variance = lax.optimization_barrier(jnp.mean(centred * centred, axis=-1, keepdims=True))
        standardized_input = centred * lax.rsqrt(variance + epsilon)
        normed = low(standardized_input * layer_norm_gain + ln_bias)
        u_pre = low_back(jnp.dot(normed, w_up, precision=highest))
        v_pre = low_back(jnp.dot(normed, w_val, precision=highest))
        v_act = low_back(low(gelu_exact(v_pre)))
        value_groups = v_act.reshape(L, groups, 64).transpose(1, 0, 2)[:, None]

        def per_group(triple):
            return ssm_mix(triple[0], triple[1], triple[2], seq_starts[None])
        mixed_groups = lax.map(jax.checkpoint(per_group), (value_groups, rate_groups, coef_groups))
        ssm_y = mixed_groups[:, 0].transpose(1, 0, 2).reshape(L, E)
        y_round = low_back(low(ssm_y))
        y_proj = low_back(jnp.dot(y_round, w_mix, precision=highest))
        gate_out = low(gelu_exact(u_pre) * y_proj)
        return seq_tokens + jnp.dot(gate_out, w_down, precision=highest)
    return lax.map(jax.checkpoint(per_sequence), (all_tokens, starts))

def reference(tokens, starts, layer_norm_gain, ln_bias, w_up, w_val, w_mix, w_down, decay_rate, mix_coef, out_grad):
    all_tokens = tokens.astype(jnp.float32).reshape(SEQS, L, D)

    def as_function(seq_tokens, gain, bias, up_w, val_w, mix_w, down_w, rates, coefs):
        return forward(seq_tokens, starts, gain, bias, up_w, val_w, mix_w, down_w, rates, coefs)
    block_out, pullback = jax.vjp(as_function, all_tokens, layer_norm_gain.astype(jnp.float32), ln_bias.astype(jnp.float32), w_up.astype(jnp.float32), w_val.astype(jnp.float32), w_mix.astype(jnp.float32), w_down.astype(jnp.float32), decay_rate.astype(jnp.float32), mix_coef.astype(jnp.float32))
    gradients = pullback(out_grad.astype(jnp.float32).reshape(SEQS, L, D))
    return (block_out.reshape(TOKENS, D).astype(jnp.bfloat16), gradients[0].reshape(TOKENS, D), gradients[1], gradients[2], gradients[3], gradients[4], gradients[5], gradients[6], gradients[7], gradients[8])
```

```python
import jax
import jax.numpy as jnp
from jax import lax
from jax.experimental import pallas as pl
from jax.experimental.pallas import tpu as pltpu
from jax.sharding import PartitionSpec as P

T=128; G8=8; SEG=4
f32=jnp.float32; bf16=jnp.bfloat16
NT=(((1,),(1,)),((),())); TN=(((0,),(0,)),((),())); NN=(((1,),(0,)),((),()))
def mm(a,b,d=NN): return lax.dot_general(a,b,d,preferred_element_type=f32)
def iota(shape,d): return lax.broadcasted_iota(jnp.int32,shape,d)

def powers(rate_row, pt_ref, c):
    n=rate_row.shape[1]
    steps=iota((8,n),0).astype(f32)
    r8=jnp.broadcast_to(rate_row,(8,n))
    blk=jnp.exp(-r8*steps)
    fade=jnp.exp(-8.0*r8)
    rows=8
    parts=[blk]
    while rows<T:
        parts=parts+[p*fade for p in parts]
        fade=fade*fade
        rows*=2
    for i in range(0,len(parts),2):
        pt_ref[c,i*8:i*8+16,:]=jnp.concatenate(parts[i:i+2],0).astype(bf16)

def flip_matrix():
    return (iota((T,T),0)+iota((T,T),1)==T-1).astype(f32).astype(bf16)

def put(ref,c,val,R):
    for q in range(val.shape[1]//T): ref[q,pl.ds(c,R,stride=G8),:]=val[:,q*T:(q+1)*T]
def take(ref,c,R):
    return jnp.concatenate([ref[q,pl.ds(c,R,stride=G8),:] for q in range(ref.shape[0])],1)
def tiles(v): return jnp.stack([v[:,q*T:(q+1)*T] for q in range(v.shape[1]//T)])
def untile(v): return jnp.concatenate([v[q] for q in range(v.shape[0])],1)
def seg_masks(ins, g):
    return jnp.concatenate([(ins==g*SEG+k).astype(f32) for k in range(SEG)],0)

def rep(x): return jnp.concatenate([x]*SEG,0)
def fold(o,m,R):
    o=o*m
    out=o[0:R]
    for k in range(1,SEG): out=out+o[k*R:(k+1)*R]
    return out

def fwd_kernel(groups,keep,x,rate,coef,ins,insj,head,tailj,y,hs,toe,pt,ss,near):
    R=ins.shape[0]; n=rate.shape[1]
    J=flip_matrix()
    xf=x[...].reshape(G8*R,T)
    xj=mm(xf,J).astype(bf16)
    tail=tailj[...]
    ins0=ins[...]
    m0=seg_masks(ins0,0); m0b=m0.astype(bf16)
    cf=coef[...]; rt=rate[...]
    cfh=cf.astype(bf16); cfl=(cf-cfh.astype(f32)).astype(bf16)
    cf2=jnp.concatenate([cfh,cfl],0)
    tri=iota((T,T),1)>=iota((T,T),0)
    for c in range(G8):
        powers(rt[c:c+1],pt,c)
        p=pt[c]
        s=mm(xj[c*R:(c+1)*R]*tail,p)
        put(ss,c,s,R)
        k2=mm(cf2,p,NT)
        k=k2[c:c+1]+k2[G8+c:G8+c+1]
        kb=pltpu.roll(jnp.broadcast_to(k,(T,T)),0,1,stride=1,stride_axis=0)
        tp=jnp.where(tri,kb,0.0).astype(bf16)
        toe[c]=tp
        near[c]=fold(mm(rep(xf[c*R:(c+1)*R])*m0b,tp),m0,R)
    fade=tiles(jnp.exp(-float(T)*rt)); ce=tiles(cf*jnp.exp(-rt))
    h=jnp.zeros((n//T,G8,T),f32)
    for b in range(R):
        hs[0,:,b*G8:(b+1)*G8,:]=h
        s=ss[:,b*G8:(b+1)*G8,:]
        ss[:,b*G8:(b+1)*G8,:]=h*ce
        h=h*(fade*keep[b])+s
    @pl.loop(1,groups[0])
    def _(g):
        m=seg_masks(ins[...],g)
        for c in range(G8):
            near[c]+=fold(mm(rep(x[c])*m.astype(bf16),toe[c]),m,R)
    hd=head[...]
    for c in range(G8):
        a=take(ss,c,R).astype(bf16)
        far=mm(a,pt[c],NT)
        y[c]=(near[c]+hd*far).astype(bf16)

def bwd_kernel(groups,keep,x,dy,rate,coef,ins,insj,head,tailj,hs,toe,dv,drate,dcoef,pt,s1,e0,e1,near,gacc,nr):
    R=ins.shape[0]; n=rate.shape[1]
    J=flip_matrix()
    xj=mm(x[...].reshape(G8*R,T),J).astype(bf16)
    dyf=dy[...].reshape(G8*R,T)
    dyj=mm(dyf,J).astype(bf16)
    tail=tailj[...]; hdb=head[...].astype(bf16)
    mn=seg_masks(ins[...],0).astype(bf16); mj=seg_masks(insj[...],0); mjb=mj.astype(bf16)
    rt=rate[...]; cf=coef[...]
    lag=iota((R,T),1).astype(f32).astype(bf16)
    lag1=(iota((R,T),1)+1).astype(f32).astype(bf16)
    lagf=iota((1,T),1).astype(f32)
    valid=iota((T,T),0)+iota((T,T),1)>=T-1
    row16=iota((16,T),0)
    def lags(d,xx,md,mx):
        o=mm(rep(d)*md,rep(xx)*mx,TN)
        o=pltpu.roll(jnp.where(valid,o,0.0),1,1,stride=1,stride_axis=0)
        return jnp.sum(o,axis=0,keepdims=True)
    for c in range(G8):
        sl=slice(c*R,(c+1)*R)
        near[c]=fold(mm(rep(dyj[sl])*mjb,toe[c]),mj,R)
        gacc[c:c+1,:]=lags(dyf[sl],xj[sl],mn,mjb)
    @pl.loop(1,groups[0])
    def _(g):
        m=seg_masks(ins[...],g).astype(bf16); k=seg_masks(insj[...],g)
        kb=k.astype(bf16)
        for c in range(G8):
            d=dy[c]; xx=x[c]
            dj=mm(d,J).astype(bf16); xxj=mm(xx,J).astype(bf16)
            near[c]+=fold(mm(rep(dj)*kb,toe[c]),k,R)
            gacc[c:c+1,:]+=lags(d,xxj,m,kb)
    for c in range(G8):
        sl=slice(c*R,(c+1)*R)
        powers(rt[c:c+1],pt,c)
        gr=gacc[c:c+1,:]; gl=gr*lagf
        gh=gr.astype(bf16).astype(f32); glh=gl.astype(bf16).astype(f32)
        gm=jnp.where(row16==0,gh,jnp.where(row16==1,gr-gh,jnp.where(row16==2,glh,jnp.where(row16==3,gl-glh,0.0)))).astype(bf16)
        xt=xj[sl]*tail; dh=dyf[sl]*hdb
        o=mm(jnp.concatenate([xt*lag,dh,dh*lag1,gm],0),pt[c])
        put(s1,c,o[0:R],R)
        put(e0,c,o[R:2*R],R)
        put(e1,c,o[2*R:3*R],R)
        nr[c:c+1,:]=o[3*R:3*R+1]+o[3*R+1:3*R+2]
        nr[G8+c:G8+c+1,:]=o[3*R+2:3*R+3]+o[3*R+3:3*R+4]
    fade=tiles(jnp.exp(-float(T)*rt)); ee=tiles(jnp.exp(-rt)); ce=tiles(cf)*ee
    zero=jnp.zeros((n//T,G8,T),f32)
    dh,ac,ar,ae=zero,zero,zero,zero
    for b in range(R-1,-1,-1):
        w=slice(b*G8,(b+1)*G8)
        h=hs[0,:,w,:]; e=e0[:,w,:]; kf=fade*keep[b]
        ar=ar+dh*(kf*(float(T)*h)+s1[:,w,:])
        ae=ae+h*e1[:,w,:]
        ac=ac+h*e
        s1[:,w,:]=dh
        dh=ce*e+kf*dh
    dcoef[...]=nr[0:G8,:]+untile(ee*ac)
    drate[...]=-(cf*nr[G8:2*G8,:]+untile(ar+ce*ae))
    for c in range(G8):
        a=take(s1,c,R).astype(bf16)
        far=mm(a,pt[c],NT)
        near[c]=near[c]+tail.astype(f32)*far
    dvj=near[...].reshape(G8*R,T).astype(bf16)
    dv[...]=mm(dvj,J).astype(bf16).reshape(G8,R,T)

def ssm_masks(starts):
    S,L=starts.shape; B=L//T; R=S*B
    st=starts.reshape(R,T)
    tri=(iota((T,T),0)<=iota((T,T),1)).astype(bf16)
    cum=mm(st.astype(bf16),tri).astype(jnp.int32)
    ins=cum-st[:,:1]
    first=iota((R,1),0)%B==0
    cont=(st[:,:1]==0)&~first
    last=ins[:,-1:]
    head=((ins==0)&cont).astype(f32)
    rev=(iota((T,T),0)+iota((T,T),1)==T-1).astype(bf16)
    insj=mm(ins.astype(bf16),rev).astype(jnp.int32)
    tailj=(insj==last).astype(bf16)
    keep=(cont&(last==0)).astype(f32)[:,0]
    groups=(jnp.max(last)//SEG+1).reshape(1).astype(jnp.int32)
    return groups,keep,ins,insj,head,tailj

def ssm_fwd(x,rate,coef,masks):
    C,R,_=x.shape; n=rate.shape[1]
    groups,keep,ins,insj,head,tailj=masks
    sm=pl.BlockSpec(memory_space=pltpu.SMEM)
    full=pl.BlockSpec((R,T),lambda i:(0,0))
    ch=pl.BlockSpec((G8,R,T),lambda i:(i,0,0))
    par=pl.BlockSpec((G8,n),lambda i:(i,0))
    return pl.pallas_call(fwd_kernel,grid=(C//G8,),
        in_specs=[sm,sm,ch,par,par,full,full,full,full],
        out_specs=[ch,pl.BlockSpec((1,n//T,R*G8,T),lambda i:(i,0,0,0)),pl.BlockSpec((G8,T,T),lambda i:(i,0,0))],
        out_shape=[jax.ShapeDtypeStruct((C,R,T),bf16),jax.ShapeDtypeStruct((C//G8,n//T,R*G8,T),f32),jax.ShapeDtypeStruct((C,T,T),bf16)],
        scratch_shapes=[pltpu.VMEM((G8,T,n),bf16),pltpu.VMEM((n//T,R*G8,T),f32),pltpu.VMEM((G8,R,T),f32)],
        compiler_params=pltpu.CompilerParams(vmem_limit_bytes=40*2**20),
        name="ssm_fwd")(groups,keep,x,rate,coef,ins,insj,head,tailj)

def ssm_bwd(x,dy,rate,coef,masks,hs,toe):
    C,R,_=x.shape; n=rate.shape[1]
    groups,keep,ins,insj,head,tailj=masks
    sm=pl.BlockSpec(memory_space=pltpu.SMEM)
    full=pl.BlockSpec((R,T),lambda i:(0,0))
    ch=pl.BlockSpec((G8,R,T),lambda i:(i,0,0))
    par=pl.BlockSpec((G8,n),lambda i:(i,0))
    big=pltpu.VMEM((n//T,R*G8,T),f32)
    return pl.pallas_call(bwd_kernel,grid=(C//G8,),
        in_specs=[sm,sm,ch,ch,par,par,full,full,full,full,pl.BlockSpec((1,n//T,R*G8,T),lambda i:(i,0,0,0)),pl.BlockSpec((G8,T,T),lambda i:(i,0,0))],
        out_specs=[ch,par,par],
        out_shape=[jax.ShapeDtypeStruct((C,R,T),bf16),jax.ShapeDtypeStruct((C,n),f32),jax.ShapeDtypeStruct((C,n),f32)],
        scratch_shapes=[pltpu.VMEM((G8,T,n),bf16),big,big,big,pltpu.VMEM((G8,R,T),f32),pltpu.VMEM((G8,T),f32),pltpu.VMEM((2*G8,n),f32)],
        compiler_params=pltpu.CompilerParams(vmem_limit_bytes=40*2**20),
        name="ssm_bwd")(groups,keep,x,dy,rate,coef,ins,insj,head,tailj,hs,toe)


epsilon = 1e-05


def gauss_cdf(a):
    return 0.5 * (1.0 + lax.erf(a * 0.7071067811865476))


def gauss_pdf(a):
    return jnp.exp(-0.5 * a * a) * 0.3989422804014327


def make_on_device(row_n, chan_n):
    row_hi = row_n // 2

    def swap(value, axis, bit):
        size = row_n if axis == "row" else chan_n
        return lax.ppermute(value, axis, [(i, i ^ (1 << bit)) for i in range(size)])

    def core_swap(value):
        return swap(value, "row", 0)

    def bits_of(size):
        return size.bit_length() - 1

    def scatter_sum(part, names, order, last_dtype):
        names = list(names)
        for step, name in enumerate(order):
            axis, bit = name
            dim = names.index(name)
            mine = (lax.axis_index(axis) >> bit) & 1
            keep = lax.dynamic_index_in_dim(part, mine, dim, keepdims=False)
            give = lax.dynamic_index_in_dim(part, 1 - mine, dim, keepdims=False)
            got = swap(give, axis, bit)
            part = keep.astype(jnp.float32) + got.astype(jnp.float32)
            if step < len(order) - 1:
                part = part.astype(give.dtype)
            else:
                part = part.astype(last_dtype)
            names.pop(dim)
        return part

    row_bits = [("row", k) for k in range(bits_of(row_n) - 1, 0, -1)]
    core_bit = ("row", 0)
    chan_bits = [("chan", k) for k in range(bits_of(chan_n) - 1, -1, -1)]
    near_y = chan_bits[2:]
    along_z = chan_bits[:2][::-1]

    def on_device(
        tokens,
        starts,
        layer_norm_gain,
        ln_bias,
        w_up,
        w_val,
        w_mix,
        w_down,
        decay_rate,
        mix_coef,
        out_grad,
    ):
        own, width = tokens.shape
        ff = w_up.shape[1]
        inner = w_val.shape[1]
        part_ff = ff // row_n
        core = lax.axis_index("row") % 2
        mm = lambda a, b, ca, cb: lax.dot_general(
            a, b, (((ca,), (cb,)), ((), ())), preferred_element_type=jnp.float32
        )
        masks = ssm_masks(starts)
        inputs_f = tokens.astype(jnp.float32)
        row_mean = jnp.mean(inputs_f, axis=1, keepdims=True)
        centred = inputs_f - row_mean
        inv_std = lax.rsqrt(jnp.mean(centred * centred, axis=1, keepdims=True) + epsilon)
        x_hat = centred * inv_std
        normed = (x_hat * layer_norm_gain + ln_bias).astype(jnp.bfloat16)
        v_pre = mm(w_val, normed, 0, 1)
        v_cdf = gauss_cdf(v_pre)
        v_act = (v_pre * v_cdf).astype(jnp.bfloat16)
        v_slope = v_cdf + v_pre * gauss_pdf(v_pre)
        v_chan = lax.all_to_all(
            v_act.reshape(inner, own // T, T), "chan", split_axis=0, concat_axis=1, tiled=True
        )
        pair_normed = jnp.concatenate([normed, core_swap(normed)], 0)
        pair_grad = jnp.concatenate([out_grad, core_swap(out_grad)], 0)
        halves = lambda w, d: lax.dynamic_index_in_dim(
            w.reshape(w.shape[:d] + (row_hi, 2, part_ff) + w.shape[d + 1 :]), core, d + 1, keepdims=False
        ).reshape(w.shape[:d] + (ff // 2,) + w.shape[d + 1 :])
        up_half = halves(w_up, 1)
        mix_half = halves(w_mix, 1)
        down_half = halves(w_down, 0)
        u_pre = mm(pair_normed, up_half, 1, 0)
        d_gate = mm(pair_grad, down_half, 1, 1)
        u_cdf = gauss_cdf(u_pre)
        u_act = u_pre * u_cdf
        d_yproj = (d_gate * u_act).astype(jnp.bfloat16)
        d_slope = d_gate * (u_cdf + u_pre * gauss_pdf(u_pre))
        d_y_part = mm(mix_half, d_yproj, 1, 1)
        d_y = (
            d_y_part[:, :own] + core_swap(d_y_part[:, own:].astype(jnp.bfloat16)).astype(jnp.float32)
        ).astype(jnp.bfloat16)
        d_y_chan = lax.all_to_all(
            d_y.reshape(inner, own // T, T), "chan", split_axis=0, concat_axis=1, tiled=True
        )
        y_chan, states, toeplitz = ssm_fwd(v_chan, decay_rate, mix_coef, masks)
        y_own = lax.all_to_all(y_chan, "chan", split_axis=1, concat_axis=0, tiled=True)
        y_own = y_own.reshape(inner, own)
        d_v_chan, d_rate, d_coef = ssm_bwd(
            v_chan, d_y_chan, decay_rate, mix_coef, masks, states, toeplitz
        )
        d_v = lax.all_to_all(d_v_chan, "chan", split_axis=1, concat_axis=0, tiled=True)
        pair_y = jnp.concatenate([y_own, core_swap(y_own)], 1)
        split_rows = lambda a, lead: a.reshape((2,) * lead + (-1,) + a.shape[1:])
        y_proj = mm(pair_y, mix_half, 0, 0)
        gate_out = (u_act * y_proj).astype(jnp.bfloat16)
        d_upre = (d_slope * y_proj).astype(jnp.bfloat16)
        mix_part = mm(pair_y, d_yproj, 1, 0).astype(jnp.bfloat16)
        down_part = mm(gate_out, pair_grad, 0, 0).astype(jnp.bfloat16)
        up_part = mm(pair_normed, d_upre, 0, 0).astype(jnp.bfloat16)
        all_names = row_bits + [core_bit] + chan_bits
        no_core = row_bits + chan_bits
        lead = len(all_names)
        mix_sum = scatter_sum(
            split_rows(mix_part, lead), all_names, along_z + row_bits + near_y, jnp.float32
        )
        up_sum = scatter_sum(
            split_rows(up_part, lead), all_names, row_bits + near_y + along_z, jnp.float32
        )
        down_grad = scatter_sum(
            split_rows(down_part, lead - 1), no_core, near_y + row_bits + along_z, jnp.float32
        )

        def join_cores(halfsum):
            mine = lax.dynamic_index_in_dim(halfsum, core, 0, keepdims=False)
            other = core_swap(lax.dynamic_index_in_dim(halfsum, 1 - core, 0, keepdims=False))
            shape = (mine.shape[0], row_hi, part_ff)
            low = jnp.where(core == 0, mine, other).reshape(shape)
            high = jnp.where(core == 0, other, mine).reshape(shape)
            return jnp.stack([low, high], 2).reshape(mine.shape[0], ff)

        block_part = mm(gate_out, down_half, 1, 0)
        block_out = (
            inputs_f
            + block_part[:own]
            + core_swap(block_part[own:].astype(jnp.bfloat16)).astype(jnp.float32)
        ).astype(jnp.bfloat16)
        d_normed_part = mm(d_upre, up_half, 1, 1)
        d_normed_got = core_swap(d_normed_part[own:].astype(jnp.bfloat16)).astype(jnp.float32)
        d_vpre = (d_v.reshape(inner, own).astype(jnp.float32) * v_slope).astype(jnp.bfloat16)
        val_part = mm(normed, d_vpre, 0, 1).astype(jnp.bfloat16)
        val_grad = scatter_sum(
            split_rows(val_part, lead),
            all_names,
            [core_bit] + along_z + near_y + row_bits,
            jnp.float32,
        )
        d_normed = d_normed_part[:own] + d_normed_got + mm(d_vpre, w_val, 0, 1)
        norm_part = jnp.stack([jnp.sum(d_normed * x_hat, axis=0), jnp.sum(d_normed, axis=0)], 1)
        norm_sum = scatter_sum(
            split_rows(norm_part, lead), all_names, [core_bit] + row_bits + chan_bits, jnp.float32
        )
        d_xh = d_normed * layer_norm_gain
        tokens_grad = out_grad.astype(jnp.float32) + inv_std * (
            d_xh
            - jnp.mean(d_xh, axis=1, keepdims=True)
            - x_hat * jnp.mean(d_xh * x_hat, axis=1, keepdims=True)
        )
        row_all = row_bits + [core_bit]
        states_n = decay_rate.shape[1]
        rates = jnp.stack([d_rate, d_coef]).reshape(
            (2 * d_rate.shape[0],) + (2,) * len(row_all) + (states_n // row_n,)
        )
        rates = jnp.moveaxis(rates, 0, len(row_all))
        rates = scatter_sum(rates, row_all, [core_bit] + row_bits, jnp.float32)
        rates = rates.reshape(2, d_rate.shape[0], states_n // row_n)
        return (
            block_out,
            tokens_grad,
            norm_sum[:, 0],
            norm_sum[:, 1],
            join_cores(up_sum),
            val_grad,
            join_cores(mix_sum),
            down_grad,
            rates[0],
            rates[1],
        )

    return on_device


def solution(mesh):
    spread = P(("row", "chan"), None)
    return jax.shard_map(
        make_on_device(mesh.shape["row"], mesh.shape["chan"]),
        mesh=mesh,
        in_specs=(
            spread,
            P("row", None),
            P(),
            P(),
            P(),
            P(),
            P(),
            P(),
            P("chan", None),
            P("chan", None),
            spread,
        ),
        out_specs=(
            spread,
            spread,
            P(("row", "chan")),
            P(("row", "chan")),
            spread,
            spread,
            spread,
            spread,
            P("chan", "row"),
            P("chan", "row"),
        ),
        check_vma=False,
    )
```

```python
import jax
import jax.numpy as jnp
from jax import lax
from jax.experimental import pallas as pl
from jax.experimental.pallas import tpu as pltpu
from jax.sharding import PartitionSpec as P

T=128; G8=8; SEG=4
f32=jnp.float32; bf16=jnp.bfloat16
NT=(((1,),(1,)),((),())); TN=(((0,),(0,)),((),())); NN=(((1,),(0,)),((),()))
def mm(a,b,d=NN): return lax.dot_general(a,b,d,preferred_element_type=f32)
def iota(shape,d): return lax.broadcasted_iota(jnp.int32,shape,d)

def powers(rate_row, pt_ref, c):
    n=rate_row.shape[1]
    steps=iota((8,n),0).astype(f32)
    r8=jnp.broadcast_to(rate_row,(8,n))
    blk=jnp.exp(-r8*steps)
    fade=jnp.exp(-8.0*r8)
    rows=8
    parts=[blk]
    while rows<T:
        parts=parts+[p*fade for p in parts]
        fade=fade*fade
        rows*=2
    for i in range(0,len(parts),2):
        pt_ref[c,i*8:i*8+16,:]=jnp.concatenate(parts[i:i+2],0).astype(bf16)

def flip_matrix():
    return (iota((T,T),0)+iota((T,T),1)==T-1).astype(f32).astype(bf16)

def put(ref,c,val,R):
    for q in range(val.shape[1]//T): ref[q,pl.ds(c,R,stride=G8),:]=val[:,q*T:(q+1)*T]
def take(ref,c,R):
    return jnp.concatenate([ref[q,pl.ds(c,R,stride=G8),:] for q in range(ref.shape[0])],1)
def tiles(v): return jnp.stack([v[:,q*T:(q+1)*T] for q in range(v.shape[1]//T)])
def untile(v): return jnp.concatenate([v[q] for q in range(v.shape[0])],1)
def seg_masks(ins, g):
    return jnp.concatenate([(ins==g*SEG+k).astype(f32) for k in range(SEG)],0)

def rep(x): return jnp.concatenate([x]*SEG,0)
def fold(o,m,R):
    o=o*m
    out=o[0:R]
    for k in range(1,SEG): out=out+o[k*R:(k+1)*R]
    return out

def fwd_kernel(groups,keep,x,rate,coef,ins,insj,head,tailj,y,hs,toe,pt,ss,near):
    R=ins.shape[0]; n=rate.shape[1]
    J=flip_matrix()
    xf=x[...].reshape(G8*R,T)
    xj=mm(xf,J).astype(bf16)
    tail=tailj[...]
    ins0=ins[...]
    m0=seg_masks(ins0,0); m0b=m0.astype(bf16)
    cf=coef[...]; rt=rate[...]
    cfh=cf.astype(bf16); cfl=(cf-cfh.astype(f32)).astype(bf16)
    cf2=jnp.concatenate([cfh,cfl],0)
    tri=iota((T,T),1)>=iota((T,T),0)
    for c in range(G8):
        powers(rt[c:c+1],pt,c)
        p=pt[c]
        s=mm(xj[c*R:(c+1)*R]*tail,p)
        put(ss,c,s,R)
        k2=mm(cf2,p,NT)
        k=k2[c:c+1]+k2[G8+c:G8+c+1]
        kb=pltpu.roll(jnp.broadcast_to(k,(T,T)),0,1,stride=1,stride_axis=0)
        tp=jnp.where(tri,kb,0.0).astype(bf16)
        toe[c]=tp
        near[c]=fold(mm(rep(xf[c*R:(c+1)*R])*m0b,tp),m0,R)
    fade=tiles(jnp.exp(-float(T)*rt)); ce=tiles(cf*jnp.exp(-rt))
    h=jnp.zeros((n//T,G8,T),f32)
    for b in range(R):
        hs[0,:,b*G8:(b+1)*G8,:]=h
        s=ss[:,b*G8:(b+1)*G8,:]
        ss[:,b*G8:(b+1)*G8,:]=h*ce
        h=h*(fade*keep[b])+s
    @pl.loop(1,groups[0])
    def _(g):
        m=seg_masks(ins[...],g)
        for c in range(G8):
            near[c]+=fold(mm(rep(x[c])*m.astype(bf16),toe[c]),m,R)
    hd=head[...]
    for c in range(G8):
        a=take(ss,c,R).astype(bf16)
        far=mm(a,pt[c],NT)
        y[c]=(near[c]+hd*far).astype(bf16)

def bwd_kernel(groups,keep,x,dy,rate,coef,ins,insj,head,tailj,hs,toe,dv,drate,dcoef,pt,s1,e0,e1,near,gacc,nr):
    R=ins.shape[0]; n=rate.shape[1]
    J=flip_matrix()
    xj=mm(x[...].reshape(G8*R,T),J).astype(bf16)
    dyf=dy[...].reshape(G8*R,T)
    dyj=mm(dyf,J).astype(bf16)
    tail=tailj[...]; hdb=head[...].astype(bf16)
    mn=seg_masks(ins[...],0).astype(bf16); mj=seg_masks(insj[...],0); mjb=mj.astype(bf16)
    rt=rate[...]; cf=coef[...]
    lag=iota((R,T),1).astype(f32).astype(bf16)
    lag1=(iota((R,T),1)+1).astype(f32).astype(bf16)
    lagf=iota((1,T),1).astype(f32)
    valid=iota((T,T),0)+iota((T,T),1)>=T-1
    row16=iota((16,T),0)
    def lags(d,xx,md,mx):
        o=mm(rep(d)*md,rep(xx)*mx,TN)
        o=pltpu.roll(jnp.where(valid,o,0.0),1,1,stride=1,stride_axis=0)
        return jnp.sum(o,axis=0,keepdims=True)
    for c in range(G8):
        sl=slice(c*R,(c+1)*R)
        near[c]=fold(mm(rep(dyj[sl])*mjb,toe[c]),mj,R)
        gacc[c:c+1,:]=lags(dyf[sl],xj[sl],mn,mjb)
    @pl.loop(1,groups[0])
    def _(g):
        m=seg_masks(ins[...],g).astype(bf16); k=seg_masks(insj[...],g)
        kb=k.astype(bf16)
        for c in range(G8):
            d=dy[c]; xx=x[c]
            dj=mm(d,J).astype(bf16); xxj=mm(xx,J).astype(bf16)
            near[c]+=fold(mm(rep(dj)*kb,toe[c]),k,R)
            gacc[c:c+1,:]+=lags(d,xxj,m,kb)
    for c in range(G8):
        sl=slice(c*R,(c+1)*R)
        powers(rt[c:c+1],pt,c)
        gr=gacc[c:c+1,:]; gl=gr*lagf
        gh=gr.astype(bf16).astype(f32); glh=gl.astype(bf16).astype(f32)
        gm=jnp.where(row16==0,gh,jnp.where(row16==1,gr-gh,jnp.where(row16==2,glh,jnp.where(row16==3,gl-glh,0.0)))).astype(bf16)
        xt=xj[sl]*tail; dh=dyf[sl]*hdb
        o=mm(jnp.concatenate([xt*lag,dh,dh*lag1,gm],0),pt[c])
        put(s1,c,o[0:R],R)
        put(e0,c,o[R:2*R],R)
        put(e1,c,o[2*R:3*R],R)
        nr[c:c+1,:]=o[3*R:3*R+1]+o[3*R+1:3*R+2]
        nr[G8+c:G8+c+1,:]=o[3*R+2:3*R+3]+o[3*R+3:3*R+4]
    fade=tiles(jnp.exp(-float(T)*rt)); ee=tiles(jnp.exp(-rt)); ce=tiles(cf)*ee
    zero=jnp.zeros((n//T,G8,T),f32)
    dh,ac,ar,ae=zero,zero,zero,zero
    for b in range(R-1,-1,-1):
        w=slice(b*G8,(b+1)*G8)
        h=hs[0,:,w,:]; e=e0[:,w,:]; kf=fade*keep[b]
        ar=ar+dh*(kf*(float(T)*h)+s1[:,w,:])
        ae=ae+h*e1[:,w,:]
        ac=ac+h*e
        s1[:,w,:]=dh
        dh=ce*e+kf*dh
    dcoef[...]=nr[0:G8,:]+untile(ee*ac)
    drate[...]=-(cf*nr[G8:2*G8,:]+untile(ar+ce*ae))
    for c in range(G8):
        a=take(s1,c,R).astype(bf16)
        far=mm(a,pt[c],NT)
        near[c]=near[c]+tail.astype(f32)*far
    dvj=near[...].reshape(G8*R,T).astype(bf16)
    dv[...]=mm(dvj,J).astype(bf16).reshape(G8,R,T)

def ssm_masks(starts):
    S,L=starts.shape; B=L//T; R=S*B
    st=starts.reshape(R,T)
    tri=(iota((T,T),0)<=iota((T,T),1)).astype(bf16)
    cum=mm(st.astype(bf16),tri).astype(jnp.int32)
    ins=cum-st[:,:1]
    first=iota((R,1),0)%B==0
    cont=(st[:,:1]==0)&~first
    last=ins[:,-1:]
    head=((ins==0)&cont).astype(f32)
    rev=(iota((T,T),0)+iota((T,T),1)==T-1).astype(bf16)
    insj=mm(ins.astype(bf16),rev).astype(jnp.int32)
    tailj=(insj==last).astype(bf16)
    keep=(cont&(last==0)).astype(f32)[:,0]
    groups=(jnp.max(last)//SEG+1).reshape(1).astype(jnp.int32)
    return groups,keep,ins,insj,head,tailj

def ssm_fwd(x,rate,coef,masks):
    C,R,_=x.shape; n=rate.shape[1]
    groups,keep,ins,insj,head,tailj=masks
    sm=pl.BlockSpec(memory_space=pltpu.SMEM)
    full=pl.BlockSpec((R,T),lambda i:(0,0))
    ch=pl.BlockSpec((G8,R,T),lambda i:(i,0,0))
    par=pl.BlockSpec((G8,n),lambda i:(i,0))
    return pl.pallas_call(fwd_kernel,grid=(C//G8,),
        in_specs=[sm,sm,ch,par,par,full,full,full,full],
        out_specs=[ch,pl.BlockSpec((1,n//T,R*G8,T),lambda i:(i,0,0,0)),pl.BlockSpec((G8,T,T),lambda i:(i,0,0))],
        out_shape=[jax.ShapeDtypeStruct((C,R,T),bf16),jax.ShapeDtypeStruct((C//G8,n//T,R*G8,T),f32),jax.ShapeDtypeStruct((C,T,T),bf16)],
        scratch_shapes=[pltpu.VMEM((G8,T,n),bf16),pltpu.VMEM((n//T,R*G8,T),f32),pltpu.VMEM((G8,R,T),f32)],
        compiler_params=pltpu.CompilerParams(vmem_limit_bytes=40*2**20),
        name="ssm_fwd")(groups,keep,x,rate,coef,ins,insj,head,tailj)

def ssm_bwd(x,dy,rate,coef,masks,hs,toe):
    C,R,_=x.shape; n=rate.shape[1]
    groups,keep,ins,insj,head,tailj=masks
    sm=pl.BlockSpec(memory_space=pltpu.SMEM)
    full=pl.BlockSpec((R,T),lambda i:(0,0))
    ch=pl.BlockSpec((G8,R,T),lambda i:(i,0,0))
    par=pl.BlockSpec((G8,n),lambda i:(i,0))
    big=pltpu.VMEM((n//T,R*G8,T),f32)
    return pl.pallas_call(bwd_kernel,grid=(C//G8,),
        in_specs=[sm,sm,ch,ch,par,par,full,full,full,full,pl.BlockSpec((1,n//T,R*G8,T),lambda i:(i,0,0,0)),pl.BlockSpec((G8,T,T),lambda i:(i,0,0))],
        out_specs=[ch,par,par],
        out_shape=[jax.ShapeDtypeStruct((C,R,T),bf16),jax.ShapeDtypeStruct((C,n),f32),jax.ShapeDtypeStruct((C,n),f32)],
        scratch_shapes=[pltpu.VMEM((G8,T,n),bf16),big,big,big,pltpu.VMEM((G8,R,T),f32),pltpu.VMEM((G8,T),f32),pltpu.VMEM((2*G8,n),f32)],
        compiler_params=pltpu.CompilerParams(vmem_limit_bytes=40*2**20),
        name="ssm_bwd")(groups,keep,x,dy,rate,coef,ins,insj,head,tailj,hs,toe)


epsilon = 1e-05


def gauss_cdf(a):
    return 0.5 * (1.0 + lax.erf(a * 0.7071067811865476))


def gauss_pdf(a):
    return jnp.exp(-0.5 * a * a) * 0.3989422804014327


def make_on_device(row_n, chan_n):
    row_hi = row_n // 2

    def swap(value, axis, bit):
        size = row_n if axis == "row" else chan_n
        return lax.ppermute(value, axis, [(i, i ^ (1 << bit)) for i in range(size)])

    def core_swap(value):
        return swap(value, "row", 0)

    def bits_of(size):
        return size.bit_length() - 1

    row_bits = [("row", k) for k in range(bits_of(row_n) - 1, 0, -1)]
    core_bit = ("row", 0)
    chan_bits = [("chan", k) for k in range(bits_of(chan_n) - 1, -1, -1)]
    y_bits = chan_bits[2:]
    z_bits = chan_bits[:2][::-1]
    if len(row_bits) == len(y_bits):
        crossed = list(zip(row_bits + y_bits, y_bits + row_bits))
    else:
        crossed = [(b, b) for b in row_bits + y_bits]
    straight = lambda bits: [(b, b) for b in bits]

    def partner(pair):
        moves = []
        for row in range(row_n):
            for chan in range(chan_n):
                axis, bit = pair[row % 2]
                to_row = row ^ (1 << bit) if axis == "row" else row
                to_chan = chan ^ (1 << bit) if axis == "chan" else chan
                moves.append((row * chan_n + chan, to_row * chan_n + to_chan))
        return moves

    class Reduction:
        def __init__(self, part, names, order, core):
            self.part = part.reshape((2,) * len(names) + (-1,) + part.shape[1:])
            self.names = (list(names), list(names))
            self.order = list(order)
            self.core = core

        def half(self, other):
            pair = self.order[0]

            def of(core_id):
                axis, bit = pair[core_id]
                mine = (lax.axis_index(axis) >> bit) & 1
                dim = self.names[core_id].index((axis, bit))
                return lax.dynamic_index_in_dim(
                    self.part, 1 - mine if other else mine, dim, keepdims=False
                )

            if pair[0] == pair[1]:
                return of(0)
            return jnp.where(self.core == 0, of(0), of(1))

        def give(self):
            return self.half(True)

        def send(self, give):
            return lax.ppermute(give, ("row", "chan"), partner(self.order[0]))

        def take(self, got):
            total = self.half(False).astype(jnp.float32) + got.astype(jnp.float32)
            pair = self.order.pop(0)
            for core_id in (0, 1):
                self.names[core_id].remove(pair[core_id])
            self.part = total.astype(got.dtype) if self.order else total

    def on_device(
        tokens,
        starts,
        layer_norm_gain,
        ln_bias,
        w_up,
        w_val,
        w_mix,
        w_down,
        decay_rate,
        mix_coef,
        out_grad,
    ):
        own, width = tokens.shape
        ff = w_up.shape[1]
        inner = w_val.shape[1]
        part_ff = ff // row_n
        core = lax.axis_index("row") % 2
        mm = lambda a, b, ca, cb: lax.dot_general(
            a, b, (((ca,), (cb,)), ((), ())), preferred_element_type=jnp.float32
        )
        masks = ssm_masks(starts)
        inputs_f = tokens.astype(jnp.float32)
        row_mean = jnp.mean(inputs_f, axis=1, keepdims=True)
        centred = inputs_f - row_mean
        inv_std = lax.rsqrt(jnp.mean(centred * centred, axis=1, keepdims=True) + epsilon)
        x_hat = centred * inv_std
        normed = (x_hat * layer_norm_gain + ln_bias).astype(jnp.bfloat16)
        v_pre = mm(w_val, normed, 0, 1)
        v_cdf = gauss_cdf(v_pre)
        v_act = (v_pre * v_cdf).astype(jnp.bfloat16)
        v_slope = v_cdf + v_pre * gauss_pdf(v_pre)
        v_chan = lax.all_to_all(
            v_act.reshape(inner, own // T, T), "chan", split_axis=0, concat_axis=1, tiled=True
        )
        pair_normed = jnp.concatenate([normed, core_swap(normed)], 0)
        pair_grad = jnp.concatenate([out_grad, core_swap(out_grad)], 0)
        halves = lambda w, d: jnp.concatenate(
            [
                lax.dynamic_slice_in_dim(w, (2 * k + core) * part_ff, part_ff, d)
                for k in range(row_hi)
            ],
            d,
        )
        up_half = halves(w_up, 1)
        mix_half = halves(w_mix, 1)
        down_half = halves(w_down, 0)
        u_pre = mm(pair_normed, up_half, 1, 0)
        d_gate = mm(pair_grad, down_half, 1, 1)
        u_cdf = gauss_cdf(u_pre)
        u_act = u_pre * u_cdf
        d_yproj = (d_gate * u_act).astype(jnp.bfloat16)
        d_slope = d_gate * (u_cdf + u_pre * gauss_pdf(u_pre))
        d_y_part = mm(mix_half, d_yproj, 1, 1)
        d_y = (
            d_y_part[:, :own] + core_swap(d_y_part[:, own:].astype(jnp.bfloat16)).astype(jnp.float32)
        ).astype(jnp.bfloat16)
        d_y_chan = lax.all_to_all(
            d_y.reshape(inner, own // T, T), "chan", split_axis=0, concat_axis=1, tiled=True
        )
        v_chan, d_y_chan = lax.optimization_barrier((v_chan, d_y_chan))
        y_chan, states, toeplitz = ssm_fwd(v_chan, decay_rate, mix_coef, masks)
        y_own = lax.all_to_all(y_chan, "chan", split_axis=1, concat_axis=0, tiled=True)
        y_own = y_own.reshape(inner, own)
        d_v_chan, d_rate, d_coef = ssm_bwd(
            v_chan, d_y_chan, decay_rate, mix_coef, masks, states, toeplitz
        )
        d_v = lax.all_to_all(d_v_chan, "chan", split_axis=1, concat_axis=0, tiled=True)
        pair_y = jnp.concatenate([y_own, core_swap(y_own)], 1)
        after = lax.optimization_barrier
        all_names = row_bits + [core_bit] + chan_bits
        no_core = row_bits + chan_bits
        low = lambda a: a.astype(jnp.bfloat16)
        wide = lambda a: a.astype(jnp.float32)
        mix = Reduction(low(mm(pair_y, d_yproj, 1, 0)), all_names, straight(z_bits) + crossed, core)
        mix_give, pair_y = after((mix.give(), pair_y))
        y_proj = mm(pair_y, mix_half, 0, 0)
        gate_out = low(u_act * y_proj)
        d_upre = low(d_slope * y_proj)
        up = Reduction(
            low(mm(pair_normed, d_upre, 0, 0)), all_names, crossed + straight(z_bits), core
        )
        up_give, gate_out, d_upre = after((up.give(), gate_out, d_upre))

        up_got = up.send(up_give)
        mix_got = mix.send(mix_give)
        down = Reduction(
            low(mm(gate_out, pair_grad, 0, 0)), no_core, crossed + straight(z_bits), core
        )
        down_give = down.give()
        block_part = mm(gate_out, down_half, 1, 0)
        block_give = low(block_part[own:])
        up_got, mix_got, down_give, block_give, d_upre, d_v, d_rate, d_coef = after(
            (up_got, mix_got, down_give, block_give, d_upre, d_v, d_rate, d_coef)
        )

        mix.take(mix_got)
        mix_give = mix.give()
        down_got = down.send(down_give)
        mix_got = mix.send(mix_give)
        block_got = core_swap(block_give)
        up.take(up_got)
        up_give = up.give()
        d_vpre = low(d_v.reshape(inner, own).astype(jnp.float32) * v_slope)
        d_normed_part = mm(d_upre, up_half, 1, 1)
        d_normed_give = low(d_normed_part[own:])
        val = Reduction(
            low(mm(normed, d_vpre, 0, 1)),
            all_names,
            straight([core_bit] + z_bits) + crossed,
            core,
        )
        val_give = val.give()
        row_all = row_bits + [core_bit]
        states_n = decay_rate.shape[1]
        rates = jnp.concatenate([d_rate, d_coef], 0)
        rates = jnp.stack(jnp.split(rates, row_n, 1)).reshape(-1, states_n // row_n)
        rates = Reduction(rates, row_all, straight([core_bit] + row_bits), core)
        rates_give = rates.give()
        down_got, mix_got, up_give, val_give, d_normed_give, block_got, d_vpre, rates_give = after(
            (down_got, mix_got, up_give, val_give, d_normed_give, block_got, d_vpre, rates_give)
        )

        up_got = up.send(up_give)
        val_got = val.send(val_give)
        d_normed_got = core_swap(d_normed_give)
        rates_got = rates.send(rates_give)
        down.take(down_got)
        down_give = down.give()
        mix.take(mix_got)
        mix_give = mix.give()
        block_out = low(inputs_f + block_part[:own] + wide(block_got))
        val_normed = mm(d_vpre, w_val, 0, 1)
        up_got, val_got, rates_got, d_normed_got, down_give, mix_give, val_normed = after(
            (up_got, val_got, rates_got, d_normed_got, down_give, mix_give, val_normed)
        )

        up.take(up_got)
        val.take(val_got)
        up_give, val_give = up.give(), val.give()
        down_got = down.send(down_give)
        up_got = up.send(up_give)
        val_got = val.send(val_give)
        rates.take(rates_got)
        rates_give = rates.give()
        d_normed = d_normed_part[:own] + wide(d_normed_got) + val_normed
        norm_part = jnp.stack([jnp.sum(d_normed * x_hat, axis=0), jnp.sum(d_normed, axis=0)])
        norm_part = jnp.swapaxes(norm_part.reshape(2, row_n * chan_n, -1), 0, 1)
        d_xh = d_normed * layer_norm_gain
        tokens_grad = out_grad.astype(jnp.float32) + inv_std * (
            d_xh
            - jnp.mean(d_xh, axis=1, keepdims=True)
            - x_hat * jnp.mean(d_xh * x_hat, axis=1, keepdims=True)
        )
        up_got, val_got, down_got, rates_give, norm_part = after(
            (up_got, val_got, down_got, rates_give, norm_part)
        )

        up.take(up_got)
        down.take(down_got)
        val.take(val_got)
        up_got = up.send(up.give())
        down_got = down.send(down.give())
        val_got = val.send(val.give())
        mix_got = mix.send(mix_give)
        rates_got = rates.send(rates_give)
        norm_all = lax.all_to_all(norm_part, ("row", "chan"), split_axis=0, concat_axis=0, tiled=True)
        up_got, down_got, val_got, mix_got, rates_got = after(
            (up_got, down_got, val_got, mix_got, rates_got)
        )

        up.take(up_got)
        down.take(down_got)
        val.take(val_got)
        mix.take(mix_got)
        rates.take(rates_got)
        while down.order or val.order or mix.order or rates.order or up.order:
            for r in (down, up, val, mix, rates):
                if r.order:
                    r.take(r.send(r.give()))

        def join_cores(halfsum):
            mine = lax.dynamic_index_in_dim(halfsum, core, 0, keepdims=False)
            other = core_swap(lax.dynamic_index_in_dim(halfsum, 1 - core, 0, keepdims=False))
            shape = (mine.shape[0], row_hi, part_ff)
            first = jnp.where(core == 0, mine, other).reshape(shape)
            second = jnp.where(core == 0, other, mine).reshape(shape)
            return jnp.stack([first, second], 2).reshape(mine.shape[0], ff)

        norm_sum = jnp.sum(norm_all, axis=0)
        rate_sum = rates.part.reshape(2, d_rate.shape[0], states_n // row_n)
        return (
            block_out,
            tokens_grad,
            norm_sum[0],
            norm_sum[1],
            join_cores(up.part),
            val.part,
            join_cores(mix.part),
            down.part,
            rate_sum[0],
            rate_sum[1],
        )

    return on_device


def solution(mesh):
    spread = P(("row", "chan"), None)
    return jax.shard_map(
        make_on_device(mesh.shape["row"], mesh.shape["chan"]),
        mesh=mesh,
        in_specs=(
            spread,
            P("row", None),
            P(),
            P(),
            P(),
            P(),
            P(),
            P(),
            P("chan", None),
            P("chan", None),
            spread,
        ),
        out_specs=(
            spread,
            spread,
            P(("row", "chan")),
            P(("row", "chan")),
            spread,
            spread,
            spread,
            spread,
            P("chan", "row"),
            P("chan", "row"),
        ),
        check_vma=False,
    )
```

```python
import jax
import jax.numpy as jnp
from jax import lax
from jax.experimental import pallas as pl
from jax.experimental.pallas import tpu as pltpu
from jax.sharding import PartitionSpec as P

T = 128
SUB = 8
GROUP = 16
SEG = 4
f32 = jnp.float32
bf16 = jnp.bfloat16
NT = (((1,), (1,)), ((), ()))
TN = (((0,), (0,)), ((), ()))
NN = (((1,), (0,)), ((), ()))


def mm(a, b, d=NN):
    return lax.dot_general(a, b, d, preferred_element_type=f32)


def iota(shape, d):
    return lax.broadcasted_iota(jnp.int32, shape, d)


def powers(rate_row, pt_ref, c):
    n = rate_row.shape[1]
    steps = iota((8, n), 0).astype(f32)
    r8 = jnp.broadcast_to(rate_row, (8, n))
    parts = [jnp.exp(-r8 * steps)]
    fade = jnp.exp(-8.0 * r8)
    while len(parts) < T // 8:
        parts = parts + [p * fade for p in parts]
        fade = fade * fade
    for i in range(0, len(parts), 2):
        pt_ref[c, i * 8 : i * 8 + 16, :] = jnp.concatenate(parts[i : i + 2], 0).astype(bf16)


def put(ref, c, val, rows):
    for q in range(val.shape[1] // T):
        ref[q, pl.ds(c, rows, stride=SUB), :] = val[:, q * T : (q + 1) * T]


def take(ref, c, rows):
    return jnp.concatenate(
        [ref[q, pl.ds(c, rows, stride=SUB), :] for q in range(ref.shape[0])], 1
    )


def tiles(v):
    return jnp.stack([v[:, q * T : (q + 1) * T] for q in range(v.shape[1] // T)])


def untile(v):
    return jnp.concatenate([v[q] for q in range(v.shape[0])], 1)


def flip_matrix():
    return (iota((T, T), 0) + iota((T, T), 1) == T - 1).astype(f32).astype(bf16)


def seg_masks(ins, g):
    return jnp.concatenate([(ins == g * SEG + k).astype(f32) for k in range(SEG)], 0)


def rep(x):
    return jnp.concatenate([x] * SEG, 0)


def fold(o, m, rows):
    o = o * m
    out = o[0:rows]
    for k in range(1, SEG):
        out = out + o[k * rows : (k + 1) * rows]
    return out


def far_part(a, p, rows):
    hi = a.astype(bf16)
    lo = (a - hi.astype(f32)).astype(bf16)
    o = mm(jnp.concatenate([hi, lo], 0), p, NT)
    return o[:rows] + o[rows:]


def lanes_of(ref, c, rows):
    return ref[pl.ds(c, rows, stride=GROUP), :]


def fwd_kernel(groups, keep, x, rate, coef, ins, insj, head, tailj, y, hs, toe, pt, ss, near, xs, kr):
    rows = ins.shape[0]
    n = rate.shape[1]
    flip = flip_matrix()
    xs[...] = x[...].astype(f32).reshape(rows * GROUP, T)
    tail = tailj[...]
    hd = head[...]
    m0 = seg_masks(ins[...], 0)
    m0b = m0.astype(bf16)
    tri = iota((T, T), 1) >= iota((T, T), 0)
    for sub in range(GROUP // SUB):
        lo = sub * SUB
        cf = coef[lo : lo + SUB, :]
        rt = rate[lo : lo + SUB, :]
        cfh = cf.astype(bf16)
        cfl = (cf - cfh.astype(f32)).astype(bf16)
        cf2 = jnp.concatenate([cfh, cfl], 0)
        xj = []
        for c in range(SUB):
            xc = lanes_of(xs, lo + c, rows).astype(bf16)
            xj.append(mm(xc, flip).astype(bf16) * tail)
        for c in range(SUB):
            powers(rt[c : c + 1], pt, c)
            p = pt[c]
            put(ss, c, mm(xj[c], p), rows)
            k2 = mm(cf2, p, NT)
            kr[c : c + 1, :] = k2[c : c + 1] + k2[SUB + c : SUB + c + 1]
        for c in range(SUB):
            k = jnp.broadcast_to(kr[c : c + 1, :], (T, T))
            kb = pltpu.roll(k, 0, 1, stride=1, stride_axis=0)
            tp = jnp.where(tri, kb, 0.0).astype(bf16)
            toe[lo + c] = tp
            xc = lanes_of(xs, lo + c, rows).astype(bf16)
            near[c] = fold(mm(rep(xc) * m0b, tp), m0, rows)
        fade = tiles(jnp.exp(-float(T) * rt))
        ce = tiles(cf * jnp.exp(-rt))
        h = jnp.zeros((n // T, SUB, T), f32)
        for b in range(rows):
            w = slice(b * SUB, (b + 1) * SUB)
            hs[sub, :, w, :] = h
            s = ss[:, w, :]
            ss[:, w, :] = h * ce
            h = h * (fade * keep[b]) + s

        @pl.loop(1, groups[0])
        def _(g):
            m = seg_masks(ins[...], g)
            for c in range(SUB):
                xc = lanes_of(xs, lo + c, rows).astype(bf16)
                near[c] += fold(mm(rep(xc) * m.astype(bf16), toe[lo + c]), m, rows)

        for c in range(SUB):
            far = far_part(take(ss, c, rows), pt[c], rows)
            xs[pl.ds(lo + c, rows, stride=GROUP), :] = near[c] + hd * far
    y[...] = xs[...].reshape(rows, GROUP, T).astype(bf16)


def bwd_kernel(
    groups, keep, x, dy, rate, coef, ins, insj, head, tailj, hs, toe,
    dv, drate, dcoef, pt, s1, e0, e1, near, gacc, nr, xs, ys,
):
    rows = ins.shape[0]
    n = rate.shape[1]
    flip = flip_matrix()
    xs[...] = x[...].astype(f32).reshape(rows * GROUP, T)
    ys[...] = dy[...].astype(f32).reshape(rows * GROUP, T)
    tail = tailj[...]
    hdb = head[...].astype(bf16)
    mn = seg_masks(ins[...], 0).astype(bf16)
    mj = seg_masks(insj[...], 0)
    mjb = mj.astype(bf16)
    lag = iota((rows, T), 1).astype(f32).astype(bf16)
    lag1 = (iota((rows, T), 1) + 1).astype(f32).astype(bf16)
    lagf = iota((1, T), 1).astype(f32)
    valid = iota((T, T), 0) + iota((T, T), 1) >= T - 1
    row16 = iota((16, T), 0)

    def lags(d, xx, md, mx):
        o = mm(rep(d) * md, rep(xx) * mx, TN)
        o = pltpu.roll(jnp.where(valid, o, 0.0), 1, 1, stride=1, stride_axis=0)
        return jnp.sum(o, axis=0, keepdims=True)

    for sub in range(GROUP // SUB):
        lo = sub * SUB
        rt = rate[lo : lo + SUB, :]
        cf = coef[lo : lo + SUB, :]
        xa = jnp.concatenate([lanes_of(xs, lo + c, rows) for c in range(SUB)], 0).astype(bf16)
        da = jnp.concatenate([lanes_of(ys, lo + c, rows) for c in range(SUB)], 0).astype(bf16)
        xja = mm(xa, flip).astype(bf16)
        dja = mm(da, flip).astype(bf16)
        for c in range(SUB):
            sl = slice(c * rows, (c + 1) * rows)
            near[c] = fold(mm(rep(dja[sl]) * mjb, toe[lo + c]), mj, rows)
            gacc[c : c + 1, :] = lags(da[sl], xja[sl], mn, mjb)

        @pl.loop(1, groups[0])
        def _(g):
            m = seg_masks(ins[...], g).astype(bf16)
            k = seg_masks(insj[...], g)
            kb = k.astype(bf16)
            for c in range(SUB):
                d = lanes_of(ys, lo + c, rows).astype(bf16)
                xx = lanes_of(xs, lo + c, rows).astype(bf16)
                dj = mm(d, flip).astype(bf16)
                xj = mm(xx, flip).astype(bf16)
                near[c] += fold(mm(rep(dj) * kb, toe[lo + c]), k, rows)
                gacc[c : c + 1, :] += lags(d, xj, m, kb)

        for c in range(SUB):
            sl = slice(c * rows, (c + 1) * rows)
            powers(rt[c : c + 1], pt, c)
            gr = gacc[c : c + 1, :]
            gl = gr * lagf
            gh = gr.astype(bf16).astype(f32)
            glh = gl.astype(bf16).astype(f32)
            gm = jnp.where(row16 == 2, glh, jnp.where(row16 == 3, gl - glh, 0.0))
            gm = jnp.where(row16 == 0, gh, jnp.where(row16 == 1, gr - gh, gm)).astype(bf16)
            dh = da[sl] * hdb
            o = mm(jnp.concatenate([xja[sl] * tail * lag, dh, dh * lag1, gm], 0), pt[c])
            put(s1, c, o[0:rows], rows)
            put(e0, c, o[rows : 2 * rows], rows)
            put(e1, c, o[2 * rows : 3 * rows], rows)
            k = 3 * rows
            nr[c : c + 1, :] = o[k : k + 1] + o[k + 1 : k + 2]
            nr[SUB + c : SUB + c + 1, :] = o[k + 2 : k + 3] + o[k + 3 : k + 4]
        fade = tiles(jnp.exp(-float(T) * rt))
        ee = tiles(jnp.exp(-rt))
        ce = tiles(cf) * ee
        zero = jnp.zeros((n // T, SUB, T), f32)
        dh, ac, ar, ae = zero, zero, zero, zero
        for b in range(rows - 1, -1, -1):
            w = slice(b * SUB, (b + 1) * SUB)
            h = hs[sub, :, w, :]
            e = e0[:, w, :]
            kf = fade * keep[b]
            ar = ar + dh * (kf * (float(T) * h) + s1[:, w, :])
            ae = ae + h * e1[:, w, :]
            ac = ac + h * e
            s1[:, w, :] = dh
            dh = ce * e + kf * dh
        for c in range(SUB):
            far = far_part(take(s1, c, rows), pt[c], rows)
            near[c] = near[c] + tail.astype(f32) * far
        dva = mm(near[...].reshape(SUB * rows, T).astype(bf16), flip)
        for c in range(SUB):
            xs[pl.ds(lo + c, rows, stride=GROUP), :] = dva[c * rows : (c + 1) * rows]
        dcoef[lo : lo + SUB, :] = nr[0:SUB, :] + untile(ee * ac)
        drate[lo : lo + SUB, :] = -(cf * nr[SUB : 2 * SUB, :] + untile(ar + ce * ae))
    dv[...] = xs[...].reshape(rows, GROUP, T).astype(bf16)


def ssm_masks(starts):
    seqs, length = starts.shape
    blocks = length // T
    rows = seqs * blocks
    st = starts.reshape(rows, T)
    tri = (iota((T, T), 0) <= iota((T, T), 1)).astype(bf16)
    ins = mm(st.astype(bf16), tri).astype(jnp.int32) - st[:, :1]
    cont = (st[:, :1] == 0) & (iota((rows, 1), 0) % blocks != 0)
    last = ins[:, -1:]
    head = ((ins == 0) & cont).astype(f32)
    back = (iota((T, T), 0) + iota((T, T), 1) == T - 1).astype(bf16)
    insj = mm(ins.astype(bf16), back).astype(jnp.int32)
    tailj = (insj == last).astype(bf16)
    keep = (cont & (last == 0)).astype(f32)[:, 0]
    groups = (jnp.max(last) // SEG + 1).reshape(1).astype(jnp.int32)
    return groups, keep, ins, insj, head, tailj


def ssm_specs(rows, n):
    full = pl.BlockSpec((rows, T), lambda i: (0, 0))
    return dict(
        sm=pl.BlockSpec(memory_space=pltpu.SMEM),
        full=full,
        ch=pl.BlockSpec((rows, GROUP, T), lambda i: (0, i, 0)),
        par=pl.BlockSpec((GROUP, n), lambda i: (i, 0)),
        hs=pl.BlockSpec((GROUP // SUB, n // T, rows * SUB, T), lambda i: (i, 0, 0, 0)),
        toe=pl.BlockSpec((GROUP, T, T), lambda i: (i, 0, 0)),
        big=pltpu.VMEM((n // T, rows * SUB, T), f32),
        pt=pltpu.VMEM((SUB, T, n), bf16),
        near=pltpu.VMEM((SUB, rows, T), f32),
        xs=pltpu.VMEM((rows * GROUP, T), f32),
        cost=pl.CostEstimate(flops=2 * 10**10, bytes_accessed=10**7, transcendentals=0),
    )


def ssm_fwd(x, rate, coef, masks):
    rows, chans, _ = x.shape
    n = rate.shape[1]
    s = ssm_specs(rows, n)
    return pl.pallas_call(
        fwd_kernel,
        grid=(chans // GROUP,),
        in_specs=[s["sm"], s["sm"], s["ch"], s["par"], s["par"]] + [s["full"]] * 4,
        out_specs=[s["ch"], s["hs"], s["toe"]],
        out_shape=[
            pltpu.HBM(x.shape, bf16),
            pltpu.HBM((chans // SUB, n // T, rows * SUB, T), f32),
            pltpu.HBM((chans, T, T), bf16),
        ],
        scratch_shapes=[s["pt"], s["big"], s["near"], s["xs"], pltpu.VMEM((SUB, T), f32)],
        compiler_params=pltpu.CompilerParams(vmem_limit_bytes=40 * 2**20),
        cost_estimate=s["cost"],
        name="ssm_fwd",
    )(masks[0], masks[1], x, rate, coef, *masks[2:])


def ssm_bwd(x, dy, rate, coef, masks, hs, toe):
    rows, chans, _ = x.shape
    n = rate.shape[1]
    s = ssm_specs(rows, n)
    return pl.pallas_call(
        bwd_kernel,
        grid=(chans // GROUP,),
        in_specs=[s["sm"], s["sm"], s["ch"], s["ch"], s["par"], s["par"]]
        + [s["full"]] * 4
        + [s["hs"], s["toe"]],
        out_specs=[s["ch"], s["par"], s["par"]],
        out_shape=[
            pltpu.HBM(x.shape, bf16),
            pltpu.HBM((chans, n), f32),
            pltpu.HBM((chans, n), f32),
        ],
        scratch_shapes=[
            s["pt"],
            s["big"],
            s["big"],
            s["big"],
            s["near"],
            pltpu.VMEM((SUB, T), f32),
            pltpu.VMEM((2 * SUB, n), f32),
            s["xs"],
            s["xs"],
        ],
        compiler_params=pltpu.CompilerParams(vmem_limit_bytes=40 * 2**20),
        cost_estimate=s["cost"],
        name="ssm_bwd",
    )(masks[0], masks[1], x, dy, rate, coef, *masks[2:], *from_hbm(hs, toe))


epsilon = 1e-05
TILE = 768


def gauss_cdf(a):
    return 0.5 * (1.0 + lax.erf(a * 0.7071067811865476))


def gauss_pdf(a):
    return jnp.exp(-0.5 * a * a) * 0.3989422804014327


def struct(shape, dtype):
    return jax.ShapeDtypeStruct(shape, dtype)


def in_hbm(shape, dtype):
    return pltpu.HBM(shape, dtype)


def from_hbm(*arrays):
    return tuple(pltpu.with_memory_space_constraint(a, pltpu.HBM) for a in arrays)


def whole(shape):
    return pl.BlockSpec(shape, lambda *_: (0,) * len(shape))


def call(kernel, name, grid, ins, outs, out_shape, args, scalars=None, scratch=(), aliases=None, vmem=24, cost=None):
    lead = [] if scalars is None else [scalars]
    return pl.pallas_call(
        kernel,
        grid_spec=pltpu.PrefetchScalarGridSpec(
            num_scalar_prefetch=len(lead),
            grid=grid,
            in_specs=ins,
            out_specs=outs,
            scratch_shapes=list(scratch),
        ),
        out_shape=out_shape,
        input_output_aliases=aliases or {},
        compiler_params=pltpu.CompilerParams(vmem_limit_bytes=vmem * 2**20),
        cost_estimate=cost and pl.CostEstimate(flops=cost, bytes_accessed=10**7, transcendentals=0),
        name=name,
    )(*lead, *args)


def normalise(x):
    centred = x - jnp.mean(x, axis=1, keepdims=True)
    inv_std = lax.rsqrt(jnp.mean(centred * centred, axis=1, keepdims=True) + epsilon)
    return centred * inv_std, inv_std


def norm_kernel(tok, gain, bias, w_val, normed, v_act, v_slope):
    x_hat, _ = normalise(tok[...].astype(f32))
    n = (x_hat * gain[...] + bias[...]).astype(bf16)
    normed[...] = n
    v = mm(n, w_val[...])
    cdf = gauss_cdf(v)
    v_act[...] = (v * cdf).T.astype(bf16).reshape(v_act.shape)
    v_slope[...] = (cdf + v * gauss_pdf(v)).T.reshape(v_slope.shape)


def norm_call(tokens, gain, bias, w_val, chan_n):
    own, width = tokens.shape
    inner = w_val.shape[1]
    quads = own // T
    spread = (chan_n, quads, inner // chan_n, T)
    block = pl.BlockSpec((chan_n, 1, inner // chan_n, T), lambda i: (0, i, 0, 0))
    rows = pl.BlockSpec((T, width), lambda i: (i, 0))
    return call(
        norm_kernel,
        "norm_val",
        (quads,),
        [rows, whole((1, width)), whole((1, width)), whole(w_val.shape)],
        [rows, block, block],
        [struct((own, width), bf16), struct(spread, bf16), struct(spread, f32)],
        from_hbm(tokens, gain[None], bias[None], w_val),
    )


def gate_kernel(
    core, n_own, n_oth, g_own, g_oth, w_up, w_mix, w_down,
    u_act, d_slope, d_yproj, normed_t, dy_own, dy_oth, ga, na, acc,
):
    j = pl.program_id(0)
    own = n_own.shape[0]

    @pl.when(j == 0)
    def _():
        for h, (n, g) in enumerate(((n_own, g_own), (n_oth, g_oth))):
            na[h * own : (h + 1) * own, :] = n[...]
            ga[h * own : (h + 1) * own, :] = g[...]
            normed_t[:, h * own : (h + 1) * own] = n[...].T

    u = mm(na[...], w_up[...])
    d = mm(ga[...], w_down[...], NT)
    cdf = gauss_cdf(u)
    act = u * cdf
    u_act[...] = act.astype(bf16)
    d_slope[...] = (d * (cdf + u * gauss_pdf(u))).astype(bf16)
    dyp = (d * act).astype(bf16)
    d_yproj[...] = dyp
    part = mm(dyp, w_mix[...], NT)

    @pl.when(j == 0)
    def _():
        acc[...] = part

    @pl.when(j > 0)
    def _():
        acc[...] += part

    @pl.when(j == pl.num_programs(0) - 1)
    def _():
        shape = (dy_own.shape[0], dy_own.shape[2], T)
        for q in range(dy_own.shape[1]):
            dy_own[:, q] = acc[q * T : (q + 1) * T, :].T.reshape(shape)
            dy_oth[:, q] = acc[own + q * T : own + (q + 1) * T, :].T.astype(bf16).reshape(shape)


def gate_call(core, normed, normed_oth, grad, grad_oth, w_up, w_mix, w_down, row_n, chan_n):
    own, width = normed.shape
    inner, ff = w_mix.shape
    per = ff // row_n // TILE
    half = ff // 2
    col = lambda j, s: (2 * (j // per) + s[0]) * per + j % per
    tok = whole((own, width))
    tile = pl.BlockSpec((2 * own, TILE), lambda j, s: (0, j))
    spread = (chan_n, own // T, inner // chan_n, T)
    return call(
        gate_kernel,
        "gate",
        (half // TILE,),
        [
            tok,
            tok,
            tok,
            tok,
            pl.BlockSpec((width, TILE), lambda j, s: (0, col(j, s))),
            pl.BlockSpec((inner, TILE), lambda j, s: (0, col(j, s))),
            pl.BlockSpec((TILE, width), lambda j, s: (col(j, s), 0)),
        ],
        [tile, tile, tile, whole((width, 2 * own)), whole(spread), whole(spread), whole((2 * own, width))],
        [in_hbm((2 * own, half), bf16)] * 3
        + [in_hbm((width, 2 * own), bf16), in_hbm(spread, f32), in_hbm(spread, bf16)]
        + [in_hbm((2 * own, width), bf16)],
        (normed, normed_oth, grad, grad_oth, w_up, w_mix, w_down),
        scalars=core,
        scratch=[
            pltpu.VMEM((2 * own, width), bf16),
            pltpu.VMEM((2 * own, inner), f32),
        ],
        vmem=56,
    )


def mine_a(s):
    return jnp.where(s[0] == 0, s[1], s[2])


def mine_b(s):
    return jnp.where(s[0] == 0, s[2], s[1])


def row_block(s, a, b, core, high, low):
    x = jnp.where(s[0] == 0, a, b)
    y = jnp.where(s[0] == 0, b, a)
    return x * 16 + core * 8 + high * 4 + low * 2 + y


def mid_kernel(
    s, y_own, y_oth, w_mix, u_act, d_slope, d_yproj, normed_t,
    gate, d_upre, u_give, u_keep, m_give, m_keep, yt, yn, us, ms,
):
    inner = yt.shape[0]

    own = yn.shape[0] // 2

    @pl.when(pl.program_id(0) == 0)
    def _():
        for h, y in enumerate((y_own, y_oth)):
            for q in range(y.shape[1]):
                part = y[:, q].reshape(inner, T)
                at = slice(h * own + q * T, h * own + (q + 1) * T)
                yt[:, at] = part
                yn[at, :] = part.T

    yp = mm(yn[...], w_mix[...])
    gate[...] = (u_act[...].astype(f32) * yp).astype(bf16)
    du = (d_slope[...].astype(f32) * yp).astype(bf16)
    d_upre[...] = du
    us[...] = mm(normed_t[...], du).astype(bf16)
    ms[...] = mm(yt[...], d_yproj[...]).astype(bf16)
    m = u_give.shape[1]
    for sel, out in ((1, u_give), (0, u_keep)):
        a = mine_a(s) ^ sel
        for b in (0, 1):
            for low in (0, 1):
                for high in (0, 1):
                    for core in (0, 1):
                        at = pl.multiple_of(row_block(s, a, b, core, high, low) * m, m)
                        out[b * 8 + low * 4 + high * 2 + core] = us[pl.ds(at, m), :]
    m = m_give.shape[1]
    for sel, out in ((1, m_give), (0, m_keep)):
        low = s[3] ^ sel
        for high in (0, 1):
            for a in (0, 1):
                for b in (0, 1):
                    for core in (0, 1):
                        at = pl.multiple_of(row_block(s, a, b, core, high, low) * m, m)
                        out[high * 8 + a * 4 + b * 2 + core] = ms[pl.ds(at, m), :]


def mid_call(scal, y_own, y_oth, w_mix, u_act, d_slope, d_yproj, normed_t, row_n):
    inner, ff = w_mix.shape
    half = u_act.shape[1]
    own = u_act.shape[0] // 2
    width = normed_t.shape[0]
    per = ff // row_n // TILE
    col = lambda j, s: (2 * (j // per) + s[0]) * per + j % per
    tile = pl.BlockSpec((2 * own, TILE), lambda j, s: (0, j))
    um, mx = width // 32, inner // 32
    ub = pl.BlockSpec((16, um, TILE), lambda j, s: (0, 0, j))
    mb = pl.BlockSpec((16, mx, TILE), lambda j, s: (0, 0, j))
    return call(
        mid_kernel,
        "mix_up",
        (half // TILE,),
        [
            whole(y_own.shape),
            whole(y_own.shape),
            pl.BlockSpec((inner, TILE), lambda j, s: (0, col(j, s))),
            tile,
            tile,
            tile,
            whole(normed_t.shape),
        ],
        [tile, tile, ub, ub, mb, mb],
        [in_hbm((2 * own, half), bf16)] * 2
        + [in_hbm((16, um, half), bf16)] * 2
        + [in_hbm((16, mx, half), bf16)] * 2,
        (y_own, y_oth, w_mix, u_act, d_slope, d_yproj, normed_t),
        scalars=scal,
        scratch=[
            pltpu.VMEM((inner, 2 * own), bf16),
            pltpu.VMEM((2 * own, inner), bf16),
            pltpu.VMEM((width, TILE), bf16),
            pltpu.VMEM((inner, TILE), bf16),
        ],
        vmem=56,
        cost=10**10,
    )


def block_kernel(s, gate, d_upre, w_down, w_up, block_own, dn_own, oth, acc):
    j = pl.program_id(0)
    own = block_own.shape[0]
    sums = (mm(gate[...], w_down[...]), mm(d_upre[...], w_up[...], NT))

    @pl.when(j == 0)
    def _():
        for k in (0, 1):
            acc[k] = sums[k]

    @pl.when(j > 0)
    def _():
        for k in (0, 1):
            acc[k] += sums[k]

    @pl.when(j == pl.num_programs(0) - 1)
    def _():
        block_own[...] = acc[0, :own]
        dn_own[...] = acc[1, :own]
        oth[...] = acc[:, own:].astype(bf16)


def block_call(scal, gate, d_upre, w_down, w_up, row_n):
    ff, width = w_down.shape
    own = gate.shape[0] // 2
    part = ff // row_n
    tile = pl.BlockSpec((2 * own, part), lambda j, s: (0, j))
    return call(
        block_kernel,
        "block",
        (row_n // 2,),
        [
            tile,
            tile,
            pl.BlockSpec((part, width), lambda j, s: (2 * j + s[0], 0)),
            pl.BlockSpec((width, part), lambda j, s: (0, 2 * j + s[0])),
        ],
        [whole((own, width)), whole((own, width)), whole((2, own, width))],
        [in_hbm((own, width), f32), in_hbm((own, width), f32), in_hbm((2, own, width), bf16)],
        (gate, d_upre, w_down, w_up),
        scalars=scal,
        scratch=[pltpu.VMEM((2, 2 * own, width), f32)],
        vmem=56,
    )


def down_val_kernel(s, down_g, down_k, v_own, v_oth, normed_t, d_give, d_keep, vs, vt):
    i = pl.program_id(0)
    inner, pair = vt.shape
    m = vs.shape[0] // 32
    rows = down_g.shape[0]

    @pl.when(i == 0)
    def _():
        for h, v in enumerate((v_own, v_oth)):
            for q in range(v.shape[1]):
                at = h * pair // 2 + q * T
                vt[:, at : at + T] = v[:, q].reshape(inner, T)
        vs[...] = mm(normed_t[...], vt[...], NT)

    b, low, high = i // 4, (i // 2) % 2, i % 2
    for sel, down, out in ((1, down_g, d_give), (0, down_k, d_keep)):
        out[0, 0:rows, :] = down[...]
        a = mine_a(s) ^ sel
        cut = []
        for core in (0, 1):
            at = pl.multiple_of(row_block(s, a, b, core, high, low) * m, m)
            cut.append(vs[pl.ds(at, m), :])
        parts = [jnp.concatenate([c[r * 8 : r * 8 + 8] for c in cut], 0) for r in range(m // 8)]
        out[0, rows : rows + 16, :] = jnp.concatenate(parts, 1).astype(bf16)


def down_val_call(scal, down, d_vpre, v_oth, normed_t):
    half = v_oth.shape
    inner = half[0] * half[2]
    width, pair = normed_t.shape
    rows = down.shape[0] // 16

    def block_of(sel):
        def at(i, s):
            a, b, low, high = mine_a(s) ^ sel, i // 4, (i // 2) % 2, i % 2
            x = jnp.where(s[0] == 0, a, b)
            y = jnp.where(s[0] == 0, b, a)
            return x * 8 + high * 4 + low * 2 + y, 0

        return pl.BlockSpec((rows, width), at)

    buf = (8, rows + 16, width)
    out = pl.BlockSpec((1, rows + 16, width), lambda i, s: (i, 0, 0))
    return call(
        down_val_kernel,
        "down_val",
        (8,),
        [
            block_of(1),
            block_of(0),
            pl.BlockSpec(half, lambda i, s: (s[0], 0, 0, 0)),
            whole(half),
            whole(normed_t.shape),
        ],
        [out, out],
        [struct(buf, bf16)] * 2,
        (down, down, d_vpre, v_oth, normed_t),
        scalars=scal,
        scratch=[pltpu.VMEM((width, inner), f32), pltpu.VMEM((inner, pair), bf16)],
    )


def step_kernel(bit, keep_g, got_g, keep_k, got_k, give, keep):
    give[...] = (keep_g[0].astype(f32) + got_g[0].astype(f32)).astype(bf16)
    keep[...] = (keep_k[0].astype(f32) + got_k[0].astype(f32)).astype(bf16)


def step_call(bit, keep, got):
    n, rows, cols = keep.shape
    n //= 2
    nb = max(1, n // 4)
    view = (2, n, rows, cols)
    other = pl.BlockSpec((1, nb, rows, cols), lambda i, b: (1 - b[0], i, 0, 0))
    same = pl.BlockSpec((1, nb, rows, cols), lambda i, b: (b[0], i, 0, 0))
    out = pl.BlockSpec((nb, rows, cols), lambda i, b: (i, 0, 0))
    keep, got = keep.reshape(view), got.reshape(view)
    return call(
        step_kernel,
        "halve",
        (n // nb,),
        [other, other, same, same],
        [out, out],
        [struct((n, rows, cols), bf16)] * 2,
        (keep, got, keep, got),
        scalars=bit,
    )


def tail_kernel(
    tok, grad, gain, block_own, got, dn_own, d_vpre, w_val, block_out, tokens_grad, norm_part, acc
):
    i = pl.program_id(0)
    x = tok[...].astype(f32)
    x_hat, inv_std = normalise(x)
    block_out[...] = (x + block_own[...] + got[0].astype(f32)).astype(bf16)
    dv = d_vpre[...].reshape(w_val.shape[1], T).T
    dn = dn_own[...] + got[1].astype(f32) + mm(dv, w_val[...], NT)
    dx = dn * gain[...]
    tokens_grad[...] = grad[...].astype(f32) + inv_std * (
        dx
        - jnp.mean(dx, axis=1, keepdims=True)
        - x_hat * jnp.mean(dx * x_hat, axis=1, keepdims=True)
    )
    sums = jnp.concatenate(
        [jnp.sum(dn * x_hat, axis=0, keepdims=True), jnp.sum(dn, axis=0, keepdims=True)], 0
    )

    @pl.when(i == 0)
    def _():
        acc[...] = sums

    @pl.when(i > 0)
    def _():
        acc[...] += sums

    @pl.when(i == pl.num_programs(0) - 1)
    def _():
        parts, lanes = norm_part.shape
        w = acc.shape[1] // parts
        for k in range(parts):
            cut = acc[:, k * w : (k + 1) * w]
            blank = jnp.zeros((1, lanes - 2 * w), f32)
            norm_part[k : k + 1, :] = jnp.concatenate([cut[0:1], cut[1:2], blank], 1)


def tail_call(tokens, grad, gain, block_own, got, dn_own, d_vpre, w_val, parts):
    own, width = tokens.shape
    rows = pl.BlockSpec((T, width), lambda i: (i, 0))
    chan_n, _, group, _ = d_vpre.shape
    return call(
        tail_kernel,
        "norm_back",
        (own // T,),
        [
            rows,
            rows,
            whole((1, width)),
            rows,
            pl.BlockSpec((2, T, width), lambda i: (0, i, 0)),
            rows,
            pl.BlockSpec((chan_n, 1, group, T), lambda i: (0, i, 0, 0)),
            whole(w_val.shape),
        ],
        [rows, rows, whole((parts, T))],
        [struct((own, width), bf16), struct((own, width), f32), struct((parts, T), f32)],
        from_hbm(tokens, grad, gain[None], block_own, got, dn_own, d_vpre, w_val),
        scratch=[pltpu.VMEM((2, width), f32)],
    )


def finish_kernel(s, u_keep, u_got, m_keep, m_got, d_keep, d_got, down, mine, other):
    d = d_keep[0].astype(f32) + d_got[0].astype(f32)
    rows = down.shape[0]
    down[...] = d[:rows]
    half = d.shape[1]
    um, mx = u_keep.shape[1], m_keep.shape[1]
    for out, core in ((mine, s[0]), (other, 1 - s[0])):
        out[0:um, :] = u_keep[core].astype(f32) + u_got[core].astype(f32)
        out[um : um + mx, :] = m_keep[core].astype(f32) + m_got[core].astype(f32)
        out[um + mx :, 0:half] = jnp.where(core == 0, d[rows : rows + 8], d[rows + 8 :])
        out[um + mx :, half:] = jnp.zeros((8, out.shape[1] - half), f32)


def finish_call(scal, up, mix, down):
    um, mx, half = up[0].shape[1], mix[0].shape[1], up[0].shape[2]
    rows, width = down[0].shape[1:]
    args = (*up, *mix, *down)
    pack = (um + mx + 8, half)
    return call(
        finish_kernel,
        "finish",
        (1,),
        [whole(a.shape) for a in args],
        [whole((rows - 16, width)), whole(pack), whole(pack)],
        [struct((rows - 16, width), f32), struct(pack, f32), struct(pack, f32)],
        args,
        scalars=scal,
    )


def join_kernel(s, mine, got, up, mix, val):
    um, mx = up.shape[0], mix.shape[0]
    first = s[0] == 0
    part = mine.shape[1] // 2
    for core in (0, 1):
        held = jnp.where(first, mine[...], got[...]) if core == 0 else jnp.where(first, got[...], mine[...])
        for x in (0, 1):
            to = slice((2 * x + core) * part, (2 * x + core + 1) * part)
            up[:, to] = held[0:um, x * part : (x + 1) * part]
            mix[:, to] = held[um : um + mx, x * part : (x + 1) * part]
        w = val.shape[1] // 2
        for r in range(val.shape[0] // 8):
            val[r * 8 : r * 8 + 8, core * w : (core + 1) * w] = held[um + mx :, r * w : (r + 1) * w]


def join_call(scal, mine, got, um, mx, inner):
    ff = mine.shape[1] * 2
    return call(
        join_kernel,
        "join",
        (1,),
        [whole(mine.shape)] * 2,
        [whole((um, ff)), whole((mx, ff)), whole((um, inner))],
        [struct((um, ff), f32), struct((mx, ff), f32), struct((um, inner), f32)],
        (mine, got),
        scalars=scal,
    )


def make_square(row_n, chan_n):
    def on_device(
        tokens, starts, layer_norm_gain, ln_bias, w_up, w_val, w_mix, w_down,
        decay_rate, mix_coef, out_grad,
    ):
        own, width = tokens.shape
        inner = w_val.shape[1]
        row, chan = lax.axis_index("row"), lax.axis_index("chan")
        core = row % 2
        scal = jnp.stack([core, row // 2, chan % 2, (chan // 2) % 2, chan // 4]).astype(jnp.int32)
        bit_x, bit_y = scal[1], scal[2]
        bit_a = jnp.where(core == 0, bit_x, bit_y).reshape(1)
        bit_b = jnp.where(core == 0, bit_y, bit_x).reshape(1)
        bit_low, bit_high = scal[3:4], scal[4:5]
        devices = [(r, c) for r in range(row_n) for c in range(chan_n)]
        flip_x = lambda r, c: (r ^ 2, c)
        flip_y = lambda r, c: (r, c ^ 1)
        moves = dict(
            core=lambda r, c: (r ^ 1, c),
            a=lambda r, c: flip_y(r, c) if r % 2 else flip_x(r, c),
            b=lambda r, c: flip_x(r, c) if r % 2 else flip_y(r, c),
            low=lambda r, c: (r, c ^ 2),
            high=lambda r, c: (r, c ^ 4),
            ab=lambda r, c: (r ^ 2, c ^ 1),
            z=lambda r, c: (r, c ^ 6),
        )

        def send(value, way):
            to = [moves[way](r, c) for r, c in devices]
            pairs = [(r * chan_n + c, t[0] * chan_n + t[1]) for (r, c), t in zip(devices, to)]
            return lax.ppermute(value, ("row", "chan"), pairs)

        after = lax.optimization_barrier
        trade = lambda v: lax.all_to_all(v, "chan", split_axis=0, concat_axis=0, tiled=True)
        rows = own * chan_n // T
        to_seq = lambda v: v.reshape(rows, inner // chan_n, T)
        to_tok = lambda v: v.reshape(chan_n, own // T, inner // chan_n, T)

        masks = ssm_masks(starts)
        grad_oth = send(out_grad, "core")
        normed, v_act, v_slope = norm_call(tokens, layer_norm_gain, ln_bias, w_val, chan_n)
        normed_oth = send(normed, "core")
        v_chan = to_seq(trade(v_act))
        u_act, d_slope, d_yproj, normed_t, dy_own, dy_oth, pair_grad = gate_call(
            scal, normed, normed_oth, out_grad, grad_oth, w_up, w_mix, w_down, row_n, chan_n
        )
        d_y = (dy_own + send(dy_oth, "core").astype(f32)).astype(bf16)
        v_chan, d_y = after((v_chan, d_y))
        d_y_chan = to_seq(trade(d_y))
        y_chan, states, toeplitz = ssm_fwd(v_chan, decay_rate, mix_coef, masks)
        y_chan, d_y_chan = after((y_chan, d_y_chan))
        y_own = trade(to_tok(y_chan))
        d_v_chan, d_rate, d_coef = ssm_bwd(
            v_chan, d_y_chan, decay_rate, mix_coef, masks, states, toeplitz
        )
        y_own, d_v_chan = after((y_own, d_v_chan))
        y_oth = send(y_own, "core")
        y_oth, d_v_chan = after((y_oth, d_v_chan))
        d_v = trade(to_tok(d_v_chan))
        gate_out, d_upre, u_give, u_keep, m_give, m_keep = mid_call(
            scal, y_own, y_oth, w_mix, u_act, d_slope, d_yproj, normed_t, row_n
        )
        u_give, m_give, gate_out, d_v, d_rate, d_coef = after(
            (u_give, m_give, gate_out, d_v, d_rate, d_coef)
        )

        u_got = send(u_give, "a")
        m_got = send(m_give, "low")
        rates = lax.psum_scatter(
            jnp.concatenate([d_rate, d_coef], 0), "row", scatter_dimension=1, tiled=True
        )
        half = chan_n // 2
        other_half = lambda v: lax.dynamic_slice_in_dim(v, (1 - core) * half, half, 0)
        v_give = (other_half(d_v).astype(f32) * other_half(v_slope)).astype(bf16)
        v_got = send(v_give, "core")
        d_vpre = (d_v.astype(f32) * v_slope).astype(bf16)
        down = mm(gate_out, pair_grad, TN).astype(bf16)
        d_give, d_keep = down_val_call(scal, down, d_vpre, v_got, normed_t)
        u_got, m_got, d_give, gate_out = after((u_got, m_got, d_give, gate_out))

        d_got = send(d_give, "a")
        m_give, m_keep = step_call(bit_high, m_keep, m_got)
        m_got = send(m_give, "high")
        u_give, u_keep = step_call(bit_b, u_keep, u_got)
        block_own, dn_own, bd_give = block_call(scal, gate_out, d_upre, w_down, w_up, row_n)
        d_got, m_got, u_give, bd_give = after((d_got, m_got, u_give, bd_give))

        u_got = send(u_give, "b")
        bd_got = send(bd_give, "core")
        d_give, d_keep = step_call(bit_b, d_keep, d_got)
        u_got, d_give, bd_got = after((u_got, d_give, bd_got))

        d_got = send(d_give, "b")
        u_give, u_keep = step_call(bit_low, u_keep, u_got)
        u_got = send(u_give, "low")
        m_give, m_keep = step_call(bit_a, m_keep, m_got)
        block_out, tokens_grad, norm_part = tail_call(
            tokens, out_grad, layer_norm_gain, block_own, bd_got, dn_own, d_vpre, w_val,
            row_n * chan_n,
        )
        d_got, u_got, m_give, norm_part = after((d_got, u_got, m_give, norm_part))

        d_give, d_keep = step_call(bit_low, d_keep, d_got)
        d_got = send(d_give, "low")
        u_give, u_keep = step_call(bit_high, u_keep, u_got)
        u_got = send(u_give, "high")
        m_got = send(m_give, "a")
        norm_part = norm_part + send(norm_part, "a") + send(norm_part, "b") + send(norm_part, "ab")
        d_got, m_got, u_got, norm_part = after((d_got, m_got, u_got, norm_part))

        d_give, d_keep = step_call(bit_high, d_keep, d_got)
        d_got = send(d_give, "high")
        m_give, m_keep = step_call(bit_b, m_keep, m_got)
        m_got = send(m_give, "b")
        norm_part = (
            norm_part + send(norm_part, "low") + send(norm_part, "high") + send(norm_part, "z")
        )
        d_got, m_got, norm_part = after((d_got, m_got, norm_part))

        down_grad, mine, other = finish_call(
            scal, (u_keep, u_got), (m_keep, m_got), (d_keep, d_got)
        )
        um, mx = u_keep.shape[1], m_keep.shape[1]
        other = send(other, "core")
        norm_part = norm_part + send(norm_part, "core")
        up_grad, mix_grad, val_grad = join_call(scal, mine, other, um, mx, inner)
        norm_sum = lax.dynamic_index_in_dim(norm_part, row * chan_n + chan, 0, keepdims=False)
        w = width // (row_n * chan_n)
        return (
            block_out,
            tokens_grad,
            norm_sum[:w],
            norm_sum[w : 2 * w],
            up_grad,
            val_grad,
            mix_grad,
            down_grad,
            rates[: decay_rate.shape[0]],
            rates[decay_rate.shape[0] :],
        )

    return on_device


def make_general(row_n, chan_n):
    row_hi = row_n // 2

    def swap(value, axis, bit):
        size = row_n if axis == "row" else chan_n
        return lax.ppermute(value, axis, [(i, i ^ (1 << bit)) for i in range(size)])

    def core_swap(value):
        return swap(value, "row", 0)

    def bits_of(size):
        return size.bit_length() - 1

    def scatter_sum(part, names, order, last_dtype):
        names = list(names)
        for step, name in enumerate(order):
            axis, bit = name
            dim = names.index(name)
            mine = (lax.axis_index(axis) >> bit) & 1
            keep = lax.dynamic_index_in_dim(part, mine, dim, keepdims=False)
            give = lax.dynamic_index_in_dim(part, 1 - mine, dim, keepdims=False)
            got = swap(give, axis, bit)
            part = keep.astype(jnp.float32) + got.astype(jnp.float32)
            if step < len(order) - 1:
                part = part.astype(give.dtype)
            else:
                part = part.astype(last_dtype)
            names.pop(dim)
        return part

    row_bits = [("row", k) for k in range(bits_of(row_n) - 1, 0, -1)]
    core_bit = ("row", 0)
    chan_bits = [("chan", k) for k in range(bits_of(chan_n) - 1, -1, -1)]
    near_y = chan_bits[2:]
    along_z = chan_bits[:2][::-1]

    def on_device(
        tokens,
        starts,
        layer_norm_gain,
        ln_bias,
        w_up,
        w_val,
        w_mix,
        w_down,
        decay_rate,
        mix_coef,
        out_grad,
    ):
        own, width = tokens.shape
        ff = w_up.shape[1]
        inner = w_val.shape[1]
        part_ff = ff // row_n
        core = lax.axis_index("row") % 2
        mm = lambda a, b, ca, cb: lax.dot_general(
            a, b, (((ca,), (cb,)), ((), ())), preferred_element_type=jnp.float32
        )
        masks = ssm_masks(starts)
        inputs_f = tokens.astype(jnp.float32)
        row_mean = jnp.mean(inputs_f, axis=1, keepdims=True)
        centred = inputs_f - row_mean
        inv_std = lax.rsqrt(jnp.mean(centred * centred, axis=1, keepdims=True) + epsilon)
        x_hat = centred * inv_std
        normed = (x_hat * layer_norm_gain + ln_bias).astype(jnp.bfloat16)
        v_pre = mm(w_val, normed, 0, 1)
        v_cdf = gauss_cdf(v_pre)
        v_act = (v_pre * v_cdf).astype(jnp.bfloat16)
        v_slope = v_cdf + v_pre * gauss_pdf(v_pre)
        v_chan = lax.all_to_all(
            v_act.reshape(inner, own // T, T), "chan", split_axis=0, concat_axis=1, tiled=True
        )
        v_chan = jnp.swapaxes(v_chan, 0, 1)
        pair_normed = jnp.concatenate([normed, core_swap(normed)], 0)
        pair_grad = jnp.concatenate([out_grad, core_swap(out_grad)], 0)
        halves = lambda w, d: lax.dynamic_index_in_dim(
            w.reshape(w.shape[:d] + (row_hi, 2, part_ff) + w.shape[d + 1 :]), core, d + 1, keepdims=False
        ).reshape(w.shape[:d] + (ff // 2,) + w.shape[d + 1 :])
        up_half = halves(w_up, 1)
        mix_half = halves(w_mix, 1)
        down_half = halves(w_down, 0)
        u_pre = mm(pair_normed, up_half, 1, 0)
        d_gate = mm(pair_grad, down_half, 1, 1)
        u_cdf = gauss_cdf(u_pre)
        u_act = u_pre * u_cdf
        d_yproj = (d_gate * u_act).astype(jnp.bfloat16)
        d_slope = d_gate * (u_cdf + u_pre * gauss_pdf(u_pre))
        d_y_part = mm(mix_half, d_yproj, 1, 1)
        d_y = (
            d_y_part[:, :own] + core_swap(d_y_part[:, own:].astype(jnp.bfloat16)).astype(jnp.float32)
        ).astype(jnp.bfloat16)
        d_y_chan = lax.all_to_all(
            d_y.reshape(inner, own // T, T), "chan", split_axis=0, concat_axis=1, tiled=True
        )
        d_y_chan = jnp.swapaxes(d_y_chan, 0, 1)
        y_chan, states, toeplitz = ssm_fwd(v_chan, decay_rate, mix_coef, masks)
        y_chan = jnp.swapaxes(y_chan, 0, 1)
        y_own = lax.all_to_all(y_chan, "chan", split_axis=1, concat_axis=0, tiled=True)
        y_own = y_own.reshape(inner, own)
        d_v_chan, d_rate, d_coef = ssm_bwd(
            v_chan, d_y_chan, decay_rate, mix_coef, masks, states, toeplitz
        )
        d_v_chan = jnp.swapaxes(d_v_chan, 0, 1)
        d_v = lax.all_to_all(d_v_chan, "chan", split_axis=1, concat_axis=0, tiled=True)
        pair_y = jnp.concatenate([y_own, core_swap(y_own)], 1)
        split_rows = lambda a, lead: a.reshape((2,) * lead + (-1,) + a.shape[1:])
        y_proj = mm(pair_y, mix_half, 0, 0)
        gate_out = (u_act * y_proj).astype(jnp.bfloat16)
        d_upre = (d_slope * y_proj).astype(jnp.bfloat16)
        mix_part = mm(pair_y, d_yproj, 1, 0).astype(jnp.bfloat16)
        down_part = mm(gate_out, pair_grad, 0, 0).astype(jnp.bfloat16)
        up_part = mm(pair_normed, d_upre, 0, 0).astype(jnp.bfloat16)
        all_names = row_bits + [core_bit] + chan_bits
        no_core = row_bits + chan_bits
        lead = len(all_names)
        mix_sum = scatter_sum(
            split_rows(mix_part, lead), all_names, along_z + row_bits + near_y, jnp.float32
        )
        up_sum = scatter_sum(
            split_rows(up_part, lead), all_names, row_bits + near_y + along_z, jnp.float32
        )
        down_grad = scatter_sum(
            split_rows(down_part, lead - 1), no_core, near_y + row_bits + along_z, jnp.float32
        )

        def join_cores(halfsum):
            mine = lax.dynamic_index_in_dim(halfsum, core, 0, keepdims=False)
            other = core_swap(lax.dynamic_index_in_dim(halfsum, 1 - core, 0, keepdims=False))
            shape = (mine.shape[0], row_hi, part_ff)
            low = jnp.where(core == 0, mine, other).reshape(shape)
            high = jnp.where(core == 0, other, mine).reshape(shape)
            return jnp.stack([low, high], 2).reshape(mine.shape[0], ff)

        block_part = mm(gate_out, down_half, 1, 0)
        block_out = (
            inputs_f
            + block_part[:own]
            + core_swap(block_part[own:].astype(jnp.bfloat16)).astype(jnp.float32)
        ).astype(jnp.bfloat16)
        d_normed_part = mm(d_upre, up_half, 1, 1)
        d_normed_got = core_swap(d_normed_part[own:].astype(jnp.bfloat16)).astype(jnp.float32)
        d_vpre = (d_v.reshape(inner, own).astype(jnp.float32) * v_slope).astype(jnp.bfloat16)
        val_part = mm(normed, d_vpre, 0, 1).astype(jnp.bfloat16)
        val_grad = scatter_sum(
            split_rows(val_part, lead),
            all_names,
            [core_bit] + along_z + near_y + row_bits,
            jnp.float32,
        )
        d_normed = d_normed_part[:own] + d_normed_got + mm(d_vpre, w_val, 0, 1)
        norm_part = jnp.stack([jnp.sum(d_normed * x_hat, axis=0), jnp.sum(d_normed, axis=0)], 1)
        norm_sum = scatter_sum(
            split_rows(norm_part, lead), all_names, [core_bit] + row_bits + chan_bits, jnp.float32
        )
        d_xh = d_normed * layer_norm_gain
        tokens_grad = out_grad.astype(jnp.float32) + inv_std * (
            d_xh
            - jnp.mean(d_xh, axis=1, keepdims=True)
            - x_hat * jnp.mean(d_xh * x_hat, axis=1, keepdims=True)
        )
        row_all = row_bits + [core_bit]
        states_n = decay_rate.shape[1]
        rates = jnp.stack([d_rate, d_coef]).reshape(
            (2 * d_rate.shape[0],) + (2,) * len(row_all) + (states_n // row_n,)
        )
        rates = jnp.moveaxis(rates, 0, len(row_all))
        rates = scatter_sum(rates, row_all, [core_bit] + row_bits, jnp.float32)
        rates = rates.reshape(2, d_rate.shape[0], states_n // row_n)
        return (
            block_out,
            tokens_grad,
            norm_sum[:, 0],
            norm_sum[:, 1],
            join_cores(up_sum),
            val_grad,
            join_cores(mix_sum),
            down_grad,
            rates[0],
            rates[1],
        )

    return on_device


def solution(mesh):
    spread = P(("row", "chan"), None)
    row_n, chan_n = mesh.shape["row"], mesh.shape["chan"]
    make = make_square if (row_n, chan_n) == (4, 8) else make_general
    return jax.shard_map(
        make(row_n, chan_n),
        mesh=mesh,
        in_specs=(
            spread,
            P("row", None),
            P(),
            P(),
            P(),
            P(),
            P(),
            P(),
            P("chan", None),
            P("chan", None),
            spread,
        ),
        out_specs=(
            spread,
            spread,
            P(("row", "chan")),
            P(("row", "chan")),
            spread,
            spread,
            spread,
            spread,
            P("chan", "row"),
            P("chan", "row"),
        ),
        check_vma=False,
    )
```

```python
import jax
import jax.numpy as jnp
from jax import lax
from jax.experimental import pallas as pl
from jax.experimental.pallas import tpu as pltpu
from jax.sharding import PartitionSpec as P

T = 128
SUB = 8
GROUP = 16
SEG = 4
f32 = jnp.float32
bf16 = jnp.bfloat16
NT = (((1,), (1,)), ((), ()))
TN = (((0,), (0,)), ((), ()))
NN = (((1,), (0,)), ((), ()))


def mm(a, b, d=NN):
    return lax.dot_general(a, b, d, preferred_element_type=f32)


def iota(shape, d):
    return lax.broadcasted_iota(jnp.int32, shape, d)


def powers(rate_row, pt_ref, c):
    n = rate_row.shape[1]
    steps = iota((8, n), 0).astype(f32)
    r8 = jnp.broadcast_to(rate_row, (8, n))
    parts = [jnp.exp(-r8 * steps)]
    fade = jnp.exp(-8.0 * r8)
    while len(parts) < T // 8:
        parts = parts + [p * fade for p in parts]
        fade = fade * fade
    for i in range(0, len(parts), 2):
        pt_ref[c, i * 8 : i * 8 + 16, :] = jnp.concatenate(parts[i : i + 2], 0).astype(bf16)


def put(ref, c, val, rows):
    for q in range(val.shape[1] // T):
        ref[q, pl.ds(c, rows, stride=SUB), :] = val[:, q * T : (q + 1) * T]


def take(ref, c, rows):
    return jnp.concatenate(
        [ref[q, pl.ds(c, rows, stride=SUB), :] for q in range(ref.shape[0])], 1
    )


def tiles(v):
    return jnp.stack([v[:, q * T : (q + 1) * T] for q in range(v.shape[1] // T)])


def untile(v):
    return jnp.concatenate([v[q] for q in range(v.shape[0])], 1)


def flip_matrix():
    return (iota((T, T), 0) + iota((T, T), 1) == T - 1).astype(f32).astype(bf16)


def seg_masks(ins, g):
    return jnp.concatenate([(ins == g * SEG + k).astype(f32) for k in range(SEG)], 0)


def rep(x):
    return jnp.concatenate([x] * SEG, 0)


def fold(o, m, rows):
    o = o * m
    out = o[0:rows]
    for k in range(1, SEG):
        out = out + o[k * rows : (k + 1) * rows]
    return out


def far_part(a, p, rows):
    hi = a.astype(bf16)
    lo = (a - hi.astype(f32)).astype(bf16)
    o = mm(jnp.concatenate([hi, lo], 0), p, NT)
    return o[:rows] + o[rows:]


def lanes_of(ref, c, rows):
    return ref[pl.ds(c, rows, stride=GROUP), :]


def fwd_kernel(groups, keep, x, rate, coef, ins, insj, head, tailj, y, hs, toe, pt, ss, near, xs, kr):
    rows = ins.shape[0]
    n = rate.shape[1]
    flip = flip_matrix()
    xs[...] = x[...].astype(f32).reshape(rows * GROUP, T)
    tail = tailj[...]
    hd = head[...]
    m0 = seg_masks(ins[...], 0)
    m0b = m0.astype(bf16)
    tri = iota((T, T), 1) >= iota((T, T), 0)
    for sub in range(GROUP // SUB):
        lo = sub * SUB
        cf = coef[lo : lo + SUB, :]
        rt = rate[lo : lo + SUB, :]
        cfh = cf.astype(bf16)
        cfl = (cf - cfh.astype(f32)).astype(bf16)
        cf2 = jnp.concatenate([cfh, cfl], 0)
        xj = []
        for c in range(SUB):
            xc = lanes_of(xs, lo + c, rows).astype(bf16)
            xj.append(mm(xc, flip).astype(bf16) * tail)
        for c in range(SUB):
            powers(rt[c : c + 1], pt, c)
            p = pt[c]
            put(ss, c, mm(xj[c], p), rows)
            k2 = mm(cf2, p, NT)
            kr[c : c + 1, :] = k2[c : c + 1] + k2[SUB + c : SUB + c + 1]
        for c in range(SUB):
            k = jnp.broadcast_to(kr[c : c + 1, :], (T, T))
            kb = pltpu.roll(k, 0, 1, stride=1, stride_axis=0)
            tp = jnp.where(tri, kb, 0.0).astype(bf16)
            toe[lo + c] = tp
            xc = lanes_of(xs, lo + c, rows).astype(bf16)
            near[c] = fold(mm(rep(xc) * m0b, tp), m0, rows)
        fade = tiles(jnp.exp(-float(T) * rt))
        ce = tiles(cf * jnp.exp(-rt))
        h = jnp.zeros((n // T, SUB, T), f32)
        for b in range(rows):
            w = slice(b * SUB, (b + 1) * SUB)
            hs[sub, :, w, :] = h
            s = ss[:, w, :]
            ss[:, w, :] = h * ce
            h = h * (fade * keep[b]) + s

        @pl.loop(1, groups[0])
        def _(g):
            m = seg_masks(ins[...], g)
            for c in range(SUB):
                xc = lanes_of(xs, lo + c, rows).astype(bf16)
                near[c] += fold(mm(rep(xc) * m.astype(bf16), toe[lo + c]), m, rows)

        for c in range(SUB):
            far = far_part(take(ss, c, rows), pt[c], rows)
            xs[pl.ds(lo + c, rows, stride=GROUP), :] = near[c] + hd * far
    y[...] = xs[...].reshape(rows, GROUP, T).astype(bf16)


def bwd_kernel(
    groups, keep, x, dy, rate, coef, ins, insj, head, tailj, hs, toe,
    dv, rates, pt, s1, e0, e1, near, gacc, nr, xs, ys,
):
    rows = ins.shape[0]
    n = rate.shape[1]
    flip = flip_matrix()
    xs[...] = x[...].astype(f32).reshape(rows * GROUP, T)
    ys[...] = dy[...].astype(f32).reshape(rows * GROUP, T)
    tail = tailj[...]
    hdb = head[...].astype(bf16)
    mn = seg_masks(ins[...], 0).astype(bf16)
    mj = seg_masks(insj[...], 0)
    mjb = mj.astype(bf16)
    lag = iota((rows, T), 1).astype(f32).astype(bf16)
    lag1 = (iota((rows, T), 1) + 1).astype(f32).astype(bf16)
    lagf = iota((1, T), 1).astype(f32)
    valid = iota((T, T), 0) + iota((T, T), 1) >= T - 1
    row16 = iota((16, T), 0)

    def lags(d, xx, md, mx):
        o = mm(rep(d) * md, rep(xx) * mx, TN)
        o = pltpu.roll(jnp.where(valid, o, 0.0), 1, 1, stride=1, stride_axis=0)
        return jnp.sum(o, axis=0, keepdims=True)

    for sub in range(GROUP // SUB):
        lo = sub * SUB
        rt = rate[lo : lo + SUB, :]
        cf = coef[lo : lo + SUB, :]
        xa = jnp.concatenate([lanes_of(xs, lo + c, rows) for c in range(SUB)], 0).astype(bf16)
        da = jnp.concatenate([lanes_of(ys, lo + c, rows) for c in range(SUB)], 0).astype(bf16)
        xja = mm(xa, flip).astype(bf16)
        dja = mm(da, flip).astype(bf16)
        for c in range(SUB):
            sl = slice(c * rows, (c + 1) * rows)
            near[c] = fold(mm(rep(dja[sl]) * mjb, toe[lo + c]), mj, rows)
            gacc[c : c + 1, :] = lags(da[sl], xja[sl], mn, mjb)

        @pl.loop(1, groups[0])
        def _(g):
            m = seg_masks(ins[...], g).astype(bf16)
            k = seg_masks(insj[...], g)
            kb = k.astype(bf16)
            for c in range(SUB):
                d = lanes_of(ys, lo + c, rows).astype(bf16)
                xx = lanes_of(xs, lo + c, rows).astype(bf16)
                dj = mm(d, flip).astype(bf16)
                xj = mm(xx, flip).astype(bf16)
                near[c] += fold(mm(rep(dj) * kb, toe[lo + c]), k, rows)
                gacc[c : c + 1, :] += lags(d, xj, m, kb)

        for c in range(SUB):
            sl = slice(c * rows, (c + 1) * rows)
            powers(rt[c : c + 1], pt, c)
            gr = gacc[c : c + 1, :]
            gl = gr * lagf
            gh = gr.astype(bf16).astype(f32)
            glh = gl.astype(bf16).astype(f32)
            gm = jnp.where(row16 == 2, glh, jnp.where(row16 == 3, gl - glh, 0.0))
            gm = jnp.where(row16 == 0, gh, jnp.where(row16 == 1, gr - gh, gm)).astype(bf16)
            dh = da[sl] * hdb
            o = mm(jnp.concatenate([xja[sl] * tail * lag, dh, dh * lag1, gm], 0), pt[c])
            put(s1, c, o[0:rows], rows)
            put(e0, c, o[rows : 2 * rows], rows)
            put(e1, c, o[2 * rows : 3 * rows], rows)
            k = 3 * rows
            nr[c : c + 1, :] = o[k : k + 1] + o[k + 1 : k + 2]
            nr[SUB + c : SUB + c + 1, :] = o[k + 2 : k + 3] + o[k + 3 : k + 4]
        fade = tiles(jnp.exp(-float(T) * rt))
        ee = tiles(jnp.exp(-rt))
        ce = tiles(cf) * ee
        zero = jnp.zeros((n // T, SUB, T), f32)
        dh, ac, ar, ae = zero, zero, zero, zero
        for b in range(rows - 1, -1, -1):
            w = slice(b * SUB, (b + 1) * SUB)
            h = hs[sub, :, w, :]
            e = e0[:, w, :]
            kf = fade * keep[b]
            ar = ar + dh * (kf * (float(T) * h) + s1[:, w, :])
            ae = ae + h * e1[:, w, :]
            ac = ac + h * e
            s1[:, w, :] = dh
            dh = ce * e + kf * dh
        for c in range(SUB):
            far = far_part(take(s1, c, rows), pt[c], rows)
            near[c] = near[c] + tail.astype(f32) * far
        dva = mm(near[...].reshape(SUB * rows, T).astype(bf16), flip)
        for c in range(SUB):
            xs[pl.ds(lo + c, rows, stride=GROUP), :] = dva[c * rows : (c + 1) * rows]
        cut = (lo, lo + SUB)
        dcoef = nr[0:SUB, :] + untile(ee * ac)
        drate = -(cf * nr[SUB : 2 * SUB, :] + untile(ar + ce * ae))
        lanes = rates.shape[-1]
        for row in range(n // lanes):
            at = slice(row * lanes, (row + 1) * lanes)
            rates[row % 2, row // 2, 0, cut[0] : cut[1], :] = drate[:, at]
            rates[row % 2, row // 2, 1, cut[0] : cut[1], :] = dcoef[:, at]
    dv[...] = xs[...].reshape(rows, GROUP, T).astype(bf16)


def ssm_masks(starts):
    seqs, length = starts.shape
    blocks = length // T
    rows = seqs * blocks
    st = starts.reshape(rows, T)
    tri = (iota((T, T), 0) <= iota((T, T), 1)).astype(bf16)
    ins = mm(st.astype(bf16), tri).astype(jnp.int32) - st[:, :1]
    cont = (st[:, :1] == 0) & (iota((rows, 1), 0) % blocks != 0)
    last = ins[:, -1:]
    head = ((ins == 0) & cont).astype(f32)
    back = (iota((T, T), 0) + iota((T, T), 1) == T - 1).astype(bf16)
    insj = mm(ins.astype(bf16), back).astype(jnp.int32)
    tailj = (insj == last).astype(bf16)
    keep = (cont & (last == 0)).astype(f32)[:, 0]
    groups = (jnp.max(last) // SEG + 1).reshape(1).astype(jnp.int32)
    return groups, keep, ins, insj, head, tailj


def ssm_specs(rows, n):
    full = pl.BlockSpec((rows, T), lambda i: (0, 0))
    return dict(
        sm=pl.BlockSpec(memory_space=pltpu.SMEM),
        full=full,
        ch=pl.BlockSpec((rows, GROUP, T), lambda i: (0, i, 0)),
        par=pl.BlockSpec((GROUP, n), lambda i: (i, 0)),
        hs=pl.BlockSpec((GROUP // SUB, n // T, rows * SUB, T), lambda i: (i, 0, 0, 0)),
        toe=pl.BlockSpec((GROUP, T, T), lambda i: (i, 0, 0)),
        big=pltpu.VMEM((n // T, rows * SUB, T), f32),
        pt=pltpu.VMEM((SUB, T, n), bf16),
        near=pltpu.VMEM((SUB, rows, T), f32),
        xs=pltpu.VMEM((rows * GROUP, T), f32),
        cost=pl.CostEstimate(flops=2 * 10**10, bytes_accessed=10**7, transcendentals=0),
    )


def ssm_fwd(x, rate, coef, masks):
    rows, chans, _ = x.shape
    n = rate.shape[1]
    s = ssm_specs(rows, n)
    return pl.pallas_call(
        fwd_kernel,
        grid=(chans // GROUP,),
        in_specs=[s["sm"], s["sm"], s["ch"], s["par"], s["par"]] + [s["full"]] * 4,
        out_specs=[s["ch"], s["hs"], s["toe"]],
        out_shape=[
            pltpu.HBM(x.shape, bf16),
            pltpu.HBM((chans // SUB, n // T, rows * SUB, T), f32),
            pltpu.HBM((chans, T, T), bf16),
        ],
        scratch_shapes=[s["pt"], s["big"], s["near"], s["xs"], pltpu.VMEM((SUB, T), f32)],
        compiler_params=pltpu.CompilerParams(vmem_limit_bytes=16 * 2**20),
        cost_estimate=s["cost"],
        name="ssm_fwd",
    )(masks[0], masks[1], x, rate, coef, *masks[2:])


def ssm_bwd(x, dy, rate, coef, masks, hs, toe, row_n):
    rows, chans, _ = x.shape
    n = rate.shape[1]
    s = ssm_specs(rows, n)
    return pl.pallas_call(
        bwd_kernel,
        grid=(chans // GROUP,),
        in_specs=[s["sm"], s["sm"], s["ch"], s["ch"], s["par"], s["par"]]
        + [s["full"]] * 4
        + [s["hs"], s["toe"]],
        out_specs=[
            s["ch"],
            pl.BlockSpec((2, row_n // 2, 2, GROUP, n // row_n), lambda i: (0, 0, 0, i, 0)),
        ],
        out_shape=[
            pltpu.HBM(x.shape, bf16),
            jax.ShapeDtypeStruct((2, row_n // 2, 2, chans, n // row_n), f32),
        ],
        scratch_shapes=[
            s["pt"],
            s["big"],
            s["big"],
            s["big"],
            s["near"],
            pltpu.VMEM((SUB, T), f32),
            pltpu.VMEM((2 * SUB, n), f32),
            s["xs"],
            s["xs"],
        ],
        compiler_params=pltpu.CompilerParams(vmem_limit_bytes=16 * 2**20),
        cost_estimate=s["cost"],
        name="ssm_bwd",
    )(masks[0], masks[1], x, dy, rate, coef, *masks[2:], *from_hbm(hs, toe))


epsilon = 1e-05
TILE = 768


def gauss_cdf(a):
    return 0.5 * (1.0 + lax.erf(a * 0.7071067811865476))


def gauss_pdf(a):
    return jnp.exp(-0.5 * a * a) * 0.3989422804014327


def struct(shape, dtype):
    return jax.ShapeDtypeStruct(shape, dtype)


def in_hbm(shape, dtype):
    return pltpu.HBM(shape, dtype)


def from_hbm(*arrays):
    return tuple(pltpu.with_memory_space_constraint(a, pltpu.HBM) for a in arrays)


def whole(shape):
    return pl.BlockSpec(shape, lambda *_: (0,) * len(shape))


def call(kernel, name, grid, ins, outs, out_shape, args, scalars=None, scratch=(), aliases=None, vmem=24, cost=None):
    lead = [] if scalars is None else [scalars]
    return pl.pallas_call(
        kernel,
        grid_spec=pltpu.PrefetchScalarGridSpec(
            num_scalar_prefetch=len(lead),
            grid=grid,
            in_specs=ins,
            out_specs=outs,
            scratch_shapes=list(scratch),
        ),
        out_shape=out_shape,
        input_output_aliases=aliases or {},
        compiler_params=pltpu.CompilerParams(vmem_limit_bytes=vmem * 2**20),
        cost_estimate=cost and pl.CostEstimate(flops=cost, bytes_accessed=10**7, transcendentals=0),
        name=name,
    )(*lead, *args)


def normalise(x):
    centred = x - jnp.mean(x, axis=1, keepdims=True)
    inv_std = lax.rsqrt(jnp.mean(centred * centred, axis=1, keepdims=True) + epsilon)
    return centred * inv_std, inv_std


def norm_kernel(tok, gain, bias, w_val, normed, v_act, v_slope):
    x_hat, _ = normalise(tok[...].astype(f32))
    n = (x_hat * gain[...] + bias[...]).astype(bf16)
    normed[...] = n
    v = mm(n, w_val[...])
    cdf = gauss_cdf(v)
    v_act[...] = (v * cdf).T.astype(bf16).reshape(v_act.shape)
    v_slope[...] = (cdf + v * gauss_pdf(v)).T.reshape(v_slope.shape)


def norm_call(tokens, gain, bias, w_val, chan_n):
    own, width = tokens.shape
    inner = w_val.shape[1]
    quads = own // T
    spread = (chan_n, quads, inner // chan_n, T)
    block = pl.BlockSpec((chan_n, 1, inner // chan_n, T), lambda i: (0, i, 0, 0))
    rows = pl.BlockSpec((T, width), lambda i: (i, 0))
    return call(
        norm_kernel,
        "norm_val",
        (quads,),
        [rows, whole((1, width)), whole((1, width)), whole(w_val.shape)],
        [rows, block, block],
        [struct((own, width), bf16), struct(spread, bf16), struct(spread, f32)],
        from_hbm(tokens, gain[None], bias[None], w_val),
    )


def gate_kernel(
    core, n_own, n_oth, g_own, g_oth, w_up, w_mix, w_down,
    u_act, d_slope, d_yproj, normed_t, dy_own, dy_oth, ga, na, acc,
):
    j = pl.program_id(0)
    own = n_own.shape[0]

    @pl.when(j == 0)
    def _():
        for h, (n, g) in enumerate(((n_own, g_own), (n_oth, g_oth))):
            na[h * own : (h + 1) * own, :] = n[...]
            ga[h * own : (h + 1) * own, :] = g[...]
            normed_t[:, h * own : (h + 1) * own] = n[...].T

    u = mm(na[...], w_up[...])
    d = mm(ga[...], w_down[...], NT)
    cdf = gauss_cdf(u)
    act = u * cdf
    u_act[...] = act.astype(bf16)
    d_slope[...] = (d * (cdf + u * gauss_pdf(u))).astype(bf16)
    dyp = (d * act).astype(bf16)
    d_yproj[...] = dyp
    part = mm(dyp, w_mix[...], NT)

    @pl.when(j == 0)
    def _():
        acc[...] = part

    @pl.when(j > 0)
    def _():
        acc[...] += part

    @pl.when(j == pl.num_programs(0) - 1)
    def _():
        shape = (dy_own.shape[0], dy_own.shape[2], T)
        for q in range(dy_own.shape[1]):
            dy_own[:, q] = acc[q * T : (q + 1) * T, :].T.reshape(shape)
            dy_oth[:, q] = acc[own + q * T : own + (q + 1) * T, :].T.astype(bf16).reshape(shape)


def gate_call(core, normed, normed_oth, grad, grad_oth, w_up, w_mix, w_down, row_n, chan_n):
    own, width = normed.shape
    inner, ff = w_mix.shape
    per = ff // row_n // TILE
    half = ff // 2
    col = lambda j, s: (2 * (j // per) + s[0]) * per + j % per
    tok = whole((own, width))
    tile = pl.BlockSpec((2 * own, TILE), lambda j, s: (0, j))
    spread = (chan_n, own // T, inner // chan_n, T)
    return call(
        gate_kernel,
        "gate",
        (half // TILE,),
        [
            tok,
            tok,
            tok,
            tok,
            pl.BlockSpec((width, TILE), lambda j, s: (0, col(j, s))),
            pl.BlockSpec((inner, TILE), lambda j, s: (0, col(j, s))),
            pl.BlockSpec((TILE, width), lambda j, s: (col(j, s), 0)),
        ],
        [tile, tile, tile, whole((width, 2 * own)), whole(spread), whole(spread), whole((2 * own, width))],
        [in_hbm((2 * own, half), bf16)] * 3
        + [in_hbm((width, 2 * own), bf16), in_hbm(spread, f32), in_hbm(spread, bf16)]
        + [in_hbm((2 * own, width), bf16)],
        from_hbm(normed, normed_oth, grad, grad_oth, w_up, w_mix, w_down),
        scalars=core,
        scratch=[
            pltpu.VMEM((2 * own, width), bf16),
            pltpu.VMEM((2 * own, inner), f32),
        ],
        vmem=56,
    )


def mine_a(s):
    return jnp.where(s[0] == 0, s[1], s[2])


def mine_b(s):
    return jnp.where(s[0] == 0, s[2], s[1])


def row_block(s, a, b, core, high, low):
    x = jnp.where(s[0] == 0, a, b)
    y = jnp.where(s[0] == 0, b, a)
    return x * 16 + core * 8 + high * 4 + low * 2 + y


def mid_kernel(
    s, y_own, y_oth, w_mix, u_act, d_slope, d_yproj, normed_t,
    gate, d_upre, u_give, u_keep, m_give, m_keep, yt, yn, us, ms,
):
    inner = yt.shape[0]

    own = yn.shape[0] // 2

    @pl.when(pl.program_id(0) == 0)
    def _():
        for h, y in enumerate((y_own, y_oth)):
            for q in range(y.shape[1]):
                part = y[:, q].reshape(inner, T)
                at = slice(h * own + q * T, h * own + (q + 1) * T)
                yt[:, at] = part
                yn[at, :] = part.T

    yp = mm(yn[...], w_mix[...])
    gate[...] = (u_act[...].astype(f32) * yp).astype(bf16)
    du = (d_slope[...].astype(f32) * yp).astype(bf16)
    d_upre[...] = du
    us[...] = mm(normed_t[...], du).astype(bf16)
    ms[...] = mm(yt[...], d_yproj[...]).astype(bf16)
    m = u_give.shape[1]
    for sel, out in ((1, u_give), (0, u_keep)):
        a = mine_a(s) ^ sel
        for b in (0, 1):
            for low in (0, 1):
                for high in (0, 1):
                    for core in (0, 1):
                        at = pl.multiple_of(row_block(s, a, b, core, high, low) * m, m)
                        out[b * 8 + low * 4 + high * 2 + core] = us[pl.ds(at, m), :]
    m = m_give.shape[1]
    for sel, out in ((1, m_give), (0, m_keep)):
        low = s[3] ^ sel
        for high in (0, 1):
            for a in (0, 1):
                for b in (0, 1):
                    for core in (0, 1):
                        at = pl.multiple_of(row_block(s, a, b, core, high, low) * m, m)
                        out[high * 8 + a * 4 + b * 2 + core] = ms[pl.ds(at, m), :]


def mid_call(scal, y_own, y_oth, w_mix, u_act, d_slope, d_yproj, normed_t, row_n):
    inner, ff = w_mix.shape
    half = u_act.shape[1]
    own = u_act.shape[0] // 2
    width = normed_t.shape[0]
    per = ff // row_n // TILE
    col = lambda j, s: (2 * (j // per) + s[0]) * per + j % per
    tile = pl.BlockSpec((2 * own, TILE), lambda j, s: (0, j))
    um, mx = width // 32, inner // 32
    ub = pl.BlockSpec((16, um, TILE), lambda j, s: (0, 0, j))
    mb = pl.BlockSpec((16, mx, TILE), lambda j, s: (0, 0, j))
    return call(
        mid_kernel,
        "mix_up",
        (half // TILE,),
        [
            whole(y_own.shape),
            whole(y_own.shape),
            pl.BlockSpec((inner, TILE), lambda j, s: (0, col(j, s))),
            tile,
            tile,
            tile,
            whole(normed_t.shape),
        ],
        [tile, tile, ub, ub, mb, mb],
        [in_hbm((2 * own, half), bf16)] * 2
        + [in_hbm((16, um, half), bf16)] * 2
        + [in_hbm((16, mx, half), bf16)] * 2,
        from_hbm(y_own, y_oth, w_mix, u_act, d_slope, d_yproj, normed_t),
        scalars=scal,
        scratch=[
            pltpu.VMEM((inner, 2 * own), bf16),
            pltpu.VMEM((2 * own, inner), bf16),
            pltpu.VMEM((width, TILE), bf16),
            pltpu.VMEM((inner, TILE), bf16),
        ],
        vmem=56,
        cost=10**10,
    )


def block_kernel(s, gate, d_upre, w_down, w_up, block_own, dn_own, oth, acc):
    j = pl.program_id(0)
    own = block_own.shape[0]
    sums = (mm(gate[...], w_down[...]), mm(d_upre[...], w_up[...], NT))

    @pl.when(j == 0)
    def _():
        for k in (0, 1):
            acc[k] = sums[k]

    @pl.when(j > 0)
    def _():
        for k in (0, 1):
            acc[k] += sums[k]

    @pl.when(j == pl.num_programs(0) - 1)
    def _():
        block_own[...] = acc[0, :own]
        dn_own[...] = acc[1, :own]
        oth[...] = acc[:, own:].astype(bf16)


def block_call(scal, gate, d_upre, w_down, w_up, row_n):
    ff, width = w_down.shape
    own = gate.shape[0] // 2
    part = ff // row_n
    tile = pl.BlockSpec((2 * own, part), lambda j, s: (0, j))
    return call(
        block_kernel,
        "block",
        (row_n // 2,),
        [
            tile,
            tile,
            pl.BlockSpec((part, width), lambda j, s: (2 * j + s[0], 0)),
            pl.BlockSpec((width, part), lambda j, s: (0, 2 * j + s[0])),
        ],
        [whole((own, width)), whole((own, width)), whole((2, own, width))],
        [in_hbm((own, width), f32), in_hbm((own, width), f32), in_hbm((2, own, width), bf16)],
        from_hbm(gate, d_upre, w_down, w_up),
        scalars=scal,
        scratch=[pltpu.VMEM((2, 2 * own, width), f32)],
        vmem=56,
    )


def down_val_kernel(s, down_g, down_k, v_own, v_oth, normed_t, d_give, d_keep, vs, vt):
    i = pl.program_id(0)
    inner, pair = vt.shape
    m = vs.shape[0] // 32
    rows = down_g.shape[0]

    @pl.when(i == 0)
    def _():
        for h, v in enumerate((v_own, v_oth)):
            for q in range(v.shape[1]):
                at = h * pair // 2 + q * T
                vt[:, at : at + T] = v[:, q].reshape(inner, T)
        vs[...] = mm(normed_t[...], vt[...], NT)

    b, low, high = i // 4, (i // 2) % 2, i % 2
    for sel, down, out in ((1, down_g, d_give), (0, down_k, d_keep)):
        out[0, 0:rows, :] = down[...]
        a = mine_a(s) ^ sel
        cut = []
        for core in (0, 1):
            at = pl.multiple_of(row_block(s, a, b, core, high, low) * m, m)
            cut.append(vs[pl.ds(at, m), :])
        parts = [jnp.concatenate([c[r * 8 : r * 8 + 8] for c in cut], 0) for r in range(m // 8)]
        out[0, rows : rows + 16, :] = jnp.concatenate(parts, 1).astype(bf16)


def down_val_call(scal, down, d_vpre, v_oth, normed_t):
    half = v_oth.shape
    inner = half[0] * half[2]
    width, pair = normed_t.shape
    rows = down.shape[0] // 16

    def block_of(sel):
        def at(i, s):
            a, b, low, high = mine_a(s) ^ sel, i // 4, (i // 2) % 2, i % 2
            x = jnp.where(s[0] == 0, a, b)
            y = jnp.where(s[0] == 0, b, a)
            return x * 8 + high * 4 + low * 2 + y, 0

        return pl.BlockSpec((rows, width), at)

    buf = (8, rows + 16, width)
    out = pl.BlockSpec((1, rows + 16, width), lambda i, s: (i, 0, 0))
    return call(
        down_val_kernel,
        "down_val",
        (8,),
        [
            block_of(1),
            block_of(0),
            pl.BlockSpec(half, lambda i, s: (s[0], 0, 0, 0)),
            whole(half),
            whole(normed_t.shape),
        ],
        [out, out],
        [struct(buf, bf16)] * 2,
        (down, down, d_vpre, v_oth, normed_t),
        scalars=scal,
        scratch=[pltpu.VMEM((width, inner), f32), pltpu.VMEM((inner, pair), bf16)],
    )


def step_kernel(bit, keep_g, got_g, keep_k, got_k, give, keep):
    give[...] = (keep_g[0].astype(f32) + got_g[0].astype(f32)).astype(bf16)
    keep[...] = (keep_k[0].astype(f32) + got_k[0].astype(f32)).astype(bf16)


def step_call(bit, keep, got):
    n, rows, cols = keep.shape
    n //= 2
    nb = max(1, n // 4)
    view = (2, n, rows, cols)
    other = pl.BlockSpec((1, nb, rows, cols), lambda i, b: (1 - b[0], i, 0, 0))
    same = pl.BlockSpec((1, nb, rows, cols), lambda i, b: (b[0], i, 0, 0))
    out = pl.BlockSpec((nb, rows, cols), lambda i, b: (i, 0, 0))
    keep, got = keep.reshape(view), got.reshape(view)
    return call(
        step_kernel,
        "halve",
        (n // nb,),
        [other, other, same, same],
        [out, out],
        [struct((n, rows, cols), bf16)] * 2,
        (keep, got, keep, got),
        scalars=bit,
    )


def tail_kernel(
    tok, grad, gain, block_own, got, dn_own, d_vpre, w_val, block_out, tokens_grad, norm_part, acc
):
    i = pl.program_id(0)
    x = tok[...].astype(f32)
    x_hat, inv_std = normalise(x)
    block_out[...] = (x + block_own[...] + got[0].astype(f32)).astype(bf16)
    dv = d_vpre[...].reshape(w_val.shape[1], T).T
    dn = dn_own[...] + got[1].astype(f32) + mm(dv, w_val[...], NT)
    dx = dn * gain[...]
    tokens_grad[...] = grad[...].astype(f32) + inv_std * (
        dx
        - jnp.mean(dx, axis=1, keepdims=True)
        - x_hat * jnp.mean(dx * x_hat, axis=1, keepdims=True)
    )
    sums = jnp.concatenate(
        [jnp.sum(dn * x_hat, axis=0, keepdims=True), jnp.sum(dn, axis=0, keepdims=True)], 0
    )

    @pl.when(i == 0)
    def _():
        acc[...] = sums

    @pl.when(i > 0)
    def _():
        acc[...] += sums

    @pl.when(i == pl.num_programs(0) - 1)
    def _():
        parts, lanes = norm_part.shape
        w = acc.shape[1] // parts
        for k in range(parts):
            cut = acc[:, k * w : (k + 1) * w]
            blank = jnp.zeros((1, lanes - 2 * w), f32)
            norm_part[k : k + 1, :] = jnp.concatenate([cut[0:1], cut[1:2], blank], 1)


def tail_call(tokens, grad, gain, block_own, got, dn_own, d_vpre, w_val, parts):
    own, width = tokens.shape
    rows = pl.BlockSpec((T, width), lambda i: (i, 0))
    chan_n, _, group, _ = d_vpre.shape
    return call(
        tail_kernel,
        "norm_back",
        (own // T,),
        [
            rows,
            rows,
            whole((1, width)),
            rows,
            pl.BlockSpec((2, T, width), lambda i: (0, i, 0)),
            rows,
            pl.BlockSpec((chan_n, 1, group, T), lambda i: (0, i, 0, 0)),
            whole(w_val.shape),
        ],
        [rows, rows, whole((parts, T))],
        [struct((own, width), bf16), struct((own, width), f32), struct((parts, T), f32)],
        from_hbm(tokens, grad, gain[None], block_own, got, dn_own, d_vpre, w_val),
        scratch=[pltpu.VMEM((2, width), f32)],
    )


def finish_kernel(s, u_keep, u_got, m_keep, m_got, d_keep, d_got, norm, down, mine, other):
    d = d_keep[0].astype(f32) + d_got[0].astype(f32)
    rows = down.shape[0]
    down[...] = d[:rows]
    half = d.shape[1]
    um, mx = u_keep.shape[1], m_keep.shape[1]
    tail = um + mx + 8
    for out, core, owner in ((mine, s[0], s[5]), (other, 1 - s[0], s[6])):
        out[0:um, :] = u_keep[core].astype(f32) + u_got[core].astype(f32)
        out[um : um + mx, :] = m_keep[core].astype(f32) + m_got[core].astype(f32)
        out[um + mx : tail, 0:half] = jnp.where(core == 0, d[rows : rows + 8], d[rows + 8 :])
        out[um + mx : tail, half:] = jnp.zeros((8, out.shape[1] - half), f32)
        out[tail:, :] = jnp.zeros((8, out.shape[1]), f32)
        out[tail : tail + 1, 0:T] = norm[pl.ds(owner, 1), :]


def finish_call(scal, up, mix, down, norm):
    um, mx, half = up[0].shape[1], mix[0].shape[1], up[0].shape[2]
    rows, width = down[0].shape[1:]
    args = (*up, *mix, *down, norm)
    pack = (um + mx + 16, half)
    return call(
        finish_kernel,
        "finish",
        (1,),
        [whole(a.shape) for a in args],
        [whole((rows - 16, width)), whole(pack), whole(pack)],
        [struct((rows - 16, width), f32), struct(pack, f32), struct(pack, f32)],
        args,
        scalars=scal,
    )


def join_kernel(s, mine, got, up, mix, val, norm):
    um, mx = up.shape[0], mix.shape[0]
    first = s[0] == 0
    part = mine.shape[1] // 2
    for core in (0, 1):
        held = jnp.where(first, mine[...], got[...]) if core == 0 else jnp.where(first, got[...], mine[...])
        for x in (0, 1):
            to = slice((2 * x + core) * part, (2 * x + core + 1) * part)
            up[:, to] = held[0:um, x * part : (x + 1) * part]
            mix[:, to] = held[um : um + mx, x * part : (x + 1) * part]
        w = val.shape[1] // 2
        for r in range(val.shape[0] // 8):
            at = slice(r * w, (r + 1) * w)
            val[r * 8 : r * 8 + 8, core * w : (core + 1) * w] = held[um + mx : um + mx + 8, at]
    norm[...] = mine[um + mx + 8 :, 0:T] + got[um + mx + 8 :, 0:T]


def join_call(scal, mine, got, um, mx, inner):
    ff = mine.shape[1] * 2
    return call(
        join_kernel,
        "join",
        (1,),
        [whole(mine.shape)] * 2,
        [whole((um, ff)), whole((mx, ff)), whole((um, inner)), whole((8, T))],
        [
            struct((um, ff), f32),
            struct((mx, ff), f32),
            struct((um, inner), f32),
            struct((8, T), f32),
        ],
        (mine, got),
        scalars=scal,
    )


def make_square(row_n, chan_n):
    def on_device(
        tokens, starts, layer_norm_gain, ln_bias, w_up, w_val, w_mix, w_down,
        decay_rate, mix_coef, out_grad,
    ):
        own, width = tokens.shape
        inner = w_val.shape[1]
        row, chan = lax.axis_index("row"), lax.axis_index("chan")
        core = row % 2
        me = row * chan_n + chan
        there = (row ^ 1) * chan_n + chan
        scal = jnp.stack([core, row // 2, chan % 2, (chan // 2) % 2, chan // 4, me, there])
        scal = scal.astype(jnp.int32)
        bit_x, bit_y = scal[1], scal[2]
        bit_a = jnp.where(core == 0, bit_x, bit_y).reshape(1)
        bit_b = jnp.where(core == 0, bit_y, bit_x).reshape(1)
        bit_low, bit_high = scal[3:4], scal[4:5]
        devices = [(r, c) for r in range(row_n) for c in range(chan_n)]
        flip_x = lambda r, c: (r ^ 2, c)
        flip_y = lambda r, c: (r, c ^ 1)
        moves = dict(
            core=lambda r, c: (r ^ 1, c),
            a=lambda r, c: flip_y(r, c) if r % 2 else flip_x(r, c),
            b=lambda r, c: flip_x(r, c) if r % 2 else flip_y(r, c),
            low=lambda r, c: (r, c ^ 2),
            high=lambda r, c: (r, c ^ 4),
            x=lambda r, c: (r ^ 2, c),
            ab=lambda r, c: (r ^ 2, c ^ 1),
            z=lambda r, c: (r, c ^ 6),
        )

        def send(value, way):
            to = [moves[way](r, c) for r, c in devices]
            pairs = [(r * chan_n + c, t[0] * chan_n + t[1]) for (r, c), t in zip(devices, to)]
            return lax.ppermute(value, ("row", "chan"), pairs)

        after = lax.optimization_barrier
        trade = lambda v: lax.all_to_all(v, "chan", split_axis=0, concat_axis=0, tiled=True)
        rows = own * chan_n // T
        to_seq = lambda v: v.reshape(rows, inner // chan_n, T)
        to_tok = lambda v: v.reshape(chan_n, own // T, inner // chan_n, T)

        masks = ssm_masks(starts)
        grad_oth = send(out_grad, "core")
        normed, v_act, v_slope = norm_call(tokens, layer_norm_gain, ln_bias, w_val, chan_n)
        normed_oth = send(normed, "core")
        v_chan = to_seq(trade(v_act))
        u_act, d_slope, d_yproj, normed_t, dy_own, dy_oth, pair_grad = gate_call(
            scal, normed, normed_oth, out_grad, grad_oth, w_up, w_mix, w_down, row_n, chan_n
        )
        d_y = (dy_own + send(dy_oth, "core").astype(f32)).astype(bf16)
        v_chan, d_y = after((v_chan, d_y))
        d_y_chan = to_seq(trade(d_y))
        y_chan, states, toeplitz = ssm_fwd(v_chan, decay_rate, mix_coef, masks)
        y_chan, d_y_chan = after((y_chan, d_y_chan))
        y_own = trade(to_tok(y_chan))
        d_v_chan, rates = ssm_bwd(
            v_chan, d_y_chan, decay_rate, mix_coef, masks, states, toeplitz, row_n
        )
        y_own, d_v_chan = after((y_own, d_v_chan))
        y_oth = send(y_own, "core")
        y_oth, d_v_chan = after((y_oth, d_v_chan))
        d_v = trade(to_tok(d_v_chan))
        gate_out, d_upre, u_give, u_keep, m_give, m_keep = mid_call(
            scal, y_own, y_oth, w_mix, u_act, d_slope, d_yproj, normed_t, row_n
        )
        u_give, m_give, gate_out, d_v, rates = after((u_give, m_give, gate_out, d_v, rates))

        u_got = send(u_give, "a")
        m_got = send(m_give, "low")
        rates_give = lax.dynamic_index_in_dim(rates, 1 - core, 0, keepdims=False)
        rates_got = send(rates_give, "core")
        half = chan_n // 2
        other_half = lambda v: lax.dynamic_slice_in_dim(v, (1 - core) * half, half, 0)
        v_give = (other_half(d_v).astype(f32) * other_half(v_slope)).astype(bf16)
        v_got = send(v_give, "core")
        d_vpre = (d_v.astype(f32) * v_slope).astype(bf16)
        down = mm(gate_out, pair_grad, TN).astype(bf16)
        d_give, d_keep = down_val_call(scal, down, d_vpre, v_got, normed_t)
        u_got, m_got, d_give, gate_out, rates_got = after(
            (u_got, m_got, d_give, gate_out, rates_got)
        )

        d_got = send(d_give, "a")
        m_give, m_keep = step_call(bit_high, m_keep, m_got)
        m_got = send(m_give, "high")
        u_give, u_keep = step_call(bit_b, u_keep, u_got)
        block_own, dn_own, bd_give = block_call(scal, gate_out, d_upre, w_down, w_up, row_n)
        d_got, m_got, u_give, bd_give = after((d_got, m_got, u_give, bd_give))

        u_got = send(u_give, "b")
        bd_got = send(bd_give, "core")
        d_give, d_keep = step_call(bit_b, d_keep, d_got)
        rates = lax.dynamic_index_in_dim(rates, core, 0, keepdims=False) + rates_got
        rates_give = lax.dynamic_index_in_dim(rates, 1 - bit_x, 0, keepdims=False)
        block_out, tokens_grad, norm_part = tail_call(
            tokens, out_grad, layer_norm_gain, block_own, bd_got, dn_own, d_vpre, w_val,
            row_n * chan_n,
        )
        u_got, d_give, norm_part, rates_give = after((u_got, d_give, norm_part, rates_give))

        rates_got = send(rates_give, "x")
        d_got = send(d_give, "b")
        u_give, u_keep = step_call(bit_low, u_keep, u_got)
        u_got = send(u_give, "low")
        m_give, m_keep = step_call(bit_a, m_keep, m_got)
        norm_part = norm_part + send(norm_part, "low")
        d_got, u_got, m_give, norm_part, rates_got = after(
            (d_got, u_got, m_give, norm_part, rates_got)
        )
        rates = lax.dynamic_index_in_dim(rates, bit_x, 0, keepdims=False) + rates_got

        d_give, d_keep = step_call(bit_low, d_keep, d_got)
        d_got = send(d_give, "low")
        u_give, u_keep = step_call(bit_high, u_keep, u_got)
        u_got = send(u_give, "high")
        m_got = send(m_give, "a")
        norm_part = norm_part + send(norm_part, "a")
        norm_part = norm_part + send(norm_part, "b")
        d_got, m_got, u_got, norm_part = after((d_got, m_got, u_got, norm_part))

        d_give, d_keep = step_call(bit_high, d_keep, d_got)
        d_got = send(d_give, "high")
        m_give, m_keep = step_call(bit_b, m_keep, m_got)
        m_got = send(m_give, "b")
        norm_part = norm_part + send(norm_part, "high")
        d_got, m_got, norm_part = after((d_got, m_got, norm_part))

        down_grad, mine, other = finish_call(
            scal, (u_keep, u_got), (m_keep, m_got), (d_keep, d_got), norm_part
        )
        um, mx = u_keep.shape[1], m_keep.shape[1]
        other = send(other, "core")
        up_grad, mix_grad, val_grad, norm_sum = join_call(scal, mine, other, um, mx, inner)
        norm_sum = norm_sum[0]
        w = width // (row_n * chan_n)
        return (
            block_out,
            tokens_grad,
            norm_sum[:w],
            norm_sum[w : 2 * w],
            up_grad,
            val_grad,
            mix_grad,
            down_grad,
            rates[0],
            rates[1],
        )

    return on_device


def make_general(row_n, chan_n):
    row_hi = row_n // 2

    def swap(value, axis, bit):
        size = row_n if axis == "row" else chan_n
        return lax.ppermute(value, axis, [(i, i ^ (1 << bit)) for i in range(size)])

    def core_swap(value):
        return swap(value, "row", 0)

    def bits_of(size):
        return size.bit_length() - 1

    def scatter_sum(part, names, order, last_dtype):
        names = list(names)
        for step, name in enumerate(order):
            axis, bit = name
            dim = names.index(name)
            mine = (lax.axis_index(axis) >> bit) & 1
            keep = lax.dynamic_index_in_dim(part, mine, dim, keepdims=False)
            give = lax.dynamic_index_in_dim(part, 1 - mine, dim, keepdims=False)
            got = swap(give, axis, bit)
            part = keep.astype(jnp.float32) + got.astype(jnp.float32)
            if step < len(order) - 1:
                part = part.astype(give.dtype)
            else:
                part = part.astype(last_dtype)
            names.pop(dim)
        return part

    row_bits = [("row", k) for k in range(bits_of(row_n) - 1, 0, -1)]
    core_bit = ("row", 0)
    chan_bits = [("chan", k) for k in range(bits_of(chan_n) - 1, -1, -1)]
    near_y = chan_bits[2:]
    along_z = chan_bits[:2][::-1]

    def on_device(
        tokens,
        starts,
        layer_norm_gain,
        ln_bias,
        w_up,
        w_val,
        w_mix,
        w_down,
        decay_rate,
        mix_coef,
        out_grad,
    ):
        own, width = tokens.shape
        ff = w_up.shape[1]
        inner = w_val.shape[1]
        part_ff = ff // row_n
        core = lax.axis_index("row") % 2
        mm = lambda a, b, ca, cb: lax.dot_general(
            a, b, (((ca,), (cb,)), ((), ())), preferred_element_type=jnp.float32
        )
        masks = ssm_masks(starts)
        inputs_f = tokens.astype(jnp.float32)
        row_mean = jnp.mean(inputs_f, axis=1, keepdims=True)
        centred = inputs_f - row_mean
        inv_std = lax.rsqrt(jnp.mean(centred * centred, axis=1, keepdims=True) + epsilon)
        x_hat = centred * inv_std
        normed = (x_hat * layer_norm_gain + ln_bias).astype(jnp.bfloat16)
        v_pre = mm(w_val, normed, 0, 1)
        v_cdf = gauss_cdf(v_pre)
        v_act = (v_pre * v_cdf).astype(jnp.bfloat16)
        v_slope = v_cdf + v_pre * gauss_pdf(v_pre)
        v_chan = lax.all_to_all(
            v_act.reshape(inner, own // T, T), "chan", split_axis=0, concat_axis=1, tiled=True
        )
        v_chan = jnp.swapaxes(v_chan, 0, 1)
        pair_normed = jnp.concatenate([normed, core_swap(normed)], 0)
        pair_grad = jnp.concatenate([out_grad, core_swap(out_grad)], 0)
        halves = lambda w, d: lax.dynamic_index_in_dim(
            w.reshape(w.shape[:d] + (row_hi, 2, part_ff) + w.shape[d + 1 :]), core, d + 1, keepdims=False
        ).reshape(w.shape[:d] + (ff // 2,) + w.shape[d + 1 :])
        up_half = halves(w_up, 1)
        mix_half = halves(w_mix, 1)
        down_half = halves(w_down, 0)
        u_pre = mm(pair_normed, up_half, 1, 0)
        d_gate = mm(pair_grad, down_half, 1, 1)
        u_cdf = gauss_cdf(u_pre)
        u_act = u_pre * u_cdf
        d_yproj = (d_gate * u_act).astype(jnp.bfloat16)
        d_slope = d_gate * (u_cdf + u_pre * gauss_pdf(u_pre))
        d_y_part = mm(mix_half, d_yproj, 1, 1)
        d_y = (
            d_y_part[:, :own] + core_swap(d_y_part[:, own:].astype(jnp.bfloat16)).astype(jnp.float32)
        ).astype(jnp.bfloat16)
        d_y_chan = lax.all_to_all(
            d_y.reshape(inner, own // T, T), "chan", split_axis=0, concat_axis=1, tiled=True
        )
        d_y_chan = jnp.swapaxes(d_y_chan, 0, 1)
        y_chan, states, toeplitz = ssm_fwd(v_chan, decay_rate, mix_coef, masks)
        y_chan = jnp.swapaxes(y_chan, 0, 1)
        y_own = lax.all_to_all(y_chan, "chan", split_axis=1, concat_axis=0, tiled=True)
        y_own = y_own.reshape(inner, own)
        d_v_chan, rates = ssm_bwd(
            v_chan, d_y_chan, decay_rate, mix_coef, masks, states, toeplitz, row_n
        )
        d_v_chan = jnp.swapaxes(d_v_chan, 0, 1)
        d_v = lax.all_to_all(d_v_chan, "chan", split_axis=1, concat_axis=0, tiled=True)
        pair_y = jnp.concatenate([y_own, core_swap(y_own)], 1)
        split_rows = lambda a, lead: a.reshape((2,) * lead + (-1,) + a.shape[1:])
        y_proj = mm(pair_y, mix_half, 0, 0)
        gate_out = (u_act * y_proj).astype(jnp.bfloat16)
        d_upre = (d_slope * y_proj).astype(jnp.bfloat16)
        mix_part = mm(pair_y, d_yproj, 1, 0).astype(jnp.bfloat16)
        down_part = mm(gate_out, pair_grad, 0, 0).astype(jnp.bfloat16)
        up_part = mm(pair_normed, d_upre, 0, 0).astype(jnp.bfloat16)
        all_names = row_bits + [core_bit] + chan_bits
        no_core = row_bits + chan_bits
        lead = len(all_names)
        mix_sum = scatter_sum(
            split_rows(mix_part, lead), all_names, along_z + row_bits + near_y, jnp.float32
        )
        up_sum = scatter_sum(
            split_rows(up_part, lead), all_names, row_bits + near_y + along_z, jnp.float32
        )
        down_grad = scatter_sum(
            split_rows(down_part, lead - 1), no_core, near_y + row_bits + along_z, jnp.float32
        )

        def join_cores(halfsum):
            mine = lax.dynamic_index_in_dim(halfsum, core, 0, keepdims=False)
            other = core_swap(lax.dynamic_index_in_dim(halfsum, 1 - core, 0, keepdims=False))
            shape = (mine.shape[0], row_hi, part_ff)
            low = jnp.where(core == 0, mine, other).reshape(shape)
            high = jnp.where(core == 0, other, mine).reshape(shape)
            return jnp.stack([low, high], 2).reshape(mine.shape[0], ff)

        block_part = mm(gate_out, down_half, 1, 0)
        block_out = (
            inputs_f
            + block_part[:own]
            + core_swap(block_part[own:].astype(jnp.bfloat16)).astype(jnp.float32)
        ).astype(jnp.bfloat16)
        d_normed_part = mm(d_upre, up_half, 1, 1)
        d_normed_got = core_swap(d_normed_part[own:].astype(jnp.bfloat16)).astype(jnp.float32)
        d_vpre = (d_v.reshape(inner, own).astype(jnp.float32) * v_slope).astype(jnp.bfloat16)
        val_part = mm(normed, d_vpre, 0, 1).astype(jnp.bfloat16)
        val_grad = scatter_sum(
            split_rows(val_part, lead),
            all_names,
            [core_bit] + along_z + near_y + row_bits,
            jnp.float32,
        )
        d_normed = d_normed_part[:own] + d_normed_got + mm(d_vpre, w_val, 0, 1)
        norm_part = jnp.stack([jnp.sum(d_normed * x_hat, axis=0), jnp.sum(d_normed, axis=0)], 1)
        norm_sum = scatter_sum(
            split_rows(norm_part, lead), all_names, [core_bit] + row_bits + chan_bits, jnp.float32
        )
        d_xh = d_normed * layer_norm_gain
        tokens_grad = out_grad.astype(jnp.float32) + inv_std * (
            d_xh
            - jnp.mean(d_xh, axis=1, keepdims=True)
            - x_hat * jnp.mean(d_xh * x_hat, axis=1, keepdims=True)
        )
        row_all = [core_bit] + row_bits
        chans, lanes = rates.shape[-2:]
        rates = rates.reshape((2,) * len(row_all) + (2 * chans, lanes))
        rates = scatter_sum(rates, row_all, row_all, jnp.float32).reshape(2, chans, lanes)
        return (
            block_out,
            tokens_grad,
            norm_sum[:, 0],
            norm_sum[:, 1],
            join_cores(up_sum),
            val_grad,
            join_cores(mix_sum),
            down_grad,
            rates[0],
            rates[1],
        )

    return on_device


def solution(mesh):
    spread = P(("row", "chan"), None)
    row_n, chan_n = mesh.shape["row"], mesh.shape["chan"]
    make = make_square if (row_n, chan_n) == (4, 8) else make_general
    return jax.shard_map(
        make(row_n, chan_n),
        mesh=mesh,
        in_specs=(
            spread,
            P("row", None),
            P(),
            P(),
            P(),
            P(),
            P(),
            P(),
            P("chan", None),
            P("chan", None),
            spread,
        ),
        out_specs=(
            spread,
            spread,
            P(("row", "chan")),
            P(("row", "chan")),
            spread,
            spread,
            spread,
            spread,
            P("chan", "row"),
            P("chan", "row"),
        ),
        check_vma=False,
    )
```

```python
import jax
import jax.numpy as jnp
from jax import lax
from jax.experimental import pallas as pl
from jax.experimental.pallas import tpu as pltpu
from jax.sharding import PartitionSpec as P

T = 128
SUB = 8
GROUP = 16
SEG = 4
f32 = jnp.float32
bf16 = jnp.bfloat16
NT = (((1,), (1,)), ((), ()))
TN = (((0,), (0,)), ((), ()))
NN = (((1,), (0,)), ((), ()))


def mm(a, b, d=NN):
    return lax.dot_general(a, b, d, preferred_element_type=f32)


def iota(shape, d):
    return lax.broadcasted_iota(jnp.int32, shape, d)


def powers(rate_row, pt_ref, c):
    n = rate_row.shape[1]
    steps = iota((8, n), 0).astype(f32)
    r8 = jnp.broadcast_to(rate_row, (8, n))
    parts = [jnp.exp(-r8 * steps)]
    fade = jnp.exp(-8.0 * r8)
    while len(parts) < T // 8:
        parts = parts + [p * fade for p in parts]
        fade = fade * fade
    for i in range(0, len(parts), 2):
        pt_ref[c, i * 8 : i * 8 + 16, :] = jnp.concatenate(parts[i : i + 2], 0).astype(bf16)


def put(ref, c, val, rows):
    for q in range(val.shape[1] // T):
        ref[q, pl.ds(c, rows, stride=SUB), :] = val[:, q * T : (q + 1) * T]


def take(ref, c, rows):
    return jnp.concatenate(
        [ref[q, pl.ds(c, rows, stride=SUB), :] for q in range(ref.shape[0])], 1
    )


def tiles(v):
    return jnp.stack([v[:, q * T : (q + 1) * T] for q in range(v.shape[1] // T)])


def untile(v):
    return jnp.concatenate([v[q] for q in range(v.shape[0])], 1)


def flip_matrix():
    return (iota((T, T), 0) + iota((T, T), 1) == T - 1).astype(f32).astype(bf16)


def seg_masks(ins, g):
    return jnp.concatenate([(ins == g * SEG + k).astype(f32) for k in range(SEG)], 0)


def rep(x):
    return jnp.concatenate([x] * SEG, 0)


def fold(o, m, rows):
    o = o * m
    out = o[0:rows]
    for k in range(1, SEG):
        out = out + o[k * rows : (k + 1) * rows]
    return out


def far_part(a, p, rows):
    hi = a.astype(bf16)
    lo = (a - hi.astype(f32)).astype(bf16)
    o = mm(jnp.concatenate([hi, lo], 0), p, NT)
    return o[:rows] + o[rows:]


def lanes_of(ref, c, rows):
    return ref[pl.ds(c, rows, stride=GROUP), :]


def fwd_kernel(groups, keep, x, rate, coef, ins, insj, head, tailj, y, hs, toe, pt, ss, near, xs, kr):
    rows = ins.shape[0]
    n = rate.shape[1]
    flip = flip_matrix()
    xs[...] = x[...].astype(f32).reshape(rows * GROUP, T)
    tail = tailj[...]
    hd = head[...]
    m0 = seg_masks(ins[...], 0)
    m0b = m0.astype(bf16)
    tri = iota((T, T), 1) >= iota((T, T), 0)
    for sub in range(GROUP // SUB):
        lo = sub * SUB
        cf = coef[lo : lo + SUB, :]
        rt = rate[lo : lo + SUB, :]
        cfh = cf.astype(bf16)
        cfl = (cf - cfh.astype(f32)).astype(bf16)
        cf2 = jnp.concatenate([cfh, cfl], 0)
        xj = []
        for c in range(SUB):
            xc = lanes_of(xs, lo + c, rows).astype(bf16)
            xj.append(mm(xc, flip).astype(bf16) * tail)
        for c in range(SUB):
            powers(rt[c : c + 1], pt, c)
            k2 = mm(cf2, pt[c], NT)
            kr[c : c + 1, :] = k2[c : c + 1] + k2[SUB + c : SUB + c + 1]
        for c in range(SUB):
            put(ss, c, mm(xj[c], pt[c]), rows)
        for c in range(SUB):
            k = jnp.broadcast_to(kr[c : c + 1, :], (T, T))
            kb = pltpu.roll(k, 0, 1, stride=1, stride_axis=0)
            tp = jnp.where(tri, kb, 0.0).astype(bf16)
            toe[lo + c] = tp
            xc = lanes_of(xs, lo + c, rows).astype(bf16)
            near[c] = fold(mm(rep(xc) * m0b, tp), m0, rows)
        fade = tiles(jnp.exp(-float(T) * rt))
        ce = tiles(cf * jnp.exp(-rt))
        h = jnp.zeros((n // T, SUB, T), f32)
        for b in range(rows):
            w = slice(b * SUB, (b + 1) * SUB)
            hs[sub, :, w, :] = h
            s = ss[:, w, :]
            ss[:, w, :] = h * ce
            h = h * (fade * keep[b]) + s

        @pl.loop(1, groups[0])
        def _(g):
            m = seg_masks(ins[...], g)
            for c in range(SUB):
                xc = lanes_of(xs, lo + c, rows).astype(bf16)
                near[c] += fold(mm(rep(xc) * m.astype(bf16), toe[lo + c]), m, rows)

        for c in range(SUB):
            far = far_part(take(ss, c, rows), pt[c], rows)
            xs[pl.ds(lo + c, rows, stride=GROUP), :] = near[c] + hd * far
    y[...] = xs[...].reshape(rows, GROUP, T).astype(bf16)


def bwd_kernel(
    groups, keep, x, dy, rate, coef, ins, insj, head, tailj, hs, toe, *rest
):
    dv, rates, pt, s1, e0, e1, near, gacc, nr, xs, ys = rest[-11:]
    rows = ins.shape[0]
    n = rate.shape[1]
    flip = flip_matrix()
    xs[...] = x[...].astype(f32).reshape(rows * GROUP, T)
    ys[...] = dy[...].astype(f32).reshape(rows * GROUP, T)
    tail = tailj[...]
    hdb = head[...].astype(bf16)
    mn = seg_masks(ins[...], 0).astype(bf16)
    mj = seg_masks(insj[...], 0)
    mjb = mj.astype(bf16)
    lag = iota((rows, T), 1).astype(f32).astype(bf16)
    lag1 = (iota((rows, T), 1) + 1).astype(f32).astype(bf16)
    lagf = iota((1, T), 1).astype(f32)
    valid = iota((T, T), 0) + iota((T, T), 1) >= T - 1
    row16 = iota((16, T), 0)

    def lags(d, xx, md, mx):
        o = mm(rep(d) * md, rep(xx) * mx, TN)
        o = pltpu.roll(jnp.where(valid, o, 0.0), 1, 1, stride=1, stride_axis=0)
        return jnp.sum(o, axis=0, keepdims=True)

    for sub in range(GROUP // SUB):
        lo = sub * SUB
        rt = rate[lo : lo + SUB, :]
        cf = coef[lo : lo + SUB, :]
        xa = jnp.concatenate([lanes_of(xs, lo + c, rows) for c in range(SUB)], 0).astype(bf16)
        da = jnp.concatenate([lanes_of(ys, lo + c, rows) for c in range(SUB)], 0).astype(bf16)
        xja = mm(xa, flip).astype(bf16)
        dja = mm(da, flip).astype(bf16)
        for c in range(SUB):
            sl = slice(c * rows, (c + 1) * rows)
            near[c] = fold(mm(rep(dja[sl]) * mjb, toe[lo + c]), mj, rows)
            gacc[c : c + 1, :] = lags(da[sl], xja[sl], mn, mjb)

        @pl.loop(1, groups[0])
        def _(g):
            m = seg_masks(ins[...], g).astype(bf16)
            k = seg_masks(insj[...], g)
            kb = k.astype(bf16)
            for c in range(SUB):
                d = lanes_of(ys, lo + c, rows).astype(bf16)
                xx = lanes_of(xs, lo + c, rows).astype(bf16)
                dj = mm(d, flip).astype(bf16)
                xj = mm(xx, flip).astype(bf16)
                near[c] += fold(mm(rep(dj) * kb, toe[lo + c]), k, rows)
                gacc[c : c + 1, :] += lags(d, xj, m, kb)

        for c in range(SUB):
            sl = slice(c * rows, (c + 1) * rows)
            powers(rt[c : c + 1], pt, c)
            gr = gacc[c : c + 1, :]
            gl = gr * lagf
            gh = gr.astype(bf16).astype(f32)
            glh = gl.astype(bf16).astype(f32)
            gm = jnp.where(row16 == 2, glh, jnp.where(row16 == 3, gl - glh, 0.0))
            gm = jnp.where(row16 == 0, gh, jnp.where(row16 == 1, gr - gh, gm)).astype(bf16)
            dh = da[sl] * hdb
            o = mm(jnp.concatenate([xja[sl] * tail * lag, dh, dh * lag1, gm], 0), pt[c])
            put(s1, c, o[0:rows], rows)
            put(e0, c, o[rows : 2 * rows], rows)
            put(e1, c, o[2 * rows : 3 * rows], rows)
            k = 3 * rows
            nr[c : c + 1, :] = o[k : k + 1] + o[k + 1 : k + 2]
            nr[SUB + c : SUB + c + 1, :] = o[k + 2 : k + 3] + o[k + 3 : k + 4]
        fade = tiles(jnp.exp(-float(T) * rt))
        ee = tiles(jnp.exp(-rt))
        ce = tiles(cf) * ee
        zero = jnp.zeros((n // T, SUB, T), f32)
        dh, ac, ar, ae = zero, zero, zero, zero
        for b in range(rows - 1, -1, -1):
            w = slice(b * SUB, (b + 1) * SUB)
            h = hs[sub, :, w, :]
            e = e0[:, w, :]
            kf = fade * keep[b]
            ar = ar + dh * (kf * (float(T) * h) + s1[:, w, :])
            ae = ae + h * e1[:, w, :]
            ac = ac + h * e
            s1[:, w, :] = dh
            dh = ce * e + kf * dh
        for c in range(SUB):
            far = far_part(take(s1, c, rows), pt[c], rows)
            near[c] = near[c] + tail.astype(f32) * far
        dva = mm(near[...].reshape(SUB * rows, T).astype(bf16), flip)
        for c in range(SUB):
            xs[pl.ds(lo + c, rows, stride=GROUP), :] = dva[c * rows : (c + 1) * rows]
        cut = (lo, lo + SUB)
        dcoef = nr[0:SUB, :] + untile(ee * ac)
        drate = -(cf * nr[SUB : 2 * SUB, :] + untile(ar + ce * ae))
        lanes = rates.shape[-1]
        for row in range(n // lanes):
            at = slice(row * lanes, (row + 1) * lanes)
            rates[row % 2, row // 2, 0, cut[0] : cut[1], :] = drate[:, at]
            rates[row % 2, row // 2, 1, cut[0] : cut[1], :] = dcoef[:, at]
    dv[...] = xs[...].reshape(rows, GROUP, T).astype(bf16)


def ssm_masks(starts):
    seqs, length = starts.shape
    blocks = length // T
    rows = seqs * blocks
    st = starts.reshape(rows, T)
    tri = (iota((T, T), 0) <= iota((T, T), 1)).astype(bf16)
    ins = mm(st.astype(bf16), tri).astype(jnp.int32) - st[:, :1]
    cont = (st[:, :1] == 0) & (iota((rows, 1), 0) % blocks != 0)
    last = ins[:, -1:]
    head = ((ins == 0) & cont).astype(f32)
    back = (iota((T, T), 0) + iota((T, T), 1) == T - 1).astype(bf16)
    insj = mm(ins.astype(bf16), back).astype(jnp.int32)
    tailj = (insj == last).astype(bf16)
    keep = (cont & (last == 0)).astype(f32)[:, 0]
    groups = (jnp.max(last) // SEG + 1).reshape(1).astype(jnp.int32)
    return groups, keep, ins, insj, head, tailj


def ssm_specs(rows, n, first=0):
    full = pl.BlockSpec((rows, T), lambda i: (0, 0))
    return dict(
        sm=pl.BlockSpec(memory_space=pltpu.SMEM),
        full=full,
        ch=pl.BlockSpec((rows, GROUP, T), lambda i: (0, i + first, 0)),
        par=pl.BlockSpec((GROUP, n), lambda i: (i + first, 0)),
        hs=pl.BlockSpec((GROUP // SUB, n // T, rows * SUB, T), lambda i: (i + first, 0, 0, 0)),
        toe=pl.BlockSpec((GROUP, T, T), lambda i: (i + first, 0, 0)),
        big=pltpu.VMEM((n // T, rows * SUB, T), f32),
        pt=pltpu.VMEM((SUB, T, n), bf16),
        near=pltpu.VMEM((SUB, rows, T), f32),
        xs=pltpu.VMEM((rows * GROUP, T), f32),
        cost=pl.CostEstimate(flops=2 * 10**10, bytes_accessed=10**7, transcendentals=0),
    )


def ssm_fwd(x, rate, coef, masks):
    rows, chans, _ = x.shape
    n = rate.shape[1]
    s = ssm_specs(rows, n)
    return pl.pallas_call(
        fwd_kernel,
        grid=(chans // GROUP,),
        in_specs=[s["sm"], s["sm"], s["ch"], s["par"], s["par"]] + [s["full"]] * 4,
        out_specs=[s["ch"], s["hs"], s["toe"]],
        out_shape=[
            pltpu.HBM(x.shape, bf16),
            pltpu.HBM((chans // SUB, n // T, rows * SUB, T), f32),
            pltpu.HBM((chans, T, T), bf16),
        ],
        scratch_shapes=[s["pt"], s["big"], s["near"], s["xs"], pltpu.VMEM((SUB, T), f32)],
        compiler_params=pltpu.CompilerParams(vmem_limit_bytes=16 * 2**20),
        cost_estimate=s["cost"],
        name="ssm_fwd",
    )(masks[0], masks[1], x, rate, coef, *masks[2:])


def ssm_bwd(x, dy, rate, coef, masks, hs, toe, row_n, part=0, parts=1, held=()):
    rows, chans, _ = x.shape
    n = rate.shape[1]
    steps = chans // GROUP // parts
    s = ssm_specs(rows, n, part * steps)
    raw = pl.BlockSpec(memory_space=pl.ANY)
    return pl.pallas_call(
        bwd_kernel,
        grid=(steps,),
        in_specs=[s["sm"], s["sm"], s["ch"], s["ch"], s["par"], s["par"]]
        + [s["full"]] * 4
        + [s["hs"], s["toe"]]
        + [raw] * len(held),
        out_specs=[
            s["ch"],
            pl.BlockSpec((2, row_n // 2, 2, GROUP, n // row_n), lambda i: (0, 0, 0, i + part * steps, 0)),
        ],
        out_shape=[
            pltpu.HBM(x.shape, bf16),
            jax.ShapeDtypeStruct((2, row_n // 2, 2, chans, n // row_n), f32),
        ],
        scratch_shapes=[
            s["pt"],
            s["big"],
            s["big"],
            s["big"],
            s["near"],
            pltpu.VMEM((SUB, T), f32),
            pltpu.VMEM((2 * SUB, n), f32),
            s["xs"],
            s["xs"],
        ],
        compiler_params=pltpu.CompilerParams(vmem_limit_bytes=16 * 2**20),
        cost_estimate=s["cost"],
        input_output_aliases={12 + i: i for i in range(len(held))},
        name="ssm_bwd",
    )(masks[0], masks[1], x, dy, rate, coef, *masks[2:], *from_hbm(hs, toe), *held)


epsilon = 1e-05
TILE = 768
BLOCK_COLS = 256


def gauss_cdf(a):
    return 0.5 * (1.0 + lax.erf(a * 0.7071067811865476))


def gauss_pdf(a):
    return jnp.exp(-0.5 * a * a) * 0.3989422804014327


def struct(shape, dtype):
    return jax.ShapeDtypeStruct(shape, dtype)


def in_hbm(shape, dtype):
    return pltpu.HBM(shape, dtype)


def from_hbm(*arrays):
    return tuple(pltpu.with_memory_space_constraint(a, pltpu.HBM) for a in arrays)


def whole(shape):
    return pl.BlockSpec(shape, lambda *_: (0,) * len(shape))


def call(kernel, name, grid, ins, outs, out_shape, args, scalars=None, scratch=(), aliases=None, vmem=24, cost=None):
    lead = [] if scalars is None else [scalars]
    return pl.pallas_call(
        kernel,
        grid_spec=pltpu.PrefetchScalarGridSpec(
            num_scalar_prefetch=len(lead),
            grid=grid,
            in_specs=ins,
            out_specs=outs,
            scratch_shapes=list(scratch),
        ),
        out_shape=out_shape,
        input_output_aliases=aliases or {},
        compiler_params=pltpu.CompilerParams(vmem_limit_bytes=vmem * 2**20),
        cost_estimate=cost and pl.CostEstimate(flops=cost, bytes_accessed=10**7, transcendentals=0),
        name=name,
    )(*lead, *args)


def normalise(x):
    centred = x - jnp.mean(x, axis=1, keepdims=True)
    inv_std = lax.rsqrt(jnp.mean(centred * centred, axis=1, keepdims=True) + epsilon)
    return centred * inv_std, inv_std


def norm_kernel(tok, gain, bias, w_val, normed, v_act, v_slope):
    x_hat, _ = normalise(tok[...].astype(f32))
    n = (x_hat * gain[...] + bias[...]).astype(bf16)
    normed[...] = n
    v = mm(n, w_val[...])
    cdf = gauss_cdf(v)
    v_act[...] = (v * cdf).T.astype(bf16).reshape(v_act.shape)
    v_slope[...] = (cdf + v * gauss_pdf(v)).T.reshape(v_slope.shape)


def norm_call(tokens, gain, bias, w_val, chan_n):
    own, width = tokens.shape
    inner = w_val.shape[1]
    quads = own // T
    spread = (chan_n, quads, inner // chan_n, T)
    block = pl.BlockSpec((chan_n, 1, inner // chan_n, T), lambda i: (0, i, 0, 0))
    rows = pl.BlockSpec((T, width), lambda i: (i, 0))
    return call(
        norm_kernel,
        "norm_val",
        (quads,),
        [rows, whole((1, width)), whole((1, width)), whole(w_val.shape)],
        [rows, block, block],
        [struct((own, width), bf16), struct(spread, bf16), struct(spread, f32)],
        from_hbm(tokens, gain[None], bias[None], w_val),
    )


def gate_tile(normed, grad, w_up, w_mix, w_down, u_act, d_slope, d_yproj):
    u = mm(normed, w_up[...])
    d = mm(grad, w_down[...], NT)
    cdf = gauss_cdf(u)
    act = u * cdf
    u_act[...] = act.astype(bf16)
    d_slope[...] = (d * (cdf + u * gauss_pdf(u))).astype(bf16)
    dyp = (d * act).astype(bf16)
    d_yproj[...] = dyp
    return mm(dyp, w_mix[...], NT)


def gate_first_kernel(
    core, n_own, n_oth, g_own, g_oth, w_up, w_mix, w_down,
    u_act, d_slope, d_yproj, na, ga, acc,
):
    own = n_own.shape[0]
    for h, (n, g) in enumerate(((n_own, g_own), (n_oth, g_oth))):
        na[h * own : (h + 1) * own, :] = n[...]
        ga[h * own : (h + 1) * own, :] = g[...]
    acc[...] = gate_tile(na[...], ga[...], w_up, w_mix, w_down, u_act, d_slope, d_yproj)


def gate_last_kernel(
    core, na, ga, acc, w_up, w_mix, w_down, _u, _s, _d,
    u_act, d_slope, d_yproj, normed_t, dy_own, dy_oth, sums,
):
    j = pl.program_id(0)
    own = na.shape[0] // 2

    @pl.when(j == 0)
    def _():
        sums[...] = acc[...]
        normed_t[...] = na[...].T

    sums[...] += gate_tile(na[...], ga[...], w_up, w_mix, w_down, u_act, d_slope, d_yproj)

    @pl.when(j == pl.num_programs(0) - 1)
    def _():
        shape = (dy_own.shape[0], dy_own.shape[2], T)
        for q in range(dy_own.shape[1]):
            dy_own[:, q] = sums[q * T : (q + 1) * T, :].T.reshape(shape)
            dy_oth[:, q] = sums[own + q * T : own + (q + 1) * T, :].T.astype(bf16).reshape(shape)


def gate_specs(own, w_mix, row_n, first):
    inner, ff = w_mix.shape
    part = ff // row_n
    col = lambda j, s: 2 * (j + first) + s[0]
    return [
        lambda width: pl.BlockSpec((width, part), lambda j, s: (0, col(j, s))),
        pl.BlockSpec((inner, part), lambda j, s: (0, col(j, s))),
        lambda width: pl.BlockSpec((part, width), lambda j, s: (col(j, s), 0)),
        pl.BlockSpec((2 * own, part), lambda j, s: (0, j + first)),
    ]


def gate_first(core, normed, normed_oth, grad, grad_oth, w_up, w_mix, w_down, row_n):
    own, width = normed.shape
    inner, ff = w_mix.shape
    up, mix, down, tile = gate_specs(own, w_mix, row_n, 0)
    tok = whole((own, width))
    pair = (2 * own, width)
    return call(
        gate_first_kernel,
        "gate_first",
        (1,),
        [tok, tok, tok, tok, up(width), mix, down(width)],
        [tile, tile, tile, whole(pair), whole(pair), whole((2 * own, inner))],
        [in_hbm((2 * own, ff // 2), bf16)] * 3
        + [in_hbm(pair, bf16), in_hbm(pair, bf16), in_hbm((2 * own, inner), f32)],
        from_hbm(normed, normed_oth, grad, grad_oth, w_up, w_mix, w_down),
        scalars=core,
        vmem=44,
    )


def gate_last(core, pair_normed, pair_grad, acc, w_up, w_mix, w_down, held, row_n, chan_n):
    own, width = pair_normed.shape[0] // 2, pair_normed.shape[1]
    inner, ff = w_mix.shape
    up, mix, down, tile = gate_specs(own, w_mix, row_n, 1)
    pair = (2 * own, width)
    raw = pl.BlockSpec(memory_space=pl.ANY)
    spread = (chan_n, own // T, inner // chan_n, T)
    return call(
        gate_last_kernel,
        "gate_last",
        (row_n // 2 - 1,),
        [whole(pair), whole(pair), whole(acc.shape), up(width), mix, down(width), raw, raw, raw],
        [tile, tile, tile, whole((width, 2 * own)), whole(spread), whole(spread)],
        [in_hbm((2 * own, ff // 2), bf16)] * 3
        + [in_hbm((width, 2 * own), bf16), in_hbm(spread, f32), in_hbm(spread, bf16)],
        from_hbm(pair_normed, pair_grad, acc, w_up, w_mix, w_down, *held),
        scalars=core,
        scratch=[pltpu.VMEM(acc.shape, f32)],
        aliases={7: 0, 8: 1, 9: 2},
        vmem=48,
    )


def mine_a(s):
    return jnp.where(s[0] == 0, s[1], s[2])


def mine_b(s):
    return jnp.where(s[0] == 0, s[2], s[1])


def row_block(s, a, b, core, high, low):
    x = jnp.where(s[0] == 0, a, b)
    y = jnp.where(s[0] == 0, b, a)
    return x * 16 + core * 8 + high * 4 + low * 2 + y


def mid_kernel(
    s, y_own, y_oth, w_mix, u_act, d_slope, d_yproj, normed_t,
    gate, d_upre, u_give, u_keep, m_give, m_keep, yt, yn, us, ms,
):
    inner = yt.shape[0]

    own = yn.shape[0] // 2

    @pl.when(pl.program_id(0) == 0)
    def _():
        for h, y in enumerate((y_own, y_oth)):
            for q in range(y.shape[1]):
                part = y[:, q].reshape(inner, T)
                at = slice(h * own + q * T, h * own + (q + 1) * T)
                yt[:, at] = part
                yn[at, :] = part.T

    yp = mm(yn[...], w_mix[...])
    gate[...] = (u_act[...].astype(f32) * yp).astype(bf16)
    du = (d_slope[...].astype(f32) * yp).astype(bf16)
    d_upre[...] = du
    us[...] = mm(normed_t[...], du).astype(bf16)
    ms[...] = mm(yt[...], d_yproj[...]).astype(bf16)
    m = u_give.shape[1]
    for sel, out in ((1, u_give), (0, u_keep)):
        a = mine_a(s) ^ sel
        for b in (0, 1):
            for low in (0, 1):
                for high in (0, 1):
                    for core in (0, 1):
                        at = pl.multiple_of(row_block(s, a, b, core, high, low) * m, m)
                        out[b * 8 + low * 4 + high * 2 + core] = us[pl.ds(at, m), :]
    m = m_give.shape[1]
    for sel, out in ((1, m_give), (0, m_keep)):
        low = s[3] ^ sel
        for high in (0, 1):
            for a in (0, 1):
                for b in (0, 1):
                    for core in (0, 1):
                        at = pl.multiple_of(row_block(s, a, b, core, high, low) * m, m)
                        out[high * 8 + a * 4 + b * 2 + core] = ms[pl.ds(at, m), :]


def mid_call(scal, y_own, y_oth, w_mix, u_act, d_slope, d_yproj, normed_t, row_n):
    inner, ff = w_mix.shape
    half = u_act.shape[1]
    own = u_act.shape[0] // 2
    width = normed_t.shape[0]
    per = ff // row_n // TILE
    col = lambda j, s: (2 * (j // per) + s[0]) * per + j % per
    tile = pl.BlockSpec((2 * own, TILE), lambda j, s: (0, j))
    um, mx = width // 32, inner // 32
    ub = pl.BlockSpec((16, um, TILE), lambda j, s: (0, 0, j))
    mb = pl.BlockSpec((16, mx, TILE), lambda j, s: (0, 0, j))
    return call(
        mid_kernel,
        "mix_up",
        (half // TILE,),
        [
            whole(y_own.shape),
            whole(y_own.shape),
            pl.BlockSpec((inner, TILE), lambda j, s: (0, col(j, s))),
            tile,
            tile,
            tile,
            whole(normed_t.shape),
        ],
        [tile, tile, ub, ub, mb, mb],
        [in_hbm((2 * own, half), bf16)] * 2
        + [in_hbm((16, um, half), bf16)] * 2
        + [in_hbm((16, mx, half), bf16)] * 2,
        from_hbm(y_own, y_oth, w_mix, u_act, d_slope, d_yproj, normed_t),
        scalars=scal,
        scratch=[
            pltpu.VMEM((inner, 2 * own), bf16),
            pltpu.VMEM((2 * own, inner), bf16),
            pltpu.VMEM((width, TILE), bf16),
            pltpu.VMEM((inner, TILE), bf16),
        ],
        vmem=32,
        cost=10**10,
    )


def block_kernel(s, gate, d_upre, *refs):
    half = (len(refs) - 3) // 2
    downs, ups, (block_own, dn_own, oth) = refs[:half], refs[half : 2 * half], refs[2 * half :]
    own = block_own.shape[0]
    part = downs[0].shape[0]
    cut = lambda ref, k: ref[:, k * part : (k + 1) * part]
    block = sum(mm(cut(gate, k), w[...]) for k, w in enumerate(downs))
    dn = sum(mm(cut(d_upre, k), w[...], NT) for k, w in enumerate(ups))
    block_own[...] = block[:own]
    dn_own[...] = dn[:own]
    oth[0] = block[own:].astype(bf16)
    oth[1] = dn[own:].astype(bf16)


def block_call(scal, gate, d_upre, w_down, w_up, row_n):
    ff, width = w_down.shape
    own = gate.shape[0] // 2
    part = ff // row_n
    cols = BLOCK_COLS
    out = pl.BlockSpec((own, cols), lambda j, s: (0, j))
    ks = range(row_n // 2)
    return call(
        block_kernel,
        "block",
        (width // cols,),
        [whole(gate.shape), whole(d_upre.shape)]
        + [pl.BlockSpec((part, cols), lambda j, s, k=k: (2 * k + s[0], j)) for k in ks]
        + [pl.BlockSpec((cols, part), lambda j, s, k=k: (j, 2 * k + s[0])) for k in ks],
        [out, out, pl.BlockSpec((2, own, cols), lambda j, s: (0, 0, j))],
        [in_hbm((own, width), f32), in_hbm((own, width), f32), in_hbm((2, own, width), bf16)],
        from_hbm(gate, d_upre, *[w_down for _ in ks], *[w_up for _ in ks]),
        scalars=scal,
        vmem=36,
    )


def split_kernel(s, down_g, down_k, d_give, d_keep):
    d_give[0] = down_g[...]
    d_keep[0] = down_k[...]


def split_call(scal, down):
    rows, width = down.shape[0] // 16, down.shape[1]

    def block_of(sel):
        def at(i, s):
            a, b, low, high = mine_a(s) ^ sel, i // 4, (i // 2) % 2, i % 2
            x = jnp.where(s[0] == 0, a, b)
            y = jnp.where(s[0] == 0, b, a)
            return x * 8 + high * 4 + low * 2 + y, 0

        return pl.BlockSpec((rows, width), at)

    out = pl.BlockSpec((1, rows, width), lambda i, s: (i, 0, 0))
    return call(
        split_kernel,
        "split",
        (8,),
        [block_of(1), block_of(0)],
        [out, out],
        [struct((8, rows, width), bf16)] * 2,
        (down, down),
        scalars=scal,
    )


def val_kernel(s, v_own, v_oth, normed_t, v_give, v_keep, vs, vt):
    inner, pair = vt.shape
    for h, v in enumerate((v_own, v_oth)):
        for q in range(v.shape[1]):
            at = h * pair // 2 + q * T
            vt[:, at : at + T] = v[:, q].reshape(inner, T)
    vs[...] = mm(normed_t[...], vt[...], NT)
    m = vs.shape[0] // 32
    for sel, out in ((1, v_give), (0, v_keep)):
        a = mine_a(s) ^ sel
        for b in (0, 1):
            for low in (0, 1):
                for high in (0, 1):
                    cut = []
                    for core in (0, 1):
                        at = pl.multiple_of(row_block(s, a, b, core, high, low) * m, m)
                        cut.append(vs[pl.ds(at, m), :])
                    parts = [
                        jnp.concatenate([c[r * 8 : r * 8 + 8] for c in cut], 0)
                        for r in range(m // 8)
                    ]
                    out[b * 4 + low * 2 + high] = jnp.concatenate(parts, 1).astype(bf16)


def val_call(scal, d_vpre, v_oth, normed_t):
    half = v_oth.shape
    inner = half[0] * half[2]
    width, pair = normed_t.shape
    buf = (8, 16, width)
    return call(
        val_kernel,
        "val",
        (1,),
        [
            pl.BlockSpec(half, lambda i, s: (s[0], 0, 0, 0)),
            whole(half),
            whole(normed_t.shape),
        ],
        [whole(buf), whole(buf)],
        [struct(buf, bf16)] * 2,
        (d_vpre, v_oth, normed_t),
        scalars=scal,
        scratch=[pltpu.VMEM((width, inner), f32), pltpu.VMEM((inner, pair), bf16)],
    )


def step_kernel(bit, keep_g, got_g, keep_k, got_k, give, keep):
    give[...] = (keep_g[0].astype(f32) + got_g[0].astype(f32)).astype(bf16)
    keep[...] = (keep_k[0].astype(f32) + got_k[0].astype(f32)).astype(bf16)


def step_call(bit, keep, got):
    n, rows, cols = keep.shape
    n //= 2
    nb = max(1, n // 4)
    view = (2, n, rows, cols)
    other = pl.BlockSpec((1, nb, rows, cols), lambda i, b: (1 - b[0], i, 0, 0))
    same = pl.BlockSpec((1, nb, rows, cols), lambda i, b: (b[0], i, 0, 0))
    out = pl.BlockSpec((nb, rows, cols), lambda i, b: (i, 0, 0))
    keep, got = keep.reshape(view), got.reshape(view)
    return call(
        step_kernel,
        "halve",
        (n // nb,),
        [other, other, same, same],
        [out, out],
        [struct((n, rows, cols), bf16)] * 2,
        (keep, got, keep, got),
        scalars=bit,
    )


def tail_kernel(
    tok, grad, gain, block_own, got, dn_own, d_vpre, w_val, block_out, tokens_grad, norm_part, acc
):
    i = pl.program_id(0)
    x = tok[...].astype(f32)
    x_hat, inv_std = normalise(x)
    block_out[...] = (x + block_own[...] + got[0].astype(f32)).astype(bf16)
    dv = d_vpre[...].reshape(w_val.shape[1], T).T
    dn = dn_own[...] + got[1].astype(f32) + mm(dv, w_val[...], NT)
    dx = dn * gain[...]
    tokens_grad[...] = grad[...].astype(f32) + inv_std * (
        dx
        - jnp.mean(dx, axis=1, keepdims=True)
        - x_hat * jnp.mean(dx * x_hat, axis=1, keepdims=True)
    )
    sums = jnp.concatenate(
        [jnp.sum(dn * x_hat, axis=0, keepdims=True), jnp.sum(dn, axis=0, keepdims=True)], 0
    )

    @pl.when(i == 0)
    def _():
        acc[...] = sums

    @pl.when(i > 0)
    def _():
        acc[...] += sums

    @pl.when(i == pl.num_programs(0) - 1)
    def _():
        parts, lanes = norm_part.shape
        w = acc.shape[1] // parts
        for k in range(parts):
            cut = acc[:, k * w : (k + 1) * w]
            blank = jnp.zeros((1, lanes - 2 * w), f32)
            norm_part[k : k + 1, :] = jnp.concatenate([cut[0:1], cut[1:2], blank], 1)


def tail_call(tokens, grad, gain, block_own, got, dn_own, d_vpre, w_val, parts):
    own, width = tokens.shape
    rows = pl.BlockSpec((T, width), lambda i: (i, 0))
    chan_n, _, group, _ = d_vpre.shape
    return call(
        tail_kernel,
        "norm_back",
        (own // T,),
        [
            rows,
            rows,
            whole((1, width)),
            rows,
            pl.BlockSpec((2, T, width), lambda i: (0, i, 0)),
            rows,
            pl.BlockSpec((chan_n, 1, group, T), lambda i: (0, i, 0, 0)),
            whole(w_val.shape),
        ],
        [rows, rows, whole((parts, T))],
        [struct((own, width), bf16), struct((own, width), f32), struct((parts, T), f32)],
        from_hbm(tokens, grad, gain[None], block_own, got, dn_own, d_vpre, w_val),
        scratch=[pltpu.VMEM((2, width), f32)],
    )


def finish_kernel(s, u_keep, u_got, m_keep, m_got, d_keep, d_got, v_keep, v_got, norm, down, mine, other):
    down[...] = d_keep[0].astype(f32) + d_got[0].astype(f32)
    v = v_keep[0].astype(f32) + v_got[0].astype(f32)
    half = v.shape[1]
    um, mx = u_keep.shape[1], m_keep.shape[1]
    tail = um + mx + 8
    for out, core, owner in ((mine, s[0], s[5]), (other, 1 - s[0], s[6])):
        out[0:um, :] = u_keep[core].astype(f32) + u_got[core].astype(f32)
        out[um : um + mx, :] = m_keep[core].astype(f32) + m_got[core].astype(f32)
        out[um + mx : tail, 0:half] = jnp.where(core == 0, v[:8], v[8:])
        out[um + mx : tail, half:] = jnp.zeros((8, out.shape[1] - half), f32)
        out[tail:, :] = jnp.zeros((8, out.shape[1]), f32)
        out[tail : tail + 1, 0:T] = norm[pl.ds(owner, 1), :]


def finish_call(scal, up, mix, down, val, norm):
    um, mx, half = up[0].shape[1], mix[0].shape[1], up[0].shape[2]
    rows, width = down[0].shape[1:]
    args = (*up, *mix, *down, *val, norm)
    pack = (um + mx + 16, half)
    return call(
        finish_kernel,
        "finish",
        (1,),
        [whole(a.shape) for a in args],
        [whole((rows, width)), whole(pack), whole(pack)],
        [struct((rows, width), f32), struct(pack, f32), struct(pack, f32)],
        args,
        scalars=scal,
    )


def join_kernel(s, mine, got, up, mix, val, norm):
    um, mx = up.shape[0], mix.shape[0]
    first = s[0] == 0
    part = mine.shape[1] // 2
    for core in (0, 1):
        held = jnp.where(first, mine[...], got[...]) if core == 0 else jnp.where(first, got[...], mine[...])
        for x in (0, 1):
            to = slice((2 * x + core) * part, (2 * x + core + 1) * part)
            up[:, to] = held[0:um, x * part : (x + 1) * part]
            mix[:, to] = held[um : um + mx, x * part : (x + 1) * part]
        w = val.shape[1] // 2
        for r in range(val.shape[0] // 8):
            at = slice(r * w, (r + 1) * w)
            val[r * 8 : r * 8 + 8, core * w : (core + 1) * w] = held[um + mx : um + mx + 8, at]
    norm[...] = mine[um + mx + 8 :, 0:T] + got[um + mx + 8 :, 0:T]


def join_call(scal, mine, got, um, mx, inner):
    ff = mine.shape[1] * 2
    return call(
        join_kernel,
        "join",
        (1,),
        [whole(mine.shape)] * 2,
        [whole((um, ff)), whole((mx, ff)), whole((um, inner)), whole((8, T))],
        [
            struct((um, ff), f32),
            struct((mx, ff), f32),
            struct((um, inner), f32),
            struct((8, T), f32),
        ],
        (mine, got),
        scalars=scal,
    )


def make_square(row_n, chan_n):
    def on_device(
        tokens, starts, layer_norm_gain, ln_bias, w_up, w_val, w_mix, w_down,
        decay_rate, mix_coef, out_grad,
    ):
        own, width = tokens.shape
        inner = w_val.shape[1]
        row, chan = lax.axis_index("row"), lax.axis_index("chan")
        core = row % 2
        me = row * chan_n + chan
        there = (row ^ 1) * chan_n + chan
        scal = jnp.stack([core, row // 2, chan % 2, (chan // 2) % 2, chan // 4, me, there])
        scal = scal.astype(jnp.int32)
        bit_x, bit_y = scal[1], scal[2]
        bit_a = jnp.where(core == 0, bit_x, bit_y).reshape(1)
        bit_b = jnp.where(core == 0, bit_y, bit_x).reshape(1)
        bit_low, bit_high = scal[3:4], scal[4:5]
        devices = [(r, c) for r in range(row_n) for c in range(chan_n)]
        flip_x = lambda r, c: (r ^ 2, c)
        flip_y = lambda r, c: (r, c ^ 1)
        moves = dict(
            core=lambda r, c: (r ^ 1, c),
            a=lambda r, c: flip_y(r, c) if r % 2 else flip_x(r, c),
            b=lambda r, c: flip_x(r, c) if r % 2 else flip_y(r, c),
            low=lambda r, c: (r, c ^ 2),
            high=lambda r, c: (r, c ^ 4),
            x=lambda r, c: (r ^ 2, c),
            ab=lambda r, c: (r ^ 2, c ^ 1),
            z=lambda r, c: (r, c ^ 6),
        )

        def send(value, way):
            to = [moves[way](r, c) for r, c in devices]
            pairs = [(r * chan_n + c, t[0] * chan_n + t[1]) for (r, c), t in zip(devices, to)]
            return lax.ppermute(value, ("row", "chan"), pairs)

        after = lax.optimization_barrier
        trade = lambda v: lax.all_to_all(v, "chan", split_axis=0, concat_axis=0, tiled=True)
        rows = own * chan_n // T
        to_seq = lambda v: v.reshape(rows, inner // chan_n, T)
        to_tok = lambda v: v.reshape(chan_n, own // T, inner // chan_n, T)

        masks = ssm_masks(starts)
        grad_oth = send(out_grad, "core")
        normed, v_act, v_slope = norm_call(tokens, layer_norm_gain, ln_bias, w_val, chan_n)
        normed_oth = send(normed, "core")
        v_chan = to_seq(trade(v_act))
        *gated, pair_normed, pair_grad, acc = gate_first(
            scal, normed, normed_oth, out_grad, grad_oth, w_up, w_mix, w_down, row_n
        )
        v_chan, acc = after((v_chan, acc))
        y_chan, states, toeplitz = ssm_fwd(v_chan, decay_rate, mix_coef, masks)
        y_chan, acc = after((y_chan, acc))
        y_own = trade(to_tok(y_chan))
        u_act, d_slope, d_yproj, normed_t, dy_own, dy_oth = gate_last(
            scal, pair_normed, pair_grad, acc, w_up, w_mix, w_down, gated, row_n, chan_n
        )
        d_y = (dy_own + send(dy_oth, "core").astype(f32)).astype(bf16)
        y_own, d_y = after((y_own, d_y))
        y_oth = send(y_own, "core")
        d_y_chan = to_seq(trade(d_y))
        gate_out, d_upre, u_give, u_keep, m_give, m_keep = mid_call(
            scal, y_own, y_oth, w_mix, u_act, d_slope, d_yproj, normed_t, row_n
        )
        u_give, m_give, gate_out, d_y_chan = after((u_give, m_give, gate_out, d_y_chan))
        back = lambda part, held, d_y_chan: ssm_bwd(
            v_chan, d_y_chan, decay_rate, mix_coef, masks, states, toeplitz, row_n, part, 2, held
        )

        u_got = send(u_give, "a")
        m_got = send(m_give, "low")
        down = mm(gate_out, pair_grad, TN).astype(bf16)
        d_give, d_keep = split_call(scal, down)
        held = back(0, (), d_y_chan)
        u_got, m_got, d_give, gate_out, d_y_chan, *held = after(
            (u_got, m_got, d_give, gate_out, d_y_chan, *held)
        )

        d_got = send(d_give, "a")
        m_give, m_keep = step_call(bit_high, m_keep, m_got)
        m_got = send(m_give, "high")
        d_v_chan, rates = back(1, tuple(held), d_y_chan)
        u_give, u_keep = step_call(bit_b, u_keep, u_got)
        d_v_chan, u_give, gate_out, rates = after((d_v_chan, u_give, gate_out, rates))
        d_v = trade(to_tok(d_v_chan))
        d_got, m_got, u_give = after((d_got, m_got, u_give))
        u_got = send(u_give, "b")
        block_own, dn_own, bd_give = block_call(scal, gate_out, d_upre, w_down, w_up, row_n)
        d_give, d_keep = step_call(bit_b, d_keep, d_got)
        rates_give = lax.dynamic_index_in_dim(rates, 1 - core, 0, keepdims=False)
        rates_got = send(rates_give, "core")
        u_got, d_give, bd_give, d_v, rates_got = after((u_got, d_give, bd_give, d_v, rates_got))

        d_got = send(d_give, "b")
        u_give, u_keep = step_call(bit_low, u_keep, u_got)
        u_give, d_v, m_got = after((u_give, d_v, m_got))
        u_got = send(u_give, "low")
        half = chan_n // 2
        other_half = lambda v: lax.dynamic_slice_in_dim(v, (1 - core) * half, half, 0)
        v_give = (other_half(d_v).astype(f32) * other_half(v_slope)).astype(bf16)
        v_got = send(v_give, "core")
        bd_got = send(bd_give, "core")
        d_vpre = (d_v.astype(f32) * v_slope).astype(bf16)
        v_give, v_keep = val_call(scal, d_vpre, v_got, normed_t)
        v_got = send(v_give, "a")
        m_give, m_keep = step_call(bit_a, m_keep, m_got)
        rates = lax.dynamic_index_in_dim(rates, core, 0, keepdims=False) + rates_got
        rates_give = lax.dynamic_index_in_dim(rates, 1 - bit_x, 0, keepdims=False)
        d_got, u_got, m_give, v_got, rates_give, d_vpre, bd_got = after(
            (d_got, u_got, m_give, v_got, rates_give, d_vpre, bd_got)
        )

        rates_got = send(rates_give, "x")
        d_give, d_keep = step_call(bit_low, d_keep, d_got)
        d_got = send(d_give, "low")
        u_give, u_keep = step_call(bit_high, u_keep, u_got)
        u_got = send(u_give, "high")
        m_got = send(m_give, "a")
        v_give, v_keep = step_call(bit_b, v_keep, v_got)
        v_got = send(v_give, "b")
        block_out, tokens_grad, norm_part = tail_call(
            tokens, out_grad, layer_norm_gain, block_own, bd_got, dn_own, d_vpre, w_val,
            row_n * chan_n,
        )
        d_got, m_got, u_got, v_got, norm_part, rates_got = after(
            (d_got, m_got, u_got, v_got, norm_part, rates_got)
        )
        rates = lax.dynamic_index_in_dim(rates, bit_x, 0, keepdims=False) + rates_got

        d_give, d_keep = step_call(bit_high, d_keep, d_got)
        d_got = send(d_give, "high")
        m_give, m_keep = step_call(bit_b, m_keep, m_got)
        m_got = send(m_give, "b")
        v_give, v_keep = step_call(bit_low, v_keep, v_got)
        v_got = send(v_give, "low")
        norm_part = norm_part + send(norm_part, "a") + send(norm_part, "b") + send(norm_part, "ab")
        norm_part = norm_part + send(norm_part, "low")
        d_got, m_got, v_got, norm_part = after((d_got, m_got, v_got, norm_part))

        v_give, v_keep = step_call(bit_high, v_keep, v_got)
        v_got = send(v_give, "high")
        norm_part = norm_part + send(norm_part, "high")
        down_grad, mine, other = finish_call(
            scal, (u_keep, u_got), (m_keep, m_got), (d_keep, d_got), (v_keep, v_got), norm_part
        )
        um, mx = u_keep.shape[1], m_keep.shape[1]
        other = send(other, "core")
        up_grad, mix_grad, val_grad, norm_sum = join_call(scal, mine, other, um, mx, inner)
        norm_sum = norm_sum[0]
        w = width // (row_n * chan_n)
        return (
            block_out,
            tokens_grad,
            norm_sum[:w],
            norm_sum[w : 2 * w],
            up_grad,
            val_grad,
            mix_grad,
            down_grad,
            rates[0],
            rates[1],
        )

    return on_device


def make_general(row_n, chan_n):
    row_hi = row_n // 2

    def swap(value, axis, bit):
        size = row_n if axis == "row" else chan_n
        return lax.ppermute(value, axis, [(i, i ^ (1 << bit)) for i in range(size)])

    def core_swap(value):
        return swap(value, "row", 0)

    def bits_of(size):
        return size.bit_length() - 1

    def scatter_sum(part, names, order, last_dtype):
        names = list(names)
        for step, name in enumerate(order):
            axis, bit = name
            dim = names.index(name)
            mine = (lax.axis_index(axis) >> bit) & 1
            keep = lax.dynamic_index_in_dim(part, mine, dim, keepdims=False)
            give = lax.dynamic_index_in_dim(part, 1 - mine, dim, keepdims=False)
            got = swap(give, axis, bit)
            part = keep.astype(jnp.float32) + got.astype(jnp.float32)
            if step < len(order) - 1:
                part = part.astype(give.dtype)
            else:
                part = part.astype(last_dtype)
            names.pop(dim)
        return part

    row_bits = [("row", k) for k in range(bits_of(row_n) - 1, 0, -1)]
    core_bit = ("row", 0)
    chan_bits = [("chan", k) for k in range(bits_of(chan_n) - 1, -1, -1)]
    near_y = chan_bits[2:]
    along_z = chan_bits[:2][::-1]

    def on_device(
        tokens,
        starts,
        layer_norm_gain,
        ln_bias,
        w_up,
        w_val,
        w_mix,
        w_down,
        decay_rate,
        mix_coef,
        out_grad,
    ):
        own, width = tokens.shape
        ff = w_up.shape[1]
        inner = w_val.shape[1]
        part_ff = ff // row_n
        core = lax.axis_index("row") % 2
        mm = lambda a, b, ca, cb: lax.dot_general(
            a, b, (((ca,), (cb,)), ((), ())), preferred_element_type=jnp.float32
        )
        masks = ssm_masks(starts)
        inputs_f = tokens.astype(jnp.float32)
        row_mean = jnp.mean(inputs_f, axis=1, keepdims=True)
        centred = inputs_f - row_mean
        inv_std = lax.rsqrt(jnp.mean(centred * centred, axis=1, keepdims=True) + epsilon)
        x_hat = centred * inv_std
        normed = (x_hat * layer_norm_gain + ln_bias).astype(jnp.bfloat16)
        v_pre = mm(w_val, normed, 0, 1)
        v_cdf = gauss_cdf(v_pre)
        v_act = (v_pre * v_cdf).astype(jnp.bfloat16)
        v_slope = v_cdf + v_pre * gauss_pdf(v_pre)
        v_chan = lax.all_to_all(
            v_act.reshape(inner, own // T, T), "chan", split_axis=0, concat_axis=1, tiled=True
        )
        v_chan = jnp.swapaxes(v_chan, 0, 1)
        pair_normed = jnp.concatenate([normed, core_swap(normed)], 0)
        pair_grad = jnp.concatenate([out_grad, core_swap(out_grad)], 0)
        halves = lambda w, d: lax.dynamic_index_in_dim(
            w.reshape(w.shape[:d] + (row_hi, 2, part_ff) + w.shape[d + 1 :]), core, d + 1, keepdims=False
        ).reshape(w.shape[:d] + (ff // 2,) + w.shape[d + 1 :])
        up_half = halves(w_up, 1)
        mix_half = halves(w_mix, 1)
        down_half = halves(w_down, 0)
        u_pre = mm(pair_normed, up_half, 1, 0)
        d_gate = mm(pair_grad, down_half, 1, 1)
        u_cdf = gauss_cdf(u_pre)
        u_act = u_pre * u_cdf
        d_yproj = (d_gate * u_act).astype(jnp.bfloat16)
        d_slope = d_gate * (u_cdf + u_pre * gauss_pdf(u_pre))
        d_y_part = mm(mix_half, d_yproj, 1, 1)
        d_y = (
            d_y_part[:, :own] + core_swap(d_y_part[:, own:].astype(jnp.bfloat16)).astype(jnp.float32)
        ).astype(jnp.bfloat16)
        d_y_chan = lax.all_to_all(
            d_y.reshape(inner, own // T, T), "chan", split_axis=0, concat_axis=1, tiled=True
        )
        d_y_chan = jnp.swapaxes(d_y_chan, 0, 1)
        y_chan, states, toeplitz = ssm_fwd(v_chan, decay_rate, mix_coef, masks)
        y_chan = jnp.swapaxes(y_chan, 0, 1)
        y_own = lax.all_to_all(y_chan, "chan", split_axis=1, concat_axis=0, tiled=True)
        y_own = y_own.reshape(inner, own)
        d_v_chan, rates = ssm_bwd(
            v_chan, d_y_chan, decay_rate, mix_coef, masks, states, toeplitz, row_n
        )
        d_v_chan = jnp.swapaxes(d_v_chan, 0, 1)
        d_v = lax.all_to_all(d_v_chan, "chan", split_axis=1, concat_axis=0, tiled=True)
        pair_y = jnp.concatenate([y_own, core_swap(y_own)], 1)
        split_rows = lambda a, lead: a.reshape((2,) * lead + (-1,) + a.shape[1:])
        y_proj = mm(pair_y, mix_half, 0, 0)
        gate_out = (u_act * y_proj).astype(jnp.bfloat16)
        d_upre = (d_slope * y_proj).astype(jnp.bfloat16)
        mix_part = mm(pair_y, d_yproj, 1, 0).astype(jnp.bfloat16)
        down_part = mm(gate_out, pair_grad, 0, 0).astype(jnp.bfloat16)
        up_part = mm(pair_normed, d_upre, 0, 0).astype(jnp.bfloat16)
        all_names = row_bits + [core_bit] + chan_bits
        no_core = row_bits + chan_bits
        lead = len(all_names)
        mix_sum = scatter_sum(
            split_rows(mix_part, lead), all_names, along_z + row_bits + near_y, jnp.float32
        )
        up_sum = scatter_sum(
            split_rows(up_part, lead), all_names, row_bits + near_y + along_z, jnp.float32
        )
        down_grad = scatter_sum(
            split_rows(down_part, lead - 1), no_core, near_y + row_bits + along_z, jnp.float32
        )

        def join_cores(halfsum):
            mine = lax.dynamic_index_in_dim(halfsum, core, 0, keepdims=False)
            other = core_swap(lax.dynamic_index_in_dim(halfsum, 1 - core, 0, keepdims=False))
            shape = (mine.shape[0], row_hi, part_ff)
            low = jnp.where(core == 0, mine, other).reshape(shape)
            high = jnp.where(core == 0, other, mine).reshape(shape)
            return jnp.stack([low, high], 2).reshape(mine.shape[0], ff)

        block_part = mm(gate_out, down_half, 1, 0)
        block_out = (
            inputs_f
            + block_part[:own]
            + core_swap(block_part[own:].astype(jnp.bfloat16)).astype(jnp.float32)
        ).astype(jnp.bfloat16)
        d_normed_part = mm(d_upre, up_half, 1, 1)
        d_normed_got = core_swap(d_normed_part[own:].astype(jnp.bfloat16)).astype(jnp.float32)
        d_vpre = (d_v.reshape(inner, own).astype(jnp.float32) * v_slope).astype(jnp.bfloat16)
        val_part = mm(normed, d_vpre, 0, 1).astype(jnp.bfloat16)
        val_grad = scatter_sum(
            split_rows(val_part, lead),
            all_names,
            [core_bit] + along_z + near_y + row_bits,
            jnp.float32,
        )
        d_normed = d_normed_part[:own] + d_normed_got + mm(d_vpre, w_val, 0, 1)
        norm_part = jnp.stack([jnp.sum(d_normed * x_hat, axis=0), jnp.sum(d_normed, axis=0)], 1)
        norm_sum = scatter_sum(
            split_rows(norm_part, lead), all_names, [core_bit] + row_bits + chan_bits, jnp.float32
        )
        d_xh = d_normed * layer_norm_gain
        tokens_grad = out_grad.astype(jnp.float32) + inv_std * (
            d_xh
            - jnp.mean(d_xh, axis=1, keepdims=True)
            - x_hat * jnp.mean(d_xh * x_hat, axis=1, keepdims=True)
        )
        row_all = [core_bit] + row_bits
        chans, lanes = rates.shape[-2:]
        rates = rates.reshape((2,) * len(row_all) + (2 * chans, lanes))
        rates = scatter_sum(rates, row_all, row_all, jnp.float32).reshape(2, chans, lanes)
        return (
            block_out,
            tokens_grad,
            norm_sum[:, 0],
            norm_sum[:, 1],
            join_cores(up_sum),
            val_grad,
            join_cores(mix_sum),
            down_grad,
            rates[0],
            rates[1],
        )

    return on_device


def solution(mesh):
    spread = P(("row", "chan"), None)
    row_n, chan_n = mesh.shape["row"], mesh.shape["chan"]
    make = make_square if (row_n, chan_n) == (4, 8) else make_general
    return jax.shard_map(
        make(row_n, chan_n),
        mesh=mesh,
        in_specs=(
            spread,
            P("row", None),
            P(),
            P(),
            P(),
            P(),
            P(),
            P(),
            P("chan", None),
            P("chan", None),
            spread,
        ),
        out_specs=(
            spread,
            spread,
            P(("row", "chan")),
            P(("row", "chan")),
            spread,
            spread,
            spread,
            spread,
            P("chan", "row"),
            P("chan", "row"),
        ),
        check_vma=False,
    )
```

```python
import functools

import jax
import jax.numpy as jnp
from jax import lax
from jax.experimental import pallas as pl
from jax.experimental.pallas import tpu as pltpu
from jax.sharding import PartitionSpec as P

T = 128
SUB = 8
GROUP = 16
SEG = 4
f32 = jnp.float32
bf16 = jnp.bfloat16
NT = (((1,), (1,)), ((), ()))
TN = (((0,), (0,)), ((), ()))
NN = (((1,), (0,)), ((), ()))


def mm(a, b, d=NN):
    return lax.dot_general(a, b, d, preferred_element_type=f32)


def iota(shape, d):
    return lax.broadcasted_iota(jnp.int32, shape, d)


def powers(rate_row, pt_ref, c):
    n = rate_row.shape[1]
    steps = iota((8, n), 0).astype(f32)
    r8 = jnp.broadcast_to(rate_row, (8, n))
    parts = [jnp.exp(-r8 * steps)]
    fade = jnp.exp(-8.0 * r8)
    while len(parts) < T // 8:
        parts = parts + [p * fade for p in parts]
        fade = fade * fade
    for i in range(0, len(parts), 2):
        pt_ref[c, i * 8 : i * 8 + 16, :] = jnp.concatenate(parts[i : i + 2], 0).astype(bf16)


def put(ref, c, val, rows):
    for q in range(val.shape[1] // T):
        ref[q, pl.ds(c, rows, stride=SUB), :] = val[:, q * T : (q + 1) * T]


def take(ref, c, rows):
    return jnp.concatenate(
        [ref[q, pl.ds(c, rows, stride=SUB), :] for q in range(ref.shape[0])], 1
    )


def tiles(v):
    return jnp.stack([v[:, q * T : (q + 1) * T] for q in range(v.shape[1] // T)])


def untile(v):
    return jnp.concatenate([v[q] for q in range(v.shape[0])], 1)


def flip_matrix():
    return (iota((T, T), 0) + iota((T, T), 1) == T - 1).astype(f32).astype(bf16)


def seg_masks(ins, g):
    return jnp.concatenate([(ins == g * SEG + k).astype(f32) for k in range(SEG)], 0)


def rep(x):
    return jnp.concatenate([x] * SEG, 0)


def fold(o, m, rows):
    o = o * m
    out = o[0:rows]
    for k in range(1, SEG):
        out = out + o[k * rows : (k + 1) * rows]
    return out


def far_part(a, p, rows):
    hi = a.astype(bf16)
    lo = (a - hi.astype(f32)).astype(bf16)
    o = mm(jnp.concatenate([hi, lo], 0), p, NT)
    return o[:rows] + o[rows:]


def lanes_of(ref, c, rows):
    return ref[pl.ds(c, rows, stride=GROUP), :]


def fwd_kernel(sm, x, rate, coef, ins, insj, head, tailj, y, hs, toe, pt, ss, near, xs, kr):
    rows = ins.shape[0]
    n = rate.shape[1]
    flip = flip_matrix()
    xs[...] = x[...].astype(f32).reshape(rows * GROUP, T)
    tail = tailj[...]
    hd = head[...]
    m0 = seg_masks(ins[...], 0)
    m0b = m0.astype(bf16)
    tri = iota((T, T), 1) >= iota((T, T), 0)
    for sub in range(GROUP // SUB):
        lo = sub * SUB
        cf = coef[lo : lo + SUB, :]
        rt = rate[lo : lo + SUB, :]
        cfh = cf.astype(bf16)
        cfl = (cf - cfh.astype(f32)).astype(bf16)
        cf2 = jnp.concatenate([cfh, cfl], 0)
        xj = []
        for c in range(SUB):
            xc = lanes_of(xs, lo + c, rows).astype(bf16)
            xj.append(mm(xc, flip).astype(bf16) * tail)
        for c in range(SUB):
            powers(rt[c : c + 1], pt, c)
            k2 = mm(cf2, pt[c], NT)
            kr[c : c + 1, :] = k2[c : c + 1] + k2[SUB + c : SUB + c + 1]
        for c in range(SUB):
            put(ss, c, mm(xj[c], pt[c]), rows)
        for c in range(SUB):
            k = jnp.broadcast_to(kr[c : c + 1, :], (T, T))
            kb = pltpu.roll(k, 0, 1, stride=1, stride_axis=0)
            tp = jnp.where(tri, kb, 0.0).astype(bf16)
            toe[lo + c] = tp
            xc = lanes_of(xs, lo + c, rows).astype(bf16)
            near[c] = fold(mm(rep(xc) * m0b, tp), m0, rows)
        fade = tiles(jnp.exp(-float(T) * rt))
        ce = tiles(cf * jnp.exp(-rt))
        h = jnp.zeros((n // T, SUB, T), f32)
        for b in range(rows):
            w = slice(b * SUB, (b + 1) * SUB)
            hs[sub, :, w, :] = h
            s = ss[:, w, :]
            ss[:, w, :] = h * ce
            h = h * (fade * sm[0, b].astype(f32)) + s

        @pl.loop(1, sm[1, 0])
        def _(g):
            m = seg_masks(ins[...], g)
            for c in range(SUB):
                xc = lanes_of(xs, lo + c, rows).astype(bf16)
                near[c] += fold(mm(rep(xc) * m.astype(bf16), toe[lo + c]), m, rows)

        for c in range(SUB):
            far = far_part(take(ss, c, rows), pt[c], rows)
            xs[pl.ds(lo + c, rows, stride=GROUP), :] = near[c] + hd * far
    y[...] = xs[...].reshape(rows, GROUP, T).astype(bf16)


def bwd_kernel(
    sm, x, dy, rate, coef, ins, insj, head, tailj, hs, toe, *rest
):
    dv, rates, pt, s1, e0, e1, near, gacc, nr, xs, ys = rest[-11:]
    rows = ins.shape[0]
    n = rate.shape[1]
    flip = flip_matrix()
    xs[...] = x[...].astype(f32).reshape(rows * GROUP, T)
    ys[...] = dy[...].astype(f32).reshape(rows * GROUP, T)
    tail = tailj[...]
    hdb = head[...].astype(bf16)
    mn = seg_masks(ins[...], 0).astype(bf16)
    mj = seg_masks(insj[...], 0)
    mjb = mj.astype(bf16)
    lag = iota((rows, T), 1).astype(f32).astype(bf16)
    lag1 = (iota((rows, T), 1) + 1).astype(f32).astype(bf16)
    lagf = iota((1, T), 1).astype(f32)
    valid = iota((T, T), 0) + iota((T, T), 1) >= T - 1
    row16 = iota((16, T), 0)

    def lags(d, xx, md, mx):
        o = mm(rep(d) * md, rep(xx) * mx, TN)
        o = pltpu.roll(jnp.where(valid, o, 0.0), 1, 1, stride=1, stride_axis=0)
        return jnp.sum(o, axis=0, keepdims=True)

    for sub in range(GROUP // SUB):
        lo = sub * SUB
        rt = rate[lo : lo + SUB, :]
        cf = coef[lo : lo + SUB, :]
        xa = jnp.concatenate([lanes_of(xs, lo + c, rows) for c in range(SUB)], 0).astype(bf16)
        da = jnp.concatenate([lanes_of(ys, lo + c, rows) for c in range(SUB)], 0).astype(bf16)
        xja = mm(xa, flip).astype(bf16)
        dja = mm(da, flip).astype(bf16)
        for c in range(SUB):
            sl = slice(c * rows, (c + 1) * rows)
            near[c] = fold(mm(rep(dja[sl]) * mjb, toe[lo + c]), mj, rows)
            gacc[c : c + 1, :] = lags(da[sl], xja[sl], mn, mjb)

        @pl.loop(1, sm[1, 0])
        def _(g):
            m = seg_masks(ins[...], g).astype(bf16)
            k = seg_masks(insj[...], g)
            kb = k.astype(bf16)
            for c in range(SUB):
                d = lanes_of(ys, lo + c, rows).astype(bf16)
                xx = lanes_of(xs, lo + c, rows).astype(bf16)
                dj = mm(d, flip).astype(bf16)
                xj = mm(xx, flip).astype(bf16)
                near[c] += fold(mm(rep(dj) * kb, toe[lo + c]), k, rows)
                gacc[c : c + 1, :] += lags(d, xj, m, kb)

        for c in range(SUB):
            sl = slice(c * rows, (c + 1) * rows)
            powers(rt[c : c + 1], pt, c)
            gr = gacc[c : c + 1, :]
            gl = gr * lagf
            gh = gr.astype(bf16).astype(f32)
            glh = gl.astype(bf16).astype(f32)
            gm = jnp.where(row16 == 2, glh, jnp.where(row16 == 3, gl - glh, 0.0))
            gm = jnp.where(row16 == 0, gh, jnp.where(row16 == 1, gr - gh, gm)).astype(bf16)
            dh = da[sl] * hdb
            o = mm(jnp.concatenate([xja[sl] * tail * lag, dh, dh * lag1, gm], 0), pt[c])
            put(s1, c, o[0:rows], rows)
            put(e0, c, o[rows : 2 * rows], rows)
            put(e1, c, o[2 * rows : 3 * rows], rows)
            k = 3 * rows
            nr[c : c + 1, :] = o[k : k + 1] + o[k + 1 : k + 2]
            nr[SUB + c : SUB + c + 1, :] = o[k + 2 : k + 3] + o[k + 3 : k + 4]
        fade = tiles(jnp.exp(-float(T) * rt))
        ee = tiles(jnp.exp(-rt))
        ce = tiles(cf) * ee
        zero = jnp.zeros((n // T, SUB, T), f32)
        dh, ac, ar, ae = zero, zero, zero, zero
        for b in range(rows - 1, -1, -1):
            w = slice(b * SUB, (b + 1) * SUB)
            h = hs[sub, :, w, :]
            e = e0[:, w, :]
            kf = fade * sm[0, b].astype(f32)
            ar = ar + dh * (kf * (float(T) * h) + s1[:, w, :])
            ae = ae + h * e1[:, w, :]
            ac = ac + h * e
            s1[:, w, :] = dh
            dh = ce * e + kf * dh
        for c in range(SUB):
            far = far_part(take(s1, c, rows), pt[c], rows)
            near[c] = near[c] + tail.astype(f32) * far
        dva = mm(near[...].reshape(SUB * rows, T).astype(bf16), flip)
        for c in range(SUB):
            xs[pl.ds(lo + c, rows, stride=GROUP), :] = dva[c * rows : (c + 1) * rows]
        cut = (lo, lo + SUB)
        dcoef = nr[0:SUB, :] + untile(ee * ac)
        drate = -(cf * nr[SUB : 2 * SUB, :] + untile(ar + ce * ae))
        lanes = rates.shape[-1]
        for row in range(n // lanes):
            at = slice(row * lanes, (row + 1) * lanes)
            rates[row % 2, row // 2, 0, cut[0] : cut[1], :] = drate[:, at]
            rates[row % 2, row // 2, 1, cut[0] : cut[1], :] = dcoef[:, at]
    dv[...] = xs[...].reshape(rows, GROUP, T).astype(bf16)


def mask_kernel(st, sm, ins, insj, head, tailj, *, blocks):
    rows = st.shape[0]
    s = st[...]
    tri = (iota((T, T), 0) <= iota((T, T), 1)).astype(f32).astype(bf16)
    first = s[:, 0:1]
    seg = mm(s.astype(f32).astype(bf16), tri) - first.astype(f32)
    last = seg[:, T - 1 : T]
    cont = (first == 0) & (iota((rows, 1), 0) % blocks != 0)
    back = mm(seg.astype(bf16), flip_matrix())
    ins[...] = seg.astype(jnp.int32)
    insj[...] = back.astype(jnp.int32)
    head[...] = jnp.where((seg == 0) & cont, 1.0, 0.0)
    tailj[...] = jnp.where(back == last, 1.0, 0.0).astype(bf16)
    keep = jnp.where(cont & (last == 0), 1, 0)
    place = iota((rows, T), 0) == iota((rows, T), 1)
    keep = jnp.sum(jnp.where(place, keep, 0), axis=0, keepdims=True)
    most = jnp.max(jnp.broadcast_to(last.astype(jnp.int32), (rows, T)), axis=0, keepdims=True)
    row = iota((8, T), 0)
    sm[...] = jnp.where(row == 0, keep, jnp.where(row == 1, most // SEG + 1, 0))


def ssm_masks(starts):
    seqs, length = starts.shape
    blocks = length // T
    rows = seqs * blocks
    shape = (rows, T)
    kinds = (jnp.int32, jnp.int32, f32, bf16)
    return pl.pallas_call(
        functools.partial(mask_kernel, blocks=blocks),
        out_shape=[jax.ShapeDtypeStruct((8, T), jnp.int32)]
        + [jax.ShapeDtypeStruct(shape, kind) for kind in kinds],
        name="masks",
    )(starts.reshape(shape))


def ssm_specs(rows, n, first=0):
    full = pl.BlockSpec((rows, T), lambda i: (0, 0))
    return dict(
        sm=pl.BlockSpec(memory_space=pltpu.SMEM),
        full=full,
        ch=pl.BlockSpec((rows, GROUP, T), lambda i: (0, i + first, 0)),
        par=pl.BlockSpec((GROUP, n), lambda i: (i + first, 0)),
        hs=pl.BlockSpec((GROUP // SUB, n // T, rows * SUB, T), lambda i: (i + first, 0, 0, 0)),
        toe=pl.BlockSpec((GROUP, T, T), lambda i: (i + first, 0, 0)),
        big=pltpu.VMEM((n // T, rows * SUB, T), f32),
        pt=pltpu.VMEM((SUB, T, n), bf16),
        near=pltpu.VMEM((SUB, rows, T), f32),
        xs=pltpu.VMEM((rows * GROUP, T), f32),
        cost=pl.CostEstimate(flops=2 * 10**10, bytes_accessed=10**7, transcendentals=0),
    )


def ssm_fwd(x, rate, coef, masks):
    rows, chans, _ = x.shape
    n = rate.shape[1]
    s = ssm_specs(rows, n)
    return pl.pallas_call(
        fwd_kernel,
        grid=(chans // GROUP,),
        in_specs=[s["sm"], s["ch"], s["par"], s["par"]] + [s["full"]] * 4,
        out_specs=[s["ch"], s["hs"], s["toe"]],
        out_shape=[
            pltpu.HBM(x.shape, bf16),
            pltpu.HBM((chans // SUB, n // T, rows * SUB, T), f32),
            pltpu.HBM((chans, T, T), bf16),
        ],
        scratch_shapes=[s["pt"], s["big"], s["near"], s["xs"], pltpu.VMEM((SUB, T), f32)],
        compiler_params=pltpu.CompilerParams(vmem_limit_bytes=16 * 2**20),
        cost_estimate=s["cost"],
        name="ssm_fwd",
    )(masks[0], x, rate, coef, *masks[1:])


def ssm_bwd(x, dy, rate, coef, masks, hs, toe, row_n, part=0, parts=1, held=()):
    rows, chans, _ = x.shape
    n = rate.shape[1]
    steps = chans // GROUP // parts
    s = ssm_specs(rows, n, part * steps)
    raw = pl.BlockSpec(memory_space=pl.ANY)
    return pl.pallas_call(
        bwd_kernel,
        grid=(steps,),
        in_specs=[s["sm"], s["ch"], s["ch"], s["par"], s["par"]]
        + [s["full"]] * 4
        + [s["hs"], s["toe"]]
        + [raw] * len(held),
        out_specs=[
            s["ch"],
            pl.BlockSpec((2, row_n // 2, 2, GROUP, n // row_n), lambda i: (0, 0, 0, i + part * steps, 0)),
        ],
        out_shape=[
            pltpu.HBM(x.shape, bf16),
            jax.ShapeDtypeStruct((2, row_n // 2, 2, chans, n // row_n), f32),
        ],
        scratch_shapes=[
            s["pt"],
            s["big"],
            s["big"],
            s["big"],
            s["near"],
            pltpu.VMEM((SUB, T), f32),
            pltpu.VMEM((2 * SUB, n), f32),
            s["xs"],
            s["xs"],
        ],
        compiler_params=pltpu.CompilerParams(vmem_limit_bytes=16 * 2**20),
        cost_estimate=s["cost"],
        input_output_aliases={11 + i: i for i in range(len(held))},
        name="ssm_bwd",
    )(masks[0], x, dy, rate, coef, *masks[1:], *from_hbm(hs, toe), *held)


epsilon = 1e-05
TILE = 768
BLOCK_COLS = 256


def gauss_cdf(a):
    return 0.5 * (1.0 + lax.erf(a * 0.7071067811865476))


def gauss_pdf(a):
    return jnp.exp(-0.5 * a * a) * 0.3989422804014327


def struct(shape, dtype):
    return jax.ShapeDtypeStruct(shape, dtype)


def in_hbm(shape, dtype):
    return pltpu.HBM(shape, dtype)


def from_hbm(*arrays):
    return tuple(pltpu.with_memory_space_constraint(a, pltpu.HBM) for a in arrays)


def whole(shape):
    return pl.BlockSpec(shape, lambda *_: (0,) * len(shape))


def call(kernel, name, grid, ins, outs, out_shape, args, scalars=None, scratch=(), aliases=None, vmem=24, cost=None):
    lead = [] if scalars is None else [scalars]
    return pl.pallas_call(
        kernel,
        grid_spec=pltpu.PrefetchScalarGridSpec(
            num_scalar_prefetch=len(lead),
            grid=grid,
            in_specs=ins,
            out_specs=outs,
            scratch_shapes=list(scratch),
        ),
        out_shape=out_shape,
        input_output_aliases=aliases or {},
        compiler_params=pltpu.CompilerParams(vmem_limit_bytes=vmem * 2**20),
        cost_estimate=cost and pl.CostEstimate(flops=cost, bytes_accessed=10**7, transcendentals=0),
        name=name,
    )(*lead, *args)


def normalise(x):
    centred = x - jnp.mean(x, axis=1, keepdims=True)
    inv_std = lax.rsqrt(jnp.mean(centred * centred, axis=1, keepdims=True) + epsilon)
    return centred * inv_std, inv_std


def norm_kernel(tok, gain, bias, w_val, normed, v_act, v_slope):
    x_hat, _ = normalise(tok[...].astype(f32))
    n = (x_hat * gain[...] + bias[...]).astype(bf16)
    normed[...] = n
    v = mm(n, w_val[...])
    cdf = gauss_cdf(v)
    v_act[...] = (v * cdf).T.astype(bf16).reshape(v_act.shape)
    v_slope[...] = (cdf + v * gauss_pdf(v)).T.reshape(v_slope.shape)


def norm_call(tokens, gain, bias, w_val, chan_n):
    own, width = tokens.shape
    inner = w_val.shape[1]
    quads = own // T
    spread = (chan_n, quads, inner // chan_n, T)
    block = pl.BlockSpec((chan_n, 1, inner // chan_n, T), lambda i: (0, i, 0, 0))
    rows = pl.BlockSpec((T, width), lambda i: (i, 0))
    return call(
        norm_kernel,
        "norm_val",
        (quads,),
        [rows, whole((1, width)), whole((1, width)), whole(w_val.shape)],
        [rows, block, block],
        [struct((own, width), bf16), struct(spread, bf16), in_hbm(spread, f32)],
        from_hbm(tokens, gain[None], bias[None], w_val),
    )


def gate_tile(normed, grad, w_up, w_mix, w_down, u_act, d_slope, d_yproj):
    u = mm(normed, w_up[...])
    d = mm(grad, w_down[...], NT)
    cdf = gauss_cdf(u)
    act = u * cdf
    u_act[...] = act.astype(bf16)
    d_slope[...] = (d * (cdf + u * gauss_pdf(u))).astype(bf16)
    dyp = (d * act).astype(bf16)
    d_yproj[...] = dyp
    return mm(dyp, w_mix[...], NT)


def gate_first_kernel(
    core, n_own, n_oth, g_own, g_oth, w_up, w_mix, w_down,
    u_act, d_slope, d_yproj, na, ga, acc,
):
    own = n_own.shape[0]
    for h, (n, g) in enumerate(((n_own, g_own), (n_oth, g_oth))):
        na[h * own : (h + 1) * own, :] = n[...]
        ga[h * own : (h + 1) * own, :] = g[...]
    acc[...] = gate_tile(na[...], ga[...], w_up, w_mix, w_down, u_act, d_slope, d_yproj)


def gate_last_kernel(
    core, na, ga, acc, w_up, w_mix, w_down, _u, _s, _d,
    u_act, d_slope, d_yproj, normed_t, dy_own, dy_oth, sums,
):
    j = pl.program_id(0)
    own = na.shape[0] // 2

    @pl.when(j == 0)
    def _():
        sums[...] = acc[...]
        normed_t[...] = na[...].T

    sums[...] += gate_tile(na[...], ga[...], w_up, w_mix, w_down, u_act, d_slope, d_yproj)

    @pl.when(j == pl.num_programs(0) - 1)
    def _():
        shape = (dy_own.shape[0], dy_own.shape[2], T)
        for q in range(dy_own.shape[1]):
            dy_own[:, q] = sums[q * T : (q + 1) * T, :].T.reshape(shape)
            dy_oth[:, q] = sums[own + q * T : own + (q + 1) * T, :].T.astype(bf16).reshape(shape)


def gate_specs(own, w_mix, row_n, first):
    inner, ff = w_mix.shape
    part = ff // row_n
    col = lambda j, s: 2 * (j + first) + s[0]
    return [
        lambda width: pl.BlockSpec((width, part), lambda j, s: (0, col(j, s))),
        pl.BlockSpec((inner, part), lambda j, s: (0, col(j, s))),
        lambda width: pl.BlockSpec((part, width), lambda j, s: (col(j, s), 0)),
        pl.BlockSpec((2 * own, part), lambda j, s: (0, j + first)),
    ]


def gate_first(core, normed, normed_oth, grad, grad_oth, w_up, w_mix, w_down, row_n):
    own, width = normed.shape
    inner, ff = w_mix.shape
    up, mix, down, tile = gate_specs(own, w_mix, row_n, 0)
    tok = whole((own, width))
    pair = (2 * own, width)
    return call(
        gate_first_kernel,
        "gate_first",
        (1,),
        [tok, tok, tok, tok, up(width), mix, down(width)],
        [tile, tile, tile, whole(pair), whole(pair), whole((2 * own, inner))],
        [in_hbm((2 * own, ff // 2), bf16)] * 3
        + [in_hbm(pair, bf16), in_hbm(pair, bf16), in_hbm((2 * own, inner), f32)],
        from_hbm(normed, normed_oth, grad, grad_oth, w_up, w_mix, w_down),
        scalars=core,
        vmem=44,
    )


def gate_last(core, pair_normed, pair_grad, acc, w_up, w_mix, w_down, held, row_n, chan_n):
    own, width = pair_normed.shape[0] // 2, pair_normed.shape[1]
    inner, ff = w_mix.shape
    up, mix, down, tile = gate_specs(own, w_mix, row_n, 1)
    pair = (2 * own, width)
    raw = pl.BlockSpec(memory_space=pl.ANY)
    spread = (chan_n, own // T, inner // chan_n, T)
    return call(
        gate_last_kernel,
        "gate_last",
        (row_n // 2 - 1,),
        [whole(pair), whole(pair), whole(acc.shape), up(width), mix, down(width), raw, raw, raw],
        [tile, tile, tile, whole((width, 2 * own)), whole(spread), whole(spread)],
        [in_hbm((2 * own, ff // 2), bf16)] * 3
        + [in_hbm((width, 2 * own), bf16), in_hbm(spread, f32), in_hbm(spread, bf16)],
        from_hbm(pair_normed, pair_grad, acc, w_up, w_mix, w_down, *held),
        scalars=core,
        scratch=[pltpu.VMEM(acc.shape, f32)],
        aliases={7: 0, 8: 1, 9: 2},
        vmem=48,
    )


def mine_a(s):
    return jnp.where(s[0] == 0, s[1], s[2])


def mine_b(s):
    return jnp.where(s[0] == 0, s[2], s[1])


def row_block(s, a, b, core, high, low):
    x = jnp.where(s[0] == 0, a, b)
    y = jnp.where(s[0] == 0, b, a)
    return x * 16 + core * 8 + high * 4 + low * 2 + y


def mid_kernel(
    s, y_own, y_oth, w_mix, u_act, d_slope, d_yproj, normed_t,
    gate, d_upre, u_give, u_keep, m_give, m_keep, yt, yn, us, ms,
):
    inner = yt.shape[0]

    own = yn.shape[0] // 2

    @pl.when(pl.program_id(0) == 0)
    def _():
        for h, y in enumerate((y_own, y_oth)):
            for q in range(y.shape[1]):
                part = y[:, q].reshape(inner, T)
                at = slice(h * own + q * T, h * own + (q + 1) * T)
                yt[:, at] = part
                yn[at, :] = part.T

    yp = mm(yn[...], w_mix[...])
    gate[...] = (u_act[...].astype(f32) * yp).astype(bf16)
    du = (d_slope[...].astype(f32) * yp).astype(bf16)
    d_upre[...] = du
    us[...] = mm(normed_t[...], du).astype(bf16)
    ms[...] = mm(yt[...], d_yproj[...]).astype(bf16)
    m = u_give.shape[1]
    for sel, out in ((1, u_give), (0, u_keep)):
        a = mine_a(s) ^ sel
        for b in (0, 1):
            for low in (0, 1):
                for high in (0, 1):
                    for core in (0, 1):
                        at = pl.multiple_of(row_block(s, a, b, core, high, low) * m, m)
                        out[b * 8 + low * 4 + high * 2 + core] = us[pl.ds(at, m), :]
    m = m_give.shape[1]
    for sel, out in ((1, m_give), (0, m_keep)):
        low = s[3] ^ sel
        for high in (0, 1):
            for a in (0, 1):
                for b in (0, 1):
                    for core in (0, 1):
                        at = pl.multiple_of(row_block(s, a, b, core, high, low) * m, m)
                        out[high * 8 + a * 4 + b * 2 + core] = ms[pl.ds(at, m), :]


def mid_call(scal, y_own, y_oth, w_mix, u_act, d_slope, d_yproj, normed_t, row_n):
    inner, ff = w_mix.shape
    half = u_act.shape[1]
    own = u_act.shape[0] // 2
    width = normed_t.shape[0]
    per = ff // row_n // TILE
    col = lambda j, s: (2 * (j // per) + s[0]) * per + j % per
    tile = pl.BlockSpec((2 * own, TILE), lambda j, s: (0, j))
    um, mx = width // 32, inner // 32
    ub = pl.BlockSpec((16, um, TILE), lambda j, s: (0, 0, j))
    mb = pl.BlockSpec((16, mx, TILE), lambda j, s: (0, 0, j))
    return call(
        mid_kernel,
        "mix_up",
        (half // TILE,),
        [
            whole(y_own.shape),
            whole(y_own.shape),
            pl.BlockSpec((inner, TILE), lambda j, s: (0, col(j, s))),
            tile,
            tile,
            tile,
            whole(normed_t.shape),
        ],
        [tile, tile, ub, ub, mb, mb],
        [in_hbm((2 * own, half), bf16)] * 2
        + [in_hbm((16, um, half), bf16)] * 2
        + [in_hbm((16, mx, half), bf16)] * 2,
        from_hbm(y_own, y_oth, w_mix, u_act, d_slope, d_yproj, normed_t),
        scalars=scal,
        scratch=[
            pltpu.VMEM((inner, 2 * own), bf16),
            pltpu.VMEM((2 * own, inner), bf16),
            pltpu.VMEM((width, TILE), bf16),
            pltpu.VMEM((inner, TILE), bf16),
        ],
        vmem=32,
        cost=10**10,
    )


def block_kernel(s, gate, d_upre, *refs):
    half = (len(refs) - 3) // 2
    downs, ups, (block_own, dn_own, oth) = refs[:half], refs[half : 2 * half], refs[2 * half :]
    own = block_own.shape[0]
    part = downs[0].shape[0]
    cut = lambda ref, k: ref[:, k * part : (k + 1) * part]
    block = sum(mm(cut(gate, k), w[...]) for k, w in enumerate(downs))
    dn = sum(mm(cut(d_upre, k), w[...], NT) for k, w in enumerate(ups))
    block_own[...] = block[:own]
    dn_own[...] = dn[:own]
    oth[0] = block[own:].astype(bf16)
    oth[1] = dn[own:].astype(bf16)


def block_call(scal, gate, d_upre, w_down, w_up, row_n):
    ff, width = w_down.shape
    own = gate.shape[0] // 2
    part = ff // row_n
    cols = BLOCK_COLS
    out = pl.BlockSpec((own, cols), lambda j, s: (0, j))
    ks = range(row_n // 2)
    return call(
        block_kernel,
        "block",
        (width // cols,),
        [whole(gate.shape), whole(d_upre.shape)]
        + [pl.BlockSpec((part, cols), lambda j, s, k=k: (2 * k + s[0], j)) for k in ks]
        + [pl.BlockSpec((cols, part), lambda j, s, k=k: (j, 2 * k + s[0])) for k in ks],
        [out, out, pl.BlockSpec((2, own, cols), lambda j, s: (0, 0, j))],
        [in_hbm((own, width), f32), in_hbm((own, width), f32), in_hbm((2, own, width), bf16)],
        from_hbm(gate, d_upre, *[w_down for _ in ks], *[w_up for _ in ks]),
        scalars=scal,
        vmem=36,
    )


def split_kernel(s, down_g, down_k, d_give, d_keep):
    d_give[0] = down_g[...]
    d_keep[0] = down_k[...]


def split_call(scal, down):
    rows, width = down.shape[0] // 16, down.shape[1]

    def block_of(sel):
        def at(i, s):
            a, b, low, high = mine_a(s) ^ sel, i // 4, (i // 2) % 2, i % 2
            x = jnp.where(s[0] == 0, a, b)
            y = jnp.where(s[0] == 0, b, a)
            return x * 8 + high * 4 + low * 2 + y, 0

        return pl.BlockSpec((rows, width), at)

    out = pl.BlockSpec((1, rows, width), lambda i, s: (i, 0, 0))
    return call(
        split_kernel,
        "split",
        (8,),
        [block_of(1), block_of(0)],
        [out, out],
        [struct((8, rows, width), bf16)] * 2,
        (down, down),
        scalars=scal,
    )


def val_kernel(s, v_own, v_oth, normed_t, v_give, v_keep, vs, vt):
    inner, pair = vt.shape
    for h, v in enumerate((v_own, v_oth)):
        for q in range(v.shape[1]):
            at = h * pair // 2 + q * T
            vt[:, at : at + T] = v[:, q].reshape(inner, T)
    vs[...] = mm(normed_t[...], vt[...], NT)
    m = vs.shape[0] // 32
    for sel, out in ((1, v_give), (0, v_keep)):
        a = mine_a(s) ^ sel
        for b in (0, 1):
            for low in (0, 1):
                for high in (0, 1):
                    cut = []
                    for core in (0, 1):
                        at = pl.multiple_of(row_block(s, a, b, core, high, low) * m, m)
                        cut.append(vs[pl.ds(at, m), :])
                    parts = [
                        jnp.concatenate([c[r * 8 : r * 8 + 8] for c in cut], 0)
                        for r in range(m // 8)
                    ]
                    out[b * 4 + low * 2 + high] = jnp.concatenate(parts, 1).astype(bf16)


def val_call(scal, d_vpre, v_oth, normed_t):
    half = v_oth.shape
    inner = half[0] * half[2]
    width, pair = normed_t.shape
    buf = (8, 16, width)
    return call(
        val_kernel,
        "val",
        (1,),
        [
            pl.BlockSpec(half, lambda i, s: (s[0], 0, 0, 0)),
            whole(half),
            whole(normed_t.shape),
        ],
        [whole(buf), whole(buf)],
        [struct(buf, bf16)] * 2,
        (d_vpre, v_oth, normed_t),
        scalars=scal,
        scratch=[pltpu.VMEM((width, inner), f32), pltpu.VMEM((inner, pair), bf16)],
    )


def step_kernel(bit, keep_g, got_g, keep_k, got_k, give, keep):
    give[...] = (keep_g[0].astype(f32) + got_g[0].astype(f32)).astype(bf16)
    keep[...] = (keep_k[0].astype(f32) + got_k[0].astype(f32)).astype(bf16)


def step_call(bit, keep, got):
    n, rows, cols = keep.shape
    n //= 2
    nb = max(1, n // 4)
    view = (2, n, rows, cols)
    other = pl.BlockSpec((1, nb, rows, cols), lambda i, b: (1 - b[0], i, 0, 0))
    same = pl.BlockSpec((1, nb, rows, cols), lambda i, b: (b[0], i, 0, 0))
    out = pl.BlockSpec((nb, rows, cols), lambda i, b: (i, 0, 0))
    keep, got = keep.reshape(view), got.reshape(view)
    return call(
        step_kernel,
        "halve",
        (n // nb,),
        [other, other, same, same],
        [out, out],
        [struct((n, rows, cols), bf16)] * 2,
        (keep, got, keep, got),
        scalars=bit,
    )


def tail_kernel(
    tok, grad, gain, block_own, got, dn_own, d_vpre, w_val, block_out, tokens_grad, norm_part, acc
):
    i = pl.program_id(0)
    x = tok[...].astype(f32)
    x_hat, inv_std = normalise(x)
    block_out[...] = (x + block_own[...] + got[0].astype(f32)).astype(bf16)
    dv = d_vpre[...].reshape(w_val.shape[1], T).T
    dn = dn_own[...] + got[1].astype(f32) + mm(dv, w_val[...], NT)
    dx = dn * gain[...]
    tokens_grad[...] = grad[...].astype(f32) + inv_std * (
        dx
        - jnp.mean(dx, axis=1, keepdims=True)
        - x_hat * jnp.mean(dx * x_hat, axis=1, keepdims=True)
    )
    sums = jnp.concatenate(
        [jnp.sum(dn * x_hat, axis=0, keepdims=True), jnp.sum(dn, axis=0, keepdims=True)], 0
    )

    @pl.when(i == 0)
    def _():
        acc[...] = sums

    @pl.when(i > 0)
    def _():
        acc[...] += sums

    @pl.when(i == pl.num_programs(0) - 1)
    def _():
        parts, lanes = norm_part.shape
        w = acc.shape[1] // parts
        for k in range(parts):
            cut = acc[:, k * w : (k + 1) * w]
            blank = jnp.zeros((1, lanes - 2 * w), f32)
            norm_part[k : k + 1, :] = jnp.concatenate([cut[0:1], cut[1:2], blank], 1)


def tail_call(tokens, grad, gain, block_own, got, dn_own, d_vpre, w_val, parts):
    own, width = tokens.shape
    rows = pl.BlockSpec((T, width), lambda i: (i, 0))
    chan_n, _, group, _ = d_vpre.shape
    return call(
        tail_kernel,
        "norm_back",
        (own // T,),
        [
            rows,
            rows,
            whole((1, width)),
            rows,
            pl.BlockSpec((2, T, width), lambda i: (0, i, 0)),
            rows,
            pl.BlockSpec((chan_n, 1, group, T), lambda i: (0, i, 0, 0)),
            whole(w_val.shape),
        ],
        [rows, rows, whole((parts, T))],
        [struct((own, width), bf16), struct((own, width), f32), struct((parts, T), f32)],
        from_hbm(tokens, grad, gain[None], block_own, got, dn_own, d_vpre, w_val),
        scratch=[pltpu.VMEM((2, width), f32)],
    )


def finish_kernel(s, u_keep, u_got, m_keep, m_got, d_keep, d_got, v_keep, *rest):
    *v_gots, norm, down, mine, other = rest
    down[...] = d_keep[0].astype(f32) + d_got[0].astype(f32)
    v = sum([g[0].astype(f32) for g in v_gots], v_keep[0].astype(f32))
    half = v.shape[1]
    um, mx = u_keep.shape[1], m_keep.shape[1]
    tail = um + mx + 8
    for out, core, owner in ((mine, s[0], s[5]), (other, 1 - s[0], s[6])):
        out[0:um, :] = u_keep[core].astype(f32) + u_got[core].astype(f32)
        out[um : um + mx, :] = m_keep[core].astype(f32) + m_got[core].astype(f32)
        out[um + mx : tail, 0:half] = jnp.where(core == 0, v[:8], v[8:])
        out[um + mx : tail, half:] = jnp.zeros((8, out.shape[1] - half), f32)
        out[tail:, :] = jnp.zeros((8, out.shape[1]), f32)
        out[tail : tail + 1, 0:T] = norm[pl.ds(owner, 1), :]


def finish_call(scal, up, mix, down, val, norm):
    um, mx, half = up[0].shape[1], mix[0].shape[1], up[0].shape[2]
    rows, width = down[0].shape[1:]
    args = (*up, *mix, *down, *val, norm)
    pack = (um + mx + 16, half)
    return call(
        finish_kernel,
        "finish",
        (1,),
        [whole(a.shape) for a in args],
        [whole((rows, width)), whole(pack), whole(pack)],
        [struct((rows, width), f32), struct(pack, f32), struct(pack, f32)],
        args,
        scalars=scal,
    )


def join_kernel(s, mine, got, up, mix, val, norm):
    um, mx = up.shape[0], mix.shape[0]
    first = s[0] == 0
    part = mine.shape[1] // 2
    for core in (0, 1):
        held = jnp.where(first, mine[...], got[...]) if core == 0 else jnp.where(first, got[...], mine[...])
        for x in (0, 1):
            to = slice((2 * x + core) * part, (2 * x + core + 1) * part)
            up[:, to] = held[0:um, x * part : (x + 1) * part]
            mix[:, to] = held[um : um + mx, x * part : (x + 1) * part]
        w = val.shape[1] // 2
        for r in range(val.shape[0] // 8):
            at = slice(r * w, (r + 1) * w)
            val[r * 8 : r * 8 + 8, core * w : (core + 1) * w] = held[um + mx : um + mx + 8, at]
    norm[...] = mine[um + mx + 8 :, 0:T] + got[um + mx + 8 :, 0:T]


def join_call(scal, mine, got, um, mx, inner):
    ff = mine.shape[1] * 2
    return call(
        join_kernel,
        "join",
        (1,),
        [whole(mine.shape)] * 2,
        [whole((um, ff)), whole((mx, ff)), whole((um, inner)), whole((8, T))],
        [
            struct((um, ff), f32),
            struct((mx, ff), f32),
            struct((um, inner), f32),
            struct((8, T), f32),
        ],
        (mine, got),
        scalars=scal,
    )


def make_square(row_n, chan_n):
    def on_device(
        tokens, starts, layer_norm_gain, ln_bias, w_up, w_val, w_mix, w_down,
        decay_rate, mix_coef, out_grad,
    ):
        own, width = tokens.shape
        inner = w_val.shape[1]
        row, chan = lax.axis_index("row"), lax.axis_index("chan")
        core = row % 2
        me = row * chan_n + chan
        there = (row ^ 1) * chan_n + chan
        y_bit = chan % 2
        b_bit = jnp.where(core == 0, y_bit, row // 2)
        scal = jnp.stack([core, row // 2, y_bit, (chan // 2) % 2, chan // 4, me, there, b_bit])
        scal = scal.astype(jnp.int32)
        bit_x, bit_y = scal[1], scal[2]
        bit_a = jnp.where(core == 0, bit_x, bit_y).reshape(1)
        bit_b = jnp.where(core == 0, bit_y, bit_x).reshape(1)
        bit_low, bit_high = scal[3:4], scal[4:5]
        devices = [(r, c) for r in range(row_n) for c in range(chan_n)]
        flip_x = lambda r, c: (r ^ 2, c)
        flip_y = lambda r, c: (r, c ^ 1)
        moves = dict(
            core=lambda r, c: (r ^ 1, c),
            a=lambda r, c: flip_y(r, c) if r % 2 else flip_x(r, c),
            b=lambda r, c: flip_x(r, c) if r % 2 else flip_y(r, c),
            low=lambda r, c: (r, c ^ 2),
            high=lambda r, c: (r, c ^ 4),
            x=lambda r, c: (r ^ 2, c),
            ab=lambda r, c: (r ^ 2, c ^ 1),
            z=lambda r, c: (r, c ^ 6),
        )

        def send(value, way):
            to = [moves[way](r, c) for r, c in devices]
            pairs = [(r * chan_n + c, t[0] * chan_n + t[1]) for (r, c), t in zip(devices, to)]
            return lax.ppermute(value, ("row", "chan"), pairs)

        after = lax.optimization_barrier
        trade = lambda v: lax.all_to_all(v, "chan", split_axis=0, concat_axis=0, tiled=True)
        rows = own * chan_n // T
        to_seq = lambda v: v.reshape(rows, inner // chan_n, T)
        to_tok = lambda v: v.reshape(chan_n, own // T, inner // chan_n, T)

        masks = ssm_masks(starts)
        grad_oth = send(out_grad, "core")
        normed, v_act, v_slope = norm_call(tokens, layer_norm_gain, ln_bias, w_val, chan_n)
        normed_oth = send(normed, "core")
        v_chan = to_seq(trade(v_act))
        *gated, pair_normed, pair_grad, acc = gate_first(
            scal, normed, normed_oth, out_grad, grad_oth, w_up, w_mix, w_down, row_n
        )
        v_chan, acc = after((v_chan, acc))
        y_chan, states, toeplitz = ssm_fwd(v_chan, decay_rate, mix_coef, masks)
        y_chan, acc = after((y_chan, acc))
        y_own = trade(to_tok(y_chan))
        u_act, d_slope, d_yproj, normed_t, dy_own, dy_oth = gate_last(
            scal, pair_normed, pair_grad, acc, w_up, w_mix, w_down, gated, row_n, chan_n
        )
        d_y = (dy_own + send(dy_oth, "core").astype(f32)).astype(bf16)
        y_own, d_y = after((y_own, d_y))
        y_oth = send(y_own, "core")
        d_y_chan = to_seq(trade(d_y))
        gate_out, d_upre, u_give, u_keep, m_give, m_keep = mid_call(
            scal, y_own, y_oth, w_mix, u_act, d_slope, d_yproj, normed_t, row_n
        )
        u_give, m_give, gate_out, d_y_chan = after((u_give, m_give, gate_out, d_y_chan))
        back = lambda part, held, d_y_chan: ssm_bwd(
            v_chan, d_y_chan, decay_rate, mix_coef, masks, states, toeplitz, row_n, part, 2, held
        )

        u_got = send(u_give, "a")
        m_got = send(m_give, "low")
        down = mm(gate_out, pair_grad, TN).astype(bf16)
        d_give, d_keep = split_call(scal, down)
        held = back(0, (), d_y_chan)
        u_got, m_got, d_give, gate_out, d_y_chan, *held = after(
            (u_got, m_got, d_give, gate_out, d_y_chan, *held)
        )

        d_got = send(d_give, "a")
        m_give, m_keep = step_call(bit_high, m_keep, m_got)
        m_got = send(m_give, "high")
        d_v_chan, rates = back(1, tuple(held), d_y_chan)
        u_give, u_keep = step_call(bit_b, u_keep, u_got)
        d_v_chan, u_give, gate_out, rates = after((d_v_chan, u_give, gate_out, rates))
        d_v = trade(to_tok(d_v_chan))
        d_got, m_got, u_give = after((d_got, m_got, u_give))
        u_got = send(u_give, "b")
        block_own, dn_own, bd_give = block_call(scal, gate_out, d_upre, w_down, w_up, row_n)
        d_give, d_keep = step_call(bit_b, d_keep, d_got)
        rates_give = lax.dynamic_index_in_dim(rates, 1 - core, 0, keepdims=False)
        rates_got = send(rates_give, "core")
        u_got, d_give, bd_give, d_v, rates_got = after((u_got, d_give, bd_give, d_v, rates_got))

        d_got = send(d_give, "b")
        u_give, u_keep = step_call(bit_low, u_keep, u_got)
        u_give, d_v, m_got = after((u_give, d_v, m_got))
        u_got = send(u_give, "low")
        half = chan_n // 2
        other_half = lambda v: lax.dynamic_slice_in_dim(v, (1 - core) * half, half, 0)
        v_give = (other_half(d_v).astype(f32) * other_half(v_slope)).astype(bf16)
        v_got = send(v_give, "core")
        bd_got = send(bd_give, "core")
        d_vpre = (d_v.astype(f32) * v_slope).astype(bf16)
        v_give, v_keep = val_call(scal, d_vpre, v_got, normed_t)
        v_got = send(v_give, "a")
        v_give, d_vpre = after((v_give, d_vpre))
        block_out, tokens_grad, norm_part = tail_call(
            tokens, out_grad, layer_norm_gain, block_own, bd_got, dn_own, d_vpre, w_val,
            row_n * chan_n,
        )
        d_got, u_got, m_got, v_got, norm_part = after((d_got, u_got, m_got, v_got, norm_part))

        d_give, d_keep = step_call(bit_low, d_keep, d_got)
        d_got = send(d_give, "low")
        u_give, u_keep = step_call(bit_high, u_keep, u_got)
        u_give, norm_part = after((u_give, norm_part))
        u_got = send(u_give, "high")
        m_give, m_keep = step_call(bit_a, m_keep, m_got)
        m_got = send(m_give, "a")
        rates = lax.dynamic_index_in_dim(rates, core, 0, keepdims=False) + rates_got
        rates_give = lax.dynamic_index_in_dim(rates, 1 - bit_x, 0, keepdims=False)
        v_give, v_keep = step_call(bit_b, v_keep, v_got)
        v_got = send(v_give, "b")
        norm_part = norm_part + send(norm_part, "a")
        norm_part = norm_part + send(norm_part, "b")
        d_got, m_got, u_got, v_got, norm_part, rates_give = after(
            (d_got, m_got, u_got, v_got, norm_part, rates_give)
        )

        d_give, d_keep = step_call(bit_high, d_keep, d_got)
        d_give, norm_part, rates_give = after((d_give, norm_part, rates_give))
        d_got = send(d_give, "high")
        rates_got = send(rates_give, "x")
        m_give, m_keep = step_call(bit_b, m_keep, m_got)
        m_got = send(m_give, "b")
        v_give, v_keep = step_call(bit_low, v_keep, v_got)
        v_got = send(v_give, "low")
        norm_part = norm_part + send(norm_part, "low")
        d_got, m_got, norm_part, v_got, rates_got = after(
            (d_got, m_got, norm_part, v_got, rates_got)
        )
        rates = lax.dynamic_index_in_dim(rates, bit_x, 0, keepdims=False) + rates_got

        v_give, v_keep = step_call(bit_high, v_keep, v_got)
        v_got = send(v_give, "high")
        norm_part = norm_part + send(norm_part, "high")
        down_grad, mine, other = finish_call(
            scal, (u_keep, u_got), (m_keep, m_got), (d_keep, d_got), (v_keep, v_got), norm_part
        )
        um, mx = u_keep.shape[1], m_keep.shape[1]
        other = send(other, "core")
        up_grad, mix_grad, val_grad, norm_sum = join_call(scal, mine, other, um, mx, inner)
        norm_sum = norm_sum[0]
        w = width // (row_n * chan_n)
        return (
            block_out,
            tokens_grad,
            norm_sum[:w],
            norm_sum[w : 2 * w],
            up_grad,
            val_grad,
            mix_grad,
            down_grad,
            rates[0],
            rates[1],
        )

    return on_device


def make_general(row_n, chan_n):
    row_hi = row_n // 2

    def swap(value, axis, bit):
        size = row_n if axis == "row" else chan_n
        return lax.ppermute(value, axis, [(i, i ^ (1 << bit)) for i in range(size)])

    def core_swap(value):
        return swap(value, "row", 0)

    def bits_of(size):
        return size.bit_length() - 1

    def scatter_sum(part, names, order, last_dtype):
        names = list(names)
        for step, name in enumerate(order):
            axis, bit = name
            dim = names.index(name)
            mine = (lax.axis_index(axis) >> bit) & 1
            keep = lax.dynamic_index_in_dim(part, mine, dim, keepdims=False)
            give = lax.dynamic_index_in_dim(part, 1 - mine, dim, keepdims=False)
            got = swap(give, axis, bit)
            part = keep.astype(jnp.float32) + got.astype(jnp.float32)
            if step < len(order) - 1:
                part = part.astype(give.dtype)
            else:
                part = part.astype(last_dtype)
            names.pop(dim)
        return part

    row_bits = [("row", k) for k in range(bits_of(row_n) - 1, 0, -1)]
    core_bit = ("row", 0)
    chan_bits = [("chan", k) for k in range(bits_of(chan_n) - 1, -1, -1)]
    near_y = chan_bits[2:]
    along_z = chan_bits[:2][::-1]

    def on_device(
        tokens,
        starts,
        layer_norm_gain,
        ln_bias,
        w_up,
        w_val,
        w_mix,
        w_down,
        decay_rate,
        mix_coef,
        out_grad,
    ):
        own, width = tokens.shape
        ff = w_up.shape[1]
        inner = w_val.shape[1]
        part_ff = ff // row_n
        core = lax.axis_index("row") % 2
        mm = lambda a, b, ca, cb: lax.dot_general(
            a, b, (((ca,), (cb,)), ((), ())), preferred_element_type=jnp.float32
        )
        masks = ssm_masks(starts)
        inputs_f = tokens.astype(jnp.float32)
        row_mean = jnp.mean(inputs_f, axis=1, keepdims=True)
        centred = inputs_f - row_mean
        inv_std = lax.rsqrt(jnp.mean(centred * centred, axis=1, keepdims=True) + epsilon)
        x_hat = centred * inv_std
        normed = (x_hat * layer_norm_gain + ln_bias).astype(jnp.bfloat16)
        v_pre = mm(w_val, normed, 0, 1)
        v_cdf = gauss_cdf(v_pre)
        v_act = (v_pre * v_cdf).astype(jnp.bfloat16)
        v_slope = v_cdf + v_pre * gauss_pdf(v_pre)
        v_chan = lax.all_to_all(
            v_act.reshape(inner, own // T, T), "chan", split_axis=0, concat_axis=1, tiled=True
        )
        v_chan = jnp.swapaxes(v_chan, 0, 1)
        pair_normed = jnp.concatenate([normed, core_swap(normed)], 0)
        pair_grad = jnp.concatenate([out_grad, core_swap(out_grad)], 0)
        halves = lambda w, d: lax.dynamic_index_in_dim(
            w.reshape(w.shape[:d] + (row_hi, 2, part_ff) + w.shape[d + 1 :]), core, d + 1, keepdims=False
        ).reshape(w.shape[:d] + (ff // 2,) + w.shape[d + 1 :])
        up_half = halves(w_up, 1)
        mix_half = halves(w_mix, 1)
        down_half = halves(w_down, 0)
        u_pre = mm(pair_normed, up_half, 1, 0)
        d_gate = mm(pair_grad, down_half, 1, 1)
        u_cdf = gauss_cdf(u_pre)
        u_act = u_pre * u_cdf
        d_yproj = (d_gate * u_act).astype(jnp.bfloat16)
        d_slope = d_gate * (u_cdf + u_pre * gauss_pdf(u_pre))
        d_y_part = mm(mix_half, d_yproj, 1, 1)
        d_y = (
            d_y_part[:, :own] + core_swap(d_y_part[:, own:].astype(jnp.bfloat16)).astype(jnp.float32)
        ).astype(jnp.bfloat16)
        d_y_chan = lax.all_to_all(
            d_y.reshape(inner, own // T, T), "chan", split_axis=0, concat_axis=1, tiled=True
        )
        d_y_chan = jnp.swapaxes(d_y_chan, 0, 1)
        y_chan, states, toeplitz = ssm_fwd(v_chan, decay_rate, mix_coef, masks)
        y_chan = jnp.swapaxes(y_chan, 0, 1)
        y_own = lax.all_to_all(y_chan, "chan", split_axis=1, concat_axis=0, tiled=True)
        y_own = y_own.reshape(inner, own)
        d_v_chan, rates = ssm_bwd(
            v_chan, d_y_chan, decay_rate, mix_coef, masks, states, toeplitz, row_n
        )
        d_v_chan = jnp.swapaxes(d_v_chan, 0, 1)
        d_v = lax.all_to_all(d_v_chan, "chan", split_axis=1, concat_axis=0, tiled=True)
        pair_y = jnp.concatenate([y_own, core_swap(y_own)], 1)
        split_rows = lambda a, lead: a.reshape((2,) * lead + (-1,) + a.shape[1:])
        y_proj = mm(pair_y, mix_half, 0, 0)
        gate_out = (u_act * y_proj).astype(jnp.bfloat16)
        d_upre = (d_slope * y_proj).astype(jnp.bfloat16)
        mix_part = mm(pair_y, d_yproj, 1, 0).astype(jnp.bfloat16)
        down_part = mm(gate_out, pair_grad, 0, 0).astype(jnp.bfloat16)
        up_part = mm(pair_normed, d_upre, 0, 0).astype(jnp.bfloat16)
        all_names = row_bits + [core_bit] + chan_bits
        no_core = row_bits + chan_bits
        lead = len(all_names)
        mix_sum = scatter_sum(
            split_rows(mix_part, lead), all_names, along_z + row_bits + near_y, jnp.float32
        )
        up_sum = scatter_sum(
            split_rows(up_part, lead), all_names, row_bits + near_y + along_z, jnp.float32
        )
        down_grad = scatter_sum(
            split_rows(down_part, lead - 1), no_core, near_y + row_bits + along_z, jnp.float32
        )

        def join_cores(halfsum):
            mine = lax.dynamic_index_in_dim(halfsum, core, 0, keepdims=False)
            other = core_swap(lax.dynamic_index_in_dim(halfsum, 1 - core, 0, keepdims=False))
            shape = (mine.shape[0], row_hi, part_ff)
            low = jnp.where(core == 0, mine, other).reshape(shape)
            high = jnp.where(core == 0, other, mine).reshape(shape)
            return jnp.stack([low, high], 2).reshape(mine.shape[0], ff)

        block_part = mm(gate_out, down_half, 1, 0)
        block_out = (
            inputs_f
            + block_part[:own]
            + core_swap(block_part[own:].astype(jnp.bfloat16)).astype(jnp.float32)
        ).astype(jnp.bfloat16)
        d_normed_part = mm(d_upre, up_half, 1, 1)
        d_normed_got = core_swap(d_normed_part[own:].astype(jnp.bfloat16)).astype(jnp.float32)
        d_vpre = (d_v.reshape(inner, own).astype(jnp.float32) * v_slope).astype(jnp.bfloat16)
        val_part = mm(normed, d_vpre, 0, 1).astype(jnp.bfloat16)
        val_grad = scatter_sum(
            split_rows(val_part, lead),
            all_names,
            [core_bit] + along_z + near_y + row_bits,
            jnp.float32,
        )
        d_normed = d_normed_part[:own] + d_normed_got + mm(d_vpre, w_val, 0, 1)
        norm_part = jnp.stack([jnp.sum(d_normed * x_hat, axis=0), jnp.sum(d_normed, axis=0)], 1)
        norm_sum = scatter_sum(
            split_rows(norm_part, lead), all_names, [core_bit] + row_bits + chan_bits, jnp.float32
        )
        d_xh = d_normed * layer_norm_gain
        tokens_grad = out_grad.astype(jnp.float32) + inv_std * (
            d_xh
            - jnp.mean(d_xh, axis=1, keepdims=True)
            - x_hat * jnp.mean(d_xh * x_hat, axis=1, keepdims=True)
        )
        row_all = [core_bit] + row_bits
        chans, lanes = rates.shape[-2:]
        rates = rates.reshape((2,) * len(row_all) + (2 * chans, lanes))
        rates = scatter_sum(rates, row_all, row_all, jnp.float32).reshape(2, chans, lanes)
        return (
            block_out,
            tokens_grad,
            norm_sum[:, 0],
            norm_sum[:, 1],
            join_cores(up_sum),
            val_grad,
            join_cores(mix_sum),
            down_grad,
            rates[0],
            rates[1],
        )

    return on_device


def solution(mesh):
    spread = P(("row", "chan"), None)
    row_n, chan_n = mesh.shape["row"], mesh.shape["chan"]
    make = make_square if (row_n, chan_n) == (4, 8) else make_general
    return jax.shard_map(
        make(row_n, chan_n),
        mesh=mesh,
        in_specs=(
            spread,
            P("row", None),
            P(),
            P(),
            P(),
            P(),
            P(),
            P(),
            P("chan", None),
            P("chan", None),
            spread,
        ),
        out_specs=(
            spread,
            spread,
            P(("row", "chan")),
            P(("row", "chan")),
            spread,
            spread,
            spread,
            spread,
            P("chan", "row"),
            P("chan", "row"),
        ),
        check_vma=False,
    )
```

```python
import functools

import jax
import jax.numpy as jnp
from jax import lax
from jax.experimental import pallas as pl
from jax.experimental.pallas import tpu as pltpu
from jax.sharding import PartitionSpec as P

T = 128
SUB = 8
GROUP = 16
SEG = 4
f32 = jnp.float32
bf16 = jnp.bfloat16
NT = (((1,), (1,)), ((), ()))
TN = (((0,), (0,)), ((), ()))
NN = (((1,), (0,)), ((), ()))


def mm(a, b, d=NN):
    return lax.dot_general(a, b, d, preferred_element_type=f32)


def iota(shape, d):
    return lax.broadcasted_iota(jnp.int32, shape, d)


def powers(rate_row, pt_ref, c):
    n = rate_row.shape[1]
    steps = iota((8, n), 0).astype(f32)
    r8 = jnp.broadcast_to(rate_row, (8, n))
    parts = [jnp.exp(-r8 * steps)]
    fade = jnp.exp(-8.0 * r8)
    while len(parts) < T // 8:
        parts = parts + [p * fade for p in parts]
        fade = fade * fade
    for i in range(0, len(parts), 2):
        pt_ref[c, i * 8 : i * 8 + 16, :] = jnp.concatenate(parts[i : i + 2], 0).astype(bf16)


def put(ref, c, val, rows):
    for q in range(val.shape[1] // T):
        ref[q, pl.ds(c, rows, stride=SUB), :] = val[:, q * T : (q + 1) * T]


def take(ref, c, rows):
    return jnp.concatenate(
        [ref[q, pl.ds(c, rows, stride=SUB), :] for q in range(ref.shape[0])], 1
    )


def tiles(v):
    return jnp.stack([v[:, q * T : (q + 1) * T] for q in range(v.shape[1] // T)])


def untile(v):
    return jnp.concatenate([v[q] for q in range(v.shape[0])], 1)


def flip_matrix():
    return (iota((T, T), 0) + iota((T, T), 1) == T - 1).astype(f32).astype(bf16)


def seg_masks(ins, g):
    return jnp.concatenate([(ins == g * SEG + k).astype(f32) for k in range(SEG)], 0)


def rep(x):
    return jnp.concatenate([x] * SEG, 0)


def fold(o, m, rows):
    o = o * m
    out = o[0:rows]
    for k in range(1, SEG):
        out = out + o[k * rows : (k + 1) * rows]
    return out


def far_part(a, p, rows):
    hi = a.astype(bf16)
    lo = (a - hi.astype(f32)).astype(bf16)
    o = mm(jnp.concatenate([hi, lo], 0), p, NT)
    return o[:rows] + o[rows:]


def lanes_of(ref, c, rows):
    return ref[pl.ds(c, rows, stride=GROUP), :]


def fwd_kernel(sm, x, rate, coef, ins, insj, head, tailj, y, hs, toe, pt, ss, near, xs, kr):
    rows = ins.shape[0]
    n = rate.shape[1]
    flip = flip_matrix()
    xs[...] = x[...].astype(f32).reshape(rows * GROUP, T)
    tail = tailj[...]
    hd = head[...]
    m0 = seg_masks(ins[...], 0)
    m0b = m0.astype(bf16)
    tri = iota((T, T), 1) >= iota((T, T), 0)
    for sub in range(GROUP // SUB):
        lo = sub * SUB
        cf = coef[lo : lo + SUB, :]
        rt = rate[lo : lo + SUB, :]
        cfh = cf.astype(bf16)
        cfl = (cf - cfh.astype(f32)).astype(bf16)
        cf2 = jnp.concatenate([cfh, cfl], 0)
        xj = []
        for c in range(SUB):
            xc = lanes_of(xs, lo + c, rows).astype(bf16)
            xj.append(mm(xc, flip).astype(bf16) * tail)
        for c in range(SUB):
            powers(rt[c : c + 1], pt, c)
            k2 = mm(cf2, pt[c], NT)
            kr[c : c + 1, :] = k2[c : c + 1] + k2[SUB + c : SUB + c + 1]
        for c in range(SUB):
            put(ss, c, mm(xj[c], pt[c]), rows)
        for c in range(SUB):
            k = jnp.broadcast_to(kr[c : c + 1, :], (T, T))
            kb = pltpu.roll(k, 0, 1, stride=1, stride_axis=0)
            tp = jnp.where(tri, kb, 0.0).astype(bf16)
            toe[lo + c] = tp
            xc = lanes_of(xs, lo + c, rows).astype(bf16)
            near[c] = fold(mm(rep(xc) * m0b, tp), m0, rows)
        fade = tiles(jnp.exp(-float(T) * rt))
        ce = tiles(cf * jnp.exp(-rt))
        h = jnp.zeros((n // T, SUB, T), f32)
        for b in range(rows):
            w = slice(b * SUB, (b + 1) * SUB)
            hs[sub, :, w, :] = h
            s = ss[:, w, :]
            ss[:, w, :] = h * ce
            h = h * (fade * sm[0, b].astype(f32)) + s

        @pl.loop(1, sm[1, 0])
        def _(g):
            m = seg_masks(ins[...], g)
            for c in range(SUB):
                xc = lanes_of(xs, lo + c, rows).astype(bf16)
                near[c] += fold(mm(rep(xc) * m.astype(bf16), toe[lo + c]), m, rows)

        for c in range(SUB):
            far = far_part(take(ss, c, rows), pt[c], rows)
            xs[pl.ds(lo + c, rows, stride=GROUP), :] = near[c] + hd * far
    y[...] = xs[...].reshape(rows, GROUP, T).astype(bf16)


def bwd_kernel(
    sm, x, dy, rate, coef, ins, insj, head, tailj, hs, toe, *rest
):
    dv, rates, pt, s1, e0, e1, near, gacc, nr, xs, ys = rest[-11:]
    rows = ins.shape[0]
    n = rate.shape[1]
    flip = flip_matrix()
    xs[...] = x[...].astype(f32).reshape(rows * GROUP, T)
    ys[...] = dy[...].astype(f32).reshape(rows * GROUP, T)
    tail = tailj[...]
    hdb = head[...].astype(bf16)
    mn = seg_masks(ins[...], 0).astype(bf16)
    mj = seg_masks(insj[...], 0)
    mjb = mj.astype(bf16)
    lag = iota((rows, T), 1).astype(f32).astype(bf16)
    lag1 = (iota((rows, T), 1) + 1).astype(f32).astype(bf16)
    lagf = iota((1, T), 1).astype(f32)
    valid = iota((T, T), 0) + iota((T, T), 1) >= T - 1
    row16 = iota((16, T), 0)

    def lags(d, xx, md, mx):
        o = mm(rep(d) * md, rep(xx) * mx, TN)
        o = pltpu.roll(jnp.where(valid, o, 0.0), 1, 1, stride=1, stride_axis=0)
        return jnp.sum(o, axis=0, keepdims=True)

    for sub in range(GROUP // SUB):
        lo = sub * SUB
        rt = rate[lo : lo + SUB, :]
        cf = coef[lo : lo + SUB, :]
        xa = jnp.concatenate([lanes_of(xs, lo + c, rows) for c in range(SUB)], 0).astype(bf16)
        da = jnp.concatenate([lanes_of(ys, lo + c, rows) for c in range(SUB)], 0).astype(bf16)
        xja = mm(xa, flip).astype(bf16)
        dja = mm(da, flip).astype(bf16)
        for c in range(SUB):
            sl = slice(c * rows, (c + 1) * rows)
            near[c] = fold(mm(rep(dja[sl]) * mjb, toe[lo + c]), mj, rows)
            gacc[c : c + 1, :] = lags(da[sl], xja[sl], mn, mjb)

        @pl.loop(1, sm[1, 0])
        def _(g):
            m = seg_masks(ins[...], g).astype(bf16)
            k = seg_masks(insj[...], g)
            kb = k.astype(bf16)
            for c in range(SUB):
                d = lanes_of(ys, lo + c, rows).astype(bf16)
                xx = lanes_of(xs, lo + c, rows).astype(bf16)
                dj = mm(d, flip).astype(bf16)
                xj = mm(xx, flip).astype(bf16)
                near[c] += fold(mm(rep(dj) * kb, toe[lo + c]), k, rows)
                gacc[c : c + 1, :] += lags(d, xj, m, kb)

        for c in range(SUB):
            sl = slice(c * rows, (c + 1) * rows)
            powers(rt[c : c + 1], pt, c)
            gr = gacc[c : c + 1, :]
            gl = gr * lagf
            gh = gr.astype(bf16).astype(f32)
            glh = gl.astype(bf16).astype(f32)
            gm = jnp.where(row16 == 2, glh, jnp.where(row16 == 3, gl - glh, 0.0))
            gm = jnp.where(row16 == 0, gh, jnp.where(row16 == 1, gr - gh, gm)).astype(bf16)
            dh = da[sl] * hdb
            o = mm(jnp.concatenate([xja[sl] * tail * lag, dh, dh * lag1, gm], 0), pt[c])
            put(s1, c, o[0:rows], rows)
            put(e0, c, o[rows : 2 * rows], rows)
            put(e1, c, o[2 * rows : 3 * rows], rows)
            k = 3 * rows
            nr[c : c + 1, :] = o[k : k + 1] + o[k + 1 : k + 2]
            nr[SUB + c : SUB + c + 1, :] = o[k + 2 : k + 3] + o[k + 3 : k + 4]
        fade = tiles(jnp.exp(-float(T) * rt))
        ee = tiles(jnp.exp(-rt))
        ce = tiles(cf) * ee
        zero = jnp.zeros((n // T, SUB, T), f32)
        dh, ac, ar, ae = zero, zero, zero, zero
        for b in range(rows - 1, -1, -1):
            w = slice(b * SUB, (b + 1) * SUB)
            h = hs[sub, :, w, :]
            e = e0[:, w, :]
            kf = fade * sm[0, b].astype(f32)
            ar = ar + dh * (kf * (float(T) * h) + s1[:, w, :])
            ae = ae + h * e1[:, w, :]
            ac = ac + h * e
            s1[:, w, :] = dh
            dh = ce * e + kf * dh
        for c in range(SUB):
            far = far_part(take(s1, c, rows), pt[c], rows)
            near[c] = near[c] + tail.astype(f32) * far
        dva = mm(near[...].reshape(SUB * rows, T).astype(bf16), flip)
        for c in range(SUB):
            xs[pl.ds(lo + c, rows, stride=GROUP), :] = dva[c * rows : (c + 1) * rows]
        cut = (lo, lo + SUB)
        dcoef = nr[0:SUB, :] + untile(ee * ac)
        drate = -(cf * nr[SUB : 2 * SUB, :] + untile(ar + ce * ae))
        lanes = rates.shape[-1]
        for row in range(n // lanes):
            at = slice(row * lanes, (row + 1) * lanes)
            rates[row % 2, row // 2, 0, cut[0] : cut[1], :] = drate[:, at]
            rates[row % 2, row // 2, 1, cut[0] : cut[1], :] = dcoef[:, at]
    dv[...] = xs[...].reshape(rows, GROUP, T).astype(bf16)


def mask_kernel(st, sm, ins, insj, head, tailj, *, blocks):
    rows = st.shape[0]
    s = st[...]
    tri = (iota((T, T), 0) <= iota((T, T), 1)).astype(f32).astype(bf16)
    first = s[:, 0:1]
    seg = mm(s.astype(f32).astype(bf16), tri) - first.astype(f32)
    last = seg[:, T - 1 : T]
    cont = (first == 0) & (iota((rows, 1), 0) % blocks != 0)
    back = mm(seg.astype(bf16), flip_matrix())
    ins[...] = seg.astype(jnp.int32)
    insj[...] = back.astype(jnp.int32)
    head[...] = jnp.where((seg == 0) & cont, 1.0, 0.0)
    tailj[...] = jnp.where(back == last, 1.0, 0.0).astype(bf16)
    keep = jnp.where(cont & (last == 0), 1, 0)
    place = iota((rows, T), 0) == iota((rows, T), 1)
    keep = jnp.sum(jnp.where(place, keep, 0), axis=0, keepdims=True)
    most = jnp.max(jnp.broadcast_to(last.astype(jnp.int32), (rows, T)), axis=0, keepdims=True)
    row = iota((8, T), 0)
    sm[...] = jnp.where(row == 0, keep, jnp.where(row == 1, most // SEG + 1, 0))


def ssm_masks(starts):
    seqs, length = starts.shape
    blocks = length // T
    rows = seqs * blocks
    shape = (rows, T)
    kinds = (jnp.int32, jnp.int32, f32, bf16)
    return pl.pallas_call(
        functools.partial(mask_kernel, blocks=blocks),
        out_shape=[jax.ShapeDtypeStruct((8, T), jnp.int32)]
        + [jax.ShapeDtypeStruct(shape, kind) for kind in kinds],
        name="masks",
    )(starts.reshape(shape))


def ssm_specs(rows, n, first=0):
    full = pl.BlockSpec((rows, T), lambda i: (0, 0))
    return dict(
        sm=pl.BlockSpec(memory_space=pltpu.SMEM),
        full=full,
        ch=pl.BlockSpec((rows, GROUP, T), lambda i: (0, i + first, 0)),
        par=pl.BlockSpec((GROUP, n), lambda i: (i + first, 0)),
        hs=pl.BlockSpec((GROUP // SUB, n // T, rows * SUB, T), lambda i: (i + first, 0, 0, 0)),
        toe=pl.BlockSpec((GROUP, T, T), lambda i: (i + first, 0, 0)),
        big=pltpu.VMEM((n // T, rows * SUB, T), f32),
        pt=pltpu.VMEM((SUB, T, n), bf16),
        near=pltpu.VMEM((SUB, rows, T), f32),
        xs=pltpu.VMEM((rows * GROUP, T), f32),
        cost=pl.CostEstimate(flops=2 * 10**10, bytes_accessed=10**7, transcendentals=0),
    )


def ssm_fwd(x, rate, coef, masks):
    rows, chans, _ = x.shape
    n = rate.shape[1]
    s = ssm_specs(rows, n)
    return pl.pallas_call(
        fwd_kernel,
        grid=(chans // GROUP,),
        in_specs=[s["sm"], s["ch"], s["par"], s["par"]] + [s["full"]] * 4,
        out_specs=[s["ch"], s["hs"], s["toe"]],
        out_shape=[
            pltpu.HBM(x.shape, bf16),
            pltpu.HBM((chans // SUB, n // T, rows * SUB, T), f32),
            pltpu.HBM((chans, T, T), bf16),
        ],
        scratch_shapes=[s["pt"], s["big"], s["near"], s["xs"], pltpu.VMEM((SUB, T), f32)],
        compiler_params=pltpu.CompilerParams(vmem_limit_bytes=16 * 2**20),
        cost_estimate=s["cost"],
        name="ssm_fwd",
    )(masks[0], x, rate, coef, *masks[1:])


def ssm_bwd(x, dy, rate, coef, masks, hs, toe, row_n, part=0, parts=1, held=()):
    rows, chans, _ = x.shape
    n = rate.shape[1]
    steps = chans // GROUP // parts
    s = ssm_specs(rows, n, part * steps)
    raw = pl.BlockSpec(memory_space=pl.ANY)
    return pl.pallas_call(
        bwd_kernel,
        grid=(steps,),
        in_specs=[s["sm"], s["ch"], s["ch"], s["par"], s["par"]]
        + [s["full"]] * 4
        + [s["hs"], s["toe"]]
        + [raw] * len(held),
        out_specs=[
            s["ch"],
            pl.BlockSpec((2, row_n // 2, 2, GROUP, n // row_n), lambda i: (0, 0, 0, i + part * steps, 0)),
        ],
        out_shape=[
            pltpu.HBM(x.shape, bf16),
            jax.ShapeDtypeStruct((2, row_n // 2, 2, chans, n // row_n), f32),
        ],
        scratch_shapes=[
            s["pt"],
            s["big"],
            s["big"],
            s["big"],
            s["near"],
            pltpu.VMEM((SUB, T), f32),
            pltpu.VMEM((2 * SUB, n), f32),
            s["xs"],
            s["xs"],
        ],
        compiler_params=pltpu.CompilerParams(vmem_limit_bytes=16 * 2**20),
        cost_estimate=s["cost"],
        input_output_aliases={11 + i: i for i in range(len(held))},
        name="ssm_bwd",
    )(masks[0], x, dy, rate, coef, *masks[1:], *from_hbm(hs, toe), *held)


epsilon = 1e-05
TILE = 768
BLOCK_COLS = 256
NORM_STEPS = 2
TAIL_STEPS = 2


def gauss_cdf(a):
    return 0.5 * (1.0 + lax.erf(a * 0.7071067811865476))


def gauss_pdf(a):
    return jnp.exp(-0.5 * a * a) * 0.3989422804014327


def struct(shape, dtype):
    return jax.ShapeDtypeStruct(shape, dtype)


def in_hbm(shape, dtype):
    return pltpu.HBM(shape, dtype)


def from_hbm(*arrays):
    return tuple(pltpu.with_memory_space_constraint(a, pltpu.HBM) for a in arrays)


def whole(shape):
    return pl.BlockSpec(shape, lambda *_: (0,) * len(shape))


def call(kernel, name, grid, ins, outs, out_shape, args, scalars=None, scratch=(), aliases=None, vmem=24, cost=None):
    lead = [] if scalars is None else [scalars]
    return pl.pallas_call(
        kernel,
        grid_spec=pltpu.PrefetchScalarGridSpec(
            num_scalar_prefetch=len(lead),
            grid=grid,
            in_specs=ins,
            out_specs=outs,
            scratch_shapes=list(scratch),
        ),
        out_shape=out_shape,
        input_output_aliases=aliases or {},
        compiler_params=pltpu.CompilerParams(vmem_limit_bytes=vmem * 2**20),
        cost_estimate=cost and pl.CostEstimate(flops=cost, bytes_accessed=10**7, transcendentals=0),
        name=name,
    )(*lead, *args)


def normalise(x):
    centred = x - jnp.mean(x, axis=1, keepdims=True)
    inv_std = lax.rsqrt(jnp.mean(centred * centred, axis=1, keepdims=True) + epsilon)
    return centred * inv_std, inv_std


def norm_kernel(tok, gain, bias, w_val, normed, v_act, v_slope):
    x_hat, _ = normalise(tok[...].astype(f32))
    n = (x_hat * gain[...] + bias[...]).astype(bf16)
    normed[...] = n
    v = mm(n, w_val[...])
    cdf = gauss_cdf(v)
    act = (v * cdf).T.astype(bf16)
    slope = (cdf + v * gauss_pdf(v)).T
    shape = (v_act.shape[0], v_act.shape[2], T)
    for q in range(v_act.shape[1]):
        cut = slice(q * T, (q + 1) * T)
        v_act[:, q] = act[:, cut].reshape(shape)
        v_slope[:, q] = slope[:, cut].reshape(shape)


def norm_call(tokens, gain, bias, w_val, chan_n):
    own, width = tokens.shape
    inner = w_val.shape[1]
    quads = own // T
    spread = (chan_n, quads, inner // chan_n, T)
    steps = NORM_STEPS
    block = pl.BlockSpec((chan_n, quads // steps, inner // chan_n, T), lambda i: (0, i, 0, 0))
    rows = pl.BlockSpec((own // steps, width), lambda i: (i, 0))
    return call(
        norm_kernel,
        "norm_val",
        (steps,),
        [rows, whole((1, width)), whole((1, width)), whole(w_val.shape)],
        [rows, block, block],
        [struct((own, width), bf16), struct(spread, bf16), in_hbm(spread, f32)],
        from_hbm(tokens, gain[None], bias[None], w_val),
    )


def gate_tile(normed, grad, w_up, w_mix, w_down, u_act, d_slope, d_yproj):
    u = mm(normed, w_up[...])
    d = mm(grad, w_down[...], NT)
    cdf = gauss_cdf(u)
    act = u * cdf
    u_act[...] = act.astype(bf16)
    d_slope[...] = (d * (cdf + u * gauss_pdf(u))).astype(bf16)
    dyp = (d * act).astype(bf16)
    d_yproj[...] = dyp
    return mm(dyp, w_mix[...], NT)


def gate_first_kernel(
    core, n_own, n_oth, g_own, g_oth, w_up, w_mix, w_down,
    u_act, d_slope, d_yproj, na, ga, acc,
):
    own = n_own.shape[0]
    for h, (n, g) in enumerate(((n_own, g_own), (n_oth, g_oth))):
        na[h * own : (h + 1) * own, :] = n[...]
        ga[h * own : (h + 1) * own, :] = g[...]
    acc[...] = gate_tile(na[...], ga[...], w_up, w_mix, w_down, u_act, d_slope, d_yproj)


def gate_last_kernel(
    core, na, ga, acc, w_up, w_mix, w_down, _u, _s, _d,
    u_act, d_slope, d_yproj, normed_t, dy_own, dy_oth, sums,
):
    j = pl.program_id(0)
    own = na.shape[0] // 2

    @pl.when(j == 0)
    def _():
        sums[...] = acc[...]
        normed_t[...] = na[...].T

    sums[...] += gate_tile(na[...], ga[...], w_up, w_mix, w_down, u_act, d_slope, d_yproj)

    @pl.when(j == pl.num_programs(0) - 1)
    def _():
        shape = (dy_own.shape[0], dy_own.shape[2], T)
        for q in range(dy_own.shape[1]):
            dy_own[:, q] = sums[q * T : (q + 1) * T, :].T.reshape(shape)
            dy_oth[:, q] = sums[own + q * T : own + (q + 1) * T, :].T.astype(bf16).reshape(shape)


def gate_specs(own, w_mix, row_n, first):
    inner, ff = w_mix.shape
    part = ff // row_n
    col = lambda j, s: 2 * (j + first) + s[0]
    return [
        lambda width: pl.BlockSpec((width, part), lambda j, s: (0, col(j, s))),
        pl.BlockSpec((inner, part), lambda j, s: (0, col(j, s))),
        lambda width: pl.BlockSpec((part, width), lambda j, s: (col(j, s), 0)),
        pl.BlockSpec((2 * own, part), lambda j, s: (0, j + first)),
    ]


def gate_first(core, normed, normed_oth, grad, grad_oth, w_up, w_mix, w_down, row_n):
    own, width = normed.shape
    inner, ff = w_mix.shape
    up, mix, down, tile = gate_specs(own, w_mix, row_n, 0)
    tok = whole((own, width))
    pair = (2 * own, width)
    return call(
        gate_first_kernel,
        "gate_first",
        (1,),
        [tok, tok, tok, tok, up(width), mix, down(width)],
        [tile, tile, tile, whole(pair), whole(pair), whole((2 * own, inner))],
        [in_hbm((2 * own, ff // 2), bf16)] * 3
        + [in_hbm(pair, bf16), in_hbm(pair, bf16), in_hbm((2 * own, inner), f32)],
        from_hbm(normed, normed_oth, grad, grad_oth, w_up, w_mix, w_down),
        scalars=core,
        vmem=44,
    )


def gate_last(core, pair_normed, pair_grad, acc, w_up, w_mix, w_down, held, row_n, chan_n):
    own, width = pair_normed.shape[0] // 2, pair_normed.shape[1]
    inner, ff = w_mix.shape
    up, mix, down, tile = gate_specs(own, w_mix, row_n, 1)
    pair = (2 * own, width)
    raw = pl.BlockSpec(memory_space=pl.ANY)
    spread = (chan_n, own // T, inner // chan_n, T)
    return call(
        gate_last_kernel,
        "gate_last",
        (row_n // 2 - 1,),
        [whole(pair), whole(pair), whole(acc.shape), up(width), mix, down(width), raw, raw, raw],
        [tile, tile, tile, whole((width, 2 * own)), whole(spread), whole(spread)],
        [in_hbm((2 * own, ff // 2), bf16)] * 3
        + [in_hbm((width, 2 * own), bf16), in_hbm(spread, f32), in_hbm(spread, bf16)],
        from_hbm(pair_normed, pair_grad, acc, w_up, w_mix, w_down, *held),
        scalars=core,
        scratch=[pltpu.VMEM(acc.shape, f32)],
        aliases={7: 0, 8: 1, 9: 2},
        vmem=48,
    )


def mine_a(s):
    return jnp.where(s[0] == 0, s[1], s[2])


def mine_b(s):
    return jnp.where(s[0] == 0, s[2], s[1])


def row_block(s, a, b, core, high, low):
    x = jnp.where(s[0] == 0, a, b)
    y = jnp.where(s[0] == 0, b, a)
    return x * 16 + core * 8 + high * 4 + low * 2 + y


def mid_kernel(
    s, y_own, y_oth, w_mix, u_act, d_slope, d_yproj, normed_t,
    gate, d_upre, u_give, u_keep, m_give, m_keep, yt, yn, us, ms,
):
    inner = yt.shape[0]

    own = yn.shape[0] // 2

    @pl.when(pl.program_id(0) == 0)
    def _():
        for h, y in enumerate((y_own, y_oth)):
            for q in range(y.shape[1]):
                part = y[:, q].reshape(inner, T)
                at = slice(h * own + q * T, h * own + (q + 1) * T)
                yt[:, at] = part
                yn[at, :] = part.T

    yp = mm(yn[...], w_mix[...])
    gate[...] = (u_act[...].astype(f32) * yp).astype(bf16)
    du = (d_slope[...].astype(f32) * yp).astype(bf16)
    d_upre[...] = du
    us[...] = mm(normed_t[...], du).astype(bf16)
    ms[...] = mm(yt[...], d_yproj[...]).astype(bf16)
    m = u_give.shape[1]
    for sel, out in ((1, u_give), (0, u_keep)):
        a = mine_a(s) ^ sel
        for b in (0, 1):
            for low in (0, 1):
                for high in (0, 1):
                    for core in (0, 1):
                        at = pl.multiple_of(row_block(s, a, b, core, high, low) * m, m)
                        out[b * 8 + low * 4 + high * 2 + core] = us[pl.ds(at, m), :]
    m = m_give.shape[1]
    for sel, out in ((1, m_give), (0, m_keep)):
        low = s[3] ^ sel
        for high in (0, 1):
            for a in (0, 1):
                for b in (0, 1):
                    for core in (0, 1):
                        at = pl.multiple_of(row_block(s, a, b, core, high, low) * m, m)
                        out[high * 8 + a * 4 + b * 2 + core] = ms[pl.ds(at, m), :]


def mid_call(scal, y_own, y_oth, w_mix, u_act, d_slope, d_yproj, normed_t, row_n):
    inner, ff = w_mix.shape
    half = u_act.shape[1]
    own = u_act.shape[0] // 2
    width = normed_t.shape[0]
    per = ff // row_n // TILE
    col = lambda j, s: (2 * (j // per) + s[0]) * per + j % per
    tile = pl.BlockSpec((2 * own, TILE), lambda j, s: (0, j))
    um, mx = width // 32, inner // 32
    ub = pl.BlockSpec((16, um, TILE), lambda j, s: (0, 0, j))
    mb = pl.BlockSpec((16, mx, TILE), lambda j, s: (0, 0, j))
    return call(
        mid_kernel,
        "mix_up",
        (half // TILE,),
        [
            whole(y_own.shape),
            whole(y_own.shape),
            pl.BlockSpec((inner, TILE), lambda j, s: (0, col(j, s))),
            tile,
            tile,
            tile,
            whole(normed_t.shape),
        ],
        [tile, tile, ub, ub, mb, mb],
        [in_hbm((2 * own, half), bf16)] * 2
        + [in_hbm((16, um, half), bf16)] * 2
        + [in_hbm((16, mx, half), bf16)] * 2,
        (y_own, y_oth, *from_hbm(w_mix, u_act, d_slope, d_yproj, normed_t)),
        scalars=scal,
        scratch=[
            pltpu.VMEM((inner, 2 * own), bf16),
            pltpu.VMEM((2 * own, inner), bf16),
            pltpu.VMEM((width, TILE), bf16),
            pltpu.VMEM((inner, TILE), bf16),
        ],
        vmem=32,
        cost=10**10,
    )


def block_kernel(s, gate, d_upre, *refs):
    half = (len(refs) - 3) // 2
    downs, ups, (block_own, dn_own, oth) = refs[:half], refs[half : 2 * half], refs[2 * half :]
    own = block_own.shape[0]
    part = downs[0].shape[0]
    cut = lambda ref, k: ref[:, k * part : (k + 1) * part]
    block = sum(mm(cut(gate, k), w[...]) for k, w in enumerate(downs))
    dn = sum(mm(cut(d_upre, k), w[...], NT) for k, w in enumerate(ups))
    block_own[...] = block[:own]
    dn_own[...] = dn[:own]
    oth[0] = block[own:].astype(bf16)
    oth[1] = dn[own:].astype(bf16)


def block_call(scal, gate, d_upre, w_down, w_up, row_n):
    ff, width = w_down.shape
    own = gate.shape[0] // 2
    part = ff // row_n
    cols = BLOCK_COLS
    out = pl.BlockSpec((own, cols), lambda j, s: (0, j))
    ks = range(row_n // 2)
    return call(
        block_kernel,
        "block",
        (width // cols,),
        [whole(gate.shape), whole(d_upre.shape)]
        + [pl.BlockSpec((part, cols), lambda j, s, k=k: (2 * k + s[0], j)) for k in ks]
        + [pl.BlockSpec((cols, part), lambda j, s, k=k: (j, 2 * k + s[0])) for k in ks],
        [out, out, pl.BlockSpec((2, own, cols), lambda j, s: (0, 0, j))],
        [in_hbm((own, width), f32), in_hbm((own, width), f32), in_hbm((2, own, width), bf16)],
        from_hbm(gate, d_upre, *[w_down for _ in ks], *[w_up for _ in ks]),
        scalars=scal,
        vmem=36,
    )


def split_kernel(s, down_g, down_k, d_give, d_keep):
    for src, dst in ((down_g, d_give), (down_k, d_keep)):
        for low in (0, 1):
            for high in (0, 1):
                dst[low * 2 + high] = src[high * 2 + low]


def split_call(scal, down):
    rows, width = down.shape[0] // 16, down.shape[1]
    view = down.reshape(2, 4, 2, rows, width)

    def block_of(sel):
        def at(i, s):
            a = mine_a(s) ^ sel
            return jnp.where(s[0] == 0, a, i), 0, jnp.where(s[0] == 0, i, a), 0, 0

        return pl.BlockSpec((None, 4, None, rows, width), at)

    out = pl.BlockSpec((4, rows, width), lambda i, s: (i, 0, 0))
    return call(
        split_kernel,
        "split",
        (2,),
        [block_of(1), block_of(0)],
        [out, out],
        [struct((8, rows, width), bf16)] * 2,
        (view, view),
        scalars=scal,
    )


def val_kernel(s, v_own, v_oth, normed_t, v_give, v_keep, vs, vt):
    inner, pair = vt.shape
    for h, v in enumerate((v_own, v_oth)):
        for q in range(v.shape[1]):
            at = h * pair // 2 + q * T
            vt[:, at : at + T] = v[:, q].reshape(inner, T)
    vs[...] = mm(normed_t[...], vt[...], NT)
    m = vs.shape[0] // 32
    for sel, out in ((1, v_give), (0, v_keep)):
        a = mine_a(s) ^ sel
        for b in (0, 1):
            for low in (0, 1):
                for high in (0, 1):
                    cut = []
                    for core in (0, 1):
                        at = pl.multiple_of(row_block(s, a, b, core, high, low) * m, m)
                        cut.append(vs[pl.ds(at, m), :])
                    parts = [
                        jnp.concatenate([c[r * 8 : r * 8 + 8] for c in cut], 0)
                        for r in range(m // 8)
                    ]
                    out[b * 4 + low * 2 + high] = jnp.concatenate(parts, 1).astype(bf16)


def val_call(scal, d_vpre, v_oth, normed_t):
    half = v_oth.shape
    inner = half[0] * half[2]
    width, pair = normed_t.shape
    buf = (8, 16, width)
    return call(
        val_kernel,
        "val",
        (1,),
        [
            pl.BlockSpec(half, lambda i, s: (s[0], 0, 0, 0)),
            whole(half),
            whole(normed_t.shape),
        ],
        [whole(buf), whole(buf)],
        [struct(buf, bf16)] * 2,
        (d_vpre, v_oth, normed_t),
        scalars=scal,
        scratch=[pltpu.VMEM((width, inner), f32), pltpu.VMEM((inner, pair), bf16)],
    )


def step_kernel(bit, keep_g, got_g, keep_k, got_k, give, keep):
    give[...] = (keep_g[0].astype(f32) + got_g[0].astype(f32)).astype(bf16)
    keep[...] = (keep_k[0].astype(f32) + got_k[0].astype(f32)).astype(bf16)


def step_call(bit, keep, got):
    n, rows, cols = keep.shape
    n //= 2
    nb = max(1, n // 4)
    view = (2, n, rows, cols)
    other = pl.BlockSpec((1, nb, rows, cols), lambda i, b: (1 - b[0], i, 0, 0))
    same = pl.BlockSpec((1, nb, rows, cols), lambda i, b: (b[0], i, 0, 0))
    out = pl.BlockSpec((nb, rows, cols), lambda i, b: (i, 0, 0))
    keep, got = keep.reshape(view), got.reshape(view)
    return call(
        step_kernel,
        "halve",
        (n // nb,),
        [other, other, same, same],
        [out, out],
        [struct((n, rows, cols), bf16)] * 2,
        (keep, got, keep, got),
        scalars=bit,
    )


def tail_kernel(
    tok, grad, gain, block_own, got, dn_own, d_vpre, w_val, block_out, tokens_grad, norm_part, acc
):
    i = pl.program_id(0)
    x = tok[...].astype(f32)
    x_hat, inv_std = normalise(x)
    block_out[...] = (x + block_own[...] + got[0].astype(f32)).astype(bf16)
    dv = jnp.concatenate(
        [d_vpre[:, q].reshape(w_val.shape[1], T).T for q in range(d_vpre.shape[1])], 0
    )
    dn = dn_own[...] + got[1].astype(f32) + mm(dv, w_val[...], NT)
    dx = dn * gain[...]
    tokens_grad[...] = grad[...].astype(f32) + inv_std * (
        dx
        - jnp.mean(dx, axis=1, keepdims=True)
        - x_hat * jnp.mean(dx * x_hat, axis=1, keepdims=True)
    )
    sums = jnp.concatenate(
        [jnp.sum(dn * x_hat, axis=0, keepdims=True), jnp.sum(dn, axis=0, keepdims=True)], 0
    )

    @pl.when(i == 0)
    def _():
        acc[...] = sums

    @pl.when(i > 0)
    def _():
        acc[...] += sums

    @pl.when(i == pl.num_programs(0) - 1)
    def _():
        parts, lanes = norm_part.shape
        w = acc.shape[1] // parts
        for k in range(parts):
            cut = acc[:, k * w : (k + 1) * w]
            blank = jnp.zeros((1, lanes - 2 * w), f32)
            norm_part[k : k + 1, :] = jnp.concatenate([cut[0:1], cut[1:2], blank], 1)


def tail_call(tokens, grad, gain, block_own, got, dn_own, d_vpre, w_val, parts):
    own, width = tokens.shape
    steps = TAIL_STEPS
    rows = pl.BlockSpec((own // steps, width), lambda i: (i, 0))
    chan_n, quads, group, _ = d_vpre.shape
    return call(
        tail_kernel,
        "norm_back",
        (steps,),
        [
            rows,
            rows,
            whole((1, width)),
            rows,
            pl.BlockSpec((2, own // steps, width), lambda i: (0, i, 0)),
            rows,
            pl.BlockSpec((chan_n, quads // steps, group, T), lambda i: (0, i, 0, 0)),
            whole(w_val.shape),
        ],
        [rows, rows, whole((parts, T))],
        [struct((own, width), bf16), struct((own, width), f32), struct((parts, T), f32)],
        from_hbm(tokens, grad, gain[None], block_own, got, dn_own, d_vpre, w_val),
        scratch=[pltpu.VMEM((2, width), f32)],
        vmem=32,
    )


def finish_kernel(s, u_keep, u_got, m_keep, m_got, d_keep, d_got, v_keep, *rest):
    *v_gots, norm, down, mine, other = rest
    down[...] = d_keep[0].astype(f32) + d_got[0].astype(f32)
    v = sum([g[0].astype(f32) for g in v_gots], v_keep[0].astype(f32))
    half = v.shape[1]
    um, mx = u_keep.shape[1], m_keep.shape[1]
    tail = um + mx + 8
    for out, core, owner in ((mine, s[0], s[5]), (other, 1 - s[0], s[6])):
        out[0:um, :] = u_keep[core].astype(f32) + u_got[core].astype(f32)
        out[um : um + mx, :] = m_keep[core].astype(f32) + m_got[core].astype(f32)
        out[um + mx : tail, 0:half] = jnp.where(core == 0, v[:8], v[8:])
        out[um + mx : tail, half:] = jnp.zeros((8, out.shape[1] - half), f32)
        out[tail:, :] = jnp.zeros((8, out.shape[1]), f32)
        out[tail : tail + 1, 0:T] = norm[pl.ds(owner, 1), :]


def finish_call(scal, up, mix, down, val, norm):
    um, mx, half = up[0].shape[1], mix[0].shape[1], up[0].shape[2]
    rows, width = down[0].shape[1:]
    args = (*up, *mix, *down, *val, norm)
    pack = (um + mx + 16, half)
    return call(
        finish_kernel,
        "finish",
        (1,),
        [whole(a.shape) for a in args],
        [whole((rows, width)), whole(pack), whole(pack)],
        [struct((rows, width), f32), struct(pack, f32), struct(pack, f32)],
        args,
        scalars=scal,
    )


def join_kernel(s, mine, got, up, mix, val, norm):
    um, mx = up.shape[0], mix.shape[0]
    first = s[0] == 0
    part = mine.shape[1] // 2
    for core in (0, 1):
        held = jnp.where(first, mine[...], got[...]) if core == 0 else jnp.where(first, got[...], mine[...])
        for x in (0, 1):
            to = slice((2 * x + core) * part, (2 * x + core + 1) * part)
            up[:, to] = held[0:um, x * part : (x + 1) * part]
            mix[:, to] = held[um : um + mx, x * part : (x + 1) * part]
        w = val.shape[1] // 2
        for r in range(val.shape[0] // 8):
            at = slice(r * w, (r + 1) * w)
            val[r * 8 : r * 8 + 8, core * w : (core + 1) * w] = held[um + mx : um + mx + 8, at]
    norm[...] = mine[um + mx + 8 :, 0:T] + got[um + mx + 8 :, 0:T]


def join_call(scal, mine, got, um, mx, inner):
    ff = mine.shape[1] * 2
    return call(
        join_kernel,
        "join",
        (1,),
        [whole(mine.shape)] * 2,
        [whole((um, ff)), whole((mx, ff)), whole((um, inner)), whole((8, T))],
        [
            struct((um, ff), f32),
            struct((mx, ff), f32),
            struct((um, inner), f32),
            struct((8, T), f32),
        ],
        (mine, got),
        scalars=scal,
    )


def make_square(row_n, chan_n):
    def on_device(
        tokens, starts, layer_norm_gain, ln_bias, w_up, w_val, w_mix, w_down,
        decay_rate, mix_coef, out_grad,
    ):
        own, width = tokens.shape
        inner = w_val.shape[1]
        row, chan = lax.axis_index("row"), lax.axis_index("chan")
        core = row % 2
        me = row * chan_n + chan
        there = (row ^ 1) * chan_n + chan
        y_bit = chan % 2
        b_bit = jnp.where(core == 0, y_bit, row // 2)
        scal = jnp.stack([core, row // 2, y_bit, (chan // 2) % 2, chan // 4, me, there, b_bit])
        scal = scal.astype(jnp.int32)
        bit_x, bit_y = scal[1], scal[2]
        bit_a = jnp.where(core == 0, bit_x, bit_y).reshape(1)
        bit_b = jnp.where(core == 0, bit_y, bit_x).reshape(1)
        bit_low, bit_high = scal[3:4], scal[4:5]
        devices = [(r, c) for r in range(row_n) for c in range(chan_n)]
        flip_x = lambda r, c: (r ^ 2, c)
        flip_y = lambda r, c: (r, c ^ 1)
        moves = dict(
            core=lambda r, c: (r ^ 1, c),
            a=lambda r, c: flip_y(r, c) if r % 2 else flip_x(r, c),
            b=lambda r, c: flip_x(r, c) if r % 2 else flip_y(r, c),
            low=lambda r, c: (r, c ^ 2),
            high=lambda r, c: (r, c ^ 4),
            x=lambda r, c: (r ^ 2, c),
            ab=lambda r, c: (r ^ 2, c ^ 1),
            z=lambda r, c: (r, c ^ 6),
        )

        def send(value, way):
            to = [moves[way](r, c) for r, c in devices]
            pairs = [(r * chan_n + c, t[0] * chan_n + t[1]) for (r, c), t in zip(devices, to)]
            return lax.ppermute(value, ("row", "chan"), pairs)

        after = lax.optimization_barrier
        trade = lambda v: lax.all_to_all(v, "chan", split_axis=0, concat_axis=0, tiled=True)
        rows = own * chan_n // T
        to_seq = lambda v: v.reshape(rows, inner // chan_n, T)
        to_tok = lambda v: v.reshape(chan_n, own // T, inner // chan_n, T)

        masks = ssm_masks(starts)
        grad_oth = send(out_grad, "core")
        normed, v_act, v_slope = norm_call(tokens, layer_norm_gain, ln_bias, w_val, chan_n)
        normed_oth = send(normed, "core")
        v_chan = to_seq(trade(v_act))
        *gated, pair_normed, pair_grad, acc = gate_first(
            scal, normed, normed_oth, out_grad, grad_oth, w_up, w_mix, w_down, row_n
        )
        v_chan, acc = after((v_chan, acc))
        y_chan, states, toeplitz = ssm_fwd(v_chan, decay_rate, mix_coef, masks)
        y_chan, acc = after((y_chan, acc))
        y_own = trade(to_tok(y_chan))
        u_act, d_slope, d_yproj, normed_t, dy_own, dy_oth = gate_last(
            scal, pair_normed, pair_grad, acc, w_up, w_mix, w_down, gated, row_n, chan_n
        )
        d_y = (dy_own + send(dy_oth, "core").astype(f32)).astype(bf16)
        y_own, d_y = after((y_own, d_y))
        y_oth = send(y_own, "core")
        d_y_chan = to_seq(trade(d_y))
        gate_out, d_upre, u_give, u_keep, m_give, m_keep = mid_call(
            scal, y_own, y_oth, w_mix, u_act, d_slope, d_yproj, normed_t, row_n
        )
        u_give, m_give, gate_out, d_y_chan = after((u_give, m_give, gate_out, d_y_chan))
        back = lambda part, held, d_y_chan: ssm_bwd(
            v_chan, d_y_chan, decay_rate, mix_coef, masks, states, toeplitz, row_n, part, 2, held
        )

        u_got = send(u_give, "a")
        m_got = send(m_give, "low")
        down = mm(gate_out, pair_grad, TN).astype(bf16)
        d_give, d_keep = split_call(scal, down)
        held = back(0, (), d_y_chan)
        u_got, m_got, d_give, gate_out, d_y_chan, *held = after(
            (u_got, m_got, d_give, gate_out, d_y_chan, *held)
        )

        d_got = send(d_give, "a")
        m_give, m_keep = step_call(bit_high, m_keep, m_got)
        m_got = send(m_give, "high")
        d_v_chan, rates = back(1, tuple(held), d_y_chan)
        u_give, u_keep = step_call(bit_b, u_keep, u_got)
        d_v_chan, u_give, gate_out, rates = after((d_v_chan, u_give, gate_out, rates))
        d_v = trade(to_tok(d_v_chan))
        d_got, m_got, u_give = after((d_got, m_got, u_give))
        u_got = send(u_give, "b")
        block_own, dn_own, bd_give = block_call(scal, gate_out, d_upre, w_down, w_up, row_n)
        d_give, d_keep = step_call(bit_b, d_keep, d_got)
        rates_give = lax.dynamic_index_in_dim(rates, 1 - core, 0, keepdims=False)
        rates_got = send(rates_give, "core")
        u_got, d_give, bd_give, d_v, rates_got = after((u_got, d_give, bd_give, d_v, rates_got))

        d_got = send(d_give, "b")
        u_give, u_keep = step_call(bit_low, u_keep, u_got)
        u_give, d_v, m_got = after((u_give, d_v, m_got))
        u_got = send(u_give, "low")
        half = chan_n // 2
        other_half = lambda v: lax.dynamic_slice_in_dim(v, (1 - core) * half, half, 0)
        v_give = (other_half(d_v).astype(f32) * other_half(v_slope)).astype(bf16)
        v_got = send(v_give, "core")
        bd_got = send(bd_give, "core")
        d_vpre = (d_v.astype(f32) * v_slope).astype(bf16)
        v_give, v_keep = val_call(scal, d_vpre, v_got, normed_t)
        v_got = send(v_give, "a")
        v_give, d_vpre = after((v_give, d_vpre))
        block_out, tokens_grad, norm_part = tail_call(
            tokens, out_grad, layer_norm_gain, block_own, bd_got, dn_own, d_vpre, w_val,
            row_n * chan_n,
        )
        d_got, u_got, m_got, v_got, norm_part = after((d_got, u_got, m_got, v_got, norm_part))

        d_give, d_keep = step_call(bit_low, d_keep, d_got)
        d_got = send(d_give, "low")
        u_give, u_keep = step_call(bit_high, u_keep, u_got)
        u_give, norm_part, m_got, v_got = after((u_give, norm_part, m_got, v_got))
        u_got = send(u_give, "high")
        m_give, m_keep = step_call(bit_a, m_keep, m_got)
        m_got = send(m_give, "a")
        rates = lax.dynamic_index_in_dim(rates, core, 0, keepdims=False) + rates_got
        rates_give = lax.dynamic_index_in_dim(rates, 1 - bit_x, 0, keepdims=False)
        v_give, v_keep = step_call(bit_b, v_keep, v_got)
        v_got = send(v_give, "b")
        norm_part = norm_part + send(norm_part, "a")
        norm_part = norm_part + send(norm_part, "b")
        d_got, m_got, u_got, v_got, norm_part, rates_give = after(
            (d_got, m_got, u_got, v_got, norm_part, rates_give)
        )

        d_give, d_keep = step_call(bit_high, d_keep, d_got)
        d_give, norm_part, rates_give = after((d_give, norm_part, rates_give))
        d_got = send(d_give, "high")
        rates_got = send(rates_give, "x")
        m_give, m_keep = step_call(bit_b, m_keep, m_got)
        m_got = send(m_give, "b")
        v_give, v_keep = step_call(bit_low, v_keep, v_got)
        v_got = send(v_give, "low")
        norm_part = norm_part + send(norm_part, "low")
        d_got, m_got, norm_part, v_got, rates_got = after(
            (d_got, m_got, norm_part, v_got, rates_got)
        )
        rates = lax.dynamic_index_in_dim(rates, bit_x, 0, keepdims=False) + rates_got

        v_give, v_keep = step_call(bit_high, v_keep, v_got)
        v_got = send(v_give, "high")
        norm_part = norm_part + send(norm_part, "high")
        down_grad, mine, other = finish_call(
            scal, (u_keep, u_got), (m_keep, m_got), (d_keep, d_got), (v_keep, v_got), norm_part
        )
        um, mx = u_keep.shape[1], m_keep.shape[1]
        other = send(other, "core")
        up_grad, mix_grad, val_grad, norm_sum = join_call(scal, mine, other, um, mx, inner)
        norm_sum = norm_sum[0]
        w = width // (row_n * chan_n)
        return (
            block_out,
            tokens_grad,
            norm_sum[:w],
            norm_sum[w : 2 * w],
            up_grad,
            val_grad,
            mix_grad,
            down_grad,
            rates[0],
            rates[1],
        )

    return on_device


def make_general(row_n, chan_n):
    row_hi = row_n // 2

    def swap(value, axis, bit):
        size = row_n if axis == "row" else chan_n
        return lax.ppermute(value, axis, [(i, i ^ (1 << bit)) for i in range(size)])

    def core_swap(value):
        return swap(value, "row", 0)

    def bits_of(size):
        return size.bit_length() - 1

    def scatter_sum(part, names, order, last_dtype):
        names = list(names)
        for step, name in enumerate(order):
            axis, bit = name
            dim = names.index(name)
            mine = (lax.axis_index(axis) >> bit) & 1
            keep = lax.dynamic_index_in_dim(part, mine, dim, keepdims=False)
            give = lax.dynamic_index_in_dim(part, 1 - mine, dim, keepdims=False)
            got = swap(give, axis, bit)
            part = keep.astype(jnp.float32) + got.astype(jnp.float32)
            if step < len(order) - 1:
                part = part.astype(give.dtype)
            else:
                part = part.astype(last_dtype)
            names.pop(dim)
        return part

    row_bits = [("row", k) for k in range(bits_of(row_n) - 1, 0, -1)]
    core_bit = ("row", 0)
    chan_bits = [("chan", k) for k in range(bits_of(chan_n) - 1, -1, -1)]
    near_y = chan_bits[2:]
    along_z = chan_bits[:2][::-1]

    def on_device(
        tokens,
        starts,
        layer_norm_gain,
        ln_bias,
        w_up,
        w_val,
        w_mix,
        w_down,
        decay_rate,
        mix_coef,
        out_grad,
    ):
        own, width = tokens.shape
        ff = w_up.shape[1]
        inner = w_val.shape[1]
        part_ff = ff // row_n
        core = lax.axis_index("row") % 2
        mm = lambda a, b, ca, cb: lax.dot_general(
            a, b, (((ca,), (cb,)), ((), ())), preferred_element_type=jnp.float32
        )
        masks = ssm_masks(starts)
        inputs_f = tokens.astype(jnp.float32)
        row_mean = jnp.mean(inputs_f, axis=1, keepdims=True)
        centred = inputs_f - row_mean
        inv_std = lax.rsqrt(jnp.mean(centred * centred, axis=1, keepdims=True) + epsilon)
        x_hat = centred * inv_std
        normed = (x_hat * layer_norm_gain + ln_bias).astype(jnp.bfloat16)
        v_pre = mm(w_val, normed, 0, 1)
        v_cdf = gauss_cdf(v_pre)
        v_act = (v_pre * v_cdf).astype(jnp.bfloat16)
        v_slope = v_cdf + v_pre * gauss_pdf(v_pre)
        v_chan = lax.all_to_all(
            v_act.reshape(inner, own // T, T), "chan", split_axis=0, concat_axis=1, tiled=True
        )
        v_chan = jnp.swapaxes(v_chan, 0, 1)
        pair_normed = jnp.concatenate([normed, core_swap(normed)], 0)
        pair_grad = jnp.concatenate([out_grad, core_swap(out_grad)], 0)
        halves = lambda w, d: lax.dynamic_index_in_dim(
            w.reshape(w.shape[:d] + (row_hi, 2, part_ff) + w.shape[d + 1 :]), core, d + 1, keepdims=False
        ).reshape(w.shape[:d] + (ff // 2,) + w.shape[d + 1 :])
        up_half = halves(w_up, 1)
        mix_half = halves(w_mix, 1)
        down_half = halves(w_down, 0)
        u_pre = mm(pair_normed, up_half, 1, 0)
        d_gate = mm(pair_grad, down_half, 1, 1)
        u_cdf = gauss_cdf(u_pre)
        u_act = u_pre * u_cdf
        d_yproj = (d_gate * u_act).astype(jnp.bfloat16)
        d_slope = d_gate * (u_cdf + u_pre * gauss_pdf(u_pre))
        d_y_part = mm(mix_half, d_yproj, 1, 1)
        d_y = (
            d_y_part[:, :own] + core_swap(d_y_part[:, own:].astype(jnp.bfloat16)).astype(jnp.float32)
        ).astype(jnp.bfloat16)
        d_y_chan = lax.all_to_all(
            d_y.reshape(inner, own // T, T), "chan", split_axis=0, concat_axis=1, tiled=True
        )
        d_y_chan = jnp.swapaxes(d_y_chan, 0, 1)
        y_chan, states, toeplitz = ssm_fwd(v_chan, decay_rate, mix_coef, masks)
        y_chan = jnp.swapaxes(y_chan, 0, 1)
        y_own = lax.all_to_all(y_chan, "chan", split_axis=1, concat_axis=0, tiled=True)
        y_own = y_own.reshape(inner, own)
        d_v_chan, rates = ssm_bwd(
            v_chan, d_y_chan, decay_rate, mix_coef, masks, states, toeplitz, row_n
        )
        d_v_chan = jnp.swapaxes(d_v_chan, 0, 1)
        d_v = lax.all_to_all(d_v_chan, "chan", split_axis=1, concat_axis=0, tiled=True)
        pair_y = jnp.concatenate([y_own, core_swap(y_own)], 1)
        split_rows = lambda a, lead: a.reshape((2,) * lead + (-1,) + a.shape[1:])
        y_proj = mm(pair_y, mix_half, 0, 0)
        gate_out = (u_act * y_proj).astype(jnp.bfloat16)
        d_upre = (d_slope * y_proj).astype(jnp.bfloat16)
        mix_part = mm(pair_y, d_yproj, 1, 0).astype(jnp.bfloat16)
        down_part = mm(gate_out, pair_grad, 0, 0).astype(jnp.bfloat16)
        up_part = mm(pair_normed, d_upre, 0, 0).astype(jnp.bfloat16)
        all_names = row_bits + [core_bit] + chan_bits
        no_core = row_bits + chan_bits
        lead = len(all_names)
        mix_sum = scatter_sum(
            split_rows(mix_part, lead), all_names, along_z + row_bits + near_y, jnp.float32
        )
        up_sum = scatter_sum(
            split_rows(up_part, lead), all_names, row_bits + near_y + along_z, jnp.float32
        )
        down_grad = scatter_sum(
            split_rows(down_part, lead - 1), no_core, near_y + row_bits + along_z, jnp.float32
        )

        def join_cores(halfsum):
            mine = lax.dynamic_index_in_dim(halfsum, core, 0, keepdims=False)
            other = core_swap(lax.dynamic_index_in_dim(halfsum, 1 - core, 0, keepdims=False))
            shape = (mine.shape[0], row_hi, part_ff)
            low = jnp.where(core == 0, mine, other).reshape(shape)
            high = jnp.where(core == 0, other, mine).reshape(shape)
            return jnp.stack([low, high], 2).reshape(mine.shape[0], ff)

        block_part = mm(gate_out, down_half, 1, 0)
        block_out = (
            inputs_f
            + block_part[:own]
            + core_swap(block_part[own:].astype(jnp.bfloat16)).astype(jnp.float32)
        ).astype(jnp.bfloat16)
        d_normed_part = mm(d_upre, up_half, 1, 1)
        d_normed_got = core_swap(d_normed_part[own:].astype(jnp.bfloat16)).astype(jnp.float32)
        d_vpre = (d_v.reshape(inner, own).astype(jnp.float32) * v_slope).astype(jnp.bfloat16)
        val_part = mm(normed, d_vpre, 0, 1).astype(jnp.bfloat16)
        val_grad = scatter_sum(
            split_rows(val_part, lead),
            all_names,
            [core_bit] + along_z + near_y + row_bits,
            jnp.float32,
        )
        d_normed = d_normed_part[:own] + d_normed_got + mm(d_vpre, w_val, 0, 1)
        norm_part = jnp.stack([jnp.sum(d_normed * x_hat, axis=0), jnp.sum(d_normed, axis=0)], 1)
        norm_sum = scatter_sum(
            split_rows(norm_part, lead), all_names, [core_bit] + row_bits + chan_bits, jnp.float32
        )
        d_xh = d_normed * layer_norm_gain
        tokens_grad = out_grad.astype(jnp.float32) + inv_std * (
            d_xh
            - jnp.mean(d_xh, axis=1, keepdims=True)
            - x_hat * jnp.mean(d_xh * x_hat, axis=1, keepdims=True)
        )
        row_all = [core_bit] + row_bits
        chans, lanes = rates.shape[-2:]
        rates = rates.reshape((2,) * len(row_all) + (2 * chans, lanes))
        rates = scatter_sum(rates, row_all, row_all, jnp.float32).reshape(2, chans, lanes)
        return (
            block_out,
            tokens_grad,
            norm_sum[:, 0],
            norm_sum[:, 1],
            join_cores(up_sum),
            val_grad,
            join_cores(mix_sum),
            down_grad,
            rates[0],
            rates[1],
        )

    return on_device


def solution(mesh):
    spread = P(("row", "chan"), None)
    row_n, chan_n = mesh.shape["row"], mesh.shape["chan"]
    make = make_square if (row_n, chan_n) == (4, 8) else make_general
    return jax.shard_map(
        make(row_n, chan_n),
        mesh=mesh,
        in_specs=(
            spread,
            P("row", None),
            P(),
            P(),
            P(),
            P(),
            P(),
            P(),
            P("chan", None),
            P("chan", None),
            spread,
        ),
        out_specs=(
            spread,
            spread,
            P(("row", "chan")),
            P(("row", "chan")),
            spread,
            spread,
            spread,
            spread,
            P("chan", "row"),
            P("chan", "row"),
        ),
        check_vma=False,
    )
```

```python
import functools

import jax
import jax.numpy as jnp
from jax import lax
from jax.experimental import pallas as pl
from jax.experimental.pallas import tpu as pltpu
from jax.sharding import PartitionSpec as P

T = 128
SUB = 8
GROUP = 16
SEG = 4
f32 = jnp.float32
bf16 = jnp.bfloat16
NT = (((1,), (1,)), ((), ()))
TN = (((0,), (0,)), ((), ()))
NN = (((1,), (0,)), ((), ()))


def mm(a, b, d=NN):
    return lax.dot_general(a, b, d, preferred_element_type=f32)


def iota(shape, d):
    return lax.broadcasted_iota(jnp.int32, shape, d)


def powers(rate_row, pt_ref, c):
    n = rate_row.shape[1]
    steps = iota((8, n), 0).astype(f32)
    r8 = jnp.broadcast_to(rate_row, (8, n))
    parts = [jnp.exp(-r8 * steps)]
    fade = jnp.exp(-8.0 * r8)
    while len(parts) < T // 8:
        parts = parts + [p * fade for p in parts]
        fade = fade * fade
    for i in range(0, len(parts), 2):
        pt_ref[c, i * 8 : i * 8 + 16, :] = jnp.concatenate(parts[i : i + 2], 0).astype(bf16)


def put(ref, c, val, rows):
    for q in range(val.shape[1] // T):
        ref[q, pl.ds(c, rows, stride=SUB), :] = val[:, q * T : (q + 1) * T]


def take(ref, c, rows):
    return jnp.concatenate(
        [ref[q, pl.ds(c, rows, stride=SUB), :] for q in range(ref.shape[0])], 1
    )


def tiles(v):
    return jnp.stack([v[:, q * T : (q + 1) * T] for q in range(v.shape[1] // T)])


def untile(v):
    return jnp.concatenate([v[q] for q in range(v.shape[0])], 1)


def flip_matrix():
    return (iota((T, T), 0) + iota((T, T), 1) == T - 1).astype(f32).astype(bf16)


def seg_masks(ins, g):
    return jnp.concatenate([(ins == g * SEG + k).astype(f32) for k in range(SEG)], 0)


def rep(x):
    return jnp.concatenate([x] * SEG, 0)


def fold(o, m, rows):
    o = o * m
    out = o[0:rows]
    for k in range(1, SEG):
        out = out + o[k * rows : (k + 1) * rows]
    return out


def far_part(a, p, rows):
    hi = a.astype(bf16)
    lo = (a - hi.astype(f32)).astype(bf16)
    o = mm(jnp.concatenate([hi, lo], 0), p, NT)
    return o[:rows] + o[rows:]


def lanes_of(ref, c, rows):
    return ref[pl.ds(c, rows, stride=GROUP), :]


def fwd_kernel(sm, x, rate, coef, ins, insj, head, tailj, y, hs, toe, pt, ss, near, xs, kr):
    rows = ins.shape[0]
    n = rate.shape[1]
    flip = flip_matrix()
    xs[...] = x[...].astype(f32).reshape(rows * GROUP, T)
    tail = tailj[...]
    hd = head[...]
    m0 = seg_masks(ins[...], 0)
    m0b = m0.astype(bf16)
    tri = iota((T, T), 1) >= iota((T, T), 0)
    for sub in range(GROUP // SUB):
        lo = sub * SUB
        cf = coef[lo : lo + SUB, :]
        rt = rate[lo : lo + SUB, :]
        cfh = cf.astype(bf16)
        cfl = (cf - cfh.astype(f32)).astype(bf16)
        cf2 = jnp.concatenate([cfh, cfl], 0)
        xj = []
        for c in range(SUB):
            xc = lanes_of(xs, lo + c, rows).astype(bf16)
            xj.append(mm(xc, flip).astype(bf16) * tail)
        for c in range(SUB):
            powers(rt[c : c + 1], pt, c)
            k2 = mm(cf2, pt[c], NT)
            kr[c : c + 1, :] = k2[c : c + 1] + k2[SUB + c : SUB + c + 1]
        for c in range(SUB):
            put(ss, c, mm(xj[c], pt[c]), rows)
        for c in range(SUB):
            k = jnp.broadcast_to(kr[c : c + 1, :], (T, T))
            kb = pltpu.roll(k, 0, 1, stride=1, stride_axis=0)
            tp = jnp.where(tri, kb, 0.0).astype(bf16)
            toe[lo + c] = tp
            xc = lanes_of(xs, lo + c, rows).astype(bf16)
            near[c] = fold(mm(rep(xc) * m0b, tp), m0, rows)
        fade = tiles(jnp.exp(-float(T) * rt))
        ce = tiles(cf * jnp.exp(-rt))
        h = jnp.zeros((n // T, SUB, T), f32)
        for b in range(rows):
            w = slice(b * SUB, (b + 1) * SUB)
            hs[sub, :, w, :] = h
            s = ss[:, w, :]
            ss[:, w, :] = h * ce
            h = h * (fade * sm[0, b].astype(f32)) + s

        @pl.loop(1, sm[1, 0])
        def _(g):
            m = seg_masks(ins[...], g)
            for c in range(SUB):
                xc = lanes_of(xs, lo + c, rows).astype(bf16)
                near[c] += fold(mm(rep(xc) * m.astype(bf16), toe[lo + c]), m, rows)

        for c in range(SUB):
            far = far_part(take(ss, c, rows), pt[c], rows)
            xs[pl.ds(lo + c, rows, stride=GROUP), :] = near[c] + hd * far
    y[...] = xs[...].reshape(rows, GROUP, T).astype(bf16)


def bwd_kernel(
    sm, x, dy, rate, coef, ins, insj, head, tailj, hs, toe, *rest
):
    dv, rates, pt, s1, e0, e1, near, gacc, nr, xs, ys = rest[-11:]
    rows = ins.shape[0]
    n = rate.shape[1]
    flip = flip_matrix()
    xs[...] = x[...].astype(f32).reshape(rows * GROUP, T)
    ys[...] = dy[...].astype(f32).reshape(rows * GROUP, T)
    tail = tailj[...]
    hdb = head[...].astype(bf16)
    mn = seg_masks(ins[...], 0).astype(bf16)
    mj = seg_masks(insj[...], 0)
    mjb = mj.astype(bf16)
    lag = iota((rows, T), 1).astype(f32).astype(bf16)
    lag1 = (iota((rows, T), 1) + 1).astype(f32).astype(bf16)
    lagf = iota((1, T), 1).astype(f32)
    valid = iota((T, T), 0) + iota((T, T), 1) >= T - 1
    row16 = iota((16, T), 0)

    def lags(d, xx, md, mx):
        o = mm(rep(d) * md, rep(xx) * mx, TN)
        o = pltpu.roll(jnp.where(valid, o, 0.0), 1, 1, stride=1, stride_axis=0)
        return jnp.sum(o, axis=0, keepdims=True)

    for sub in range(GROUP // SUB):
        lo = sub * SUB
        rt = rate[lo : lo + SUB, :]
        cf = coef[lo : lo + SUB, :]
        xa = jnp.concatenate([lanes_of(xs, lo + c, rows) for c in range(SUB)], 0).astype(bf16)
        da = jnp.concatenate([lanes_of(ys, lo + c, rows) for c in range(SUB)], 0).astype(bf16)
        xja = mm(xa, flip).astype(bf16)
        dja = mm(da, flip).astype(bf16)
        for c in range(SUB):
            sl = slice(c * rows, (c + 1) * rows)
            near[c] = fold(mm(rep(dja[sl]) * mjb, toe[lo + c]), mj, rows)
            gacc[c : c + 1, :] = lags(da[sl], xja[sl], mn, mjb)

        @pl.loop(1, sm[1, 0])
        def _(g):
            m = seg_masks(ins[...], g).astype(bf16)
            k = seg_masks(insj[...], g)
            kb = k.astype(bf16)
            for c in range(SUB):
                d = lanes_of(ys, lo + c, rows).astype(bf16)
                xx = lanes_of(xs, lo + c, rows).astype(bf16)
                dj = mm(d, flip).astype(bf16)
                xj = mm(xx, flip).astype(bf16)
                near[c] += fold(mm(rep(dj) * kb, toe[lo + c]), k, rows)
                gacc[c : c + 1, :] += lags(d, xj, m, kb)

        for c in range(SUB):
            sl = slice(c * rows, (c + 1) * rows)
            powers(rt[c : c + 1], pt, c)
            gr = gacc[c : c + 1, :]
            gl = gr * lagf
            gh = gr.astype(bf16).astype(f32)
            glh = gl.astype(bf16).astype(f32)
            gm = jnp.where(row16 == 2, glh, jnp.where(row16 == 3, gl - glh, 0.0))
            gm = jnp.where(row16 == 0, gh, jnp.where(row16 == 1, gr - gh, gm)).astype(bf16)
            dh = da[sl] * hdb
            o = mm(jnp.concatenate([xja[sl] * tail * lag, dh, dh * lag1, gm], 0), pt[c])
            put(s1, c, o[0:rows], rows)
            put(e0, c, o[rows : 2 * rows], rows)
            put(e1, c, o[2 * rows : 3 * rows], rows)
            k = 3 * rows
            nr[c : c + 1, :] = o[k : k + 1] + o[k + 1 : k + 2]
            nr[SUB + c : SUB + c + 1, :] = o[k + 2 : k + 3] + o[k + 3 : k + 4]
        fade = tiles(jnp.exp(-float(T) * rt))
        ee = tiles(jnp.exp(-rt))
        ce = tiles(cf) * ee
        zero = jnp.zeros((n // T, SUB, T), f32)
        dh, ac, ar, ae = zero, zero, zero, zero
        for b in range(rows - 1, -1, -1):
            w = slice(b * SUB, (b + 1) * SUB)
            h = hs[sub, :, w, :]
            e = e0[:, w, :]
            kf = fade * sm[0, b].astype(f32)
            ar = ar + dh * (kf * (float(T) * h) + s1[:, w, :])
            ae = ae + h * e1[:, w, :]
            ac = ac + h * e
            s1[:, w, :] = dh
            dh = ce * e + kf * dh
        for c in range(SUB):
            far = far_part(take(s1, c, rows), pt[c], rows)
            near[c] = near[c] + tail.astype(f32) * far
        dva = mm(near[...].reshape(SUB * rows, T).astype(bf16), flip)
        for c in range(SUB):
            xs[pl.ds(lo + c, rows, stride=GROUP), :] = dva[c * rows : (c + 1) * rows]
        cut = (lo, lo + SUB)
        dcoef = nr[0:SUB, :] + untile(ee * ac)
        drate = -(cf * nr[SUB : 2 * SUB, :] + untile(ar + ce * ae))
        lanes = rates.shape[-1]
        for row in range(n // lanes):
            at = slice(row * lanes, (row + 1) * lanes)
            rates[row % 2, row // 2, 0, cut[0] : cut[1], :] = drate[:, at]
            rates[row % 2, row // 2, 1, cut[0] : cut[1], :] = dcoef[:, at]
    dv[...] = xs[...].reshape(rows, GROUP, T).astype(bf16)


def mask_kernel(st, sm, ins, insj, head, tailj, *, blocks):
    rows = st.shape[0]
    s = st[...]
    tri = (iota((T, T), 0) <= iota((T, T), 1)).astype(f32).astype(bf16)
    first = s[:, 0:1]
    seg = mm(s.astype(f32).astype(bf16), tri) - first.astype(f32)
    last = seg[:, T - 1 : T]
    cont = (first == 0) & (iota((rows, 1), 0) % blocks != 0)
    back = mm(seg.astype(bf16), flip_matrix())
    ins[...] = seg.astype(jnp.int32)
    insj[...] = back.astype(jnp.int32)
    head[...] = jnp.where((seg == 0) & cont, 1.0, 0.0)
    tailj[...] = jnp.where(back == last, 1.0, 0.0).astype(bf16)
    keep = jnp.where(cont & (last == 0), 1, 0)
    place = iota((rows, T), 0) == iota((rows, T), 1)
    keep = jnp.sum(jnp.where(place, keep, 0), axis=0, keepdims=True)
    most = jnp.max(jnp.broadcast_to(last.astype(jnp.int32), (rows, T)), axis=0, keepdims=True)
    row = iota((8, T), 0)
    sm[...] = jnp.where(row == 0, keep, jnp.where(row == 1, most // SEG + 1, 0))


def ssm_masks(starts):
    seqs, length = starts.shape
    blocks = length // T
    rows = seqs * blocks
    shape = (rows, T)
    kinds = (jnp.int32, jnp.int32, f32, bf16)
    return pl.pallas_call(
        functools.partial(mask_kernel, blocks=blocks),
        out_shape=[jax.ShapeDtypeStruct((8, T), jnp.int32)]
        + [jax.ShapeDtypeStruct(shape, kind) for kind in kinds],
        name="masks",
    )(starts.reshape(shape))


def ssm_specs(rows, n, first=0):
    full = pl.BlockSpec((rows, T), lambda i: (0, 0))
    return dict(
        sm=pl.BlockSpec(memory_space=pltpu.SMEM),
        full=full,
        ch=pl.BlockSpec((rows, GROUP, T), lambda i: (0, i + first, 0)),
        par=pl.BlockSpec((GROUP, n), lambda i: (i + first, 0)),
        hs=pl.BlockSpec((GROUP // SUB, n // T, rows * SUB, T), lambda i: (i + first, 0, 0, 0)),
        toe=pl.BlockSpec((GROUP, T, T), lambda i: (i + first, 0, 0)),
        big=pltpu.VMEM((n // T, rows * SUB, T), f32),
        pt=pltpu.VMEM((SUB, T, n), bf16),
        near=pltpu.VMEM((SUB, rows, T), f32),
        xs=pltpu.VMEM((rows * GROUP, T), f32),
        cost=pl.CostEstimate(flops=2 * 10**10, bytes_accessed=10**7, transcendentals=0),
    )


def ssm_fwd(x, rate, coef, masks):
    rows, chans, _ = x.shape
    n = rate.shape[1]
    s = ssm_specs(rows, n)
    return pl.pallas_call(
        fwd_kernel,
        grid=(chans // GROUP,),
        in_specs=[s["sm"], s["ch"], s["par"], s["par"]] + [s["full"]] * 4,
        out_specs=[s["ch"], s["hs"], s["toe"]],
        out_shape=[
            pltpu.HBM(x.shape, bf16),
            pltpu.HBM((chans // SUB, n // T, rows * SUB, T), f32),
            pltpu.HBM((chans, T, T), bf16),
        ],
        scratch_shapes=[s["pt"], s["big"], s["near"], s["xs"], pltpu.VMEM((SUB, T), f32)],
        compiler_params=pltpu.CompilerParams(vmem_limit_bytes=16 * 2**20),
        cost_estimate=s["cost"],
        name="ssm_fwd",
    )(masks[0], x, rate, coef, *masks[1:])


def ssm_bwd(x, dy, rate, coef, masks, hs, toe, row_n, part=0, parts=1, held=()):
    rows, chans, _ = x.shape
    n = rate.shape[1]
    steps = chans // GROUP // parts
    s = ssm_specs(rows, n, part * steps)
    raw = pl.BlockSpec(memory_space=pl.ANY)
    return pl.pallas_call(
        bwd_kernel,
        grid=(steps,),
        in_specs=[s["sm"], s["ch"], s["ch"], s["par"], s["par"]]
        + [s["full"]] * 4
        + [s["hs"], s["toe"]]
        + [raw] * len(held),
        out_specs=[
            s["ch"],
            pl.BlockSpec((2, row_n // 2, 2, GROUP, n // row_n), lambda i: (0, 0, 0, i + part * steps, 0)),
        ],
        out_shape=[
            pltpu.HBM(x.shape, bf16),
            jax.ShapeDtypeStruct((2, row_n // 2, 2, chans, n // row_n), f32),
        ],
        scratch_shapes=[
            s["pt"],
            s["big"],
            s["big"],
            s["big"],
            s["near"],
            pltpu.VMEM((SUB, T), f32),
            pltpu.VMEM((2 * SUB, n), f32),
            s["xs"],
            s["xs"],
        ],
        compiler_params=pltpu.CompilerParams(vmem_limit_bytes=16 * 2**20),
        cost_estimate=s["cost"],
        input_output_aliases={11 + i: i for i in range(len(held))},
        name="ssm_bwd",
    )(masks[0], x, dy, rate, coef, *masks[1:], *from_hbm(hs, toe), *held)


epsilon = 1e-05
TILE = 768
BLOCK_COLS = 256
NORM_STEPS = 2
TAIL_STEPS = 2


def gauss_cdf(a):
    return 0.5 * (1.0 + lax.erf(a * 0.7071067811865476))


def gauss_pdf(a):
    return jnp.exp(-0.5 * a * a) * 0.3989422804014327


def struct(shape, dtype):
    return jax.ShapeDtypeStruct(shape, dtype)


def in_hbm(shape, dtype):
    return pltpu.HBM(shape, dtype)


def from_hbm(*arrays):
    return tuple(pltpu.with_memory_space_constraint(a, pltpu.HBM) for a in arrays)


def whole(shape):
    return pl.BlockSpec(shape, lambda *_: (0,) * len(shape))


def call(kernel, name, grid, ins, outs, out_shape, args, scalars=None, scratch=(), aliases=None, vmem=24, cost=None):
    lead = [] if scalars is None else [scalars]
    return pl.pallas_call(
        kernel,
        grid_spec=pltpu.PrefetchScalarGridSpec(
            num_scalar_prefetch=len(lead),
            grid=grid,
            in_specs=ins,
            out_specs=outs,
            scratch_shapes=list(scratch),
        ),
        out_shape=out_shape,
        input_output_aliases=aliases or {},
        compiler_params=pltpu.CompilerParams(vmem_limit_bytes=vmem * 2**20),
        cost_estimate=cost and pl.CostEstimate(flops=cost, bytes_accessed=10**7, transcendentals=0),
        name=name,
    )(*lead, *args)


def normalise(x):
    centred = x - jnp.mean(x, axis=1, keepdims=True)
    inv_std = lax.rsqrt(jnp.mean(centred * centred, axis=1, keepdims=True) + epsilon)
    return centred * inv_std, inv_std


def norm_kernel(tok, gain, bias, w_val, normed, v_act, v_slope):
    x_hat, _ = normalise(tok[...].astype(f32))
    n = (x_hat * gain[...] + bias[...]).astype(bf16)
    normed[...] = n
    v = mm(n, w_val[...])
    cdf = gauss_cdf(v)
    act = (v * cdf).T.astype(bf16)
    slope = (cdf + v * gauss_pdf(v)).T
    shape = (v_act.shape[0], v_act.shape[2], T)
    for q in range(v_act.shape[1]):
        cut = slice(q * T, (q + 1) * T)
        v_act[:, q] = act[:, cut].reshape(shape)
        v_slope[:, q] = slope[:, cut].reshape(shape)


def norm_call(tokens, gain, bias, w_val, chan_n):
    own, width = tokens.shape
    inner = w_val.shape[1]
    quads = own // T
    spread = (chan_n, quads, inner // chan_n, T)
    steps = NORM_STEPS
    block = pl.BlockSpec((chan_n, quads // steps, inner // chan_n, T), lambda i: (0, i, 0, 0))
    rows = pl.BlockSpec((own // steps, width), lambda i: (i, 0))
    return call(
        norm_kernel,
        "norm_val",
        (steps,),
        [rows, whole((1, width)), whole((1, width)), whole(w_val.shape)],
        [rows, block, block],
        [struct((own, width), bf16), struct(spread, bf16), in_hbm(spread, f32)],
        from_hbm(tokens, gain[None], bias[None], w_val),
    )


def gate_tile(normed, grad, w_up, w_mix, w_down, u_act, d_slope, d_yproj):
    u = mm(normed, w_up[...])
    d = mm(grad, w_down[...], NT)
    cdf = gauss_cdf(u)
    act = u * cdf
    u_act[...] = act.astype(bf16)
    d_slope[...] = (d * (cdf + u * gauss_pdf(u))).astype(bf16)
    dyp = (d * act).astype(bf16)
    d_yproj[...] = dyp
    return mm(dyp, w_mix[...], NT)


def gate_first_kernel(
    core, n_own, n_oth, g_own, g_oth, w_up, w_mix, w_down,
    u_act, d_slope, d_yproj, na, ga, acc,
):
    own = n_own.shape[0]
    for h, (n, g) in enumerate(((n_own, g_own), (n_oth, g_oth))):
        na[h * own : (h + 1) * own, :] = n[...]
        ga[h * own : (h + 1) * own, :] = g[...]
    acc[...] = gate_tile(na[...], ga[...], w_up, w_mix, w_down, u_act, d_slope, d_yproj)


def gate_last_kernel(
    core, na, ga, acc, w_up, w_mix, w_down, _u, _s, _d,
    u_act, d_slope, d_yproj, normed_t, dy_own, dy_oth, sums,
):
    j = pl.program_id(0)
    own = na.shape[0] // 2

    @pl.when(j == 0)
    def _():
        sums[...] = acc[...]
        normed_t[...] = na[...].T

    sums[...] += gate_tile(na[...], ga[...], w_up, w_mix, w_down, u_act, d_slope, d_yproj)

    @pl.when(j == pl.num_programs(0) - 1)
    def _():
        shape = (dy_own.shape[0], dy_own.shape[2], T)
        for q in range(dy_own.shape[1]):
            dy_own[:, q] = sums[q * T : (q + 1) * T, :].T.reshape(shape)
            dy_oth[:, q] = sums[own + q * T : own + (q + 1) * T, :].T.astype(bf16).reshape(shape)


def gate_specs(own, w_mix, row_n, first):
    inner, ff = w_mix.shape
    part = ff // row_n
    col = lambda j, s: 2 * (j + first) + s[0]
    return [
        lambda width: pl.BlockSpec((width, part), lambda j, s: (0, col(j, s))),
        pl.BlockSpec((inner, part), lambda j, s: (0, col(j, s))),
        lambda width: pl.BlockSpec((part, width), lambda j, s: (col(j, s), 0)),
        pl.BlockSpec((2 * own, part), lambda j, s: (0, j + first)),
    ]


def gate_first(core, normed, normed_oth, grad, grad_oth, w_up, w_mix, w_down, row_n):
    own, width = normed.shape
    inner, ff = w_mix.shape
    up, mix, down, tile = gate_specs(own, w_mix, row_n, 0)
    tok = whole((own, width))
    pair = (2 * own, width)
    return call(
        gate_first_kernel,
        "gate_first",
        (1,),
        [tok, tok, tok, tok, up(width), mix, down(width)],
        [tile, tile, tile, whole(pair), whole(pair), whole((2 * own, inner))],
        [in_hbm((2 * own, ff // 2), bf16)] * 3
        + [in_hbm(pair, bf16), in_hbm(pair, bf16), in_hbm((2 * own, inner), f32)],
        from_hbm(normed, normed_oth, grad, grad_oth, w_up, w_mix, w_down),
        scalars=core,
        vmem=44,
    )


def gate_last(core, pair_normed, pair_grad, acc, w_up, w_mix, w_down, held, row_n, chan_n):
    own, width = pair_normed.shape[0] // 2, pair_normed.shape[1]
    inner, ff = w_mix.shape
    up, mix, down, tile = gate_specs(own, w_mix, row_n, 1)
    pair = (2 * own, width)
    raw = pl.BlockSpec(memory_space=pl.ANY)
    spread = (chan_n, own // T, inner // chan_n, T)
    return call(
        gate_last_kernel,
        "gate_last",
        (row_n // 2 - 1,),
        [whole(pair), whole(pair), whole(acc.shape), up(width), mix, down(width), raw, raw, raw],
        [tile, tile, tile, whole((width, 2 * own)), whole(spread), whole(spread)],
        [in_hbm((2 * own, ff // 2), bf16)] * 3
        + [in_hbm((width, 2 * own), bf16), in_hbm(spread, f32), in_hbm(spread, bf16)],
        from_hbm(pair_normed, pair_grad, acc, w_up, w_mix, w_down, *held),
        scalars=core,
        scratch=[pltpu.VMEM(acc.shape, f32)],
        aliases={7: 0, 8: 1, 9: 2},
        vmem=48,
    )


def mine_a(s):
    return jnp.where(s[0] == 0, s[1], s[2])


def mine_b(s):
    return jnp.where(s[0] == 0, s[2], s[1])


def row_block(s, a, b, core, high, low):
    x = jnp.where(s[0] == 0, a, b)
    y = jnp.where(s[0] == 0, b, a)
    return x * 16 + core * 8 + high * 4 + low * 2 + y


def mid_kernel(
    s, y_own, y_oth, w_mix, u_act, d_slope, d_yproj, normed_t,
    gate, d_upre, u_give, u_keep, m_give, m_keep, yt, yn, us, ms,
):
    inner = yt.shape[0]

    own = yn.shape[0] // 2

    @pl.when(pl.program_id(0) == 0)
    def _():
        for h, y in enumerate((y_own, y_oth)):
            for q in range(y.shape[1]):
                part = y[:, q].reshape(inner, T)
                at = slice(h * own + q * T, h * own + (q + 1) * T)
                yt[:, at] = part
                yn[at, :] = part.T

    yp = mm(yn[...], w_mix[...])
    gate[...] = (u_act[...].astype(f32) * yp).astype(bf16)
    du = (d_slope[...].astype(f32) * yp).astype(bf16)
    d_upre[...] = du
    us[...] = mm(normed_t[...], du).astype(bf16)
    ms[...] = mm(yt[...], d_yproj[...]).astype(bf16)
    m = u_give.shape[1]
    for sel, out in ((1, u_give), (0, u_keep)):
        a = mine_a(s) ^ sel
        for b in (0, 1):
            for low in (0, 1):
                for high in (0, 1):
                    for core in (0, 1):
                        at = pl.multiple_of(row_block(s, a, b, core, high, low) * m, m)
                        out[b * 8 + low * 4 + high * 2 + core] = us[pl.ds(at, m), :]
    m = m_give.shape[1]
    for sel, out in ((1, m_give), (0, m_keep)):
        low = s[3] ^ sel
        for high in (0, 1):
            for a in (0, 1):
                for b in (0, 1):
                    for core in (0, 1):
                        at = pl.multiple_of(row_block(s, a, b, core, high, low) * m, m)
                        out[high * 8 + a * 4 + b * 2 + core] = ms[pl.ds(at, m), :]


def mid_call(scal, y_own, y_oth, w_mix, u_act, d_slope, d_yproj, normed_t, row_n):
    inner, ff = w_mix.shape
    half = u_act.shape[1]
    own = u_act.shape[0] // 2
    width = normed_t.shape[0]
    per = ff // row_n // TILE
    col = lambda j, s: (2 * (j // per) + s[0]) * per + j % per
    tile = pl.BlockSpec((2 * own, TILE), lambda j, s: (0, j))
    um, mx = width // 32, inner // 32
    ub = pl.BlockSpec((16, um, TILE), lambda j, s: (0, 0, j))
    mb = pl.BlockSpec((16, mx, TILE), lambda j, s: (0, 0, j))
    return call(
        mid_kernel,
        "mix_up",
        (half // TILE,),
        [
            whole(y_own.shape),
            whole(y_own.shape),
            pl.BlockSpec((inner, TILE), lambda j, s: (0, col(j, s))),
            tile,
            tile,
            tile,
            whole(normed_t.shape),
        ],
        [tile, tile, ub, ub, mb, mb],
        [in_hbm((2 * own, half), bf16)] * 2
        + [in_hbm((16, um, half), bf16)] * 2
        + [in_hbm((16, mx, half), bf16)] * 2,
        (y_own, y_oth, *from_hbm(w_mix, u_act, d_slope, d_yproj, normed_t)),
        scalars=scal,
        scratch=[
            pltpu.VMEM((inner, 2 * own), bf16),
            pltpu.VMEM((2 * own, inner), bf16),
            pltpu.VMEM((width, TILE), bf16),
            pltpu.VMEM((inner, TILE), bf16),
        ],
        vmem=32,
        cost=10**10,
    )


def block_kernel(s, gate, d_upre, *refs):
    half = (len(refs) - 3) // 2
    downs, ups, (block_own, dn_own, oth) = refs[:half], refs[half : 2 * half], refs[2 * half :]
    own = block_own.shape[0]
    part = downs[0].shape[0]
    cut = lambda ref, k: ref[:, k * part : (k + 1) * part]
    block = sum(mm(cut(gate, k), w[...]) for k, w in enumerate(downs))
    dn = sum(mm(cut(d_upre, k), w[...], NT) for k, w in enumerate(ups))
    block_own[...] = block[:own]
    dn_own[...] = dn[:own]
    oth[0] = block[own:].astype(bf16)
    oth[1] = dn[own:].astype(bf16)


def block_call(scal, gate, d_upre, w_down, w_up, row_n):
    ff, width = w_down.shape
    own = gate.shape[0] // 2
    part = ff // row_n
    cols = BLOCK_COLS
    out = pl.BlockSpec((own, cols), lambda j, s: (0, j))
    ks = range(row_n // 2)
    return call(
        block_kernel,
        "block",
        (width // cols,),
        [whole(gate.shape), whole(d_upre.shape)]
        + [pl.BlockSpec((part, cols), lambda j, s, k=k: (2 * k + s[0], j)) for k in ks]
        + [pl.BlockSpec((cols, part), lambda j, s, k=k: (j, 2 * k + s[0])) for k in ks],
        [out, out, pl.BlockSpec((2, own, cols), lambda j, s: (0, 0, j))],
        [in_hbm((own, width), f32), in_hbm((own, width), f32), in_hbm((2, own, width), bf16)],
        from_hbm(gate, d_upre, *[w_down for _ in ks], *[w_up for _ in ks]),
        scalars=scal,
        vmem=36,
    )


def split_kernel(s, down_g, down_k, d_give, d_keep):
    for src, dst in ((down_g, d_give), (down_k, d_keep)):
        for low in (0, 1):
            for high in (0, 1):
                dst[low * 2 + high] = src[high * 2 + low]


def split_call(scal, down):
    rows, width = down.shape[0] // 16, down.shape[1]
    view = down.reshape(2, 4, 2, rows, width)

    def block_of(sel):
        def at(i, s):
            a = mine_a(s) ^ sel
            return jnp.where(s[0] == 0, a, i), 0, jnp.where(s[0] == 0, i, a), 0, 0

        return pl.BlockSpec((None, 4, None, rows, width), at)

    out = pl.BlockSpec((4, rows, width), lambda i, s: (i, 0, 0))
    return call(
        split_kernel,
        "split",
        (2,),
        [block_of(1), block_of(0)],
        [out, out],
        [struct((8, rows, width), bf16)] * 2,
        (view, view),
        scalars=scal,
    )


def val_kernel(s, v_own, v_oth, normed_t, v_give, v_keep, vs, vt):
    inner, pair = vt.shape
    for h, v in enumerate((v_own, v_oth)):
        for q in range(v.shape[1]):
            at = h * pair // 2 + q * T
            vt[:, at : at + T] = v[:, q].reshape(inner, T)
    vs[...] = mm(normed_t[...], vt[...], NT)
    m = vs.shape[0] // 32
    for sel, out in ((1, v_give), (0, v_keep)):
        a = mine_a(s) ^ sel
        for b in (0, 1):
            for low in (0, 1):
                for high in (0, 1):
                    cut = []
                    for core in (0, 1):
                        at = pl.multiple_of(row_block(s, a, b, core, high, low) * m, m)
                        cut.append(vs[pl.ds(at, m), :])
                    parts = [
                        jnp.concatenate([c[r * 8 : r * 8 + 8] for c in cut], 0)
                        for r in range(m // 8)
                    ]
                    out[b * 4 + low * 2 + high] = jnp.concatenate(parts, 1).astype(bf16)


def val_call(scal, d_vpre, v_oth, normed_t):
    half = v_oth.shape
    inner = half[0] * half[2]
    width, pair = normed_t.shape
    buf = (8, 16, width)
    return call(
        val_kernel,
        "val",
        (1,),
        [
            pl.BlockSpec(half, lambda i, s: (s[0], 0, 0, 0)),
            whole(half),
            whole(normed_t.shape),
        ],
        [whole(buf), whole(buf)],
        [struct(buf, bf16)] * 2,
        (d_vpre, v_oth, normed_t),
        scalars=scal,
        scratch=[pltpu.VMEM((width, inner), f32), pltpu.VMEM((inner, pair), bf16)],
    )


def step_kernel(bit, keep_g, got_g, keep_k, got_k, give, keep):
    give[...] = (keep_g[0].astype(f32) + got_g[0].astype(f32)).astype(bf16)
    keep[...] = (keep_k[0].astype(f32) + got_k[0].astype(f32)).astype(bf16)


def step_call(bit, keep, got):
    n, rows, cols = keep.shape
    n //= 2
    nb = max(1, n // 4)
    view = (2, n, rows, cols)
    other = pl.BlockSpec((1, nb, rows, cols), lambda i, b: (1 - b[0], i, 0, 0))
    same = pl.BlockSpec((1, nb, rows, cols), lambda i, b: (b[0], i, 0, 0))
    out = pl.BlockSpec((nb, rows, cols), lambda i, b: (i, 0, 0))
    keep, got = keep.reshape(view), got.reshape(view)
    return call(
        step_kernel,
        "halve",
        (n // nb,),
        [other, other, same, same],
        [out, out],
        [struct((n, rows, cols), bf16)] * 2,
        (keep, got, keep, got),
        scalars=bit,
    )


def tail_kernel(
    tok, grad, gain, block_own, got, dn_own, d_vpre, w_val, block_out, tokens_grad, norm_part, acc
):
    i = pl.program_id(0)
    x = tok[...].astype(f32)
    x_hat, inv_std = normalise(x)
    block_out[...] = (x + block_own[...] + got[0].astype(f32)).astype(bf16)
    dv = jnp.concatenate(
        [d_vpre[:, q].reshape(w_val.shape[1], T).T for q in range(d_vpre.shape[1])], 0
    )
    dn = dn_own[...] + got[1].astype(f32) + mm(dv, w_val[...], NT)
    dx = dn * gain[...]
    tokens_grad[...] = grad[...].astype(f32) + inv_std * (
        dx
        - jnp.mean(dx, axis=1, keepdims=True)
        - x_hat * jnp.mean(dx * x_hat, axis=1, keepdims=True)
    )
    sums = jnp.concatenate(
        [jnp.sum(dn * x_hat, axis=0, keepdims=True), jnp.sum(dn, axis=0, keepdims=True)], 0
    )

    @pl.when(i == 0)
    def _():
        acc[...] = sums

    @pl.when(i > 0)
    def _():
        acc[...] += sums

    @pl.when(i == pl.num_programs(0) - 1)
    def _():
        parts, lanes = norm_part.shape
        w = acc.shape[1] // parts
        for k in range(parts):
            cut = acc[:, k * w : (k + 1) * w]
            blank = jnp.zeros((1, lanes - 2 * w), f32)
            norm_part[k : k + 1, :] = jnp.concatenate([cut[0:1], cut[1:2], blank], 1)


def tail_call(tokens, grad, gain, block_own, got, dn_own, d_vpre, w_val, parts):
    own, width = tokens.shape
    steps = TAIL_STEPS
    rows = pl.BlockSpec((own // steps, width), lambda i: (i, 0))
    chan_n, quads, group, _ = d_vpre.shape
    return call(
        tail_kernel,
        "norm_back",
        (steps,),
        [
            rows,
            rows,
            whole((1, width)),
            rows,
            pl.BlockSpec((2, own // steps, width), lambda i: (0, i, 0)),
            rows,
            pl.BlockSpec((chan_n, quads // steps, group, T), lambda i: (0, i, 0, 0)),
            whole(w_val.shape),
        ],
        [rows, rows, whole((parts, T))],
        [struct((own, width), bf16), struct((own, width), f32), struct((parts, T), f32)],
        from_hbm(tokens, grad, gain[None], block_own, got, dn_own, d_vpre, w_val),
        scratch=[pltpu.VMEM((2, width), f32)],
        vmem=32,
    )


def finish_kernel(s, u_keep, u_got, m_keep, m_got, d_keep, d_got, v_keep, *rest):
    *v_gots, norm, down, mine, other = rest
    down[...] = d_keep[0].astype(f32) + d_got[0].astype(f32)
    v = sum([g[0].astype(f32) for g in v_gots], v_keep[0].astype(f32))
    half = v.shape[1]
    um, mx = u_keep.shape[1], m_keep.shape[1]
    tail = um + mx + 8
    for out, core, owner in ((mine, s[0], s[5]), (other, 1 - s[0], s[6])):
        out[0:um, :] = u_keep[core].astype(f32) + u_got[core].astype(f32)
        out[um : um + mx, :] = m_keep[core].astype(f32) + m_got[core].astype(f32)
        out[um + mx : tail, 0:half] = jnp.where(core == 0, v[:8], v[8:])
        out[um + mx : tail, half:] = jnp.zeros((8, out.shape[1] - half), f32)
        out[tail:, :] = jnp.zeros((8, out.shape[1]), f32)
        out[tail : tail + 1, 0:T] = norm[pl.ds(owner, 1), :]


def finish_call(scal, up, mix, down, val, norm):
    um, mx, half = up[0].shape[1], mix[0].shape[1], up[0].shape[2]
    rows, width = down[0].shape[1:]
    args = (*up, *mix, *down, *val, norm)
    pack = (um + mx + 16, half)
    return call(
        finish_kernel,
        "finish",
        (1,),
        [whole(a.shape) for a in args],
        [whole((rows, width)), whole(pack), whole(pack)],
        [struct((rows, width), f32), struct(pack, f32), struct(pack, f32)],
        args,
        scalars=scal,
    )


def join_kernel(s, mine, got, up, mix, val, norm):
    um, mx = up.shape[0], mix.shape[0]
    first = s[0] == 0
    part = mine.shape[1] // 2
    for core in (0, 1):
        held = jnp.where(first, mine[...], got[...]) if core == 0 else jnp.where(first, got[...], mine[...])
        for x in (0, 1):
            to = slice((2 * x + core) * part, (2 * x + core + 1) * part)
            up[:, to] = held[0:um, x * part : (x + 1) * part]
            mix[:, to] = held[um : um + mx, x * part : (x + 1) * part]
        w = val.shape[1] // 2
        for r in range(val.shape[0] // 8):
            at = slice(r * w, (r + 1) * w)
            val[r * 8 : r * 8 + 8, core * w : (core + 1) * w] = held[um + mx : um + mx + 8, at]
    norm[...] = mine[um + mx + 8 :, 0:T] + got[um + mx + 8 :, 0:T]


def join_call(scal, mine, got, um, mx, inner):
    ff = mine.shape[1] * 2
    return call(
        join_kernel,
        "join",
        (1,),
        [whole(mine.shape)] * 2,
        [whole((um, ff)), whole((mx, ff)), whole((um, inner)), whole((8, T))],
        [
            struct((um, ff), f32),
            struct((mx, ff), f32),
            struct((um, inner), f32),
            struct((8, T), f32),
        ],
        (mine, got),
        scalars=scal,
    )


def make_square(row_n, chan_n):
    def on_device(
        tokens, starts, layer_norm_gain, ln_bias, w_up, w_val, w_mix, w_down,
        decay_rate, mix_coef, out_grad,
    ):
        own, width = tokens.shape
        inner = w_val.shape[1]
        row, chan = lax.axis_index("row"), lax.axis_index("chan")
        core = row % 2
        me = row * chan_n + chan
        there = (row ^ 1) * chan_n + chan
        y_bit = chan % 2
        b_bit = jnp.where(core == 0, y_bit, row // 2)
        scal = jnp.stack([core, row // 2, y_bit, (chan // 2) % 2, chan // 4, me, there, b_bit])
        scal = scal.astype(jnp.int32)
        bit_x, bit_y = scal[1], scal[2]
        bit_a = jnp.where(core == 0, bit_x, bit_y).reshape(1)
        bit_b = jnp.where(core == 0, bit_y, bit_x).reshape(1)
        bit_low, bit_high = scal[3:4], scal[4:5]
        devices = [(r, c) for r in range(row_n) for c in range(chan_n)]
        flip_x = lambda r, c: (r ^ 2, c)
        flip_y = lambda r, c: (r, c ^ 1)
        moves = dict(
            core=lambda r, c: (r ^ 1, c),
            a=lambda r, c: flip_y(r, c) if r % 2 else flip_x(r, c),
            b=lambda r, c: flip_x(r, c) if r % 2 else flip_y(r, c),
            low=lambda r, c: (r, c ^ 2),
            high=lambda r, c: (r, c ^ 4),
            x=lambda r, c: (r ^ 2, c),
            ab=lambda r, c: (r ^ 2, c ^ 1),
            z=lambda r, c: (r, c ^ 6),
        )

        def send(value, way):
            to = [moves[way](r, c) for r, c in devices]
            pairs = [(r * chan_n + c, t[0] * chan_n + t[1]) for (r, c), t in zip(devices, to)]
            return lax.ppermute(value, ("row", "chan"), pairs)

        after = lax.optimization_barrier
        trade = lambda v: lax.all_to_all(v, "chan", split_axis=0, concat_axis=0, tiled=True)
        rows = own * chan_n // T
        to_seq = lambda v: v.reshape(rows, inner // chan_n, T)
        to_tok = lambda v: v.reshape(chan_n, own // T, inner // chan_n, T)

        masks = ssm_masks(starts)
        grad_oth = send(out_grad, "core")
        normed, v_act, v_slope = norm_call(tokens, layer_norm_gain, ln_bias, w_val, chan_n)
        normed_oth = send(normed, "core")
        v_chan = to_seq(trade(v_act))
        *gated, pair_normed, pair_grad, acc = gate_first(
            scal, normed, normed_oth, out_grad, grad_oth, w_up, w_mix, w_down, row_n
        )
        v_chan, acc = after((v_chan, acc))
        y_chan, states, toeplitz = ssm_fwd(v_chan, decay_rate, mix_coef, masks)
        y_chan, acc = after((y_chan, acc))
        y_own = trade(to_tok(y_chan))
        u_act, d_slope, d_yproj, normed_t, dy_own, dy_oth = gate_last(
            scal, pair_normed, pair_grad, acc, w_up, w_mix, w_down, gated, row_n, chan_n
        )
        d_y = (dy_own + send(dy_oth, "core").astype(f32)).astype(bf16)
        y_own, d_y = after((y_own, d_y))
        y_oth = send(y_own, "core")
        d_y_chan = to_seq(trade(d_y))
        gate_out, d_upre, u_give, u_keep, m_give, m_keep = mid_call(
            scal, y_own, y_oth, w_mix, u_act, d_slope, d_yproj, normed_t, row_n
        )
        u_give, m_give, gate_out, d_y_chan = after((u_give, m_give, gate_out, d_y_chan))
        back = lambda part, held, d_y_chan: ssm_bwd(
            v_chan, d_y_chan, decay_rate, mix_coef, masks, states, toeplitz, row_n, part, 2, held
        )

        u_got = send(u_give, "a")
        m_got = send(m_give, "low")
        down = mm(gate_out, pair_grad, TN).astype(bf16)
        d_give, d_keep = split_call(scal, down)
        held = back(0, (), d_y_chan)
        u_got, m_got, d_give, gate_out, d_y_chan, *held = after(
            (u_got, m_got, d_give, gate_out, d_y_chan, *held)
        )

        d_got = send(d_give, "a")
        m_give, m_keep = step_call(bit_high, m_keep, m_got)
        m_got = send(m_give, "high")
        d_v_chan, rates = back(1, tuple(held), d_y_chan)
        u_give, u_keep = step_call(bit_b, u_keep, u_got)
        d_v_chan, u_give, gate_out, rates = after((d_v_chan, u_give, gate_out, rates))
        d_v = trade(to_tok(d_v_chan))
        d_got, m_got, u_give = after((d_got, m_got, u_give))
        u_got = send(u_give, "b")
        block_own, dn_own, bd_give = block_call(scal, gate_out, d_upre, w_down, w_up, row_n)
        d_give, d_keep = step_call(bit_b, d_keep, d_got)
        rates_give = lax.dynamic_index_in_dim(rates, 1 - core, 0, keepdims=False)
        rates_got = send(rates_give, "core")
        u_got, d_give, bd_give, d_v, rates_got = after((u_got, d_give, bd_give, d_v, rates_got))

        d_got = send(d_give, "b")
        u_give, u_keep = step_call(bit_low, u_keep, u_got)
        u_give, d_v, m_got = after((u_give, d_v, m_got))
        u_got = send(u_give, "low")
        half = chan_n // 2
        other_half = lambda v: lax.dynamic_slice_in_dim(v, (1 - core) * half, half, 0)
        v_give = (other_half(d_v).astype(f32) * other_half(v_slope)).astype(bf16)
        v_got = send(v_give, "core")
        bd_got = send(bd_give, "core")
        d_vpre = (d_v.astype(f32) * v_slope).astype(bf16)
        v_give, v_keep = val_call(scal, d_vpre, v_got, normed_t)
        v_got = send(v_give, "a")
        v_give, d_vpre = after((v_give, d_vpre))
        block_out, tokens_grad, norm_part = tail_call(
            tokens, out_grad, layer_norm_gain, block_own, bd_got, dn_own, d_vpre, w_val,
            row_n * chan_n,
        )
        d_got, u_got, m_got, v_got, norm_part = after((d_got, u_got, m_got, v_got, norm_part))

        d_give, d_keep = step_call(bit_low, d_keep, d_got)
        d_got = send(d_give, "low")
        u_give, u_keep = step_call(bit_high, u_keep, u_got)
        u_give, norm_part, m_got, v_got = after((u_give, norm_part, m_got, v_got))
        u_got = send(u_give, "high")
        m_give, m_keep = step_call(bit_a, m_keep, m_got)
        m_got = send(m_give, "a")
        rates = lax.dynamic_index_in_dim(rates, core, 0, keepdims=False) + rates_got
        rates_give = lax.dynamic_index_in_dim(rates, 1 - bit_x, 0, keepdims=False)
        v_give, v_keep = step_call(bit_b, v_keep, v_got)
        v_got = send(v_give, "b")
        v_give, v_keep = step_call(bit_low, v_keep, v_got)
        v_got = send(v_give, "low")
        norm_part = norm_part + send(norm_part, "a")
        norm_part = norm_part + send(norm_part, "b")
        d_got, m_got, u_got, v_got, norm_part, rates_give = after(
            (d_got, m_got, u_got, v_got, norm_part, rates_give)
        )

        d_give, d_keep = step_call(bit_high, d_keep, d_got)
        d_give, norm_part, rates_give = after((d_give, norm_part, rates_give))
        d_got = send(d_give, "high")
        rates_got = send(rates_give, "x")
        m_give, m_keep = step_call(bit_b, m_keep, m_got)
        m_got = send(m_give, "b")
        v_give, v_keep = step_call(bit_high, v_keep, v_got)
        v_got = send(v_give, "high")
        norm_part = norm_part + send(norm_part, "low")
        norm_part = norm_part + send(norm_part, "high")
        d_got, m_got, norm_part, v_got, rates_got = after(
            (d_got, m_got, norm_part, v_got, rates_got)
        )
        rates = lax.dynamic_index_in_dim(rates, bit_x, 0, keepdims=False) + rates_got

        down_grad, mine, other = finish_call(
            scal, (u_keep, u_got), (m_keep, m_got), (d_keep, d_got), (v_keep, v_got), norm_part
        )
        um, mx = u_keep.shape[1], m_keep.shape[1]
        other = send(other, "core")
        up_grad, mix_grad, val_grad, norm_sum = join_call(scal, mine, other, um, mx, inner)
        norm_sum = norm_sum[0]
        w = width // (row_n * chan_n)
        return (
            block_out,
            tokens_grad,
            norm_sum[:w],
            norm_sum[w : 2 * w],
            up_grad,
            val_grad,
            mix_grad,
            down_grad,
            rates[0],
            rates[1],
        )

    return on_device


def make_general(row_n, chan_n):
    row_hi = row_n // 2

    def swap(value, axis, bit):
        size = row_n if axis == "row" else chan_n
        return lax.ppermute(value, axis, [(i, i ^ (1 << bit)) for i in range(size)])

    def core_swap(value):
        return swap(value, "row", 0)

    def bits_of(size):
        return size.bit_length() - 1

    def scatter_sum(part, names, order, last_dtype):
        names = list(names)
        for step, name in enumerate(order):
            axis, bit = name
            dim = names.index(name)
            mine = (lax.axis_index(axis) >> bit) & 1
            keep = lax.dynamic_index_in_dim(part, mine, dim, keepdims=False)
            give = lax.dynamic_index_in_dim(part, 1 - mine, dim, keepdims=False)
            got = swap(give, axis, bit)
            part = keep.astype(jnp.float32) + got.astype(jnp.float32)
            if step < len(order) - 1:
                part = part.astype(give.dtype)
            else:
                part = part.astype(last_dtype)
            names.pop(dim)
        return part

    row_bits = [("row", k) for k in range(bits_of(row_n) - 1, 0, -1)]
    core_bit = ("row", 0)
    chan_bits = [("chan", k) for k in range(bits_of(chan_n) - 1, -1, -1)]
    near_y = chan_bits[2:]
    along_z = chan_bits[:2][::-1]

    def on_device(
        tokens,
        starts,
        layer_norm_gain,
        ln_bias,
        w_up,
        w_val,
        w_mix,
        w_down,
        decay_rate,
        mix_coef,
        out_grad,
    ):
        own, width = tokens.shape
        ff = w_up.shape[1]
        inner = w_val.shape[1]
        part_ff = ff // row_n
        core = lax.axis_index("row") % 2
        mm = lambda a, b, ca, cb: lax.dot_general(
            a, b, (((ca,), (cb,)), ((), ())), preferred_element_type=jnp.float32
        )
        masks = ssm_masks(starts)
        inputs_f = tokens.astype(jnp.float32)
        row_mean = jnp.mean(inputs_f, axis=1, keepdims=True)
        centred = inputs_f - row_mean
        inv_std = lax.rsqrt(jnp.mean(centred * centred, axis=1, keepdims=True) + epsilon)
        x_hat = centred * inv_std
        normed = (x_hat * layer_norm_gain + ln_bias).astype(jnp.bfloat16)
        v_pre = mm(w_val, normed, 0, 1)
        v_cdf = gauss_cdf(v_pre)
        v_act = (v_pre * v_cdf).astype(jnp.bfloat16)
        v_slope = v_cdf + v_pre * gauss_pdf(v_pre)
        v_chan = lax.all_to_all(
            v_act.reshape(inner, own // T, T), "chan", split_axis=0, concat_axis=1, tiled=True
        )
        v_chan = jnp.swapaxes(v_chan, 0, 1)
        pair_normed = jnp.concatenate([normed, core_swap(normed)], 0)
        pair_grad = jnp.concatenate([out_grad, core_swap(out_grad)], 0)
        halves = lambda w, d: lax.dynamic_index_in_dim(
            w.reshape(w.shape[:d] + (row_hi, 2, part_ff) + w.shape[d + 1 :]), core, d + 1, keepdims=False
        ).reshape(w.shape[:d] + (ff // 2,) + w.shape[d + 1 :])
        up_half = halves(w_up, 1)
        mix_half = halves(w_mix, 1)
        down_half = halves(w_down, 0)
        u_pre = mm(pair_normed, up_half, 1, 0)
        d_gate = mm(pair_grad, down_half, 1, 1)
        u_cdf = gauss_cdf(u_pre)
        u_act = u_pre * u_cdf
        d_yproj = (d_gate * u_act).astype(jnp.bfloat16)
        d_slope = d_gate * (u_cdf + u_pre * gauss_pdf(u_pre))
        d_y_part = mm(mix_half, d_yproj, 1, 1)
        d_y = (
            d_y_part[:, :own] + core_swap(d_y_part[:, own:].astype(jnp.bfloat16)).astype(jnp.float32)
        ).astype(jnp.bfloat16)
        d_y_chan = lax.all_to_all(
            d_y.reshape(inner, own // T, T), "chan", split_axis=0, concat_axis=1, tiled=True
        )
        d_y_chan = jnp.swapaxes(d_y_chan, 0, 1)
        y_chan, states, toeplitz = ssm_fwd(v_chan, decay_rate, mix_coef, masks)
        y_chan = jnp.swapaxes(y_chan, 0, 1)
        y_own = lax.all_to_all(y_chan, "chan", split_axis=1, concat_axis=0, tiled=True)
        y_own = y_own.reshape(inner, own)
        d_v_chan, rates = ssm_bwd(
            v_chan, d_y_chan, decay_rate, mix_coef, masks, states, toeplitz, row_n
        )
        d_v_chan = jnp.swapaxes(d_v_chan, 0, 1)
        d_v = lax.all_to_all(d_v_chan, "chan", split_axis=1, concat_axis=0, tiled=True)
        pair_y = jnp.concatenate([y_own, core_swap(y_own)], 1)
        split_rows = lambda a, lead: a.reshape((2,) * lead + (-1,) + a.shape[1:])
        y_proj = mm(pair_y, mix_half, 0, 0)
        gate_out = (u_act * y_proj).astype(jnp.bfloat16)
        d_upre = (d_slope * y_proj).astype(jnp.bfloat16)
        mix_part = mm(pair_y, d_yproj, 1, 0).astype(jnp.bfloat16)
        down_part = mm(gate_out, pair_grad, 0, 0).astype(jnp.bfloat16)
        up_part = mm(pair_normed, d_upre, 0, 0).astype(jnp.bfloat16)
        all_names = row_bits + [core_bit] + chan_bits
        no_core = row_bits + chan_bits
        lead = len(all_names)
        mix_sum = scatter_sum(
            split_rows(mix_part, lead), all_names, along_z + row_bits + near_y, jnp.float32
        )
        up_sum = scatter_sum(
            split_rows(up_part, lead), all_names, row_bits + near_y + along_z, jnp.float32
        )
        down_grad = scatter_sum(
            split_rows(down_part, lead - 1), no_core, near_y + row_bits + along_z, jnp.float32
        )

        def join_cores(halfsum):
            mine = lax.dynamic_index_in_dim(halfsum, core, 0, keepdims=False)
            other = core_swap(lax.dynamic_index_in_dim(halfsum, 1 - core, 0, keepdims=False))
            shape = (mine.shape[0], row_hi, part_ff)
            low = jnp.where(core == 0, mine, other).reshape(shape)
            high = jnp.where(core == 0, other, mine).reshape(shape)
            return jnp.stack([low, high], 2).reshape(mine.shape[0], ff)

        block_part = mm(gate_out, down_half, 1, 0)
        block_out = (
            inputs_f
            + block_part[:own]
            + core_swap(block_part[own:].astype(jnp.bfloat16)).astype(jnp.float32)
        ).astype(jnp.bfloat16)
        d_normed_part = mm(d_upre, up_half, 1, 1)
        d_normed_got = core_swap(d_normed_part[own:].astype(jnp.bfloat16)).astype(jnp.float32)
        d_vpre = (d_v.reshape(inner, own).astype(jnp.float32) * v_slope).astype(jnp.bfloat16)
        val_part = mm(normed, d_vpre, 0, 1).astype(jnp.bfloat16)
        val_grad = scatter_sum(
            split_rows(val_part, lead),
            all_names,
            [core_bit] + along_z + near_y + row_bits,
            jnp.float32,
        )
        d_normed = d_normed_part[:own] + d_normed_got + mm(d_vpre, w_val, 0, 1)
        norm_part = jnp.stack([jnp.sum(d_normed * x_hat, axis=0), jnp.sum(d_normed, axis=0)], 1)
        norm_sum = scatter_sum(
            split_rows(norm_part, lead), all_names, [core_bit] + row_bits + chan_bits, jnp.float32
        )
        d_xh = d_normed * layer_norm_gain
        tokens_grad = out_grad.astype(jnp.float32) + inv_std * (
            d_xh
            - jnp.mean(d_xh, axis=1, keepdims=True)
            - x_hat * jnp.mean(d_xh * x_hat, axis=1, keepdims=True)
        )
        row_all = [core_bit] + row_bits
        chans, lanes = rates.shape[-2:]
        rates = rates.reshape((2,) * len(row_all) + (2 * chans, lanes))
        rates = scatter_sum(rates, row_all, row_all, jnp.float32).reshape(2, chans, lanes)
        return (
            block_out,
            tokens_grad,
            norm_sum[:, 0],
            norm_sum[:, 1],
            join_cores(up_sum),
            val_grad,
            join_cores(mix_sum),
            down_grad,
            rates[0],
            rates[1],
        )

    return on_device


def solution(mesh):
    spread = P(("row", "chan"), None)
    row_n, chan_n = mesh.shape["row"], mesh.shape["chan"]
    make = make_square if (row_n, chan_n) == (4, 8) else make_general
    return jax.shard_map(
        make(row_n, chan_n),
        mesh=mesh,
        in_specs=(
            spread,
            P("row", None),
            P(),
            P(),
            P(),
            P(),
            P(),
            P(),
            P("chan", None),
            P("chan", None),
            spread,
        ),
        out_specs=(
            spread,
            spread,
            P(("row", "chan")),
            P(("row", "chan")),
            spread,
            spread,
            spread,
            spread,
            P("chan", "row"),
            P("chan", "row"),
        ),
        check_vma=False,
    )
```

```python
import functools

import jax
import jax.numpy as jnp
from jax import lax
from jax.experimental import pallas as pl
from jax.experimental.pallas import tpu as pltpu
from jax.sharding import PartitionSpec as P

T = 128
SUB = 8
GROUP = 16
SEG = 4
f32 = jnp.float32
bf16 = jnp.bfloat16
NT = (((1,), (1,)), ((), ()))
TN = (((0,), (0,)), ((), ()))
NN = (((1,), (0,)), ((), ()))


def mm(a, b, d=NN):
    return lax.dot_general(a, b, d, preferred_element_type=f32)


def iota(shape, d):
    return lax.broadcasted_iota(jnp.int32, shape, d)


def powers(rate_row, pt_ref, c):
    n = rate_row.shape[1]
    steps = iota((8, n), 0).astype(f32)
    r8 = jnp.broadcast_to(rate_row, (8, n))
    parts = [jnp.exp(-r8 * steps)]
    fade = jnp.exp(-8.0 * r8)
    while len(parts) < T // 8:
        parts = parts + [p * fade for p in parts]
        fade = fade * fade
    for i in range(0, len(parts), 2):
        pt_ref[c, i * 8 : i * 8 + 16, :] = jnp.concatenate(parts[i : i + 2], 0).astype(bf16)


def put(ref, c, val, rows):
    for q in range(val.shape[1] // T):
        ref[q, pl.ds(c, rows, stride=SUB), :] = val[:, q * T : (q + 1) * T]


def take(ref, c, rows):
    return jnp.concatenate(
        [ref[q, pl.ds(c, rows, stride=SUB), :] for q in range(ref.shape[0])], 1
    )


def tiles(v):
    return jnp.stack([v[:, q * T : (q + 1) * T] for q in range(v.shape[1] // T)])


def untile(v):
    return jnp.concatenate([v[q] for q in range(v.shape[0])], 1)


def flip_matrix():
    return (iota((T, T), 0) + iota((T, T), 1) == T - 1).astype(f32).astype(bf16)


def seg_masks(ins, g):
    return jnp.concatenate([(ins == g * SEG + k).astype(f32) for k in range(SEG)], 0)


def rep(x):
    return jnp.concatenate([x] * SEG, 0)


def fold(o, m, rows):
    o = o * m
    out = o[0:rows]
    for k in range(1, SEG):
        out = out + o[k * rows : (k + 1) * rows]
    return out


def far_part(a, p, rows):
    hi = a.astype(bf16)
    lo = (a - hi.astype(f32)).astype(bf16)
    o = mm(jnp.concatenate([hi, lo], 0), p, NT)
    return o[:rows] + o[rows:]


def lanes_of(ref, c, rows):
    return ref[pl.ds(c, rows, stride=GROUP), :]


def fwd_kernel(sm, x, rate, coef, ins, insj, head, tailj, y, hs, toe, pt, ss, near, xs, kr):
    rows = ins.shape[0]
    n = rate.shape[1]
    flip = flip_matrix()
    xs[...] = x[...].astype(f32).reshape(rows * GROUP, T)
    tail = tailj[...]
    hd = head[...]
    m0 = seg_masks(ins[...], 0)
    m0b = m0.astype(bf16)
    tri = iota((T, T), 1) >= iota((T, T), 0)
    for sub in range(GROUP // SUB):
        lo = sub * SUB
        cf = coef[lo : lo + SUB, :]
        rt = rate[lo : lo + SUB, :]
        cfh = cf.astype(bf16)
        cfl = (cf - cfh.astype(f32)).astype(bf16)
        cf2 = jnp.concatenate([cfh, cfl], 0)
        xj = []
        for c in range(SUB):
            xc = lanes_of(xs, lo + c, rows).astype(bf16)
            xj.append(mm(xc, flip).astype(bf16) * tail)
        for c in range(SUB):
            powers(rt[c : c + 1], pt, c)
            k2 = mm(cf2, pt[c], NT)
            kr[c : c + 1, :] = k2[c : c + 1] + k2[SUB + c : SUB + c + 1]
        for c in range(SUB):
            put(ss, c, mm(xj[c], pt[c]), rows)
        for c in range(SUB):
            k = jnp.broadcast_to(kr[c : c + 1, :], (T, T))
            kb = pltpu.roll(k, 0, 1, stride=1, stride_axis=0)
            tp = jnp.where(tri, kb, 0.0).astype(bf16)
            toe[lo + c] = tp
            xc = lanes_of(xs, lo + c, rows).astype(bf16)
            near[c] = fold(mm(rep(xc) * m0b, tp), m0, rows)
        fade = tiles(jnp.exp(-float(T) * rt))
        ce = tiles(cf * jnp.exp(-rt))
        h = jnp.zeros((n // T, SUB, T), f32)
        for b in range(rows):
            w = slice(b * SUB, (b + 1) * SUB)
            hs[sub, :, w, :] = h
            s = ss[:, w, :]
            ss[:, w, :] = h * ce
            h = h * (fade * sm[0, b].astype(f32)) + s

        @pl.loop(1, sm[1, 0])
        def _(g):
            m = seg_masks(ins[...], g)
            for c in range(SUB):
                xc = lanes_of(xs, lo + c, rows).astype(bf16)
                near[c] += fold(mm(rep(xc) * m.astype(bf16), toe[lo + c]), m, rows)

        for c in range(SUB):
            far = far_part(take(ss, c, rows), pt[c], rows)
            xs[pl.ds(lo + c, rows, stride=GROUP), :] = near[c] + hd * far
    y[...] = xs[...].reshape(rows, GROUP, T).astype(bf16)


def bwd_kernel(
    sm, x, dy, rate, coef, ins, insj, head, tailj, hs, toe, *rest
):
    dv, rates, pt, s1, e0, e1, near, gacc, nr, xs, ys = rest[-11:]
    rows = ins.shape[0]
    n = rate.shape[1]
    flip = flip_matrix()
    xs[...] = x[...].astype(f32).reshape(rows * GROUP, T)
    ys[...] = dy[...].astype(f32).reshape(rows * GROUP, T)
    tail = tailj[...]
    hdb = head[...].astype(bf16)
    mn = seg_masks(ins[...], 0).astype(bf16)
    mj = seg_masks(insj[...], 0)
    mjb = mj.astype(bf16)
    lag = iota((rows, T), 1).astype(f32).astype(bf16)
    lag1 = (iota((rows, T), 1) + 1).astype(f32).astype(bf16)
    lagf = iota((1, T), 1).astype(f32)
    valid = iota((T, T), 0) + iota((T, T), 1) >= T - 1
    row16 = iota((16, T), 0)

    def lags(d, xx, md, mx):
        o = mm(rep(d) * md, rep(xx) * mx, TN)
        o = pltpu.roll(jnp.where(valid, o, 0.0), 1, 1, stride=1, stride_axis=0)
        return jnp.sum(o, axis=0, keepdims=True)

    for sub in range(GROUP // SUB):
        lo = sub * SUB
        rt = rate[lo : lo + SUB, :]
        cf = coef[lo : lo + SUB, :]
        xa = jnp.concatenate([lanes_of(xs, lo + c, rows) for c in range(SUB)], 0).astype(bf16)
        da = jnp.concatenate([lanes_of(ys, lo + c, rows) for c in range(SUB)], 0).astype(bf16)
        xja = mm(xa, flip).astype(bf16)
        dja = mm(da, flip).astype(bf16)
        for c in range(SUB):
            sl = slice(c * rows, (c + 1) * rows)
            near[c] = fold(mm(rep(dja[sl]) * mjb, toe[lo + c]), mj, rows)
            gacc[c : c + 1, :] = lags(da[sl], xja[sl], mn, mjb)

        @pl.loop(1, sm[1, 0])
        def _(g):
            m = seg_masks(ins[...], g).astype(bf16)
            k = seg_masks(insj[...], g)
            kb = k.astype(bf16)
            for c in range(SUB):
                d = lanes_of(ys, lo + c, rows).astype(bf16)
                xx = lanes_of(xs, lo + c, rows).astype(bf16)
                dj = mm(d, flip).astype(bf16)
                xj = mm(xx, flip).astype(bf16)
                near[c] += fold(mm(rep(dj) * kb, toe[lo + c]), k, rows)
                gacc[c : c + 1, :] += lags(d, xj, m, kb)

        for c in range(SUB):
            sl = slice(c * rows, (c + 1) * rows)
            powers(rt[c : c + 1], pt, c)
            gr = gacc[c : c + 1, :]
            gl = gr * lagf
            gh = gr.astype(bf16).astype(f32)
            glh = gl.astype(bf16).astype(f32)
            gm = jnp.where(row16 == 2, glh, jnp.where(row16 == 3, gl - glh, 0.0))
            gm = jnp.where(row16 == 0, gh, jnp.where(row16 == 1, gr - gh, gm)).astype(bf16)
            dh = da[sl] * hdb
            o = mm(jnp.concatenate([xja[sl] * tail * lag, dh, dh * lag1, gm], 0), pt[c])
            put(s1, c, o[0:rows], rows)
            put(e0, c, o[rows : 2 * rows], rows)
            put(e1, c, o[2 * rows : 3 * rows], rows)
            k = 3 * rows
            nr[c : c + 1, :] = o[k : k + 1] + o[k + 1 : k + 2]
            nr[SUB + c : SUB + c + 1, :] = o[k + 2 : k + 3] + o[k + 3 : k + 4]
        fade = tiles(jnp.exp(-float(T) * rt))
        ee = tiles(jnp.exp(-rt))
        ce = tiles(cf) * ee
        zero = jnp.zeros((n // T, SUB, T), f32)
        dh, ac, ar, ae = zero, zero, zero, zero
        for b in range(rows - 1, -1, -1):
            w = slice(b * SUB, (b + 1) * SUB)
            h = hs[sub, :, w, :]
            e = e0[:, w, :]
            kf = fade * sm[0, b].astype(f32)
            ar = ar + dh * (kf * (float(T) * h) + s1[:, w, :])
            ae = ae + h * e1[:, w, :]
            ac = ac + h * e
            s1[:, w, :] = dh
            dh = ce * e + kf * dh
        for c in range(SUB):
            far = far_part(take(s1, c, rows), pt[c], rows)
            near[c] = near[c] + tail.astype(f32) * far
        dva = mm(near[...].reshape(SUB * rows, T).astype(bf16), flip)
        for c in range(SUB):
            xs[pl.ds(lo + c, rows, stride=GROUP), :] = dva[c * rows : (c + 1) * rows]
        cut = (lo, lo + SUB)
        dcoef = nr[0:SUB, :] + untile(ee * ac)
        drate = -(cf * nr[SUB : 2 * SUB, :] + untile(ar + ce * ae))
        lanes = rates.shape[-1]
        for row in range(n // lanes):
            at = slice(row * lanes, (row + 1) * lanes)
            rates[row % 2, row // 2, 0, cut[0] : cut[1], :] = drate[:, at]
            rates[row % 2, row // 2, 1, cut[0] : cut[1], :] = dcoef[:, at]
    dv[...] = xs[...].reshape(rows, GROUP, T).astype(bf16)


def mask_kernel(st, sm, ins, insj, head, tailj, *, blocks):
    rows = st.shape[0]
    s = st[...]
    tri = (iota((T, T), 0) <= iota((T, T), 1)).astype(f32).astype(bf16)
    first = s[:, 0:1]
    seg = mm(s.astype(f32).astype(bf16), tri) - first.astype(f32)
    last = seg[:, T - 1 : T]
    cont = (first == 0) & (iota((rows, 1), 0) % blocks != 0)
    back = mm(seg.astype(bf16), flip_matrix())
    ins[...] = seg.astype(jnp.int32)
    insj[...] = back.astype(jnp.int32)
    head[...] = jnp.where((seg == 0) & cont, 1.0, 0.0)
    tailj[...] = jnp.where(back == last, 1.0, 0.0).astype(bf16)
    keep = jnp.where(cont & (last == 0), 1, 0)
    place = iota((rows, T), 0) == iota((rows, T), 1)
    keep = jnp.sum(jnp.where(place, keep, 0), axis=0, keepdims=True)
    most = jnp.max(jnp.broadcast_to(last.astype(jnp.int32), (rows, T)), axis=0, keepdims=True)
    row = iota((8, T), 0)
    sm[...] = jnp.where(row == 0, keep, jnp.where(row == 1, most // SEG + 1, 0))


def ssm_masks(starts):
    seqs, length = starts.shape
    blocks = length // T
    rows = seqs * blocks
    shape = (rows, T)
    kinds = (jnp.int32, jnp.int32, f32, bf16)
    return pl.pallas_call(
        functools.partial(mask_kernel, blocks=blocks),
        out_shape=[jax.ShapeDtypeStruct((8, T), jnp.int32)]
        + [jax.ShapeDtypeStruct(shape, kind) for kind in kinds],
        name="masks",
    )(starts.reshape(shape))


def ssm_specs(rows, n, first=0):
    full = pl.BlockSpec((rows, T), lambda i: (0, 0))
    return dict(
        sm=pl.BlockSpec(memory_space=pltpu.SMEM),
        full=full,
        ch=pl.BlockSpec((rows, GROUP, T), lambda i: (0, i + first, 0)),
        par=pl.BlockSpec((GROUP, n), lambda i: (i + first, 0)),
        hs=pl.BlockSpec((GROUP // SUB, n // T, rows * SUB, T), lambda i: (i + first, 0, 0, 0)),
        toe=pl.BlockSpec((GROUP, T, T), lambda i: (i + first, 0, 0)),
        big=pltpu.VMEM((n // T, rows * SUB, T), f32),
        pt=pltpu.VMEM((SUB, T, n), bf16),
        near=pltpu.VMEM((SUB, rows, T), f32),
        xs=pltpu.VMEM((rows * GROUP, T), f32),
        cost=pl.CostEstimate(flops=2 * 10**10, bytes_accessed=10**7, transcendentals=0),
    )


def ssm_fwd(x, rate, coef, masks):
    rows, chans, _ = x.shape
    n = rate.shape[1]
    s = ssm_specs(rows, n)
    return pl.pallas_call(
        fwd_kernel,
        grid=(chans // GROUP,),
        in_specs=[s["sm"], s["ch"], s["par"], s["par"]] + [s["full"]] * 4,
        out_specs=[s["ch"], s["hs"], s["toe"]],
        out_shape=[
            pltpu.HBM(x.shape, bf16),
            pltpu.HBM((chans // SUB, n // T, rows * SUB, T), f32),
            pltpu.HBM((chans, T, T), bf16),
        ],
        scratch_shapes=[s["pt"], s["big"], s["near"], s["xs"], pltpu.VMEM((SUB, T), f32)],
        compiler_params=pltpu.CompilerParams(vmem_limit_bytes=16 * 2**20),
        cost_estimate=s["cost"],
        name="ssm_fwd",
    )(masks[0], x, rate, coef, *masks[1:])


def ssm_bwd(x, dy, rate, coef, masks, hs, toe, row_n, part=0, parts=1, held=()):
    rows, chans, _ = x.shape
    n = rate.shape[1]
    steps = chans // GROUP // parts
    s = ssm_specs(rows, n, part * steps)
    raw = pl.BlockSpec(memory_space=pl.ANY)
    return pl.pallas_call(
        bwd_kernel,
        grid=(steps,),
        in_specs=[s["sm"], s["ch"], s["ch"], s["par"], s["par"]]
        + [s["full"]] * 4
        + [s["hs"], s["toe"]]
        + [raw] * len(held),
        out_specs=[
            s["ch"],
            pl.BlockSpec((2, row_n // 2, 2, GROUP, n // row_n), lambda i: (0, 0, 0, i + part * steps, 0)),
        ],
        out_shape=[
            pltpu.HBM(x.shape, bf16),
            jax.ShapeDtypeStruct((2, row_n // 2, 2, chans, n // row_n), f32),
        ],
        scratch_shapes=[
            s["pt"],
            s["big"],
            s["big"],
            s["big"],
            s["near"],
            pltpu.VMEM((SUB, T), f32),
            pltpu.VMEM((2 * SUB, n), f32),
            s["xs"],
            s["xs"],
        ],
        compiler_params=pltpu.CompilerParams(vmem_limit_bytes=16 * 2**20),
        cost_estimate=s["cost"],
        input_output_aliases={11 + i: i for i in range(len(held))},
        name="ssm_bwd",
    )(masks[0], x, dy, rate, coef, *masks[1:], *from_hbm(hs, toe), *held)


epsilon = 1e-05
TILE = 768
BLOCK_COLS = 256
NORM_STEPS = 2
TAIL_STEPS = 2


def gauss_cdf(a):
    return 0.5 * (1.0 + lax.erf(a * 0.7071067811865476))


def gauss_pdf(a):
    return jnp.exp(-0.5 * a * a) * 0.3989422804014327


def struct(shape, dtype):
    return jax.ShapeDtypeStruct(shape, dtype)


def in_hbm(shape, dtype):
    return pltpu.HBM(shape, dtype)


def from_hbm(*arrays):
    return tuple(pltpu.with_memory_space_constraint(a, pltpu.HBM) for a in arrays)


def whole(shape):
    return pl.BlockSpec(shape, lambda *_: (0,) * len(shape))


def call(kernel, name, grid, ins, outs, out_shape, args, scalars=None, scratch=(), aliases=None, vmem=24, cost=None):
    lead = [] if scalars is None else [scalars]
    return pl.pallas_call(
        kernel,
        grid_spec=pltpu.PrefetchScalarGridSpec(
            num_scalar_prefetch=len(lead),
            grid=grid,
            in_specs=ins,
            out_specs=outs,
            scratch_shapes=list(scratch),
        ),
        out_shape=out_shape,
        input_output_aliases=aliases or {},
        compiler_params=pltpu.CompilerParams(vmem_limit_bytes=vmem * 2**20),
        cost_estimate=cost and pl.CostEstimate(flops=cost, bytes_accessed=10**7, transcendentals=0),
        name=name,
    )(*lead, *args)


def normalise(x):
    centred = x - jnp.mean(x, axis=1, keepdims=True)
    inv_std = lax.rsqrt(jnp.mean(centred * centred, axis=1, keepdims=True) + epsilon)
    return centred * inv_std, inv_std


def norm_kernel(tok, gain, bias, w_val, normed, v_act, v_slope):
    x_hat, _ = normalise(tok[...].astype(f32))
    n = (x_hat * gain[...] + bias[...]).astype(bf16)
    normed[...] = n
    v = mm(n, w_val[...])
    cdf = gauss_cdf(v)
    act = (v * cdf).T.astype(bf16)
    slope = (cdf + v * gauss_pdf(v)).T
    shape = (v_act.shape[0], v_act.shape[2], T)
    for q in range(v_act.shape[1]):
        cut = slice(q * T, (q + 1) * T)
        v_act[:, q] = act[:, cut].reshape(shape)
        v_slope[:, q] = slope[:, cut].reshape(shape)


def norm_call(tokens, gain, bias, w_val, chan_n):
    own, width = tokens.shape
    inner = w_val.shape[1]
    quads = own // T
    spread = (chan_n, quads, inner // chan_n, T)
    steps = NORM_STEPS
    block = pl.BlockSpec((chan_n, quads // steps, inner // chan_n, T), lambda i: (0, i, 0, 0))
    rows = pl.BlockSpec((own // steps, width), lambda i: (i, 0))
    return call(
        norm_kernel,
        "norm_val",
        (steps,),
        [rows, whole((1, width)), whole((1, width)), whole(w_val.shape)],
        [rows, block, block],
        [struct((own, width), bf16), struct(spread, bf16), in_hbm(spread, f32)],
        from_hbm(tokens, gain[None], bias[None], w_val),
    )


def gate_tile(normed, grad, w_up, w_mix, w_down, u_act, d_slope, d_yproj):
    u = mm(normed, w_up[...])
    d = mm(grad, w_down[...], NT)
    cdf = gauss_cdf(u)
    act = u * cdf
    u_act[...] = act.astype(bf16)
    d_slope[...] = (d * (cdf + u * gauss_pdf(u))).astype(bf16)
    dyp = (d * act).astype(bf16)
    d_yproj[...] = dyp
    return mm(dyp, w_mix[...], NT)


def gate_first_kernel(
    core, n_own, n_oth, g_own, g_oth, w_up, w_mix, w_down,
    u_act, d_slope, d_yproj, na, ga, acc,
):
    own = n_own.shape[0]
    for h, (n, g) in enumerate(((n_own, g_own), (n_oth, g_oth))):
        na[h * own : (h + 1) * own, :] = n[...]
        ga[h * own : (h + 1) * own, :] = g[...]
    acc[...] = gate_tile(na[...], ga[...], w_up, w_mix, w_down, u_act, d_slope, d_yproj)


def gate_last_kernel(
    core, na, ga, acc, w_up, w_mix, w_down, _u, _s, _d,
    u_act, d_slope, d_yproj, normed_t, dy_own, dy_oth, sums,
):
    j = pl.program_id(0)
    own = na.shape[0] // 2

    @pl.when(j == 0)
    def _():
        sums[...] = acc[...]
        normed_t[...] = na[...].T

    sums[...] += gate_tile(na[...], ga[...], w_up, w_mix, w_down, u_act, d_slope, d_yproj)

    @pl.when(j == pl.num_programs(0) - 1)
    def _():
        shape = (dy_own.shape[0], dy_own.shape[2], T)
        for q in range(dy_own.shape[1]):
            dy_own[:, q] = sums[q * T : (q + 1) * T, :].T.reshape(shape)
            dy_oth[:, q] = sums[own + q * T : own + (q + 1) * T, :].T.astype(bf16).reshape(shape)


def gate_specs(own, w_mix, row_n, first):
    inner, ff = w_mix.shape
    part = ff // row_n
    col = lambda j, s: 2 * (j + first) + s[0]
    return [
        lambda width: pl.BlockSpec((width, part), lambda j, s: (0, col(j, s))),
        pl.BlockSpec((inner, part), lambda j, s: (0, col(j, s))),
        lambda width: pl.BlockSpec((part, width), lambda j, s: (col(j, s), 0)),
        pl.BlockSpec((2 * own, part), lambda j, s: (0, j + first)),
    ]


def gate_first(core, normed, normed_oth, grad, grad_oth, w_up, w_mix, w_down, row_n):
    own, width = normed.shape
    inner, ff = w_mix.shape
    up, mix, down, tile = gate_specs(own, w_mix, row_n, 0)
    tok = whole((own, width))
    pair = (2 * own, width)
    return call(
        gate_first_kernel,
        "gate_first",
        (1,),
        [tok, tok, tok, tok, up(width), mix, down(width)],
        [tile, tile, tile, whole(pair), whole(pair), whole((2 * own, inner))],
        [in_hbm((2 * own, ff // 2), bf16)] * 3
        + [in_hbm(pair, bf16), in_hbm(pair, bf16), in_hbm((2 * own, inner), f32)],
        from_hbm(normed, normed_oth, grad, grad_oth, w_up, w_mix, w_down),
        scalars=core,
        vmem=44,
    )


def gate_last(core, pair_normed, pair_grad, acc, w_up, w_mix, w_down, held, row_n, chan_n):
    own, width = pair_normed.shape[0] // 2, pair_normed.shape[1]
    inner, ff = w_mix.shape
    up, mix, down, tile = gate_specs(own, w_mix, row_n, 1)
    pair = (2 * own, width)
    raw = pl.BlockSpec(memory_space=pl.ANY)
    spread = (chan_n, own // T, inner // chan_n, T)
    return call(
        gate_last_kernel,
        "gate_last",
        (row_n // 2 - 1,),
        [whole(pair), whole(pair), whole(acc.shape), up(width), mix, down(width), raw, raw, raw],
        [tile, tile, tile, whole((width, 2 * own)), whole(spread), whole(spread)],
        [in_hbm((2 * own, ff // 2), bf16)] * 3
        + [in_hbm((width, 2 * own), bf16), in_hbm(spread, f32), in_hbm(spread, bf16)],
        from_hbm(pair_normed, pair_grad, acc, w_up, w_mix, w_down, *held),
        scalars=core,
        scratch=[pltpu.VMEM(acc.shape, f32)],
        aliases={7: 0, 8: 1, 9: 2},
        vmem=48,
    )


def mine_a(s):
    return jnp.where(s[0] == 0, s[1], s[2])


def mine_b(s):
    return jnp.where(s[0] == 0, s[2], s[1])


def row_block(s, a, b, core, high, low):
    x = jnp.where(s[0] == 0, a, b)
    y = jnp.where(s[0] == 0, b, a)
    return x * 16 + core * 8 + high * 4 + low * 2 + y


def mid_kernel(
    s, y_own, y_oth, w_mix, u_act, d_slope, d_yproj, normed_t,
    gate, d_upre, u_give, u_keep, m_give, m_keep, yt, yn, us, ms,
):
    inner = yt.shape[0]

    own = yn.shape[0] // 2

    @pl.when(pl.program_id(0) == 0)
    def _():
        for h, y in enumerate((y_own, y_oth)):
            for q in range(y.shape[1]):
                part = y[:, q].reshape(inner, T)
                at = slice(h * own + q * T, h * own + (q + 1) * T)
                yt[:, at] = part
                yn[at, :] = part.T

    yp = mm(yn[...], w_mix[...])
    gate[...] = (u_act[...].astype(f32) * yp).astype(bf16)
    du = (d_slope[...].astype(f32) * yp).astype(bf16)
    d_upre[...] = du
    us[...] = mm(normed_t[...], du).astype(bf16)
    ms[...] = mm(yt[...], d_yproj[...]).astype(bf16)
    m = u_give.shape[1]
    for sel, out in ((1, u_give), (0, u_keep)):
        a = mine_a(s) ^ sel
        for b in (0, 1):
            for low in (0, 1):
                for high in (0, 1):
                    for core in (0, 1):
                        at = pl.multiple_of(row_block(s, a, b, core, high, low) * m, m)
                        out[b * 8 + low * 4 + high * 2 + core] = us[pl.ds(at, m), :]
    m = m_give.shape[1]
    for sel, out in ((1, m_give), (0, m_keep)):
        low = s[3] ^ sel
        for high in (0, 1):
            for a in (0, 1):
                for b in (0, 1):
                    for core in (0, 1):
                        at = pl.multiple_of(row_block(s, a, b, core, high, low) * m, m)
                        out[high * 8 + a * 4 + b * 2 + core] = ms[pl.ds(at, m), :]


def mid_call(scal, y_own, y_oth, w_mix, u_act, d_slope, d_yproj, normed_t, row_n):
    inner, ff = w_mix.shape
    half = u_act.shape[1]
    own = u_act.shape[0] // 2
    width = normed_t.shape[0]
    per = ff // row_n // TILE
    col = lambda j, s: (2 * (j // per) + s[0]) * per + j % per
    tile = pl.BlockSpec((2 * own, TILE), lambda j, s: (0, j))
    um, mx = width // 32, inner // 32
    ub = pl.BlockSpec((16, um, TILE), lambda j, s: (0, 0, j))
    mb = pl.BlockSpec((16, mx, TILE), lambda j, s: (0, 0, j))
    return call(
        mid_kernel,
        "mix_up",
        (half // TILE,),
        [
            whole(y_own.shape),
            whole(y_own.shape),
            pl.BlockSpec((inner, TILE), lambda j, s: (0, col(j, s))),
            tile,
            tile,
            tile,
            whole(normed_t.shape),
        ],
        [tile, tile, ub, ub, mb, mb],
        [in_hbm((2 * own, half), bf16)] * 2
        + [in_hbm((16, um, half), bf16)] * 2
        + [in_hbm((16, mx, half), bf16)] * 2,
        (y_own, y_oth, *from_hbm(w_mix, u_act, d_slope, d_yproj, normed_t)),
        scalars=scal,
        scratch=[
            pltpu.VMEM((inner, 2 * own), bf16),
            pltpu.VMEM((2 * own, inner), bf16),
            pltpu.VMEM((width, TILE), bf16),
            pltpu.VMEM((inner, TILE), bf16),
        ],
        vmem=32,
        cost=10**10,
    )


def block_kernel(s, gate, d_upre, *refs):
    half = (len(refs) - 3) // 2
    downs, ups, (block_own, dn_own, oth) = refs[:half], refs[half : 2 * half], refs[2 * half :]
    own = block_own.shape[0]
    part = downs[0].shape[0]
    cut = lambda ref, k: ref[:, k * part : (k + 1) * part]
    block = sum(mm(cut(gate, k), w[...]) for k, w in enumerate(downs))
    dn = sum(mm(cut(d_upre, k), w[...], NT) for k, w in enumerate(ups))
    block_own[...] = block[:own]
    dn_own[...] = dn[:own]
    oth[0] = block[own:].astype(bf16)
    oth[1] = dn[own:].astype(bf16)


def block_call(scal, gate, d_upre, w_down, w_up, row_n):
    ff, width = w_down.shape
    own = gate.shape[0] // 2
    part = ff // row_n
    cols = BLOCK_COLS
    out = pl.BlockSpec((own, cols), lambda j, s: (0, j))
    ks = range(row_n // 2)
    return call(
        block_kernel,
        "block",
        (width // cols,),
        [whole(gate.shape), whole(d_upre.shape)]
        + [pl.BlockSpec((part, cols), lambda j, s, k=k: (2 * k + s[0], j)) for k in ks]
        + [pl.BlockSpec((cols, part), lambda j, s, k=k: (j, 2 * k + s[0])) for k in ks],
        [out, out, pl.BlockSpec((2, own, cols), lambda j, s: (0, 0, j))],
        [in_hbm((own, width), f32), in_hbm((own, width), f32), in_hbm((2, own, width), bf16)],
        from_hbm(gate, d_upre, *[w_down for _ in ks], *[w_up for _ in ks]),
        scalars=scal,
        vmem=36,
    )


def split_kernel(s, down_g, down_k, d_give, d_keep):
    for src, dst in ((down_g, d_give), (down_k, d_keep)):
        for low in (0, 1):
            for high in (0, 1):
                dst[low * 2 + high] = src[high * 2 + low]


def split_call(scal, down):
    rows, width = down.shape[0] // 16, down.shape[1]
    view = down.reshape(2, 4, 2, rows, width)

    def block_of(sel):
        def at(i, s):
            a = mine_a(s) ^ sel
            return jnp.where(s[0] == 0, a, i), 0, jnp.where(s[0] == 0, i, a), 0, 0

        return pl.BlockSpec((None, 4, None, rows, width), at)

    out = pl.BlockSpec((4, rows, width), lambda i, s: (i, 0, 0))
    return call(
        split_kernel,
        "split",
        (2,),
        [block_of(1), block_of(0)],
        [out, out],
        [struct((8, rows, width), bf16)] * 2,
        (view, view),
        scalars=scal,
    )


def val_kernel(s, v_own, v_oth, normed_t, v_give, v_keep, vs, vt):
    inner, pair = vt.shape
    for h, v in enumerate((v_own, v_oth)):
        for q in range(v.shape[1]):
            at = h * pair // 2 + q * T
            vt[:, at : at + T] = v[:, q].reshape(inner, T)
    vs[...] = mm(normed_t[...], vt[...], NT)
    m = vs.shape[0] // 32
    for sel, out in ((1, v_give), (0, v_keep)):
        a = mine_a(s) ^ sel
        for b in (0, 1):
            for low in (0, 1):
                for high in (0, 1):
                    cut = []
                    for core in (0, 1):
                        at = pl.multiple_of(row_block(s, a, b, core, high, low) * m, m)
                        cut.append(vs[pl.ds(at, m), :])
                    parts = [
                        jnp.concatenate([c[r * 8 : r * 8 + 8] for c in cut], 0)
                        for r in range(m // 8)
                    ]
                    out[b * 4 + low * 2 + high] = jnp.concatenate(parts, 1).astype(bf16)


def val_call(scal, d_vpre, v_oth, normed_t):
    half = v_oth.shape
    inner = half[0] * half[2]
    width, pair = normed_t.shape
    buf = (8, 16, width)
    return call(
        val_kernel,
        "val",
        (1,),
        [
            pl.BlockSpec(half, lambda i, s: (s[0], 0, 0, 0)),
            whole(half),
            whole(normed_t.shape),
        ],
        [whole(buf), whole(buf)],
        [struct(buf, bf16)] * 2,
        (d_vpre, v_oth, normed_t),
        scalars=scal,
        scratch=[pltpu.VMEM((width, inner), f32), pltpu.VMEM((inner, pair), bf16)],
    )


def step_kernel(bit, keep_g, got_g, keep_k, got_k, give, keep):
    give[...] = (keep_g[0].astype(f32) + got_g[0].astype(f32)).astype(bf16)
    keep[...] = (keep_k[0].astype(f32) + got_k[0].astype(f32)).astype(bf16)


def step_call(bit, keep, got):
    n, rows, cols = keep.shape
    n //= 2
    nb = max(1, n // 4)
    view = (2, n, rows, cols)
    other = pl.BlockSpec((1, nb, rows, cols), lambda i, b: (1 - b[0], i, 0, 0))
    same = pl.BlockSpec((1, nb, rows, cols), lambda i, b: (b[0], i, 0, 0))
    out = pl.BlockSpec((nb, rows, cols), lambda i, b: (i, 0, 0))
    keep, got = keep.reshape(view), got.reshape(view)
    return call(
        step_kernel,
        "halve",
        (n // nb,),
        [other, other, same, same],
        [out, out],
        [struct((n, rows, cols), bf16)] * 2,
        (keep, got, keep, got),
        scalars=bit,
    )


def tail_kernel(
    tok, grad, gain, block_own, got, dn_own, d_vpre, w_val, block_out, tokens_grad, norm_part, acc
):
    i = pl.program_id(0)
    x = tok[...].astype(f32)
    x_hat, inv_std = normalise(x)
    block_out[...] = (x + block_own[...] + got[0].astype(f32)).astype(bf16)
    dv = jnp.concatenate(
        [d_vpre[:, q].reshape(w_val.shape[1], T).T for q in range(d_vpre.shape[1])], 0
    )
    dn = dn_own[...] + got[1].astype(f32) + mm(dv, w_val[...], NT)
    dx = dn * gain[...]
    tokens_grad[...] = grad[...].astype(f32) + inv_std * (
        dx
        - jnp.mean(dx, axis=1, keepdims=True)
        - x_hat * jnp.mean(dx * x_hat, axis=1, keepdims=True)
    )
    sums = jnp.concatenate(
        [jnp.sum(dn * x_hat, axis=0, keepdims=True), jnp.sum(dn, axis=0, keepdims=True)], 0
    )

    @pl.when(i == 0)
    def _():
        acc[...] = sums

    @pl.when(i > 0)
    def _():
        acc[...] += sums

    @pl.when(i == pl.num_programs(0) - 1)
    def _():
        parts, lanes = norm_part.shape
        w = acc.shape[1] // parts
        for k in range(parts):
            cut = acc[:, k * w : (k + 1) * w]
            blank = jnp.zeros((1, lanes - 2 * w), f32)
            norm_part[k : k + 1, :] = jnp.concatenate([cut[0:1], cut[1:2], blank], 1)


def tail_call(tokens, grad, gain, block_own, got, dn_own, d_vpre, w_val, parts):
    own, width = tokens.shape
    steps = TAIL_STEPS
    rows = pl.BlockSpec((own // steps, width), lambda i: (i, 0))
    chan_n, quads, group, _ = d_vpre.shape
    return call(
        tail_kernel,
        "norm_back",
        (steps,),
        [
            rows,
            rows,
            whole((1, width)),
            rows,
            pl.BlockSpec((2, own // steps, width), lambda i: (0, i, 0)),
            rows,
            pl.BlockSpec((chan_n, quads // steps, group, T), lambda i: (0, i, 0, 0)),
            whole(w_val.shape),
        ],
        [rows, rows, whole((parts, T))],
        [struct((own, width), bf16), struct((own, width), f32), struct((parts, T), f32)],
        from_hbm(tokens, grad, gain[None], block_own, got, dn_own, d_vpre, w_val),
        scratch=[pltpu.VMEM((2, width), f32)],
        vmem=32,
    )


def finish_kernel(s, u_keep, u_got, m_keep, m_got, d_keep, d_got, v_keep, *rest):
    *v_gots, norm, down, mine, other = rest
    down[...] = d_keep[0].astype(f32) + d_got[0].astype(f32)
    v = sum([g[0].astype(f32) for g in v_gots], v_keep[0].astype(f32))
    half = v.shape[1]
    um, mx = u_keep.shape[1], m_keep.shape[1]
    tail = um + mx + 8
    for out, core, owner in ((mine, s[0], s[5]), (other, 1 - s[0], s[6])):
        out[0:um, :] = u_keep[core].astype(f32) + u_got[core].astype(f32)
        out[um : um + mx, :] = m_keep[core].astype(f32) + m_got[core].astype(f32)
        out[um + mx : tail, 0:half] = jnp.where(core == 0, v[:8], v[8:])
        out[um + mx : tail, half:] = jnp.zeros((8, out.shape[1] - half), f32)
        out[tail:, :] = jnp.zeros((8, out.shape[1]), f32)
        out[tail : tail + 1, 0:T] = norm[pl.ds(owner, 1), :]


def finish_call(scal, up, mix, down, val, norm):
    um, mx, half = up[0].shape[1], mix[0].shape[1], up[0].shape[2]
    rows, width = down[0].shape[1:]
    args = (*up, *mix, *down, *val, norm)
    pack = (um + mx + 16, half)
    return call(
        finish_kernel,
        "finish",
        (1,),
        [whole(a.shape) for a in args],
        [whole((rows, width)), whole(pack), whole(pack)],
        [struct((rows, width), f32), struct(pack, f32), struct(pack, f32)],
        args,
        scalars=scal,
    )


def join_kernel(s, mine, got, up, mix, val, norm):
    um, mx = up.shape[0], mix.shape[0]
    first = s[0] == 0
    part = mine.shape[1] // 2
    for core in (0, 1):
        held = jnp.where(first, mine[...], got[...]) if core == 0 else jnp.where(first, got[...], mine[...])
        for x in (0, 1):
            to = slice((2 * x + core) * part, (2 * x + core + 1) * part)
            up[:, to] = held[0:um, x * part : (x + 1) * part]
            mix[:, to] = held[um : um + mx, x * part : (x + 1) * part]
        w = val.shape[1] // 2
        for r in range(val.shape[0] // 8):
            at = slice(r * w, (r + 1) * w)
            val[r * 8 : r * 8 + 8, core * w : (core + 1) * w] = held[um + mx : um + mx + 8, at]
    norm[...] = mine[um + mx + 8 :, 0:T] + got[um + mx + 8 :, 0:T]


def join_call(scal, mine, got, um, mx, inner):
    ff = mine.shape[1] * 2
    return call(
        join_kernel,
        "join",
        (1,),
        [whole(mine.shape)] * 2,
        [whole((um, ff)), whole((mx, ff)), whole((um, inner)), whole((8, T))],
        [
            struct((um, ff), f32),
            struct((mx, ff), f32),
            struct((um, inner), f32),
            struct((8, T), f32),
        ],
        (mine, got),
        scalars=scal,
    )


def make_square(row_n, chan_n):
    def on_device(
        tokens, starts, layer_norm_gain, ln_bias, w_up, w_val, w_mix, w_down,
        decay_rate, mix_coef, out_grad,
    ):
        own, width = tokens.shape
        inner = w_val.shape[1]
        row, chan = lax.axis_index("row"), lax.axis_index("chan")
        core = row % 2
        me = row * chan_n + chan
        there = (row ^ 1) * chan_n + chan
        y_bit = chan % 2
        b_bit = jnp.where(core == 0, y_bit, row // 2)
        scal = jnp.stack([core, row // 2, y_bit, (chan // 2) % 2, chan // 4, me, there, b_bit])
        scal = scal.astype(jnp.int32)
        bit_x, bit_y = scal[1], scal[2]
        bit_a = jnp.where(core == 0, bit_x, bit_y).reshape(1)
        bit_b = jnp.where(core == 0, bit_y, bit_x).reshape(1)
        bit_low, bit_high = scal[3:4], scal[4:5]
        devices = [(r, c) for r in range(row_n) for c in range(chan_n)]
        flip_x = lambda r, c: (r ^ 2, c)
        flip_y = lambda r, c: (r, c ^ 1)
        moves = dict(
            core=lambda r, c: (r ^ 1, c),
            a=lambda r, c: flip_y(r, c) if r % 2 else flip_x(r, c),
            b=lambda r, c: flip_x(r, c) if r % 2 else flip_y(r, c),
            low=lambda r, c: (r, c ^ 2),
            high=lambda r, c: (r, c ^ 4),
            x=lambda r, c: (r ^ 2, c),
            ab=lambda r, c: (r ^ 2, c ^ 1),
            z=lambda r, c: (r, c ^ 6),
        )

        def send(value, way):
            to = [moves[way](r, c) for r, c in devices]
            pairs = [(r * chan_n + c, t[0] * chan_n + t[1]) for (r, c), t in zip(devices, to)]
            return lax.ppermute(value, ("row", "chan"), pairs)

        after = lax.optimization_barrier
        trade = lambda v: lax.all_to_all(v, "chan", split_axis=0, concat_axis=0, tiled=True)
        rows = own * chan_n // T
        to_seq = lambda v: v.reshape(rows, inner // chan_n, T)
        to_tok = lambda v: v.reshape(chan_n, own // T, inner // chan_n, T)

        masks = ssm_masks(starts)
        grad_oth = send(out_grad, "core")
        normed, v_act, v_slope = norm_call(tokens, layer_norm_gain, ln_bias, w_val, chan_n)
        normed_oth = send(normed, "core")
        v_chan = to_seq(trade(v_act))
        *gated, pair_normed, pair_grad, acc = gate_first(
            scal, normed, normed_oth, out_grad, grad_oth, w_up, w_mix, w_down, row_n
        )
        v_chan, acc = after((v_chan, acc))
        y_chan, states, toeplitz = ssm_fwd(v_chan, decay_rate, mix_coef, masks)
        y_chan, acc = after((y_chan, acc))
        y_own = trade(to_tok(y_chan))
        u_act, d_slope, d_yproj, normed_t, dy_own, dy_oth = gate_last(
            scal, pair_normed, pair_grad, acc, w_up, w_mix, w_down, gated, row_n, chan_n
        )
        d_y = (dy_own + send(dy_oth, "core").astype(f32)).astype(bf16)
        y_own, d_y = after((y_own, d_y))
        y_oth = send(y_own, "core")
        d_y_chan = to_seq(trade(d_y))
        gate_out, d_upre, u_give, u_keep, m_give, m_keep = mid_call(
            scal, y_own, y_oth, w_mix, u_act, d_slope, d_yproj, normed_t, row_n
        )
        u_give, m_give, gate_out, d_y_chan = after((u_give, m_give, gate_out, d_y_chan))
        back = lambda part, held, d_y_chan: ssm_bwd(
            v_chan, d_y_chan, decay_rate, mix_coef, masks, states, toeplitz, row_n, part, 2, held
        )

        u_got = send(u_give, "a")
        m_got = send(m_give, "low")
        down = mm(gate_out, pair_grad, TN).astype(bf16)
        d_give, d_keep = split_call(scal, down)
        held = back(0, (), d_y_chan)
        u_got, m_got, d_give, gate_out, d_y_chan, *held = after(
            (u_got, m_got, d_give, gate_out, d_y_chan, *held)
        )

        d_got = send(d_give, "a")
        m_give, m_keep = step_call(bit_high, m_keep, m_got)
        m_got = send(m_give, "high")
        d_v_chan, rates = back(1, tuple(held), d_y_chan)
        u_give, u_keep = step_call(bit_b, u_keep, u_got)
        d_v_chan, u_give, gate_out, rates = after((d_v_chan, u_give, gate_out, rates))
        d_v = trade(to_tok(d_v_chan))
        d_got, m_got, u_give = after((d_got, m_got, u_give))
        u_got = send(u_give, "b")
        block_own, dn_own, bd_give = block_call(scal, gate_out, d_upre, w_down, w_up, row_n)
        d_give, d_keep = step_call(bit_b, d_keep, d_got)
        rates_give = lax.dynamic_index_in_dim(rates, 1 - core, 0, keepdims=False)
        rates_got = send(rates_give, "core")
        u_got, d_give, bd_give, d_v, rates_got = after((u_got, d_give, bd_give, d_v, rates_got))

        d_got = send(d_give, "b")
        u_give, u_keep = step_call(bit_low, u_keep, u_got)
        u_give, d_v, m_got = after((u_give, d_v, m_got))
        u_got = send(u_give, "low")
        half = chan_n // 2
        other_half = lambda v: lax.dynamic_slice_in_dim(v, (1 - core) * half, half, 0)
        v_give = (other_half(d_v).astype(f32) * other_half(v_slope)).astype(bf16)
        v_got = send(v_give, "core")
        bd_got = send(bd_give, "core")
        d_vpre = (d_v.astype(f32) * v_slope).astype(bf16)
        v_give, v_keep = val_call(scal, d_vpre, v_got, normed_t)
        v_got = send(v_give, "a")
        v_give, d_vpre = after((v_give, d_vpre))
        block_out, tokens_grad, norm_part = tail_call(
            tokens, out_grad, layer_norm_gain, block_own, bd_got, dn_own, d_vpre, w_val,
            row_n * chan_n,
        )
        d_got, u_got, m_got, v_got, norm_part = after((d_got, u_got, m_got, v_got, norm_part))

        d_give, d_keep = step_call(bit_low, d_keep, d_got)
        d_got = send(d_give, "low")
        u_give, u_keep = step_call(bit_high, u_keep, u_got)
        u_give, norm_part, v_got = after((u_give, norm_part, v_got))
        u_got = send(u_give, "high")
        rates = lax.dynamic_index_in_dim(rates, core, 0, keepdims=False) + rates_got
        rates_give = lax.dynamic_index_in_dim(rates, 1 - bit_x, 0, keepdims=False)
        v_give, v_keep = step_call(bit_b, v_keep, v_got)
        v_got = send(v_give, "b")
        v_give, v_keep = step_call(bit_low, v_keep, v_got)
        v_got = send(v_give, "low")
        norm_part = norm_part + send(norm_part, "a")
        norm_part, m_got = after((norm_part, m_got))
        m_give, m_keep = step_call(bit_a, m_keep, m_got)
        m_got = send(m_give, "a")
        norm_part = norm_part + send(norm_part, "b")
        d_got, m_got, u_got, v_got, norm_part, rates_give = after(
            (d_got, m_got, u_got, v_got, norm_part, rates_give)
        )

        d_give, d_keep = step_call(bit_high, d_keep, d_got)
        d_give, norm_part, rates_give = after((d_give, norm_part, rates_give))
        d_got = send(d_give, "high")
        rates_got = send(rates_give, "x")
        m_give, m_keep = step_call(bit_b, m_keep, m_got)
        m_got = send(m_give, "b")
        v_give, v_keep = step_call(bit_high, v_keep, v_got)
        v_got = send(v_give, "high")
        norm_part = norm_part + send(norm_part, "low")
        norm_part = norm_part + send(norm_part, "high")
        d_got, m_got, norm_part, v_got, rates_got = after(
            (d_got, m_got, norm_part, v_got, rates_got)
        )
        rates = lax.dynamic_index_in_dim(rates, bit_x, 0, keepdims=False) + rates_got

        down_grad, mine, other = finish_call(
            scal, (u_keep, u_got), (m_keep, m_got), (d_keep, d_got), (v_keep, v_got), norm_part
        )
        um, mx = u_keep.shape[1], m_keep.shape[1]
        other = send(other, "core")
        up_grad, mix_grad, val_grad, norm_sum = join_call(scal, mine, other, um, mx, inner)
        norm_sum = norm_sum[0]
        w = width // (row_n * chan_n)
        return (
            block_out,
            tokens_grad,
            norm_sum[:w],
            norm_sum[w : 2 * w],
            up_grad,
            val_grad,
            mix_grad,
            down_grad,
            rates[0],
            rates[1],
        )

    return on_device


def make_general(row_n, chan_n):
    row_hi = row_n // 2

    def swap(value, axis, bit):
        size = row_n if axis == "row" else chan_n
        return lax.ppermute(value, axis, [(i, i ^ (1 << bit)) for i in range(size)])

    def core_swap(value):
        return swap(value, "row", 0)

    def bits_of(size):
        return size.bit_length() - 1

    def scatter_sum(part, names, order, last_dtype):
        names = list(names)
        for step, name in enumerate(order):
            axis, bit = name
            dim = names.index(name)
            mine = (lax.axis_index(axis) >> bit) & 1
            keep = lax.dynamic_index_in_dim(part, mine, dim, keepdims=False)
            give = lax.dynamic_index_in_dim(part, 1 - mine, dim, keepdims=False)
            got = swap(give, axis, bit)
            part = keep.astype(jnp.float32) + got.astype(jnp.float32)
            if step < len(order) - 1:
                part = part.astype(give.dtype)
            else:
                part = part.astype(last_dtype)
            names.pop(dim)
        return part

    row_bits = [("row", k) for k in range(bits_of(row_n) - 1, 0, -1)]
    core_bit = ("row", 0)
    chan_bits = [("chan", k) for k in range(bits_of(chan_n) - 1, -1, -1)]
    near_y = chan_bits[2:]
    along_z = chan_bits[:2][::-1]

    def on_device(
        tokens,
        starts,
        layer_norm_gain,
        ln_bias,
        w_up,
        w_val,
        w_mix,
        w_down,
        decay_rate,
        mix_coef,
        out_grad,
    ):
        own, width = tokens.shape
        ff = w_up.shape[1]
        inner = w_val.shape[1]
        part_ff = ff // row_n
        core = lax.axis_index("row") % 2
        mm = lambda a, b, ca, cb: lax.dot_general(
            a, b, (((ca,), (cb,)), ((), ())), preferred_element_type=jnp.float32
        )
        masks = ssm_masks(starts)
        inputs_f = tokens.astype(jnp.float32)
        row_mean = jnp.mean(inputs_f, axis=1, keepdims=True)
        centred = inputs_f - row_mean
        inv_std = lax.rsqrt(jnp.mean(centred * centred, axis=1, keepdims=True) + epsilon)
        x_hat = centred * inv_std
        normed = (x_hat * layer_norm_gain + ln_bias).astype(jnp.bfloat16)
        v_pre = mm(w_val, normed, 0, 1)
        v_cdf = gauss_cdf(v_pre)
        v_act = (v_pre * v_cdf).astype(jnp.bfloat16)
        v_slope = v_cdf + v_pre * gauss_pdf(v_pre)
        v_chan = lax.all_to_all(
            v_act.reshape(inner, own // T, T), "chan", split_axis=0, concat_axis=1, tiled=True
        )
        v_chan = jnp.swapaxes(v_chan, 0, 1)
        pair_normed = jnp.concatenate([normed, core_swap(normed)], 0)
        pair_grad = jnp.concatenate([out_grad, core_swap(out_grad)], 0)
        halves = lambda w, d: lax.dynamic_index_in_dim(
            w.reshape(w.shape[:d] + (row_hi, 2, part_ff) + w.shape[d + 1 :]), core, d + 1, keepdims=False
        ).reshape(w.shape[:d] + (ff // 2,) + w.shape[d + 1 :])
        up_half = halves(w_up, 1)
        mix_half = halves(w_mix, 1)
        down_half = halves(w_down, 0)
        u_pre = mm(pair_normed, up_half, 1, 0)
        d_gate = mm(pair_grad, down_half, 1, 1)
        u_cdf = gauss_cdf(u_pre)
        u_act = u_pre * u_cdf
        d_yproj = (d_gate * u_act).astype(jnp.bfloat16)
        d_slope = d_gate * (u_cdf + u_pre * gauss_pdf(u_pre))
        d_y_part = mm(mix_half, d_yproj, 1, 1)
        d_y = (
            d_y_part[:, :own] + core_swap(d_y_part[:, own:].astype(jnp.bfloat16)).astype(jnp.float32)
        ).astype(jnp.bfloat16)
        d_y_chan = lax.all_to_all(
            d_y.reshape(inner, own // T, T), "chan", split_axis=0, concat_axis=1, tiled=True
        )
        d_y_chan = jnp.swapaxes(d_y_chan, 0, 1)
        y_chan, states, toeplitz = ssm_fwd(v_chan, decay_rate, mix_coef, masks)
        y_chan = jnp.swapaxes(y_chan, 0, 1)
        y_own = lax.all_to_all(y_chan, "chan", split_axis=1, concat_axis=0, tiled=True)
        y_own = y_own.reshape(inner, own)
        d_v_chan, rates = ssm_bwd(
            v_chan, d_y_chan, decay_rate, mix_coef, masks, states, toeplitz, row_n
        )
        d_v_chan = jnp.swapaxes(d_v_chan, 0, 1)
        d_v = lax.all_to_all(d_v_chan, "chan", split_axis=1, concat_axis=0, tiled=True)
        pair_y = jnp.concatenate([y_own, core_swap(y_own)], 1)
        split_rows = lambda a, lead: a.reshape((2,) * lead + (-1,) + a.shape[1:])
        y_proj = mm(pair_y, mix_half, 0, 0)
        gate_out = (u_act * y_proj).astype(jnp.bfloat16)
        d_upre = (d_slope * y_proj).astype(jnp.bfloat16)
        mix_part = mm(pair_y, d_yproj, 1, 0).astype(jnp.bfloat16)
        down_part = mm(gate_out, pair_grad, 0, 0).astype(jnp.bfloat16)
        up_part = mm(pair_normed, d_upre, 0, 0).astype(jnp.bfloat16)
        all_names = row_bits + [core_bit] + chan_bits
        no_core = row_bits + chan_bits
        lead = len(all_names)
        mix_sum = scatter_sum(
            split_rows(mix_part, lead), all_names, along_z + row_bits + near_y, jnp.float32
        )
        up_sum = scatter_sum(
            split_rows(up_part, lead), all_names, row_bits + near_y + along_z, jnp.float32
        )
        down_grad = scatter_sum(
            split_rows(down_part, lead - 1), no_core, near_y + row_bits + along_z, jnp.float32
        )

        def join_cores(halfsum):
            mine = lax.dynamic_index_in_dim(halfsum, core, 0, keepdims=False)
            other = core_swap(lax.dynamic_index_in_dim(halfsum, 1 - core, 0, keepdims=False))
            shape = (mine.shape[0], row_hi, part_ff)
            low = jnp.where(core == 0, mine, other).reshape(shape)
            high = jnp.where(core == 0, other, mine).reshape(shape)
            return jnp.stack([low, high], 2).reshape(mine.shape[0], ff)

        block_part = mm(gate_out, down_half, 1, 0)
        block_out = (
            inputs_f
            + block_part[:own]
            + core_swap(block_part[own:].astype(jnp.bfloat16)).astype(jnp.float32)
        ).astype(jnp.bfloat16)
        d_normed_part = mm(d_upre, up_half, 1, 1)
        d_normed_got = core_swap(d_normed_part[own:].astype(jnp.bfloat16)).astype(jnp.float32)
        d_vpre = (d_v.reshape(inner, own).astype(jnp.float32) * v_slope).astype(jnp.bfloat16)
        val_part = mm(normed, d_vpre, 0, 1).astype(jnp.bfloat16)
        val_grad = scatter_sum(
            split_rows(val_part, lead),
            all_names,
            [core_bit] + along_z + near_y + row_bits,
            jnp.float32,
        )
        d_normed = d_normed_part[:own] + d_normed_got + mm(d_vpre, w_val, 0, 1)
        norm_part = jnp.stack([jnp.sum(d_normed * x_hat, axis=0), jnp.sum(d_normed, axis=0)], 1)
        norm_sum = scatter_sum(
            split_rows(norm_part, lead), all_names, [core_bit] + row_bits + chan_bits, jnp.float32
        )
        d_xh = d_normed * layer_norm_gain
        tokens_grad = out_grad.astype(jnp.float32) + inv_std * (
            d_xh
            - jnp.mean(d_xh, axis=1, keepdims=True)
            - x_hat * jnp.mean(d_xh * x_hat, axis=1, keepdims=True)
        )
        row_all = [core_bit] + row_bits
        chans, lanes = rates.shape[-2:]
        rates = rates.reshape((2,) * len(row_all) + (2 * chans, lanes))
        rates = scatter_sum(rates, row_all, row_all, jnp.float32).reshape(2, chans, lanes)
        return (
            block_out,
            tokens_grad,
            norm_sum[:, 0],
            norm_sum[:, 1],
            join_cores(up_sum),
            val_grad,
            join_cores(mix_sum),
            down_grad,
            rates[0],
            rates[1],
        )

    return on_device


def solution(mesh):
    spread = P(("row", "chan"), None)
    row_n, chan_n = mesh.shape["row"], mesh.shape["chan"]
    make = make_square if (row_n, chan_n) == (4, 8) else make_general
    return jax.shard_map(
        make(row_n, chan_n),
        mesh=mesh,
        in_specs=(
            spread,
            P("row", None),
            P(),
            P(),
            P(),
            P(),
            P(),
            P(),
            P("chan", None),
            P("chan", None),
            spread,
        ),
        out_specs=(
            spread,
            spread,
            P(("row", "chan")),
            P(("row", "chan")),
            spread,
            spread,
            spread,
            spread,
            P("chan", "row"),
            P("chan", "row"),
        ),
        check_vma=False,
    )
```
